32 devices in a mesh: head: 2 (over y), blk: 16 (over z, x, core).
Axes of the slice: x: 2, y: 2, z: 4, core: 2. Of those that a mesh axis runs over, the one named last changes fastest.
Arguments:
- hidden_in: bfloat16 [1, 16, 256, 768], P(None, 'blk', 'head'), may hold values from -6 to 6
- encoded: bfloat16 [1, 1024, 768], P(None, ('head', 'blk')), may hold values from -6 to 6
- out_grad: bfloat16 [1, 16, 256, 768], P(None, 'blk', 'head'), may hold values from -6 to 6
- ln_gain: bfloat16 [3, 768], P(None, ('head', 'blk')), may hold values from 0.099609375 to 1.8984375
- ln_bias: bfloat16 [3, 768], P(None, ('head', 'blk')), may hold values from -1 to 1
- biases: bfloat16 [7, 768], P(None, ('head', 'blk')), may hold values from -1 to 1
- self_qkv: bfloat16 [768, 2304], P(('head', 'blk')), may hold values from -0.21875 to 0.21875
- self_out: bfloat16 [768, 768], P(('head', 'blk')), may hold values from -1.25 to 1.25
- cross_q: bfloat16 [768, 768], P(('head', 'blk')), may hold values from -0.21875 to 0.21875
- cross_kv: bfloat16 [768, 1536], P(('head', 'blk')), may hold values from -0.21875 to 0.21875
- cross_out: bfloat16 [768, 768], P(('head', 'blk')), may hold values from -3 to 3
- ffn_in: bfloat16 [768, 3072], P(('head', 'blk')), may hold values from -0.21875 to 0.21875
- ffn_bias: bfloat16 [3072], P(('head', 'blk')), may hold values from -1 to 1
- ffn_out: bfloat16 [3072, 768], P(('head', 'blk')), may hold values from -0.109375 to 0.109375
Outputs:
- hidden_out: bfloat16 [1, 16, 256, 768], P(None, 'blk', 'head')
- hidden_grad: float32 [1, 16, 256, 768], P(None, 'blk', 'head')
- encoded_grad: float32 [1, 1024, 768], P(None, ('head', 'blk'))
- ln_gain_grad: float32 [3, 768], P(None, ('head', 'blk'))
- ln_bias_grad: float32 [3, 768], P(None, ('head', 'blk'))
- biases_grad: float32 [7, 768], P(None, ('head', 'blk'))
- self_qkv_grad: float32 [768, 2304], P(('head', 'blk'))
- self_out_grad: float32 [768, 768], P(('head', 'blk'))
- cross_q_grad: float32 [768, 768], P(('head', 'blk'))
- cross_kv_grad: float32 [768, 1536], P(('head', 'blk'))
- cross_out_grad: float32 [768, 768], P(('head', 'blk'))
- ffn_in_grad: float32 [768, 3072], P(('head', 'blk'))
- ffn_bias_grad: float32 [3072], P(('head', 'blk'))
- ffn_out_grad: float32 [3072, 768], P(('head', 'blk'))
The draws below stay inside these ranges and needn't reach their ends.
All inputs are finite; a program needn't handle non-finite values.
Results may differ from the reference program's by a relative error of at most 0.03.
Values may be sent and summed in bfloat16 or wider, within the bound.
A program may use at most 192 MiB of HBM per device.

```python
import jax
import jax.numpy as jnp
from jax import lax

D = 768
HEADS = 12
HEAD_DIM = 64
FF = 3072
ENC = 1024
SEQS = 1
SPAN = 256
N_BLK = 16


def steps_of(own_key, shape, shards, low, largest):
    def one(position, shards_of):
        steps = jax.random.uniform(jax.random.fold_in(jax.random.fold_in(own_key, 6), position), (shards_of,), jnp.float32, low / len(shards), largest / len(shards))
        return jnp.repeat(jnp.exp(steps), shape[position] // shards_of).reshape((-1,) + (1,) * (len(shape) - position - 1))

    level = one(*shards[0])
    for cut in shards[1:]:
        level = level * one(*cut)
    return level


def noise(stream_key, extent, deviation, reach, cuts=(), kind=jnp.bfloat16):
    result = jax.random.normal(stream_key, extent, jnp.float32) * deviation
    if len(cuts) > 0:
        result = steps_of(stream_key, extent, cuts, -0.22, 0.18) * result
    return jnp.clip(result, min=-reach, max=reach).astype(kind)


def setup_inputs(seed: int = 0) -> dict:
    streams_of = jax.random.split(jax.random.key(seed), 15)
    hidden_in = noise(streams_of[0], (SEQS, N_BLK, SPAN, D), 1.0, 6.0, ((1, 16), (2, 2)))
    encoded = noise(streams_of[1], (SEQS, ENC, D), 1.0, 6.0, ((1, 32),))
    out_grad = noise(streams_of[2], (SEQS, N_BLK, SPAN, D), 1.0, 6.0, ((1, 16), (2, 2)))
    ln_gain = jnp.clip(1.0 + 0.18 * jax.random.normal(streams_of[3], (3, D), jnp.float32), 0.099609375, 1.8984375).astype(jnp.bfloat16)
    ln_bias = noise(streams_of[4], (3, D), 0.2, 1.0, ((1, 32),))
    biases = noise(streams_of[5], (7, D), 0.2, 1.0, ((1, 32),))
    self_qkv = noise(streams_of[6], (D, 3 * D), D ** -0.5, 0.21875, ((0, 32),))
    self_out = noise(streams_of[7], (D, D), (D // 32) ** -0.5, 1.25, ((0, 32),))
    cross_q = noise(streams_of[8], (D, D), D ** -0.5, 0.21875, ((0, 32),))
    cross_kv = noise(streams_of[9], (D, 2 * D), D ** -0.5, 0.21875, ((0, 32),))
    cross_out = noise(streams_of[10], (D, D), 4 ** -0.5, 3.0, ((0, 32),))
    ffn_in = noise(streams_of[11], (D, FF), D ** -0.5, 0.21875, ((0, 32),))
    ffn_bias = noise(streams_of[12], (FF,), 0.2, 1.0, ((0, 32),))
    ffn_out = noise(streams_of[13], (FF, D), FF ** -0.5, 0.109375, ((0, 32),))
    return {"hidden_in": hidden_in, "encoded": encoded, "out_grad": out_grad, "ln_gain": ln_gain, "ln_bias": ln_bias, "biases": biases, "self_qkv": self_qkv, "self_out": self_out, "cross_q": cross_q, "cross_kv": cross_kv, "cross_out": cross_out, "ffn_in": ffn_in, "ffn_bias": ffn_bias, "ffn_out": ffn_out}


PRECISE = lax.Precision.HIGHEST
EPSILON = 1e-05
SCORE_SCALE = 0.125

@jax.custom_vjp
def low(v):
    return lax.optimization_barrier(v.astype(jnp.bfloat16)).astype(jnp.float32)

@jax.custom_vjp
def low_back(v):
    return v

def low_keep(v):
    return (low(v), None)

def low_pass(kept, grad):
    return (grad,)

def back_keep(v):
    return (v, None)

def back_low(kept, grad):
    return (low(grad),)
low.defvjp(low_keep, low_pass)
low_back.defvjp(back_keep, back_low)

def both_ways(values):
    return low_back(low(values))

def layer_norm(values, gain_row, shift_row):
    centered = values - lax.optimization_barrier(jnp.mean(values, axis=-1, keepdims=True))
    spread = lax.optimization_barrier(jnp.mean(centered * centered, axis=-1, keepdims=True))
    return centered * lax.rsqrt(spread + EPSILON) * gain_row + shift_row

def product(left, right):
    return jnp.dot(left, right, precision=PRECISE, preferred_element_type=jnp.float32)

def split_heads(values):
    return values.reshape(values.shape[0], HEADS, HEAD_DIM)

def attention(queries, key_rows, value_rows, reach_ahead):
    length = queries.shape[0]
    block_rows = min(512, length)
    key_place = jnp.arange(key_rows.shape[0], dtype=jnp.int32)

    @jax.checkpoint
    def one_block(block_start):
        local_rows = lax.dynamic_slice_in_dim(queries, block_start, block_rows, 0)
        scores = jnp.einsum('qhd,khd->hqk', local_rows, key_rows, precision=PRECISE) * SCORE_SCALE
        scores = low_back(scores)
        query_place = block_start + jnp.arange(block_rows, dtype=jnp.int32)
        allowed = key_place[None, None, :] <= query_place[None, :, None] + reach_ahead
        scores = jnp.where(allowed, scores, -jnp.inf)
        row_top = lax.optimization_barrier(jnp.max(scores, axis=-1, keepdims=True))
        weights = jnp.exp(scores - row_top)
        weights = weights / lax.optimization_barrier(jnp.sum(weights, axis=-1, keepdims=True))
        return jnp.einsum('hqk,khd->qhd', low(weights), value_rows, precision=PRECISE)
    starts = jnp.arange(length // block_rows, dtype=jnp.int32) * block_rows
    return lax.map(one_block, starts).reshape(length, HEADS * HEAD_DIM)

def one_sequence(hidden, encoder, params):
    gain_rows, shift_rows, bias_rows, qkv_weight, out_weight, query_weight, memory_weight, cross_weight, inner_weight, inner_bias, outer_weight = params
    model_width = hidden.shape[-1]
    normed = low(layer_norm(hidden, gain_rows[0], shift_rows[0]))
    mixed_qkv = product(normed, qkv_weight)
    queries = both_ways(mixed_qkv[:, :model_width] + bias_rows[0])
    key_rows = both_ways(mixed_qkv[:, model_width:2 * model_width])
    value_rows = both_ways(mixed_qkv[:, 2 * model_width:] + bias_rows[1])
    attended = both_ways(attention(split_heads(queries), split_heads(key_rows), split_heads(value_rows), 0))
    after_self = hidden + low_back(product(attended, out_weight) + bias_rows[2])
    cross_normed = low(layer_norm(after_self, gain_rows[1], shift_rows[1]))
    cross_queries = both_ways(product(cross_normed, query_weight) + bias_rows[3])
    memory_mixed = product(encoder, memory_weight)
    memory_keys = both_ways(memory_mixed[:, :model_width])
    memory_values = both_ways(memory_mixed[:, model_width:] + bias_rows[4])
    cross_attended = both_ways(attention(split_heads(cross_queries), split_heads(memory_keys), split_heads(memory_values), encoder.shape[0]))
    after_cross = after_self + low_back(product(cross_attended, cross_weight) + bias_rows[5])
    ffn_normed = low(layer_norm(after_cross, gain_rows[2], shift_rows[2]))
    inner_pre = low_back(product(ffn_normed, inner_weight) + inner_bias)
    inner_act = low(jax.nn.gelu(inner_pre, approximate=False))
    return after_cross + low_back(product(inner_act, outer_weight) + bias_rows[6])

def reference(hidden_in, encoded, out_grad, ln_gain, ln_bias, biases, self_qkv, self_out, cross_q, cross_kv, cross_out, ffn_in, ffn_bias, ffn_out):
    full_shape = hidden_in.shape
    hidden = hidden_in.reshape(full_shape[0], -1, full_shape[3]).astype(jnp.float32)
    encoder = encoded.astype(jnp.float32)
    upstream = out_grad.reshape(hidden.shape).astype(jnp.float32)
    params = tuple((weight_array.astype(jnp.float32) for weight_array in (ln_gain, ln_bias, biases, self_qkv, self_out, cross_q, cross_kv, cross_out, ffn_in, ffn_bias, ffn_out)))

    def forward(hidden_all, encoder_all, param_set):

        def per_sequence(sequence_pair):
            return one_sequence(sequence_pair[0], sequence_pair[1], param_set)
        return lax.map(per_sequence, (hidden_all, encoder_all))
    output, pullback = jax.vjp(forward, hidden, encoder, params)
    hidden_grad, encoded_grad, param_grads = pullback(upstream)
    return (output.astype(jnp.bfloat16).reshape(full_shape), hidden_grad.reshape(full_shape), encoded_grad, param_grads[0], param_grads[1], param_grads[2], param_grads[3], param_grads[4], param_grads[5], param_grads[6], param_grads[7], param_grads[8], param_grads[9], param_grads[10])
```

```python
import jax
import jax.numpy as jnp
from jax import lax
from jax.experimental import pallas as pl
from jax.experimental.pallas import tpu as pltpu
from jax.sharding import PartitionSpec as P

HEADS = 12
HEAD_DIM = 64


EPSILON = 1e-05
SCORE_SCALE = 0.125


def from_behind(block, axis, distance):
    devices = range(lax.axis_size(axis))
    route = [((i - distance) % len(devices), i) for i in devices]
    return lax.ppermute(block, axis, route)


def layer_norm(values, gain_row, shift_row):
    centered = values - jnp.mean(values, axis=-1, keepdims=True)
    spread = jnp.mean(centered * centered, axis=-1, keepdims=True)
    return centered * lax.rsqrt(spread + EPSILON) * gain_row + shift_row


def norm_grads(values, gain_row, shift_row, upstream):
    result, pullback = jax.vjp(layer_norm, values, gain_row, shift_row)
    return pullback(upstream)


def exact_gelu(values):
    return jax.nn.gelu(values, approximate=False)


def project(left, right):
    return jnp.einsum("srk,kn->srn", left, right, preferred_element_type=jnp.float32)


def project_back(upstream, weight):
    return jnp.einsum("srn,kn->srk", upstream, weight, preferred_element_type=jnp.float32)


def weight_grad(left, upstream):
    return jnp.einsum("srk,srn->kn", left, upstream, preferred_element_type=jnp.float32)


def column_sum(upstream):
    return jnp.sum(upstream.astype(jnp.float32), axis=(0, 1))


def block_scores(queries, key_block, query_start, key_start):
    scores = (
        jnp.einsum("sqhd,skhd->shqk", queries, key_block, preferred_element_type=jnp.float32)
        * SCORE_SCALE
    )
    query_place = query_start + lax.iota(jnp.int32, queries.shape[1])
    key_place = key_start + lax.iota(jnp.int32, key_block.shape[1])
    allowed = key_place[None, :] <= query_place[:, None]
    return (scores, allowed)


def forward_block(carried, key_block, value_block, queries, query_start, key_start):
    row_top, row_total, weighted = carried
    scores, allowed = block_scores(queries, key_block, query_start, key_start)
    scores = jnp.where(allowed, scores, -jnp.inf)
    new_top = jnp.maximum(row_top, jnp.max(scores, axis=-1))
    weights = jnp.exp(scores - new_top[..., None])
    factor = jnp.exp(row_top - new_top)
    row_total = row_total * factor + jnp.sum(weights, axis=-1)
    addition = jnp.einsum(
        "shqk,skhd->sqhd",
        weights.astype(jnp.bfloat16),
        value_block,
        preferred_element_type=jnp.float32,
    )
    weighted = weighted * jnp.transpose(factor, (0, 2, 1))[..., None] + addition
    return (new_top, row_total, weighted)


def backward_block(
    queries, out_grads, log_total, row_delta, key_block, value_block, query_start, key_start
):
    scores, allowed = block_scores(queries, key_block, query_start, key_start)
    weights = jnp.where(allowed, jnp.exp(scores - log_total[..., None]), 0.0)
    value_grad = jnp.einsum(
        "shqk,sqhd->skhd",
        weights.astype(jnp.bfloat16),
        out_grads,
        preferred_element_type=jnp.float32,
    )
    prob_grad = jnp.einsum(
        "sqhd,skhd->shqk", out_grads, value_block, preferred_element_type=jnp.float32
    )
    score_grad = (weights * (prob_grad - row_delta[..., None])).astype(jnp.bfloat16)
    query_grad = jnp.einsum(
        "shqk,skhd->sqhd", score_grad, key_block, preferred_element_type=jnp.float32
    )
    key_grad = jnp.einsum(
        "shqk,sqhd->skhd", score_grad, queries, preferred_element_type=jnp.float32
    )
    return (query_grad, key_grad, value_grad)


def cross_forward(operands):
    queries, key_rows, value_rows = operands
    scores = (
        jnp.einsum("qhd,khd->hqk", queries, key_rows, preferred_element_type=jnp.float32)
        * SCORE_SCALE
    )
    row_top = jnp.max(scores, axis=-1, keepdims=True)
    weights = jnp.exp(scores - row_top)
    row_total = jnp.sum(weights, axis=-1, keepdims=True)
    weights_low = (weights / row_total).astype(jnp.bfloat16)
    attended = jnp.einsum(
        "hqk,khd->qhd", weights_low, value_rows, preferred_element_type=jnp.float32
    )
    return (attended, (row_top + jnp.log(row_total))[..., 0])


def cross_backward(operands):
    queries, key_rows, value_rows, log_total, out_grads = operands
    scores = (
        jnp.einsum("qhd,khd->hqk", queries, key_rows, preferred_element_type=jnp.float32)
        * SCORE_SCALE
    )
    weights = jnp.exp(scores - log_total[..., None])
    value_grad = jnp.einsum(
        "hqk,qhd->khd", weights.astype(jnp.bfloat16), out_grads, preferred_element_type=jnp.float32
    )
    prob_grad = jnp.einsum(
        "qhd,khd->hqk", out_grads, value_rows, preferred_element_type=jnp.float32
    )
    row_delta = jnp.sum(weights * prob_grad, axis=-1, keepdims=True)
    score_grad = (weights * (prob_grad - row_delta)).astype(jnp.bfloat16)
    query_grad = (
        jnp.einsum("hqk,khd->qhd", score_grad, key_rows, preferred_element_type=jnp.float32)
        * SCORE_SCALE
    )
    key_grad = (
        jnp.einsum("hqk,qhd->khd", score_grad, queries, preferred_element_type=jnp.float32)
        * SCORE_SCALE
    )
    return (query_grad, key_grad, value_grad)


def body(
    hidden_in,
    encoded,
    out_grad,
    ln_gain,
    ln_bias,
    biases,
    self_qkv,
    self_out,
    cross_q,
    cross_kv,
    cross_out,
    ffn_in,
    ffn_bias,
    ffn_out,
):
    seq_count = hidden_in.shape[0]
    row_count = hidden_in.shape[2]
    model_width = hidden_in.shape[3]
    groups = lax.axis_size("head")
    block_total = lax.axis_size("blk")
    span_rows = row_count * groups
    group_width = model_width // groups
    local_heads = HEADS // groups
    head_shape = (seq_count, span_rows, local_heads, HEAD_DIM)
    gathered = (
        lax.all_gather(ln_gain, ("head", "blk"), axis=1, tiled=True),
        lax.all_gather(ln_bias, ("head", "blk"), axis=1, tiled=True),
        lax.all_gather(biases, ("head", "blk"), axis=1, tiled=True),
        lax.all_gather(self_qkv, ("head", "blk"), axis=0, tiled=True),
        lax.all_gather(self_out, ("head", "blk"), axis=0, tiled=True),
        lax.all_gather(cross_q, ("head", "blk"), axis=0, tiled=True),
        lax.all_gather(cross_kv, ("head", "blk"), axis=0, tiled=True),
        lax.all_gather(cross_out, ("head", "blk"), axis=0, tiled=True),
        lax.all_gather(ffn_in, ("head", "blk"), axis=0, tiled=True),
        lax.all_gather(ffn_bias, ("head", "blk"), axis=0, tiled=True),
        lax.all_gather(ffn_out, ("head", "blk"), axis=0, tiled=True),
    )
    gain_rows = gathered[0].astype(jnp.float32)
    shift_rows = gathered[1].astype(jnp.float32)
    bias_rows = gathered[2].astype(jnp.float32)
    qkv_weight = gathered[3]
    out_weight = gathered[4]
    query_weight = gathered[5]
    memory_weight = gathered[6]
    cross_weight = gathered[7]
    inner_weight = gathered[8]
    inner_bias = gathered[9].astype(jnp.float32)
    outer_weight = gathered[10]
    hidden = hidden_in[:, 0].astype(jnp.float32)
    normed = layer_norm(hidden, gain_rows[0], shift_rows[0]).astype(jnp.bfloat16)
    mixed_qkv = project(normed, qkv_weight)
    mixed_qkv = mixed_qkv + jnp.concatenate(
        [bias_rows[0], jnp.zeros_like(bias_rows[0]), bias_rows[1]]
    )
    mixed_qkv = mixed_qkv.astype(jnp.bfloat16).reshape(seq_count, row_count, 3, groups, group_width)
    grouped = lax.all_to_all(mixed_qkv, "head", split_axis=3, concat_axis=1, tiled=True)
    self_queries = grouped[:, :, 0, 0].reshape(head_shape)
    self_keys = grouped[:, :, 1, 0]
    self_values = grouped[:, :, 2, 0]
    block_index = lax.axis_index("blk")
    own_start = block_index * span_rows
    stat_shape = (seq_count, local_heads, span_rows)
    initial = (
        jnp.full(stat_shape, -jnp.inf, jnp.float32),
        jnp.zeros(stat_shape, jnp.float32),
        jnp.zeros(head_shape, jnp.float32),
    )
    key_piece = lax.all_gather(self_keys, "blk", axis=1, tiled=True)
    value_piece = lax.all_gather(self_values, "blk", axis=1, tiled=True)
    piece_rows = key_piece.shape[1]
    block_count = piece_rows // span_rows
    layout = (seq_count, block_count, span_rows, local_heads, HEAD_DIM)
    key_blocks = jnp.moveaxis(key_piece.reshape(layout), 1, 0)
    value_blocks = jnp.moveaxis(value_piece.reshape(layout), 1, 0)
    block_starts = span_rows * lax.iota(jnp.int32, block_count)

    def visit(running, element):
        key_block, value_block, key_start = element

        def visit_compute(current):
            return forward_block(
                current, key_block, value_block, self_queries, own_start, key_start
            )

        def visit_unchanged(current):
            return current

        return (
            lax.cond(key_start < own_start + span_rows, visit_compute, visit_unchanged, running),
            None,
        )

    result, unused = lax.scan(visit, initial, (key_blocks, value_blocks, block_starts))
    running_top, running_total, running_sum = result
    log_total = running_top + jnp.log(running_total)
    attended = running_sum / jnp.transpose(running_total, (0, 2, 1))[..., None]
    attended_low = attended.astype(jnp.bfloat16).reshape(seq_count, span_rows, 1, group_width)
    self_mixed = lax.all_to_all(
        attended_low, "head", split_axis=1, concat_axis=2, tiled=True
    ).reshape(seq_count, row_count, model_width)
    after_self = hidden + project(self_mixed, out_weight) + bias_rows[2]
    cross_normed = layer_norm(after_self, gain_rows[1], shift_rows[1]).astype(jnp.bfloat16)
    cross_queries = (project(cross_normed, query_weight) + bias_rows[3]).astype(jnp.bfloat16)
    memory_mixed = project(encoded, memory_weight)
    memory_keys = memory_mixed[..., :model_width].astype(jnp.bfloat16)
    memory_values = (memory_mixed[..., model_width:] + bias_rows[4]).astype(jnp.bfloat16)
    all_keys, all_values = (
        lax.all_gather(memory_keys, ("head", "blk"), axis=1, tiled=True),
        lax.all_gather(memory_values, ("head", "blk"), axis=1, tiled=True),
    )
    query_heads = cross_queries.reshape(seq_count, row_count, HEADS, HEAD_DIM)
    key_heads = all_keys.reshape(seq_count, -1, HEADS, HEAD_DIM)
    value_heads = all_values.reshape(seq_count, -1, HEADS, HEAD_DIM)
    cross_result, cross_lse = lax.map(cross_forward, (query_heads, key_heads, value_heads))
    cross_mixed = cross_result.astype(jnp.bfloat16).reshape(seq_count, row_count, model_width)
    after_cross = after_self + project(cross_mixed, cross_weight) + bias_rows[5]
    ffn_normed = layer_norm(after_cross, gain_rows[2], shift_rows[2]).astype(jnp.bfloat16)
    inner_pre = project(ffn_normed, inner_weight) + inner_bias
    inner_act = exact_gelu(inner_pre).astype(jnp.bfloat16)
    output = after_cross + project(inner_act, outer_weight) + bias_rows[6]
    hidden_out = output.astype(jnp.bfloat16)[:, None]
    upstream = out_grad[:, 0].astype(jnp.float32)
    outer_low = upstream.astype(jnp.bfloat16)
    outer_weight_grad = weight_grad(inner_act, outer_low)
    act_grad = project_back(outer_low, outer_weight)
    unused_value, gelu_pull = jax.vjp(exact_gelu, inner_pre)
    pre_grad = gelu_pull(act_grad)[0].astype(jnp.bfloat16)
    inner_weight_grad = weight_grad(ffn_normed, pre_grad)
    inner_bias_grad = column_sum(pre_grad)
    back_cross, gain_grad_two, shift_grad_two = norm_grads(
        after_cross, gain_rows[2], shift_rows[2], project_back(pre_grad, inner_weight)
    )
    cross_total = upstream + back_cross
    cross_low = cross_total.astype(jnp.bfloat16)
    cross_weight_grad = weight_grad(cross_mixed, cross_low)
    cross_attn_grad = (
        project_back(cross_low, cross_weight)
        .astype(jnp.bfloat16)
        .reshape(seq_count, row_count, HEADS, HEAD_DIM)
    )
    cross_query_grads, cross_key_grads, cross_value_grads = lax.map(
        cross_backward, (query_heads, key_heads, value_heads, cross_lse, cross_attn_grad)
    )
    memory_key_grad, memory_value_grad = (
        lax.psum_scatter(
            cross_key_grads.reshape(seq_count, -1, model_width),
            ("head", "blk"),
            scatter_dimension=1,
            tiled=True,
        ),
        lax.psum_scatter(
            cross_value_grads.reshape(seq_count, -1, model_width),
            ("head", "blk"),
            scatter_dimension=1,
            tiled=True,
        ),
    )
    memory_key_low = memory_key_grad.astype(jnp.bfloat16)
    memory_value_low = memory_value_grad.astype(jnp.bfloat16)
    encoded_grad = project_back(memory_key_low, memory_weight[:, :model_width]) + project_back(
        memory_value_low, memory_weight[:, model_width:]
    )
    memory_weight_grad = weight_grad(
        encoded, jnp.concatenate([memory_key_low, memory_value_low], axis=-1)
    )
    cross_query_low = cross_query_grads.reshape(seq_count, row_count, model_width).astype(
        jnp.bfloat16
    )
    query_weight_grad = weight_grad(cross_normed, cross_query_low)
    back_self, gain_grad_one, shift_grad_one = norm_grads(
        after_self, gain_rows[1], shift_rows[1], project_back(cross_query_low, query_weight)
    )
    self_total = cross_total + back_self
    self_low = self_total.astype(jnp.bfloat16)
    out_weight_grad = weight_grad(self_mixed, self_low)
    attn_grad = (
        project_back(self_low, out_weight)
        .astype(jnp.bfloat16)
        .reshape(seq_count, row_count, groups, group_width)
    )
    grad_heads = lax.all_to_all(attn_grad, "head", split_axis=2, concat_axis=1, tiled=True).reshape(
        head_shape
    )
    row_delta = jnp.einsum("sqhd,sqhd->shq", grad_heads.astype(jnp.float32), attended)
    own_keys = self_keys.reshape(head_shape)
    own_values = self_values.reshape(head_shape)
    zero_grads = jnp.zeros(head_shape, jnp.float32)

    def key_turn(turn_index, carried):
        moving_keys, moving_values, moving_key_grads, moving_value_grads, query_grads = carried
        source = (block_index + turn_index) % block_total

        def key_compute(partial_grads):
            addition = backward_block(
                self_queries,
                grad_heads,
                log_total,
                row_delta,
                moving_keys,
                moving_values,
                own_start,
                source * span_rows,
            )
            return (
                partial_grads[0] + addition[0],
                partial_grads[1] + addition[1],
                partial_grads[2] + addition[2],
            )

        def key_unchanged(partial_grads):
            return partial_grads

        needed = (turn_index == 0) | (turn_index + block_index >= block_total)
        query_grads, moving_key_grads, moving_value_grads = lax.cond(
            needed, key_compute, key_unchanged, (query_grads, moving_key_grads, moving_value_grads)
        )
        moving_keys, moving_values = from_behind(
            (moving_keys, moving_values), "blk", block_total - 1
        )
        moving_key_grads, moving_value_grads = (
            from_behind(moving_key_grads.astype(jnp.bfloat16), "blk", block_total - 1).astype(
                moving_key_grads.dtype
            ),
            from_behind(moving_value_grads.astype(jnp.bfloat16), "blk", block_total - 1).astype(
                moving_value_grads.dtype
            ),
        )
        return (moving_keys, moving_values, moving_key_grads, moving_value_grads, query_grads)

    finished = lax.fori_loop(
        0, block_total, key_turn, (own_keys, own_values, zero_grads, zero_grads, zero_grads)
    )
    key_grads = finished[2]
    value_grads = finished[3]
    query_grads = finished[4]
    qkv_grads = jnp.stack([query_grads * SCORE_SCALE, key_grads * SCORE_SCALE, value_grads], axis=2)
    qkv_low = qkv_grads.astype(jnp.bfloat16).reshape(seq_count, span_rows, 3, 1, group_width)
    token_grads = lax.all_to_all(qkv_low, "head", split_axis=1, concat_axis=3, tiled=True).reshape(
        seq_count, row_count, 3 * model_width
    )
    qkv_weight_grad = weight_grad(normed, token_grads)
    back_input, gain_grad_zero, shift_grad_zero = norm_grads(
        hidden, gain_rows[0], shift_rows[0], project_back(token_grads, qkv_weight)
    )
    hidden_grad = (self_total + back_input)[:, None]
    bias_grad = jnp.stack(
        [
            column_sum(token_grads[..., :model_width]),
            column_sum(token_grads[..., 2 * model_width :]),
            column_sum(self_low),
            column_sum(cross_query_low),
            column_sum(memory_value_low),
            column_sum(cross_low),
            column_sum(outer_low),
        ]
    )
    gain_grad = jnp.stack([gain_grad_zero, gain_grad_one, gain_grad_two])
    shift_grad = jnp.stack([shift_grad_zero, shift_grad_one, shift_grad_two])
    reduced = (
        lax.psum_scatter(gain_grad, ("head", "blk"), scatter_dimension=1, tiled=True),
        lax.psum_scatter(shift_grad, ("head", "blk"), scatter_dimension=1, tiled=True),
        lax.psum_scatter(bias_grad, ("head", "blk"), scatter_dimension=1, tiled=True),
        lax.psum_scatter(qkv_weight_grad, ("head", "blk"), scatter_dimension=0, tiled=True),
        lax.psum_scatter(out_weight_grad, ("head", "blk"), scatter_dimension=0, tiled=True),
        lax.psum_scatter(query_weight_grad, ("head", "blk"), scatter_dimension=0, tiled=True),
        lax.psum_scatter(memory_weight_grad, ("head", "blk"), scatter_dimension=0, tiled=True),
        lax.psum_scatter(cross_weight_grad, ("head", "blk"), scatter_dimension=0, tiled=True),
        lax.psum_scatter(inner_weight_grad, ("head", "blk"), scatter_dimension=0, tiled=True),
        lax.psum_scatter(inner_bias_grad, ("head", "blk"), scatter_dimension=0, tiled=True),
        lax.psum_scatter(outer_weight_grad, ("head", "blk"), scatter_dimension=0, tiled=True),
    )
    return (
        hidden_out,
        hidden_grad,
        encoded_grad,
        reduced[0],
        reduced[1],
        reduced[2],
        reduced[3],
        reduced[4],
        reduced[5],
        reduced[6],
        reduced[7],
        reduced[8],
        reduced[9],
        reduced[10],
    )


MESH = pl.DeviceIdType.MESH
F32 = jnp.float32
BF = jnp.bfloat16
NZ, NX, NC, NH = 4, 2, 2, 2
PAIRS = 3
WIDE = 2 * HEAD_DIM


def place():
    h = lax.axis_index("head")
    b = lax.axis_index("blk")
    return h, b // 4, (b // 2) % 2, b % 2


def device_at(h, z, x, c):
    return (h, z * 4 + x * 2 + c)


def greet(h, z, x, c):
    barrier = pltpu.get_barrier_semaphore()
    others = [device_at(h, z, x, 1 - c), device_at(h, z, 1 - x, c), device_at(1 - h, z, x, c)]
    others += [device_at(h, (z + d) % NZ, x, c) for d in (1, 2, 3)]
    for other in others:
        pl.semaphore_signal(barrier, inc=1, device_id=other, device_id_type=MESH)
    pl.semaphore_wait(barrier, len(others))


def dot(a, b):
    return jnp.dot(a, b, preferred_element_type=F32)


def dot_nt(a, b):
    return lax.dot_general(a, b, (((1,), (1,)), ((), ())), preferred_element_type=F32)


def dot_tn(a, b):
    return lax.dot_general(a, b, (((0,), (0,)), ((), ())), preferred_element_type=F32)


def lane_half(shape):
    return lax.broadcasted_iota(jnp.int32, shape, len(shape) - 1) < HEAD_DIM


def stack_pair(values):
    first = lane_half(values.shape)
    zero = jnp.zeros_like(values)
    return jnp.concatenate([jnp.where(first, values, zero), jnp.where(first, zero, values)], axis=0)


def unstack_pair(stacked):
    rows = stacked.shape[0] // 2
    top, low = stacked[:rows], stacked[rows:]
    return jnp.where(lane_half(top.shape), top, low)


class Links:
    def __init__(self, send, recv):
        self.send_sems, self.recv_sems, self.count, self.open = send, recv, 0, []

    def slot(self):
        self.count += 1
        return self.count - 1

    def copy(self, source, target, k, device):
        return pltpu.make_async_remote_copy(
            source, target, self.send_sems.at[k], self.recv_sems.at[k],
            device_id=device, device_id_type=MESH,
        )

    def send(self, source, target, k, device):
        c = self.copy(source, target, k, device)
        c.start()
        self.open.append(c)

    def drain(self):
        for c in self.open:
            c.wait_send()
        self.open = []


def gather_stages(links, view, order, here):
    h, z, x, c = here
    every = slice(None)
    ks = [[links.slot() for _ in range(3)]] + [[links.slot()] for _ in range(len(order) + 1)]

    def z_start():
        for d, k in zip((1, 2, 3), ks[0]):
            links.send(view(h, z, x, c), view(h, z, x, c), k, device_at(h, (z + d) % NZ, x, c))

    def z_wait():
        for d, k in zip((1, 2, 3), ks[0]):
            got = view(h, (z - d) % NZ, x, c)
            links.copy(got, got, k, device_at(h, (z + d) % NZ, x, c)).wait_recv()

    known = {"h": h, "x": x}
    pieces = []
    for axis in order:
        sent = view(known["h"], every, known["x"], c)
        if axis == "x":
            device = device_at(h, z, 1 - x, c)
            got = view(known["h"], every, 1 - x, c)
            known["x"] = every
        else:
            device = device_at(1 - h, z, x, c)
            got = view(1 - h, every, known["x"], c)
            known["h"] = every
        pieces.append((sent, got, device))
    pieces.append((view(every, every, every, c), view(every, every, every, 1 - c), device_at(h, z, x, 1 - c)))

    def start(i):
        sent, got, device = pieces[i]
        links.send(sent, sent, ks[i + 1][0], device)

    def wait(i):
        sent, got, device = pieces[i]
        links.copy(got, got, ks[i + 1][0], device).wait_recv()

    stages = [z_start, lambda: (z_wait(), start(0))]
    for i in range(1, len(pieces)):
        stages.append(lambda i=i: (wait(i - 1), start(i)))
    return stages + [lambda: wait(len(pieces) - 1)]


def norm_stats(v):
    centered = v - jnp.mean(v, axis=-1, keepdims=True)
    inv = lax.rsqrt(jnp.mean(centered * centered, axis=-1, keepdims=True) + EPSILON)
    return centered * inv, inv


def first_kernel(
    hid, wq_in, wp_in, w2_in, enc_in, sm_in,
    wp, w2, en, wq, prm, fb, keys, vals, queries, a_span, o_wide, o_low, lse_out,
    xs, wq_all, sm_all, q2, m_ref, l_ref, acc, o_tmp, send, recv, local,
):
    here = place()
    h, z, x, c = here
    links = Links(send, recv)
    every = slice(None)
    span = 2 * hid.shape[0]
    group = 4 * span
    width = hid.shape[1]
    gw = PAIRS * WIDE

    own = [
        (hid, xs.at[z, x, c, h]), (sm_in, sm_all.at[h, z, x, c]), (wq_in.at[h], wq_all.at[h, z, x, c]),
        (wp_in, wp.at[h, z, x, c]), (w2_in, w2.at[h, z, x, c]), (enc_in, en.at[h, z, x, c]),
    ]
    own = [pltpu.make_async_copy(s, t, local.at[i]) for i, (s, t) in enumerate(own)]
    for cp in own:
        cp.start()
    greet(*here)
    core, xdev, ydev = device_at(h, z, x, 1 - c), device_at(h, z, 1 - x, c), device_at(1 - h, z, x, c)
    for cp in own:
        cp.wait()

    kx, ky = links.slot(), links.slot()
    kup, kdown = [links.slot() for _ in range(3)], [links.slot() for _ in range(3)]
    kcore = [links.slot() for _ in range(NZ)]

    kwy = links.slot()
    kwz = [links.slot() for _ in range(3)]
    kwx, kwc = links.slot(), links.slot()

    small = gather_stages(links, lambda *i: sm_all.at[i], ("x", "y"), here)

    mine = xs.at[z, x, c, h]
    links.send(mine, mine, kx, xdev)
    links.send(wq_in.at[1 - h], wq_all.at[h, z, x, c], kwy, ydev)
    small[0]()

    got = xs.at[z, 1 - x, c, h]
    links.copy(got, got, kx, xdev).wait_recv()
    mine = xs.at[z, every, c, h]
    links.send(mine, mine, ky, ydev)
    got = wq_all.at[1 - h, z, x, c]
    links.copy(got, got, kwy, ydev).wait_recv()
    mine = wq_all.at[every, z, x, c]
    for d, k in zip((1, 2, 3), kwz):
        links.send(mine, mine, k, device_at(h, (z + d) % NZ, x, c))
    small[1]()

    got = xs.at[z, every, c, 1 - h]
    links.copy(got, got, ky, ydev).wait_recv()
    up, down = device_at(h, (z + 1) % NZ, x, c), device_at(h, (z + NZ - 1) % NZ, x, c)

    def pass_on(t, direction):
        if direction > 0:
            piece = xs.at[(z - t) % NZ, every, c]
            return links.copy(piece, piece, kup[t], up), (z < NZ - 1) & (z - t >= 0)
        piece = xs.at[(z + t) % NZ, every, c]
        return links.copy(piece, piece, kdown[t], down), (z > 0) & (z + t < NZ)

    def hop_send(t):
        for direction in (1, -1):
            cp, cond = pass_on(t, direction)
            pl.when(cond)(cp.start)

    def hop_recv(t):
        piece = xs.at[(z - t) % NZ, every, c]
        pl.when(z - t >= 0)(links.copy(piece, piece, kup[t - 1], up).wait_recv)
        piece = xs.at[(z + t) % NZ, every, c]
        pl.when(z + t < NZ)(links.copy(piece, piece, kdown[t - 1], down).wait_recv)

    def core_slot(g):
        return kcore[0] + 1 + g - jnp.where(g > z, 1, 0)

    hop_send(0)
    piece = xs.at[z, every, c]
    links.send(piece, piece, kcore[0], core)
    small[2]()
    for d, k in zip((1, 2, 3), kwz):
        got = wq_all.at[every, (z - d) % NZ, x, c]
        links.copy(got, got, k, device_at(h, (z + d) % NZ, x, c)).wait_recv()
    mine = wq_all.at[every, every, x, c]
    links.send(mine, mine, kwx, xdev)

    def columns(buf, lo, n):
        return lambda *i: buf.at[i + (every, pl.ds(lo, n))]

    def rows(buf, lo, n):
        return lambda *i: buf.at[i + (pl.ds(lo, n), every)]

    ff_rows = w2_in.shape[0] // 2
    chunks = [
        (lambda *i: en.at[i], ("y", "x")),
        (columns(wp, 0, 2 * width), ("x", "y")),
        (columns(wp, 2 * width, 2 * width), ("y", "x")),
        (columns(wp, 4 * width, width), ("x", "y")),
        (columns(wp, 5 * width, 2 * width), ("y", "x")),
        (rows(w2, 0, ff_rows), ("x", "y")),
        (columns(wp, 7 * width, 2 * width), ("y", "x")),
        (rows(w2, ff_rows, ff_rows), ("x", "y")),
    ]
    pipes = [gather_stages(links, view, order, here) for view, order in chunks]

    def turn(r):
        for i, stages in enumerate(pipes):
            if 0 <= r - i < len(stages):
                stages[r - i]()

    small[3]()
    turn(0)
    small[4]()
    sm = sm_all[...].astype(F32)
    devices = NH * NZ * NX * NC
    sm = sm.reshape(devices, sm.shape[-2], sm.shape[-1])
    feature = width // devices
    prm[...] = jnp.transpose(sm[:, :feature, :].reshape(width, sm.shape[-1]))
    fb[...] = sm[:, feature, :]
    got = wq_all.at[every, every, 1 - x, c]
    links.copy(got, got, kwx, xdev).wait_recv()
    mine = wq_all.at[every, every, every, c]
    links.send(mine, mine, kwc, core)
    turn(1)
    got = wq_all.at[every, every, every, 1 - c]
    links.copy(got, got, kwc, core).wait_recv()
    wq[...] = wq_all[...].astype(F32).reshape(width, 3 * gw).astype(BF)

    gain, shift = prm[0:1, :], prm[3:4, :]
    lanes = pl.ds(pl.multiple_of(h * gw, 128), gw)
    q_bias, v_bias = prm[6:7, lanes], prm[7:8, lanes]

    def project(g, keys_too, queries_too):
        @pl.loop(0, 4)
        def _(j):
            n, _unused = norm_stats(xs[g, j // 2, j % 2].reshape(span, width).astype(F32))
            a = (n * gain + shift).astype(BF)
            at = pl.ds(pl.multiple_of(g * group + j * span, span), span)
            if queries_too:
                queries[at, :] = ((dot(a, wq[:, 0:gw]) + q_bias).astype(BF).astype(F32) * SCORE_SCALE).astype(BF)
            if keys_too:
                keys[at, :] = dot(a, wq[:, gw : 2 * gw]).astype(BF)
                vals[at, :] = (dot(a, wq[:, 2 * gw : 3 * gw]) + v_bias).astype(BF)
            if keys_too and queries_too:
                @pl.when(j == x * 2 + c)
                def _():
                    a_span[...] = a

    def attend(g, diagonal):
        at = pl.ds(pl.multiple_of(g * group, group), group)
        for p in range(PAIRS):
            part = pl.ds(p * WIDE, WIDE)
            k_pair, v_pair = keys[at, part], vals[at, part]

            @pl.loop(0, 2)
            def _(half):
                mine = pl.ds(pl.multiple_of(half * span, span), span)
                s = dot_nt(q2[p, mine, :], k_pair)
                if diagonal:
                    query = (x * 2 + c) * span + lax.broadcasted_iota(jnp.int32, s.shape, 0)
                    s = jnp.where(lax.broadcasted_iota(jnp.int32, s.shape, 1) <= query, s, -jnp.inf)
                    top = jnp.max(s, axis=-1, keepdims=True)
                    w = jnp.exp(s - top)
                    m_ref[p, mine, :] = jnp.broadcast_to(top, (span, 128))
                    l_ref[p, mine, :] = jnp.broadcast_to(jnp.sum(w, axis=-1, keepdims=True), (span, 128))
                    acc[p, mine, :] = dot(w.astype(BF), v_pair)
                else:
                    old = m_ref[p, mine, :]
                    new = jnp.maximum(old, jnp.max(s, axis=-1, keepdims=True))
                    fade = jnp.exp(old - new)
                    w = jnp.exp(s - new[:, 0:1])
                    m_ref[p, mine, :] = new
                    l_ref[p, mine, :] = l_ref[p, mine, :] * fade + jnp.sum(w, axis=-1, keepdims=True)
                    acc[p, mine, :] = acc[p, mine, :] * fade + dot(w.astype(BF), v_pair)

    got = xs.at[z, every, 1 - c]
    links.copy(got, got, kcore[0], core).wait_recv()
    project(z, True, True)
    start = pl.ds(pl.multiple_of(z * group + (x * 2 + c) * span, span), span)
    for p in range(PAIRS):
        q2[p] = stack_pair(queries[start, pl.ds(p * WIDE, WIDE)])
    attend(z, True)
    turn(2)

    def core_copy(g, cc):
        piece = xs.at[g, every, cc]
        return links.copy(piece, piece, core_slot(g), core)

    for t in (1, 2, 3):
        hop_recv(t)
        if t < NZ - 1:
            hop_send(t)
        for g, cond in ((z - t, z - t >= 0), (z + t, z + t < NZ)):
            pl.when(cond)(core_copy(g % NZ, c).start)
        turn(2 * t + 1)
        below, above = (z - t) % NZ, (z + t) % NZ

        @pl.when(z - t >= 0)
        def _():
            core_copy(below, 1 - c).wait_recv()
            project(below, True, False)
            attend(below, False)

        @pl.when(z + t < NZ)
        def _():
            core_copy(above, 1 - c).wait_recv()
            project(above, False, True)

        turn(2 * t + 2)

    lane = lax.broadcasted_iota(jnp.int32, (span, 128), 1)
    logs = jnp.zeros((span, 128), F32)
    for p in range(PAIRS):
        part = pl.ds(p * WIDE, WIDE)
        o_pair = unstack_pair(acc[p] / l_ref[p])
        o_wide[:, part] = o_pair
        o_tmp[:, :, part] = o_pair.astype(BF).reshape(2, span // 2, WIDE)
        total = m_ref[p] + jnp.log(l_ref[p])
        logs = jnp.where(lane == 2 * p, total[:span], logs)
        logs = jnp.where(lane == 2 * p + 1, total[span:], logs)
    lse_out[...] = logs
    ko = links.slot()
    links.send(o_tmp.at[1 - h], o_low.at[h], ko, ydev)
    o_low[h] = o_tmp[h]
    for r in range(9, len(pipes) + 5):
        turn(r)
    links.copy(o_low.at[1 - h], o_low.at[1 - h], ko, ydev).wait_recv()

    links.drain()
    for t in range(NZ - 1):
        for direction in (1, -1):
            cp, cond = pass_on(t, direction)
            pl.when(cond)(cp.wait_send)
    for t in (1, 2, 3):
        for g, cond in ((z - t, z - t >= 0), (z + t, z + t < NZ)):
            pl.when(cond)(core_copy(g % NZ, c).wait_send)


FIRST_SEMS = 80


def run_first(hid, wq_in, wp_in, w2_in, enc, small):
    rows, width = hid.shape
    span = 2 * rows
    total = span * NZ * NX * NC
    gw = PAIRS * WIDE
    grid = (NH, NZ, NX, NC)
    hbm, vmem = pl.BlockSpec(memory_space=pl.ANY), pl.BlockSpec(memory_space=pltpu.VMEM)
    S = jax.ShapeDtypeStruct
    outs = (
        S(grid + wp_in.shape, BF), S(grid + w2_in.shape, BF), S(grid + enc.shape, BF),
        S((width, 3 * gw), BF), S((128, width), F32), S((32, 128), F32),
        S((total, gw), BF), S((total, gw), BF), S((total, gw), BF), S((span, width), BF),
        S((span, gw), F32), S((2, rows, gw), BF), S((span, 128), F32),
    )
    return pl.pallas_call(
        first_kernel,
        out_shape=outs,
        in_specs=[hbm] * 6,
        out_specs=(hbm, hbm, hbm) + (vmem,) * 10,
        scratch_shapes=[
            pltpu.VMEM((NZ, NX, NC, NH, rows, width), BF),
            pltpu.VMEM(grid + (wq_in.shape[1], wq_in.shape[2]), BF),
            pltpu.VMEM(grid + small.shape, BF),
            pltpu.VMEM((PAIRS, 2 * span, WIDE), BF),
            pltpu.VMEM((PAIRS, 2 * span, 128), F32),
            pltpu.VMEM((PAIRS, 2 * span, 128), F32),
            pltpu.VMEM((PAIRS, 2 * span, WIDE), F32),
            pltpu.VMEM((2, rows, gw), BF),
            pltpu.SemaphoreType.DMA((FIRST_SEMS,)),
            pltpu.SemaphoreType.DMA((FIRST_SEMS,)),
            pltpu.SemaphoreType.DMA((6,)),
        ],
        compiler_params=pltpu.CompilerParams(
            collective_id=0, has_side_effects=True, vmem_limit_bytes=60 << 20
        ),
        cost_estimate=pl.CostEstimate(flops=10**10, bytes_accessed=10**8, transcendentals=10**7),
        name="gather_and_self_attention",
    )(hid, wq_in, wp_in, w2_in, enc, small)


def norm_back(dz, gain, v):
    n, inv = norm_stats(v)
    dn = dz * gain
    result = (dn - jnp.mean(dn, axis=-1, keepdims=True) - n * jnp.mean(dn * n, axis=-1, keepdims=True)) * inv
    return result, jnp.sum(dz * n, axis=0, keepdims=True), jnp.sum(dz, axis=0, keepdims=True)


def column_total(v):
    return jnp.sum(v.astype(F32), axis=0, keepdims=True)


SQRT_HALF = 0.7071067811865476
DENSITY = 0.3989422804014327


def middle_kernel(
    hid, g_in, o_low, enc, wp_hbm, w2_hbm, prm, inner_bias,
    hidden_out, g1, g2, de, d_attn, dx1_out, rows_out,
    wp, w2, kc, vc, qc, pc, oc, doc, dqc, dkc, dvc, ff, dy3, ya, dza, local,
):
    rows, width = hid.shape
    half = o_low.shape[2]
    inner = w2.shape[0]
    enc_rows = enc.shape[0]
    pairs = width // WIDE
    OUT, CQ, CK, CV, CO, FI = (i * width for i in range(6))
    bounds = [(OUT, width), (CQ, width), (CK, 2 * width), (CO, width), (FI, inner)]
    loads = [
        pltpu.make_async_copy(wp_hbm.at[:, pl.ds(lo, n)], wp.at[:, pl.ds(lo, n)], local.at[i])
        for i, (lo, n) in enumerate(bounds)
    ]
    loads.append(pltpu.make_async_copy(w2_hbm, w2, local.at[5]))
    for cp in loads:
        cp.start()
    rows_out[...] = jnp.zeros_like(rows_out)

    x0 = hid[...].astype(F32)
    loads[0].wait()
    x1 = x0 + dot(o_low[0], wp[0:half, OUT : OUT + width]) + dot(o_low[1], wp[half:width, OUT : OUT + width]) + prm[8:9]
    n1, _unused = norm_stats(x1)
    cn = (n1 * prm[1:2] + prm[4:5]).astype(BF)
    loads[1].wait()
    qc[...] = ((dot(cn, wp[:, CQ : CQ + width]) + prm[9:10]).astype(BF).astype(F32) * SCORE_SCALE).astype(BF)
    loads[2].wait()

    @pl.loop(0, 4)
    def _(i):
        at = pl.ds(pl.multiple_of(i * (enc_rows // 4), 16), enc_rows // 4)
        kc[at, :] = dot(enc[at, :], wp[:, CK : CK + width]).astype(BF)
        vc[at, :] = (dot(enc[at, :], wp[:, CV : CV + width]) + prm[10:11]).astype(BF)

    @pl.loop(0, pairs)
    def _(p):
        part = pl.ds(pl.multiple_of(p * WIDE, WIDE), WIDE)
        s = dot_nt(stack_pair(qc[:, part]), kc[:, part])
        w = jnp.exp(s - jnp.max(s, axis=-1, keepdims=True))
        w = w / jnp.sum(w, axis=-1, keepdims=True)
        pc[p] = w
        oc[:, part] = unstack_pair(dot(w.astype(BF), vc[:, part])).astype(BF)

    loads[3].wait()
    x2 = x1 + dot(oc[...], wp[:, CO : CO + width]) + prm[11:12]
    n2, _unused = norm_stats(x2)
    ff[...] = (n2 * prm[2:3] + prm[5:6]).astype(BF)
    dy3[...] = g_in[...]
    loads[4].wait()
    loads[5].wait()
    tile = 2 * half
    ya[...] = jnp.zeros_like(ya)
    dza[...] = jnp.zeros_like(dza)

    @pl.loop(0, inner // tile)
    def _(j):
        here = pl.ds(pl.multiple_of(j * tile, tile), tile)
        there = pl.ds(pl.multiple_of(FI + j * tile, 128), tile)
        u = dot(ff[...], wp[:, there]) + inner_bias[:, here]
        phi = 0.5 * (1.0 + lax.erf(u * SQRT_HALF))
        act = (u * phi).astype(BF)
        slope = phi + u * (DENSITY * jnp.exp(-0.5 * u * u))
        w2_tile = w2[here, :]
        ya[...] += dot(act, w2_tile)
        du = (dot_nt(dy3[...], w2_tile) * slope).astype(BF)
        dza[...] += dot_nt(du, wp[:, there])
        g1[:, there] = dot_tn(ff[...], du).astype(BF)
        g2[here, :] = dot_tn(act, dy3[...]).astype(BF)
        rows_out[pl.ds(pl.multiple_of(16 + 8 * j, 8), 1), :] = column_total(du)

    hidden_out[...] = (x2 + ya[...] + prm[12:13]).astype(BF)
    upstream = g_in[...].astype(F32)
    back, d_gain, d_shift = norm_back(dza[...], prm[2:3], x2)
    rows_out[2:3], rows_out[5:6] = d_gain, d_shift
    dx2 = upstream + back
    dy2 = dx2.astype(BF)
    g1[:, CO : CO + width] = dot_tn(oc[...], dy2).astype(BF)
    doc[...] = dot_nt(dy2, wp[:, CO : CO + width]).astype(BF)

    @pl.loop(0, pairs)
    def _(p):
        part = pl.ds(pl.multiple_of(p * WIDE, WIDE), WIDE)
        w = pc[p]
        do2 = stack_pair(doc[:, part])
        dp = dot_nt(do2, vc[:, part])
        ds = (w * (dp - jnp.sum(w * dp, axis=-1, keepdims=True))).astype(BF)
        dqc[:, part] = (unstack_pair(dot(ds, kc[:, part])) * SCORE_SCALE).astype(BF)
        dkc[:, part] = dot_tn(ds, stack_pair(qc[:, part])).astype(BF)
        dvc[:, part] = dot_tn(w.astype(BF), do2).astype(BF)

    @pl.loop(0, 4)
    def _(i):
        at = pl.ds(pl.multiple_of(i * (enc_rows // 4), 16), enc_rows // 4)
        de[at, :] = (dot_nt(dkc[at, :], wp[:, CK : CK + width]) + dot_nt(dvc[at, :], wp[:, CV : CV + width])).astype(BF)

    @pl.loop(0, 3)
    def _(i):
        at = pl.ds(pl.multiple_of(i * 256, 256), 256)
        g1[:, pl.ds(pl.multiple_of(CK + i * 256, 256), 256)] = dot_tn(enc[...], dkc[:, at]).astype(BF)
        g1[:, pl.ds(pl.multiple_of(CV + i * 256, 256), 256)] = dot_tn(enc[...], dvc[:, at]).astype(BF)

    dq = dqc[...]
    g1[:, CQ : CQ + width] = dot_tn(cn, dq).astype(BF)
    back, d_gain, d_shift = norm_back(dot_nt(dq, wp[:, CQ : CQ + width]), prm[1:2], x1)
    rows_out[1:2], rows_out[4:5] = d_gain, d_shift
    dx1 = dx2 + back
    dx1_out[...] = dx1
    dy1 = dx1.astype(BF)
    g1[0:half, OUT : OUT + width] = dot_tn(o_low[0], dy1).astype(BF)
    g1[half:width, OUT : OUT + width] = dot_tn(o_low[1], dy1).astype(BF)
    d_attn[0] = dot_nt(dy1, wp[0:half, OUT : OUT + width]).astype(BF)
    d_attn[1] = dot_nt(dy1, wp[half:width, OUT : OUT + width]).astype(BF)
    rows_out[8:9] = column_total(dy1)
    rows_out[9:10] = column_total(dq)
    rows_out[10:11] = column_total(dvc[...])
    rows_out[11:12] = column_total(dy2)
    rows_out[12:13] = column_total(dy3[...])


def run_middle(hid, g_in, o_low, enc, wp, w2, prm, inner_bias):
    rows, width = hid.shape
    inner = w2.shape[0]
    half = o_low.shape[2]
    enc_rows = enc.shape[0]
    pairs = width // WIDE
    hbm, vmem = pl.BlockSpec(memory_space=pl.ANY), pl.BlockSpec(memory_space=pltpu.VMEM)
    S = jax.ShapeDtypeStruct
    outs = (
        S((rows, width), BF), S(wp.shape, BF), S(w2.shape, BF), S((enc_rows, width), BF),
        S((2, rows, half), BF), S((rows, width), F32), S((16 + 8 * (inner // (2 * half)), width), F32),
    )
    return pl.pallas_call(
        middle_kernel,
        out_shape=outs,
        in_specs=[vmem, vmem, vmem, vmem, hbm, hbm, vmem, vmem],
        out_specs=(vmem,) * 7,
        scratch_shapes=[
            pltpu.VMEM(wp.shape, BF), pltpu.VMEM(w2.shape, BF),
            pltpu.VMEM((enc_rows, width), BF), pltpu.VMEM((enc_rows, width), BF),
            pltpu.VMEM((rows, width), BF), pltpu.VMEM((pairs, 2 * rows, enc_rows), F32),
            pltpu.VMEM((rows, width), BF), pltpu.VMEM((rows, width), BF), pltpu.VMEM((rows, width), BF),
            pltpu.VMEM((enc_rows, width), BF), pltpu.VMEM((enc_rows, width), BF),
            pltpu.VMEM((rows, width), BF), pltpu.VMEM((rows, width), BF),
            pltpu.VMEM((rows, width), F32), pltpu.VMEM((rows, width), F32),
            pltpu.SemaphoreType.DMA((6,)),
        ],
        compiler_params=pltpu.CompilerParams(vmem_limit_bytes=62 << 20),
        cost_estimate=pl.CostEstimate(flops=2 * 10**10, bytes_accessed=8 * 10**7, transcendentals=10**7),
        name="middle",
    )(hid, g_in, o_low, enc, wp, w2, prm, inner_bias)


def shard_loop(shape, fn):
    count = 1
    for n in shape:
        count *= n

    @pl.loop(0, count)
    def _(i):
        index = []
        for n in reversed(shape):
            index.append(i % n)
            i = i // n
        fn(tuple(reversed(index)))


def add_into(target, source):
    target[...] = (target[...].astype(F32) + source[...].astype(F32)).astype(BF)


def reduce_stages(links, source, order, here, bufs, local_sem, store):
    h, z, x, c = here
    every = slice(None)
    mine, from_core, first, second, from_z = bufs
    k_core, k_first, k_second = links.slot(), links.slot(), links.slot()
    k_z = [links.slot() for _ in range(3)]
    core = device_at(h, z, x, 1 - c)
    devices = {"x": device_at(h, z, 1 - x, c), "y": device_at(1 - h, z, x, c)}
    local = pltpu.make_async_copy(source(every, every, every, c), mine, local_sem)

    def start():
        links.send(source(every, every, every, 1 - c), from_core, k_core, core)
        local.start()

    def after_core():
        local.wait()
        links.copy(from_core, from_core, k_core, core).wait_recv()
        shard_loop((NH, NZ, NX), lambda i: add_into(mine.at[i], from_core.at[i]))
        away = mine.at[1 - h] if order[0] == "y" else mine.at[:, :, 1 - x]
        links.send(away, first, k_first, devices[order[0]])

    def after_first():
        links.copy(first, first, k_first, devices[order[0]]).wait_recv()
        if order[0] == "y":
            shard_loop((NZ, NX), lambda i: add_into(mine.at[(h,) + i], first.at[i]))
            away = mine.at[h, :, 1 - x]
        else:
            shard_loop((NH, NZ), lambda i: add_into(mine.at[i + (x,)], first.at[i]))
            away = mine.at[1 - h, :, x]
        links.send(away, second, k_second, devices[order[1]])

    def after_second():
        links.copy(second, second, k_second, devices[order[1]]).wait_recv()
        shard_loop((NZ,), lambda i: add_into(mine.at[(h,) + i + (x,)], second.at[i]))
        for d, k in zip((1, 2, 3), k_z):
            to = (z + d) % NZ
            links.send(mine.at[h, to, x], from_z.at[d - 1], k, device_at(h, to, x, c))

    def finish():
        for d, k in zip((1, 2, 3), k_z):
            links.copy(from_z.at[d - 1], from_z.at[d - 1], k, device_at(h, (z + d) % NZ, x, c)).wait_recv()
        total = mine[h, z, x].astype(F32)
        for d in range(3):
            total = total + from_z[d].astype(F32)
        store(total)

    return [start, after_core, after_first, after_second, finish]


def reduce_bufs(shard, order):
    second = (NZ,) + shard
    first = (NZ, NX) + shard if order[0] == "y" else (NH, NZ) + shard
    return [
        pltpu.VMEM((NH, NZ, NX) + shard, BF), pltpu.VMEM((NH, NZ, NX) + shard, BF),
        pltpu.VMEM(first, BF), pltpu.VMEM(second, BF), pltpu.VMEM((3,) + shard, BF),
    ]


def last_chunks(rows, width, ff_rows, enc_rows):
    return [
        ("w", 5 * width, 2 * width, ("y", "x")), ("f", 0, ff_rows // 2, ("x", "y")),
        ("w", 7 * width, 2 * width, ("y", "x")), ("f", ff_rows // 2, ff_rows // 2, ("x", "y")),
        ("w", 0, 2 * width, ("y", "x")), ("w", 2 * width, 2 * width, ("x", "y")),
        ("w", 4 * width, width, ("y", "x")), ("e", 0, enc_rows, ("x", "y")),
    ]


def last_kernel(
    hid, a_span, keys, vals, queries, wq, prm, o_wide, lse, d_attn, dx1, row_sums, fb_sums, gw_in, gf_in, ge_in,
    hidden_grad, out_w, out_f, out_e, out_q, out_s,
    do_all, st_all, q2, k2, v2, do2, dq2, dk2, dv2, gq, gs, dz_send, dz_recv, oq_recv, send, recv, local, *bufs,
):
    here = place()
    h, z, x, c = here
    links = Links(send, recv)
    every = slice(None)
    rows, width = hid.shape
    span = 2 * rows
    group = 4 * span
    gw = PAIRS * WIDE
    ydev = device_at(1 - h, z, x, c)
    greet(*here)

    ky = links.slot()
    links.send(d_attn.at[1 - h], do_all.at[z, x, c, h], ky, ydev)
    do_all[z, x, c, h] = d_attn[h]

    specs = last_chunks(rows, width, gf_in.shape[-2], ge_in.shape[-2])
    pipes = []
    for i, (name, lo, n, order) in enumerate(specs):
        if name == "w":
            view = lambda *i, lo=lo, n=n: gw_in.at[i + (every, pl.ds(lo, n))]

            def store(total, lo=lo, n=n):
                out_w[:, lo : lo + n] = total
        elif name == "f":
            view = lambda *i, lo=lo, n=n: gf_in.at[i + (pl.ds(lo, n), every)]

            def store(total, lo=lo, n=n):
                out_f[lo : lo + n, :] = total
        else:
            view = lambda *i: ge_in.at[i]

            def store(total):
                out_e[...] = total
        pipes.append(reduce_stages(links, view, order, here, bufs[5 * i : 5 * i + 5], local.at[i], store))

    def turn(r):
        for i, stages in enumerate(pipes):
            if 0 <= r - i < len(stages):
                stages[r - i]()

    turn(0)
    got = do_all.at[z, x, c, 1 - h]
    links.copy(got, got, ky, ydev).wait_recv()

    lane = lax.broadcasted_iota(jnp.int32, (span, 128), 1)
    first = lane_half((span, WIDE))
    deltas = jnp.zeros((span, 128), F32)
    d_columns, l_columns = [], []
    logs = lse[...]
    start = pl.ds(pl.multiple_of(z * group + (x * 2 + c) * span, span), span)
    for p in range(PAIRS):
        part = pl.ds(p * WIDE, WIDE)
        do = do_all[z, x, c, :, :, part].reshape(span, WIDE)
        prod = do.astype(F32) * o_wide[:, part]
        low = jnp.sum(jnp.where(first, prod, 0.0), axis=-1, keepdims=True)
        high = jnp.sum(jnp.where(first, 0.0, prod), axis=-1, keepdims=True)
        deltas = jnp.where(lane == 2 * p, low, jnp.where(lane == 2 * p + 1, high, deltas))
        d_columns.append((low, high))
        l_columns.append((logs[:, 2 * p : 2 * p + 1], logs[:, 2 * p + 1 : 2 * p + 2]))
        q2[p] = stack_pair(queries[start, part])
        k2[p] = stack_pair(keys[start, part])
        v2[p] = stack_pair(vals[start, part])
        do2[p] = stack_pair(do)
        dq2[p] = jnp.zeros_like(dq2[p])
        dk2[p] = jnp.zeros_like(dk2[p])
        dv2[p] = jnp.zeros_like(dv2[p])
    st_all[z, x, c, 0:8] = jnp.transpose(logs)[0:8]
    st_all[z, x, c, 8:16] = jnp.transpose(deltas)[0:8]
    get_do = gather_stages(links, lambda *i: do_all.at[i[1:]], ("x",), here)
    get_st = gather_stages(links, lambda *i: st_all.at[i[1:]], ("x",), here)

    def fetch(s):
        get_do[s]()
        get_st[s]()

    fetch(0)
    own_place = (x * 2 + c) * span

    def query_side(g, diagonal):
        at = pl.ds(pl.multiple_of(g * group, group), group)
        for p in range(PAIRS):
            part = pl.ds(p * WIDE, WIDE)
            for half in range(2):
                mine = pl.ds(half * span, span)
                k_pair, v_pair = keys[at, part], vals[at, part]
                w = jnp.exp(dot_nt(q2[p, mine], k_pair) - l_columns[p][half])
                if diagonal:
                    place_q = own_place + lax.broadcasted_iota(jnp.int32, w.shape, 0)
                    w = jnp.where(lax.broadcasted_iota(jnp.int32, w.shape, 1) <= place_q, w, 0.0)
                ds = (w * (dot_nt(do2[p, mine], v_pair) - d_columns[p][half])).astype(BF)
                dq2[p, mine] += dot(ds, k_pair)

    def key_side(g, diagonal):
        at = pl.ds(pl.multiple_of(g * group, group), group)
        for p in range(PAIRS):
            part = pl.ds(p * WIDE, WIDE)
            for half in range(2):
                mine = pl.ds(half * span, span)
                head = 2 * p + half
                q_pair = queries[at, part]
                do_pair = do_all[g, :, :, :, :, part].reshape(group, WIDE)
                stats = [st_all[g, i // 2, i % 2] for i in range(4)]
                log_row = jnp.concatenate([s[head : head + 1] for s in stats], axis=1)
                delta_row = jnp.concatenate([s[8 + head : 9 + head] for s in stats], axis=1)
                w = jnp.exp(dot_nt(k2[p, mine], q_pair) - log_row)
                if diagonal:
                    place_k = own_place + lax.broadcasted_iota(jnp.int32, w.shape, 0)
                    w = jnp.where(place_k <= lax.broadcasted_iota(jnp.int32, w.shape, 1), w, 0.0)
                dv2[p, mine] += dot(w.astype(BF), do_pair)
                ds = (w * (dot_nt(v2[p, mine], do_pair) - delta_row)).astype(BF)
                dk2[p, mine] += dot(ds, q_pair)

    turn(1)
    query_side(z, True)
    fetch(1)
    turn(2)
    pl.when(z - 1 >= 0)(lambda: query_side((z - 1) % NZ, False))
    fetch(2)
    turn(3)
    pl.when(z - 2 >= 0)(lambda: query_side((z - 2) % NZ, False))
    fetch(3)
    key_side(z, True)
    turn(4)
    pl.when(z - 3 >= 0)(lambda: query_side((z - 3) % NZ, False))
    pl.when(z + 1 < NZ)(lambda: key_side((z + 1) % NZ, False))
    turn(5)
    pl.when(z + 2 < NZ)(lambda: key_side((z + 2) % NZ, False))
    turn(6)
    pl.when(z + 3 < NZ)(lambda: key_side((z + 3) % NZ, False))

    dq = jnp.concatenate([unstack_pair(dq2[p]) * SCORE_SCALE for p in range(PAIRS)], axis=1).astype(BF)
    dk = jnp.concatenate([unstack_pair(dk2[p]) for p in range(PAIRS)], axis=1).astype(BF)
    dv = jnp.concatenate([unstack_pair(dv2[p]) for p in range(PAIRS)], axis=1).astype(BF)
    dz = dot_nt(dq, wq[:, 0:gw]) + dot_nt(dk, wq[:, gw : 2 * gw]) + dot_nt(dv, wq[:, 2 * gw : 3 * gw])
    dz_send[...] = dz.astype(BF).reshape(2, rows, width)
    kz = links.slot()
    links.send(dz_send.at[1 - h], dz_recv, kz, ydev)
    shards = gq.shape[:4]
    for i, d in enumerate((dq, dk, dv)):
        part = dot_tn(a_span[...], d)
        gq[:, :, :, :, :, i * gw : (i + 1) * gw] = part.reshape(shards + (gq.shape[4], gw)).astype(BF)

    mine, from_core, from_x, from_z = bufs[5 * len(specs) : 5 * len(specs) + 4]
    k_core, k_x, k_y = links.slot(), links.slot(), links.slot()
    k_z = [links.slot() for _ in range(3)]
    core, xdev = device_at(h, z, x, 1 - c), device_at(h, z, 1 - x, c)
    links.send(gq.at[:, :, :, 1 - c], from_core, k_core, core)
    turn(7)
    links.copy(dz_recv, dz_recv, kz, ydev).wait_recv()
    dz_own = dz_send[h].astype(F32) + dz_recv[...].astype(F32)
    back, d_gain, d_shift = norm_back(dz_own, prm[0:1], hid[...].astype(F32))
    hidden_grad[...] = dx1[...] + back
    sums = row_sums[0:16]
    row = lax.broadcasted_iota(jnp.int32, sums.shape, 0)
    sums = jnp.where(row == 0, d_gain, jnp.where(row == 3, d_shift, sums))
    q_sum, v_sum = column_total(dq), column_total(dv)
    q_wide = jnp.concatenate([jnp.where(h == i, q_sum, 0.0) for i in range(2)], axis=1)
    v_wide = jnp.concatenate([jnp.where(h == i, v_sum, 0.0) for i in range(2)], axis=1)
    sums = jnp.where(row == 6, q_wide, jnp.where(row == 7, v_wide, sums))
    wide = jnp.concatenate([sums, jnp.zeros((128 - 16, width), F32)], axis=0)
    devices = NH * NZ * NX * NC
    by_feature = jnp.transpose(wide).reshape(devices, width // devices, 128)
    fb = jnp.broadcast_to(fb_sums[...][:, None, :], (devices, 8, 128))
    gs[...] = jnp.concatenate([by_feature, fb], axis=1).astype(BF).reshape(gs.shape)

    def store_small(total):
        out_s[...] = total

    pipes.append(
        reduce_stages(
            links, lambda *i: gs.at[i], ("y", "x"), here,
            bufs[5 * len(specs) + 4 :], local.at[len(specs)], store_small,
        )
    )
    small = pipes.pop()
    small[0]()
    links.copy(from_core, from_core, k_core, core).wait_recv()
    shard_loop(
        (NH, NZ, NX),
        lambda i: mine.__setitem__(
            i, (gq[i + (c,)].astype(F32) + from_core[i].astype(F32)).astype(BF)
        ),
    )
    links.send(mine.at[:, :, 1 - x], from_x, k_x, xdev)
    turn(8)
    small[1]()
    links.copy(from_x, from_x, k_x, xdev).wait_recv()
    shard_loop((NH, NZ), lambda i: add_into(mine.at[i + (x,)], from_x.at[i]))
    for d, k in zip((1, 2, 3), k_z):
        to = (z + d) % NZ
        links.send(mine.at[:, to, x], from_z.at[d - 1], k, device_at(h, to, x, c))
    turn(9)
    small[2]()
    for d, k in zip((1, 2, 3), k_z):
        links.copy(from_z.at[d - 1], from_z.at[d - 1], k, device_at(h, (z + d) % NZ, x, c)).wait_recv()
    for i in range(NH):
        total = mine[i, z, x].astype(F32)
        for d in range(3):
            total = total + from_z[d, i].astype(F32)
        mine[i, z, x] = total.astype(BF)
        pl.when(h == i)(lambda total=total, i=i: out_q.__setitem__(i, total))
    links.send(mine.at[1 - h, z, x], oq_recv, k_y, ydev)
    turn(10)
    small[3]()
    turn(11)
    small[4]()
    links.copy(oq_recv, oq_recv, k_y, ydev).wait_recv()
    out_q[1 - h] = oq_recv[...].astype(F32)
    links.drain()


LAST_SEMS = 96


def run_last(hid, a_span, keys, vals, queries, wq, prm, o_wide, lse, d_attn, dx1, row_sums, fb_sums, g_w, g_f, g_e):
    rows, width = hid.shape
    span = 2 * rows
    gw = PAIRS * WIDE
    grid = (NH, NZ, NX, NC)
    w_rows, f_rows, e_rows = g_w.shape[-2], g_f.shape[-2], g_e.shape[-2]
    hbm, vmem = pl.BlockSpec(memory_space=pl.ANY), pl.BlockSpec(memory_space=pltpu.VMEM)
    S = jax.ShapeDtypeStruct
    outs = (
        S((rows, width), F32), S(g_w.shape[4:], F32), S(g_f.shape[4:], F32), S(g_e.shape[4:], F32),
        S((2, w_rows, 3 * gw), F32), S((32, 128), F32),
    )
    specs = last_chunks(rows, width, f_rows, e_rows)
    bufs = []
    for name, lo, n, order in specs:
        shard = {"w": (w_rows, n), "f": (n, width), "e": (e_rows, width)}[name]
        bufs += reduce_bufs(shard, order)
    q_shard = (w_rows, 3 * gw)
    bufs += [
        pltpu.VMEM((NH, NZ, NX) + q_shard, BF), pltpu.VMEM((NH, NZ, NX) + q_shard, BF),
        pltpu.VMEM((NH, NZ) + q_shard, BF), pltpu.VMEM((3, NH) + q_shard, BF),
    ]
    bufs += reduce_bufs((32, 128), ("y", "x"))
    stacked = pltpu.VMEM((PAIRS, 2 * span, WIDE), BF)
    stacked_f = pltpu.VMEM((PAIRS, 2 * span, WIDE), F32)
    return pl.pallas_call(
        last_kernel,
        out_shape=outs,
        in_specs=[vmem] * 13 + [hbm] * 3,
        out_specs=(vmem,) * 6,
        scratch_shapes=[
            pltpu.VMEM((NZ, NX, NC, 2, rows, gw), BF), pltpu.VMEM((NZ, NX, NC, 16, span), F32),
            stacked, stacked, stacked, stacked, stacked_f, stacked_f, stacked_f,
            pltpu.VMEM(grid + q_shard, BF), pltpu.VMEM(grid + (32, 128), BF),
            pltpu.VMEM((2, rows, width), BF), pltpu.VMEM((rows, width), BF), pltpu.VMEM(q_shard, BF),
            pltpu.SemaphoreType.DMA((LAST_SEMS,)), pltpu.SemaphoreType.DMA((LAST_SEMS,)),
            pltpu.SemaphoreType.DMA((len(specs) + 1,)),
        ] + bufs,
        compiler_params=pltpu.CompilerParams(
            collective_id=1, has_side_effects=True, vmem_limit_bytes=62 << 20
        ),
        cost_estimate=pl.CostEstimate(flops=2 * 10**10, bytes_accessed=10**8, transcendentals=10**7),
        name="reduce_and_self_attention_grad",
    )(hid, a_span, keys, vals, queries, wq, prm, o_wide, lse, d_attn, dx1, row_sums, fb_sums, g_w, g_f, g_e)


def fused_body(
    hidden_in, encoded, out_grad, ln_gain, ln_bias, biases, self_qkv, self_out, cross_q,
    cross_kv, cross_out, ffn_in, ffn_bias, ffn_out,
):
    hid = hidden_in[0, 0]
    g_in = out_grad[0, 0]
    enc = encoded[0]
    own_rows, width = self_out.shape
    devices = width // own_rows
    gw = width // 2
    wq_in = jnp.transpose(self_qkv.reshape(own_rows, 3, 2, gw), (2, 0, 1, 3)).reshape(2, own_rows, 3 * gw)
    wp_in = jnp.concatenate([self_out, cross_q, cross_kv, cross_out, ffn_in], axis=1)
    vectors = jnp.concatenate([ln_gain, ln_bias, biases], axis=0)
    small = jnp.zeros((32, 128), BF)
    small = small.at[:own_rows, : vectors.shape[0]].set(vectors.T)
    small = small.at[own_rows, : ffn_bias.shape[0]].set(ffn_bias)
    wp, w2, en, wq, prm, fb, keys, vals, queries, a_span, o_wide, o_low, lse = run_first(
        hid, wq_in, wp_in, ffn_out, enc, small
    )
    inner_bias = fb[:, : ffn_bias.shape[0]].reshape(1, -1)
    hidden_out, g_w, g_f, g_e, d_attn, dx1, row_sums = run_middle(
        hid, g_in, o_low, en.reshape(-1, width), wp.reshape(width, -1), w2.reshape(-1, width), prm, inner_bias
    )
    fb_sums = jnp.pad(row_sums[16::8].reshape(devices, -1), ((0, 0), (0, 128 - ffn_bias.shape[0])))
    grid = wp.shape[:4]
    hidden_grad, out_w, out_f, out_e, out_q, out_s = run_last(
        hid, a_span, keys, vals, queries, wq, prm, o_wide, lse, d_attn, dx1, row_sums, fb_sums,
        g_w.reshape(wp.shape), g_f.reshape(w2.shape), g_e.reshape(en.shape),
    )
    qkv = jnp.transpose(out_q.reshape(2, own_rows, 3, gw), (1, 2, 0, 3)).reshape(own_rows, 3 * width)
    vectors = out_s[:own_rows, :13].T
    return (
        hidden_out[None, None], hidden_grad[None, None], out_e[None],
        vectors[0:3], vectors[3:6], vectors[6:13], qkv,
        out_w[:, 0:width], out_w[:, width : 2 * width], out_w[:, 2 * width : 4 * width],
        out_w[:, 4 * width : 5 * width], out_w[:, 5 * width :],
        out_s[own_rows, : ffn_bias.shape[0]], out_f,
    )


def solution(mesh):
    fused = mesh.shape["head"] == NH and mesh.shape["blk"] == NZ * NX * NC
    return jax.shard_map(
        fused_body if fused else body,
        mesh=mesh,
        in_specs=(
            P(None, "blk", "head", None),
            P(None, ("head", "blk"), None),
            P(None, "blk", "head", None),
            P(None, ("head", "blk")),
            P(None, ("head", "blk")),
            P(None, ("head", "blk")),
            P(("head", "blk"), None),
            P(("head", "blk"), None),
            P(("head", "blk"), None),
            P(("head", "blk"), None),
            P(("head", "blk"), None),
            P(("head", "blk"), None),
            P(("head", "blk")),
            P(("head", "blk"), None),
        ),
        out_specs=(
            P(None, "blk", "head", None),
            P(None, "blk", "head", None),
            P(None, ("head", "blk"), None),
            P(None, ("head", "blk")),
            P(None, ("head", "blk")),
            P(None, ("head", "blk")),
            P(("head", "blk"), None),
            P(("head", "blk"), None),
            P(("head", "blk"), None),
            P(("head", "blk"), None),
            P(("head", "blk"), None),
            P(("head", "blk"), None),
            P(("head", "blk")),
            P(("head", "blk"), None),
        ),
        check_vma=False,
    )
```

```python
import jax
import jax.numpy as jnp
from jax import lax
from jax.experimental import pallas as pl
from jax.experimental.pallas import tpu as pltpu
from jax.sharding import PartitionSpec as P

HEADS = 12
HEAD_DIM = 64


EPSILON = 1e-05
SCORE_SCALE = 0.125


def from_behind(block, axis, distance):
    devices = range(lax.axis_size(axis))
    route = [((i - distance) % len(devices), i) for i in devices]
    return lax.ppermute(block, axis, route)


def layer_norm(values, gain_row, shift_row):
    centered = values - jnp.mean(values, axis=-1, keepdims=True)
    spread = jnp.mean(centered * centered, axis=-1, keepdims=True)
    return centered * lax.rsqrt(spread + EPSILON) * gain_row + shift_row


def norm_grads(values, gain_row, shift_row, upstream):
    result, pullback = jax.vjp(layer_norm, values, gain_row, shift_row)
    return pullback(upstream)


def exact_gelu(values):
    return jax.nn.gelu(values, approximate=False)


def project(left, right):
    return jnp.einsum("srk,kn->srn", left, right, preferred_element_type=jnp.float32)


def project_back(upstream, weight):
    return jnp.einsum("srn,kn->srk", upstream, weight, preferred_element_type=jnp.float32)


def weight_grad(left, upstream):
    return jnp.einsum("srk,srn->kn", left, upstream, preferred_element_type=jnp.float32)


def column_sum(upstream):
    return jnp.sum(upstream.astype(jnp.float32), axis=(0, 1))


def block_scores(queries, key_block, query_start, key_start):
    scores = (
        jnp.einsum("sqhd,skhd->shqk", queries, key_block, preferred_element_type=jnp.float32)
        * SCORE_SCALE
    )
    query_place = query_start + lax.iota(jnp.int32, queries.shape[1])
    key_place = key_start + lax.iota(jnp.int32, key_block.shape[1])
    allowed = key_place[None, :] <= query_place[:, None]
    return (scores, allowed)


def forward_block(carried, key_block, value_block, queries, query_start, key_start):
    row_top, row_total, weighted = carried
    scores, allowed = block_scores(queries, key_block, query_start, key_start)
    scores = jnp.where(allowed, scores, -jnp.inf)
    new_top = jnp.maximum(row_top, jnp.max(scores, axis=-1))
    weights = jnp.exp(scores - new_top[..., None])
    factor = jnp.exp(row_top - new_top)
    row_total = row_total * factor + jnp.sum(weights, axis=-1)
    addition = jnp.einsum(
        "shqk,skhd->sqhd",
        weights.astype(jnp.bfloat16),
        value_block,
        preferred_element_type=jnp.float32,
    )
    weighted = weighted * jnp.transpose(factor, (0, 2, 1))[..., None] + addition
    return (new_top, row_total, weighted)


def backward_block(
    queries, out_grads, log_total, row_delta, key_block, value_block, query_start, key_start
):
    scores, allowed = block_scores(queries, key_block, query_start, key_start)
    weights = jnp.where(allowed, jnp.exp(scores - log_total[..., None]), 0.0)
    value_grad = jnp.einsum(
        "shqk,sqhd->skhd",
        weights.astype(jnp.bfloat16),
        out_grads,
        preferred_element_type=jnp.float32,
    )
    prob_grad = jnp.einsum(
        "sqhd,skhd->shqk", out_grads, value_block, preferred_element_type=jnp.float32
    )
    score_grad = (weights * (prob_grad - row_delta[..., None])).astype(jnp.bfloat16)
    query_grad = jnp.einsum(
        "shqk,skhd->sqhd", score_grad, key_block, preferred_element_type=jnp.float32
    )
    key_grad = jnp.einsum(
        "shqk,sqhd->skhd", score_grad, queries, preferred_element_type=jnp.float32
    )
    return (query_grad, key_grad, value_grad)


def cross_forward(operands):
    queries, key_rows, value_rows = operands
    scores = (
        jnp.einsum("qhd,khd->hqk", queries, key_rows, preferred_element_type=jnp.float32)
        * SCORE_SCALE
    )
    row_top = jnp.max(scores, axis=-1, keepdims=True)
    weights = jnp.exp(scores - row_top)
    row_total = jnp.sum(weights, axis=-1, keepdims=True)
    weights_low = (weights / row_total).astype(jnp.bfloat16)
    attended = jnp.einsum(
        "hqk,khd->qhd", weights_low, value_rows, preferred_element_type=jnp.float32
    )
    return (attended, (row_top + jnp.log(row_total))[..., 0])


def cross_backward(operands):
    queries, key_rows, value_rows, log_total, out_grads = operands
    scores = (
        jnp.einsum("qhd,khd->hqk", queries, key_rows, preferred_element_type=jnp.float32)
        * SCORE_SCALE
    )
    weights = jnp.exp(scores - log_total[..., None])
    value_grad = jnp.einsum(
        "hqk,qhd->khd", weights.astype(jnp.bfloat16), out_grads, preferred_element_type=jnp.float32
    )
    prob_grad = jnp.einsum(
        "qhd,khd->hqk", out_grads, value_rows, preferred_element_type=jnp.float32
    )
    row_delta = jnp.sum(weights * prob_grad, axis=-1, keepdims=True)
    score_grad = (weights * (prob_grad - row_delta)).astype(jnp.bfloat16)
    query_grad = (
        jnp.einsum("hqk,khd->qhd", score_grad, key_rows, preferred_element_type=jnp.float32)
        * SCORE_SCALE
    )
    key_grad = (
        jnp.einsum("hqk,qhd->khd", score_grad, queries, preferred_element_type=jnp.float32)
        * SCORE_SCALE
    )
    return (query_grad, key_grad, value_grad)


def body(
    hidden_in,
    encoded,
    out_grad,
    ln_gain,
    ln_bias,
    biases,
    self_qkv,
    self_out,
    cross_q,
    cross_kv,
    cross_out,
    ffn_in,
    ffn_bias,
    ffn_out,
):
    seq_count = hidden_in.shape[0]
    row_count = hidden_in.shape[2]
    model_width = hidden_in.shape[3]
    groups = lax.axis_size("head")
    block_total = lax.axis_size("blk")
    span_rows = row_count * groups
    group_width = model_width // groups
    local_heads = HEADS // groups
    head_shape = (seq_count, span_rows, local_heads, HEAD_DIM)
    gathered = (
        lax.all_gather(ln_gain, ("head", "blk"), axis=1, tiled=True),
        lax.all_gather(ln_bias, ("head", "blk"), axis=1, tiled=True),
        lax.all_gather(biases, ("head", "blk"), axis=1, tiled=True),
        lax.all_gather(self_qkv, ("head", "blk"), axis=0, tiled=True),
        lax.all_gather(self_out, ("head", "blk"), axis=0, tiled=True),
        lax.all_gather(cross_q, ("head", "blk"), axis=0, tiled=True),
        lax.all_gather(cross_kv, ("head", "blk"), axis=0, tiled=True),
        lax.all_gather(cross_out, ("head", "blk"), axis=0, tiled=True),
        lax.all_gather(ffn_in, ("head", "blk"), axis=0, tiled=True),
        lax.all_gather(ffn_bias, ("head", "blk"), axis=0, tiled=True),
        lax.all_gather(ffn_out, ("head", "blk"), axis=0, tiled=True),
    )
    gain_rows = gathered[0].astype(jnp.float32)
    shift_rows = gathered[1].astype(jnp.float32)
    bias_rows = gathered[2].astype(jnp.float32)
    qkv_weight = gathered[3]
    out_weight = gathered[4]
    query_weight = gathered[5]
    memory_weight = gathered[6]
    cross_weight = gathered[7]
    inner_weight = gathered[8]
    inner_bias = gathered[9].astype(jnp.float32)
    outer_weight = gathered[10]
    hidden = hidden_in[:, 0].astype(jnp.float32)
    normed = layer_norm(hidden, gain_rows[0], shift_rows[0]).astype(jnp.bfloat16)
    mixed_qkv = project(normed, qkv_weight)
    mixed_qkv = mixed_qkv + jnp.concatenate(
        [bias_rows[0], jnp.zeros_like(bias_rows[0]), bias_rows[1]]
    )
    mixed_qkv = mixed_qkv.astype(jnp.bfloat16).reshape(seq_count, row_count, 3, groups, group_width)
    grouped = lax.all_to_all(mixed_qkv, "head", split_axis=3, concat_axis=1, tiled=True)
    self_queries = grouped[:, :, 0, 0].reshape(head_shape)
    self_keys = grouped[:, :, 1, 0]
    self_values = grouped[:, :, 2, 0]
    block_index = lax.axis_index("blk")
    own_start = block_index * span_rows
    stat_shape = (seq_count, local_heads, span_rows)
    initial = (
        jnp.full(stat_shape, -jnp.inf, jnp.float32),
        jnp.zeros(stat_shape, jnp.float32),
        jnp.zeros(head_shape, jnp.float32),
    )
    key_piece = lax.all_gather(self_keys, "blk", axis=1, tiled=True)
    value_piece = lax.all_gather(self_values, "blk", axis=1, tiled=True)
    piece_rows = key_piece.shape[1]
    block_count = piece_rows // span_rows
    layout = (seq_count, block_count, span_rows, local_heads, HEAD_DIM)
    key_blocks = jnp.moveaxis(key_piece.reshape(layout), 1, 0)
    value_blocks = jnp.moveaxis(value_piece.reshape(layout), 1, 0)
    block_starts = span_rows * lax.iota(jnp.int32, block_count)

    def visit(running, element):
        key_block, value_block, key_start = element

        def visit_compute(current):
            return forward_block(
                current, key_block, value_block, self_queries, own_start, key_start
            )

        def visit_unchanged(current):
            return current

        return (
            lax.cond(key_start < own_start + span_rows, visit_compute, visit_unchanged, running),
            None,
        )

    result, unused = lax.scan(visit, initial, (key_blocks, value_blocks, block_starts))
    running_top, running_total, running_sum = result
    log_total = running_top + jnp.log(running_total)
    attended = running_sum / jnp.transpose(running_total, (0, 2, 1))[..., None]
    attended_low = attended.astype(jnp.bfloat16).reshape(seq_count, span_rows, 1, group_width)
    self_mixed = lax.all_to_all(
        attended_low, "head", split_axis=1, concat_axis=2, tiled=True
    ).reshape(seq_count, row_count, model_width)
    after_self = hidden + project(self_mixed, out_weight) + bias_rows[2]
    cross_normed = layer_norm(after_self, gain_rows[1], shift_rows[1]).astype(jnp.bfloat16)
    cross_queries = (project(cross_normed, query_weight) + bias_rows[3]).astype(jnp.bfloat16)
    memory_mixed = project(encoded, memory_weight)
    memory_keys = memory_mixed[..., :model_width].astype(jnp.bfloat16)
    memory_values = (memory_mixed[..., model_width:] + bias_rows[4]).astype(jnp.bfloat16)
    all_keys, all_values = (
        lax.all_gather(memory_keys, ("head", "blk"), axis=1, tiled=True),
        lax.all_gather(memory_values, ("head", "blk"), axis=1, tiled=True),
    )
    query_heads = cross_queries.reshape(seq_count, row_count, HEADS, HEAD_DIM)
    key_heads = all_keys.reshape(seq_count, -1, HEADS, HEAD_DIM)
    value_heads = all_values.reshape(seq_count, -1, HEADS, HEAD_DIM)
    cross_result, cross_lse = lax.map(cross_forward, (query_heads, key_heads, value_heads))
    cross_mixed = cross_result.astype(jnp.bfloat16).reshape(seq_count, row_count, model_width)
    after_cross = after_self + project(cross_mixed, cross_weight) + bias_rows[5]
    ffn_normed = layer_norm(after_cross, gain_rows[2], shift_rows[2]).astype(jnp.bfloat16)
    inner_pre = project(ffn_normed, inner_weight) + inner_bias
    inner_act = exact_gelu(inner_pre).astype(jnp.bfloat16)
    output = after_cross + project(inner_act, outer_weight) + bias_rows[6]
    hidden_out = output.astype(jnp.bfloat16)[:, None]
    upstream = out_grad[:, 0].astype(jnp.float32)
    outer_low = upstream.astype(jnp.bfloat16)
    outer_weight_grad = weight_grad(inner_act, outer_low)
    act_grad = project_back(outer_low, outer_weight)
    unused_value, gelu_pull = jax.vjp(exact_gelu, inner_pre)
    pre_grad = gelu_pull(act_grad)[0].astype(jnp.bfloat16)
    inner_weight_grad = weight_grad(ffn_normed, pre_grad)
    inner_bias_grad = column_sum(pre_grad)
    back_cross, gain_grad_two, shift_grad_two = norm_grads(
        after_cross, gain_rows[2], shift_rows[2], project_back(pre_grad, inner_weight)
    )
    cross_total = upstream + back_cross
    cross_low = cross_total.astype(jnp.bfloat16)
    cross_weight_grad = weight_grad(cross_mixed, cross_low)
    cross_attn_grad = (
        project_back(cross_low, cross_weight)
        .astype(jnp.bfloat16)
        .reshape(seq_count, row_count, HEADS, HEAD_DIM)
    )
    cross_query_grads, cross_key_grads, cross_value_grads = lax.map(
        cross_backward, (query_heads, key_heads, value_heads, cross_lse, cross_attn_grad)
    )
    memory_key_grad, memory_value_grad = (
        lax.psum_scatter(
            cross_key_grads.reshape(seq_count, -1, model_width),
            ("head", "blk"),
            scatter_dimension=1,
            tiled=True,
        ),
        lax.psum_scatter(
            cross_value_grads.reshape(seq_count, -1, model_width),
            ("head", "blk"),
            scatter_dimension=1,
            tiled=True,
        ),
    )
    memory_key_low = memory_key_grad.astype(jnp.bfloat16)
    memory_value_low = memory_value_grad.astype(jnp.bfloat16)
    encoded_grad = project_back(memory_key_low, memory_weight[:, :model_width]) + project_back(
        memory_value_low, memory_weight[:, model_width:]
    )
    memory_weight_grad = weight_grad(
        encoded, jnp.concatenate([memory_key_low, memory_value_low], axis=-1)
    )
    cross_query_low = cross_query_grads.reshape(seq_count, row_count, model_width).astype(
        jnp.bfloat16
    )
    query_weight_grad = weight_grad(cross_normed, cross_query_low)
    back_self, gain_grad_one, shift_grad_one = norm_grads(
        after_self, gain_rows[1], shift_rows[1], project_back(cross_query_low, query_weight)
    )
    self_total = cross_total + back_self
    self_low = self_total.astype(jnp.bfloat16)
    out_weight_grad = weight_grad(self_mixed, self_low)
    attn_grad = (
        project_back(self_low, out_weight)
        .astype(jnp.bfloat16)
        .reshape(seq_count, row_count, groups, group_width)
    )
    grad_heads = lax.all_to_all(attn_grad, "head", split_axis=2, concat_axis=1, tiled=True).reshape(
        head_shape
    )
    row_delta = jnp.einsum("sqhd,sqhd->shq", grad_heads.astype(jnp.float32), attended)
    own_keys = self_keys.reshape(head_shape)
    own_values = self_values.reshape(head_shape)
    zero_grads = jnp.zeros(head_shape, jnp.float32)

    def key_turn(turn_index, carried):
        moving_keys, moving_values, moving_key_grads, moving_value_grads, query_grads = carried
        source = (block_index + turn_index) % block_total

        def key_compute(partial_grads):
            addition = backward_block(
                self_queries,
                grad_heads,
                log_total,
                row_delta,
                moving_keys,
                moving_values,
                own_start,
                source * span_rows,
            )
            return (
                partial_grads[0] + addition[0],
                partial_grads[1] + addition[1],
                partial_grads[2] + addition[2],
            )

        def key_unchanged(partial_grads):
            return partial_grads

        needed = (turn_index == 0) | (turn_index + block_index >= block_total)
        query_grads, moving_key_grads, moving_value_grads = lax.cond(
            needed, key_compute, key_unchanged, (query_grads, moving_key_grads, moving_value_grads)
        )
        moving_keys, moving_values = from_behind(
            (moving_keys, moving_values), "blk", block_total - 1
        )
        moving_key_grads, moving_value_grads = (
            from_behind(moving_key_grads.astype(jnp.bfloat16), "blk", block_total - 1).astype(
                moving_key_grads.dtype
            ),
            from_behind(moving_value_grads.astype(jnp.bfloat16), "blk", block_total - 1).astype(
                moving_value_grads.dtype
            ),
        )
        return (moving_keys, moving_values, moving_key_grads, moving_value_grads, query_grads)

    finished = lax.fori_loop(
        0, block_total, key_turn, (own_keys, own_values, zero_grads, zero_grads, zero_grads)
    )
    key_grads = finished[2]
    value_grads = finished[3]
    query_grads = finished[4]
    qkv_grads = jnp.stack([query_grads * SCORE_SCALE, key_grads * SCORE_SCALE, value_grads], axis=2)
    qkv_low = qkv_grads.astype(jnp.bfloat16).reshape(seq_count, span_rows, 3, 1, group_width)
    token_grads = lax.all_to_all(qkv_low, "head", split_axis=1, concat_axis=3, tiled=True).reshape(
        seq_count, row_count, 3 * model_width
    )
    qkv_weight_grad = weight_grad(normed, token_grads)
    back_input, gain_grad_zero, shift_grad_zero = norm_grads(
        hidden, gain_rows[0], shift_rows[0], project_back(token_grads, qkv_weight)
    )
    hidden_grad = (self_total + back_input)[:, None]
    bias_grad = jnp.stack(
        [
            column_sum(token_grads[..., :model_width]),
            column_sum(token_grads[..., 2 * model_width :]),
            column_sum(self_low),
            column_sum(cross_query_low),
            column_sum(memory_value_low),
            column_sum(cross_low),
            column_sum(outer_low),
        ]
    )
    gain_grad = jnp.stack([gain_grad_zero, gain_grad_one, gain_grad_two])
    shift_grad = jnp.stack([shift_grad_zero, shift_grad_one, shift_grad_two])
    reduced = (
        lax.psum_scatter(gain_grad, ("head", "blk"), scatter_dimension=1, tiled=True),
        lax.psum_scatter(shift_grad, ("head", "blk"), scatter_dimension=1, tiled=True),
        lax.psum_scatter(bias_grad, ("head", "blk"), scatter_dimension=1, tiled=True),
        lax.psum_scatter(qkv_weight_grad, ("head", "blk"), scatter_dimension=0, tiled=True),
        lax.psum_scatter(out_weight_grad, ("head", "blk"), scatter_dimension=0, tiled=True),
        lax.psum_scatter(query_weight_grad, ("head", "blk"), scatter_dimension=0, tiled=True),
        lax.psum_scatter(memory_weight_grad, ("head", "blk"), scatter_dimension=0, tiled=True),
        lax.psum_scatter(cross_weight_grad, ("head", "blk"), scatter_dimension=0, tiled=True),
        lax.psum_scatter(inner_weight_grad, ("head", "blk"), scatter_dimension=0, tiled=True),
        lax.psum_scatter(inner_bias_grad, ("head", "blk"), scatter_dimension=0, tiled=True),
        lax.psum_scatter(outer_weight_grad, ("head", "blk"), scatter_dimension=0, tiled=True),
    )
    return (
        hidden_out,
        hidden_grad,
        encoded_grad,
        reduced[0],
        reduced[1],
        reduced[2],
        reduced[3],
        reduced[4],
        reduced[5],
        reduced[6],
        reduced[7],
        reduced[8],
        reduced[9],
        reduced[10],
    )


MESH = pl.DeviceIdType.MESH
F32 = jnp.float32
BF = jnp.bfloat16
NZ, NX, NC, NH = 4, 2, 2, 2
PAIRS = 3
WIDE = 2 * HEAD_DIM


def place():
    h = lax.axis_index("head")
    b = lax.axis_index("blk")
    return h, b // 4, (b // 2) % 2, b % 2


def device_at(h, z, x, c):
    return (h, z * 4 + x * 2 + c)


def greet(h, z, x, c):
    barrier = pltpu.get_barrier_semaphore()
    others = [device_at(h, z, x, 1 - c), device_at(h, z, 1 - x, c), device_at(1 - h, z, x, c)]
    others += [device_at(h, (z + d) % NZ, x, c) for d in (1, 2, 3)]
    for other in others:
        pl.semaphore_signal(barrier, inc=1, device_id=other, device_id_type=MESH)
    pl.semaphore_wait(barrier, len(others))


def dot(a, b):
    return jnp.dot(a, b, preferred_element_type=F32)


def dot_nt(a, b):
    return lax.dot_general(a, b, (((1,), (1,)), ((), ())), preferred_element_type=F32)


def dot_tn(a, b):
    return lax.dot_general(a, b, (((0,), (0,)), ((), ())), preferred_element_type=F32)


def lane_half(shape):
    return lax.broadcasted_iota(jnp.int32, shape, len(shape) - 1) < HEAD_DIM


def stack_pair(values):
    first = lane_half(values.shape)
    zero = jnp.zeros_like(values)
    return jnp.concatenate([jnp.where(first, values, zero), jnp.where(first, zero, values)], axis=0)


def unstack_pair(stacked):
    rows = stacked.shape[0] // 2
    top, low = stacked[:rows], stacked[rows:]
    return jnp.where(lane_half(top.shape), top, low)


class Links:
    def __init__(self, send, recv):
        self.send_sems, self.recv_sems, self.count, self.open = send, recv, 0, []

    def slot(self):
        self.count += 1
        return self.count - 1

    def copy(self, source, target, k, device):
        return pltpu.make_async_remote_copy(
            source, target, self.send_sems.at[k], self.recv_sems.at[k],
            device_id=device, device_id_type=MESH,
        )

    def send(self, source, target, k, device):
        c = self.copy(source, target, k, device)
        c.start()
        self.open.append(c)

    def drain(self):
        for c in self.open:
            c.wait_send()
        self.open = []


def gather_stages(links, view, order, here, own=None, ready=None):
    h, z, x, c = here
    every = slice(None)
    known = {"y": h, "z": z, "x": x}
    stages = []

    def seen(core, **other):
        at = {**known, **other}
        return view(at["y"], at["z"], at["x"], core)

    for axis in order + ("c",):
        first = not stages
        sent = seen(c)
        source = own[0] if first and own is not None else sent
        if axis == "z":
            routes = [
                (links.slot(), device_at(h, (z + d) % NZ, x, c), seen(c, z=(z - d) % NZ)) for d in (1, 2, 3)
            ]
        elif axis == "x":
            routes = [(links.slot(), device_at(h, z, 1 - x, c), seen(c, x=1 - x))]
        elif axis == "y":
            routes = [(links.slot(), device_at(1 - h, z, x, c), seen(c, y=1 - h))]
        else:
            routes = [(links.slot(), device_at(h, z, x, 1 - c), seen(1 - c))]
        if axis != "c":
            known[axis] = every

        def start(first=first, sent=sent, source=source, routes=routes):
            if first and ready is not None:
                ready()
            for k, device, _got in routes:
                links.send(source, sent, k, device)

        def wait(first=first, routes=routes):
            if first and own is not None:
                own[1].wait()
            for k, device, got in routes:
                links.copy(got, got, k, device).wait_recv()

        stages.append((start, wait))

    made = [stages[0][0]]
    for (_s, wait), (start, _w) in zip(stages, stages[1:]):
        made.append(lambda wait=wait, start=start: (wait(), start()))
    return made + [stages[-1][1]]


class Pipes:
    def __init__(self):
        self.left = []

    def add(self, stages):
        self.left.append(list(stages))

    def go(self, i):
        self.left[i].pop(0)()


def norm_stats(v):
    centered = v - jnp.mean(v, axis=-1, keepdims=True)
    inv = lax.rsqrt(jnp.mean(centered * centered, axis=-1, keepdims=True) + EPSILON)
    return centered * inv, inv


(
    GO, SWAP, UNPACK, PROJECTION, WORK, SELF_DONE, RELAY, ENC, MID, CROSS, LATE, INNER, FINISH, DOC, CROSS_PAIRS, DX1, OWN,
    BY_QUERY, BY_KEY, QUERY_DONE, KEY_DONE, INPUT_GRAD,
) = range(22)
SMALL, QKV, HIDDEN, ENCODED, COLUMNS, INNER_COLUMNS, ROWS = range(7)
XY, YX, X = ("x", "y"), ("y", "x"), ("x",)
ZXY, ZYX, ZX, XZ = ("z",) + XY, ("z",) + YX, ("z",) + X, X + ("z",)
XYZ, YXZ = XY + ("z",), YX + ("z",)
FIRST_PARTS = (
    (QKV, 0, 1, XZ), (HIDDEN, 1, 4, ZXY), (HIDDEN, 3, 4, ZYX), (HIDDEN, 2, 4, ZYX), (SMALL, 0, 1, ZXY), (HIDDEN, 0, 4, ZXY),
    (INNER_COLUMNS, 0, 1, XZ), (ENCODED, 0, 2, ZYX), (COLUMNS, 2, 1, ZYX), (ENCODED, 1, 2, ZXY), (ROWS, 1, 3, ZX),
    (COLUMNS, 1, 1, ZYX), (COLUMNS, 3, 1, ZXY), (INNER_COLUMNS, 1, 1, XZ), (ROWS, 0, 3, ZX), (COLUMNS, 4, 1, ZXY),
    (ROWS, 2, 3, XZ), (COLUMNS, 0, 1, ZYX),
)
FIRST_ORDER = (
    (GO, 1), (GO, 2), (GO, 4), (SWAP, 0), (GO, 5), (GO, 1), (GO, 3), (GO, 2), (GO, 4), (GO, 0), (GO, 1), (GO, 4), (GO, 5),
    (GO, 2), (GO, 0), (GO, 3), (GO, 5), (GO, 7), (GO, 1), (GO, 9), (GO, 4), (GO, 1), (GO, 8), (GO, 4), (UNPACK, 0), (SWAP, 1),
    (GO, 2), (GO, 11), (GO, 3), (GO, 2), (GO, 12), (GO, 6), (GO, 13), (GO, 15), (GO, 0), (GO, 5), (GO, 17), (GO, 3), (GO, 7),
    (GO, 0), (PROJECTION, 0), (GO, 5), (GO, 6), (GO, 9), (GO, 3), (GO, 13), (WORK, 0), (GO, 7), (GO, 8), (GO, 9), (WORK, 1),
    (GO, 11), (WORK, 2), (WORK, 3), (GO, 8), (GO, 7), (GO, 12), (WORK, 4), (GO, 7), (GO, 9), (GO, 15), (WORK, 5), (GO, 9),
    (GO, 17), (WORK, 6), (GO, 8), (GO, 11), (WORK, 7), (GO, 8), (WORK, 8), (GO, 12), (GO, 17), (WORK, 9), (GO, 10), (GO, 15),
    (WORK, 10), (GO, 16), (WORK, 11), (GO, 6), (WORK, 12), (GO, 6), (GO, 11), (GO, 12), (WORK, 13), (GO, 11), (WORK, 14),
    (GO, 12), (GO, 14), (GO, 17), (WORK, 15), (GO, 15), (GO, 16), (GO, 17), (SELF_DONE, 0), (RELAY, 0), (GO, 13), (GO, 15),
    (RELAY, 1), (RELAY, 2), (RELAY, 3), (GO, 13), (ENC, 0), (GO, 10), (MID, 0), (CROSS, 0), (GO, 14), (CROSS, 1), (CROSS, 2),
    (GO, 10), (RELAY, 4), (LATE, 0), (GO, 10), (RELAY, 5), (RELAY, 6), (GO, 14), (GO, 16), (GO, 14), (GO, 16), (INNER, 0),
    (INNER, 1), (INNER, 2), (FINISH, 0),
)

def first_kernel(
    hid, g_in, enc_in, gains_in, shifts_in, biases_in, qkv_in, out_in, cq_in, ckv_in, co_in, inner_in, bias_in, w2_in,
    wq_out, keys_out, vals_out, queries_out, wc_out, kc_out, vc_out, g1, g2,
    prm, a_span, o_wide, o_low, lse_out, hidden_out, x1, dx2_out, cn, qc, oc, cross_lse, row_sums, en,
    wq_in, wp_in, wf_in, sm_in, vec, xs, wq_all, sm_all, wp, wf, w2, wq, keys, vals, queries, q2, m_ref, l_ref, acc, o_tmp,
    wc, w1, kc, vc, fb, ff, dy3, slope, act, du, ya, dza, yz_send, yz_recv, g1_tile, g2_tile, send, recv, local, store,
):
    here = place()
    h, z, x, c = here
    links = Links(send, recv)
    every = slice(None)
    span = 2 * hid.shape[0]
    group = 4 * span
    width = hid.shape[1]
    gw = PAIRS * WIDE
    feature = width // (NH * NZ * NX * NC)

    blocks = [(out_in, 0), (cq_in, 0), (ckv_in, 0), (ckv_in, width), (co_in, 0)]
    tiles = wf.shape[0]

    def stacked(source, lo):
        halves = [source[:, lo + k * gw : lo + (k + 1) * gw].astype(F32) for k in range(2)]
        return jnp.concatenate(halves, axis=0).astype(BF)

    for i, (source, lo) in enumerate(blocks):
        wp_in[i] = stacked(source, lo)
    for k in range(2):
        for j in range(tiles):
            wf_in[k, j] = stacked(inner_in, (k * tiles + j) * width)
    for k in range(2):
        for i in range(3):
            lo = i * width + k * gw
            wq_in[k, :, i * gw : (i + 1) * gw] = qkv_in[:, lo : lo + gw]
    vec[...] = jnp.zeros_like(vec)
    for source, lo in ((gains_in, 0), (shifts_in, 3), (biases_in, 6)):
        vec[lo : lo + source.shape[0], 0:feature] = source[...].astype(F32)
    packed = jnp.transpose(vec[...])[0 : sm_in.shape[0]]
    line = jnp.concatenate([bias_in[...].astype(F32), jnp.zeros((1, 128 - bias_in.shape[1]), F32)], axis=1)
    row = lax.broadcasted_iota(jnp.int32, packed.shape, 0)
    sm_in[...] = jnp.where(row == feature, line, packed).astype(BF)

    core, xdev, ydev = device_at(h, z, x, 1 - c), device_at(h, z, 1 - x, c), device_at(1 - h, z, x, c)

    def part(name, i, n):
        if name == SMALL:
            return lambda *d: sm_all.at[d], sm_in
        if name == QKV:
            return lambda h, z, x, c: wq_all.at[every, z, x, c], None
        if name == COLUMNS:
            return lambda *d: wp.at[(i,) + d], wp_in.at[i]
        if name == INNER_COLUMNS:
            return lambda h, z, x, c: wf.at[i, every, z, x, c], None
        source = {HIDDEN: hid, ENCODED: enc_in, ROWS: w2_in}[name]
        size = source.shape[0] // n
        cut = pl.ds(i * size, size)
        if name == HIDDEN:
            return lambda h, z, x, c: xs.at[z, x, c, h, cut], source.at[cut]
        if name == ROWS:
            return lambda h, z, x, c: w2.at[z, x, c, cut], source.at[cut]
        return lambda *d: en.at[d + (cut,)], source.at[cut]

    made = [part(*p[:3]) for p in FIRST_PARTS]
    copies = [
        None if piece is None else pltpu.make_async_copy(piece, view(h, z, x, c), local.at[i])
        for i, (view, piece) in enumerate(made)
    ]
    count = len(made)
    own_q = pltpu.make_async_copy(wq_in.at[h], wq_all.at[h, z, x, c], local.at[count])
    own_f = pltpu.make_async_copy(wf_in.at[h], wf.at[every, h, z, x, c], local.at[count + 1])
    own_g = pltpu.make_async_copy(g_in, dy3.at[h], local.at[count + 2])
    own = [own_q, own_f, own_g]
    for cp in own + [cp for cp in copies if cp is not None]:
        cp.start()
    greet(*here)
    kq, kf, kg = links.slot(), links.slot(), links.slot()
    links.send(wq_in.at[1 - h], wq_all.at[h, z, x, c], kq, ydev)

    def swapped_q():
        own_q.wait()
        got = wq_all.at[1 - h, z, x, c]
        links.copy(got, got, kq, ydev).wait_recv()

    waiting = [True]

    def swapped_f():
        if waiting:
            waiting.clear()
            own_f.wait()
            got = wf.at[every, 1 - h, z, x, c]
            links.copy(got, got, kf, ydev).wait_recv()

    pipes = Pipes()
    for (name, i, n, order), (view, piece), cp in zip(FIRST_PARTS, made, copies):
        ready = {QKV: swapped_q, INNER_COLUMNS: swapped_f}.get(name)
        pipes.add(gather_stages(links, view, order, here, None if piece is None else (piece, cp), ready))

    def swap(n):
        if n == 0:
            links.send(wf_in.at[1 - h], wf.at[every, h, z, x, c], kf, ydev)
        else:
            links.send(g_in, dy3.at[h], kg, ydev)

    def projection():
        wq[...] = wq_all[...].astype(F32).reshape(width, 3 * gw).astype(BF)
        keep(3, wq, wq_out)

    def small_done():
        sm = sm_all[...].astype(F32)
        devices = NH * NZ * NX * NC
        sm = sm.reshape(devices, sm.shape[-2], sm.shape[-1])
        prm[...] = jnp.transpose(sm[:, :feature, :].reshape(width, sm.shape[-1]))
        inner_part = w2_in.shape[0]
        for d in range(devices):
            fb[:, d * inner_part : (d + 1) * inner_part] = sm[d, feature : feature + 1, 0:inner_part]

    def project(g, keys_too, queries_too):
        gain, shift = prm[0:1, :], prm[3:4, :]
        lanes = pl.ds(pl.multiple_of(h * gw, 128), gw)
        q_bias, v_bias = prm[6:7, lanes], prm[7:8, lanes]

        @pl.loop(0, 4)
        def _(j):
            n, _unused = norm_stats(xs[g, j // 2, j % 2].reshape(span, width).astype(F32))
            a = (n * gain + shift).astype(BF)
            at = pl.ds(pl.multiple_of(g * group + j * span, span), span)
            if queries_too:
                queries[at, :] = ((dot(a, wq[:, 0:gw]) + q_bias).astype(BF).astype(F32) * SCORE_SCALE).astype(BF)
            if keys_too:
                keys[at, :] = dot(a, wq[:, gw : 2 * gw]).astype(BF)
                vals[at, :] = (dot(a, wq[:, 2 * gw : 3 * gw]) + v_bias).astype(BF)
            if keys_too and queries_too:
                @pl.when(j == x * 2 + c)
                def _():
                    a_span[...] = a

    def attend(g, diagonal, p):
        at = pl.ds(pl.multiple_of(g * group, group), group)
        if True:
            part = pl.ds(p * WIDE, WIDE)
            k_pair, v_pair = keys[at, part], vals[at, part]

            @pl.loop(0, 2)
            def _(half):
                mine = pl.ds(pl.multiple_of(half * span, span), span)
                s = dot_nt(q2[p, mine, :], k_pair)
                if diagonal:
                    query = (x * 2 + c) * span + lax.broadcasted_iota(jnp.int32, s.shape, 0)
                    s = jnp.where(lax.broadcasted_iota(jnp.int32, s.shape, 1) <= query, s, -jnp.inf)
                    top = jnp.max(s, axis=-1, keepdims=True)
                    w = jnp.exp(s - top)
                    m_ref[p, mine, :] = jnp.broadcast_to(top, (span, 128))
                    l_ref[p, mine, :] = jnp.broadcast_to(jnp.sum(w, axis=-1, keepdims=True), (span, 128))
                    acc[p, mine, :] = dot(w.astype(BF), v_pair)
                else:
                    old = m_ref[p, mine, :]
                    new = jnp.maximum(old, jnp.max(s, axis=-1, keepdims=True))
                    fade = jnp.exp(old - new)
                    w = jnp.exp(s - new[:, 0:1])
                    m_ref[p, mine, :] = new
                    l_ref[p, mine, :] = l_ref[p, mine, :] * fade + jnp.sum(w, axis=-1, keepdims=True)
                    acc[p, mine, :] = acc[p, mine, :] * fade + dot(w.astype(BF), v_pair)

    def work(n):
        t, p = n // 4, n % 4 - 1
        if t == 0 and p < 0:
            project(z, True, True)
            start = pl.ds(pl.multiple_of(z * group + (x * 2 + c) * span, span), span)
            for i in range(PAIRS):
                q2[i] = stack_pair(queries[start, pl.ds(i * WIDE, WIDE)])
        elif t == 0:
            attend(z, True, p)
        elif p < 0:
            pl.when(z - t >= 0)(lambda: project((z - t) % NZ, True, False))
            pl.when(z + t < NZ)(lambda: project((z + t) % NZ, False, True))
        else:
            pl.when(z - t >= 0)(lambda: attend((z - t) % NZ, False, p))

    lane = lax.broadcasted_iota(jnp.int32, (span, 128), 1)
    ko = links.slot()
    kept = []

    def keep(i, source, target):
        cp = pltpu.make_async_copy(source, target, store.at[i])
        cp.start()
        kept.append(cp)

    def self_done():
        keep(0, keys, keys_out)
        keep(1, vals, vals_out)
        keep(2, queries, queries_out)
        logs = jnp.zeros((span, 128), F32)
        for p in range(PAIRS):
            part = pl.ds(p * WIDE, WIDE)
            o_pair = unstack_pair(acc[p] / l_ref[p])
            o_wide[:, part] = o_pair
            o_tmp[:, :, part] = o_pair.astype(BF).reshape(2, span // 2, WIDE)
            total = m_ref[p] + jnp.log(l_ref[p])
            logs = jnp.where(lane == 2 * p, total[:span], logs)
            logs = jnp.where(lane == 2 * p + 1, total[span:], logs)
        lse_out[...] = logs
        links.send(o_tmp.at[1 - h], o_low.at[h], ko, ydev)
        o_low[h] = o_tmp[h]

    def unstack(v, hh, target):
        v = v.astype(F32).reshape(NZ * NX * NC, 2 * feature, gw)
        for half in range(2):
            target[hh * gw : (hh + 1) * gw, half * gw : (half + 1) * gw] = (
                v[:, half * feature : (half + 1) * feature, :].reshape(gw, gw).astype(BF)
            )

    def relay(i):
        for hh in range(NH):
            if i < 5:
                unstack(wp[i, hh], hh, wc.at[i])
            else:
                unstack(wf[i - 5, hh], hh, w1.at[i - 5])
        if i < 5:
            keep(4 + i, wc.at[i], wc_out.at[i])

    def encoder():
        enc_rows = kc.shape[0]

        @pl.loop(0, 2)
        def _(i):
            at = pl.ds(pl.multiple_of(i * (enc_rows // 2), 16), enc_rows // 2)
            e = en[i].reshape(enc_rows // 2, width)
            kc[at, :] = dot(e, wc[2]).astype(BF)
            vc[at, :] = (dot(e, wc[3]) + prm[10:11]).astype(BF)

        keep(9, kc, kc_out)
        keep(10, vc, vc_out)

    def after_self():
        links.copy(o_low.at[1 - h], o_low.at[1 - h], ko, ydev).wait_recv()
        total = hid[...].astype(F32) + dot(o_low[0], wc[0, 0:gw, :]) + dot(o_low[1], wc[0, gw:width, :]) + prm[8:9]
        x1[...] = total
        n, _unused = norm_stats(total)
        cn[...] = (n * prm[1:2] + prm[4:5]).astype(BF)
        qc[...] = ((dot(cn[...], wc[1]) + prm[9:10]).astype(BF).astype(F32) * SCORE_SCALE).astype(BF)
        cross_lse[...] = jnp.zeros_like(cross_lse)

    def cross(n):
        @pl.loop(2 * n, 2 * n + 2)
        def _(p):
            part = pl.ds(pl.multiple_of(p * WIDE, WIDE), WIDE)
            s = dot_nt(stack_pair(qc[:, part]), kc[:, part])
            top = jnp.max(s, axis=-1, keepdims=True)
            w = jnp.exp(s - top)
            total = jnp.sum(w, axis=-1, keepdims=True)
            cross_lse[...] = jnp.where(lane == p, top + jnp.log(total), cross_lse[...])
            oc[:, part] = unstack_pair(dot((w / total).astype(BF), vc[:, part])).astype(BF)

    def after_cross():
        total = x1[...] + dot(oc[...], wc[4]) + prm[11:12]
        dx2_out[...] = total
        n, _unused = norm_stats(total)
        ff[h] = (n * prm[2:3] + prm[5:6]).astype(BF)
        links.send(ff.at[h], ff.at[h], kn, ydev)
        row_sums[...] = jnp.zeros_like(row_sums)

    kn, kyz = links.slot(), [links.slot(), links.slot()]
    tile_copies = []

    def inner_start():
        own_g.wait()
        links.copy(dy3.at[1 - h], dy3.at[1 - h], kg, ydev).wait_recv()
        for j in range(tiles):
            w2_tile = w2[2 * j : 2 * j + 2].reshape(width, width)
            slope[j] = dot_nt(dy3[...].reshape(span, width), w2_tile)
        links.copy(ff.at[1 - h], ff.at[1 - h], kn, ydev).wait_recv()

    def inner_units():
        f_all = ff[...].reshape(span, width)
        for j in range(tiles):
            at = pl.multiple_of(h * (tiles * width) + j * width, 128)
            u = dot(f_all, w1[j]) + fb[:, pl.ds(at, width)]
            phi = 0.5 * (1.0 + lax.erf(u * SQRT_HALF))
            act[j] = (u * phi).astype(BF)
            du[j] = (slope[j] * (phi + u * (DENSITY * jnp.exp(-0.5 * u * u)))).astype(BF)
        for i, total in enumerate((ya, dza)):
            for j in range(tiles):
                if i == 0:
                    term = dot(act[j], w2[2 * j : 2 * j + 2].reshape(width, width))
                else:
                    term = dot_nt(du[j], w1[j])
                if j == 0:
                    total[...] = term
                else:
                    total[...] += term
            yz_send[i] = total[...].astype(BF).reshape(2, span // 2, width)
            links.send(yz_send.at[i, 1 - h], yz_recv.at[i], kyz[i], ydev)

    def inner_grads():
        f_all = ff[...].reshape(span, width)
        for j in range(tiles):
            row_sums[pl.ds(pl.multiple_of(16 + 8 * (h * tiles + j), 8), 1), :] = column_total(du[j])
            for hh in range(NH):
                halves = [
                    dot_tn(f_all[:, hh * gw : (hh + 1) * gw], du[j, :, half * gw : (half + 1) * gw]).reshape(
                        NZ * NX * NC, feature, gw
                    )
                    for half in range(2)
                ]
                g1_tile[j, hh] = jnp.concatenate(halves, axis=1).astype(BF).reshape(NZ, NX, NC, 2 * feature, gw)
            tile_copies.append(pltpu.make_async_copy(g1_tile.at[j], g1.at[j], store.at[11 + 2 * j]))
            tile_copies[-1].start()
            g2_tile[j] = dot_tn(act[j], dy3[...].reshape(span, width)).astype(BF).reshape(g2_tile.shape[1:])
            tile_copies.append(pltpu.make_async_copy(g2_tile.at[j], g2.at[pl.ds(2 * j, 2)], store.at[12 + 2 * j]))
            tile_copies[-1].start()

    def finish():
        for i in range(2):
            links.copy(yz_recv.at[i], yz_recv.at[i], kyz[i], ydev).wait_recv()
        mine = pl.ds(pl.multiple_of(h * (span // 2), 8), span // 2)
        x2 = dx2_out[...]
        hidden_out[...] = (x2 + ya[mine, :] + yz_recv[0].astype(F32) + prm[12:13]).astype(BF)
        back, d_gain, d_shift = norm_back(dza[mine, :] + yz_recv[1].astype(F32), prm[2:3], x2)
        row_sums[2:3, :], row_sums[5:6, :] = d_gain, d_shift
        row_sums[12:13, :] = column_total(g_in[...])
        dx2_out[...] = g_in[...].astype(F32) + back
        for cp in tile_copies + kept:
            cp.wait()

    steps = {
        GO: pipes.go, SWAP: swap, UNPACK: lambda n: small_done(), PROJECTION: lambda n: projection(), WORK: work,
        SELF_DONE: lambda n: self_done(), RELAY: relay, ENC: lambda n: encoder(), MID: lambda n: after_self(),
        CROSS: cross, LATE: lambda n: after_cross(),
        INNER: lambda n: (inner_start, inner_units, inner_grads)[n](), FINISH: lambda n: finish(),
    }
    for name, n in FIRST_ORDER:
        steps[name](n)
    links.drain()


FIRST_SEMS = 150


def run_first(hid, g_in, enc, *params):
    rows, width = hid.shape
    w2_in = params[-1]
    span = 2 * rows
    total = span * NZ * NX * NC
    gw = PAIRS * WIDE
    grid = (NH, NZ, NX, NC)
    devices = NH * NZ * NX * NC
    feature = width // devices
    enc_rows = enc.shape[0] * devices
    inner_width = w2_in.shape[0] * devices
    tiles = inner_width // width // NH
    hbm, vmem = pl.BlockSpec(memory_space=pl.ANY), pl.BlockSpec(memory_space=pltpu.VMEM)
    S = jax.ShapeDtypeStruct
    shard = (2 * feature, gw)
    wq_shape = (feature, 3 * gw)
    outs_hbm = (
        S((width, 3 * gw), BF), S((total, gw), BF), S((total, gw), BF), S((total, gw), BF),
        S((5, width, width), BF), S((enc_rows, width), BF), S((enc_rows, width), BF),
        S((tiles,) + grid + shard, BF), S(grid[1:] + w2_in.shape, BF),
    )
    outs_vmem = (
        S((128, width), F32), S((span, width), BF), S((span, gw), F32), S((2, rows, gw), BF), S((span, 128), F32),
        S((rows, width), BF), S((rows, width), F32), S((rows, width), F32), S((rows, width), BF), S((rows, width), BF),
        S((rows, width), BF), S((span, 128), F32), S((16 + 8 * tiles * NH, width), F32), S(grid + enc.shape, BF),
    )
    V = pltpu.VMEM
    return pl.pallas_call(
        first_kernel,
        out_shape=outs_hbm + outs_vmem,
        in_specs=[vmem] * 14,
        out_specs=(hbm,) * len(outs_hbm) + (vmem,) * len(outs_vmem),
        scratch_shapes=[
            V((2,) + wq_shape, BF), V((5,) + shard, BF), V((2, tiles) + shard, BF), V((32, 128), BF), V((128, 128), F32),
            V((NZ, NX, NC, NH, rows, width), BF), V(grid + wq_shape, BF), V(grid + (32, 128), BF),
            V((5,) + grid + shard, BF), V((tiles,) + grid + shard, BF), V(grid[1:] + w2_in.shape, BF),
            V((width, 3 * gw), BF), V((total, gw), BF), V((total, gw), BF), V((total, gw), BF),
            V((PAIRS, 2 * span, WIDE), BF), V((PAIRS, 2 * span, 128), F32), V((PAIRS, 2 * span, 128), F32),
            V((PAIRS, 2 * span, WIDE), F32), V((2, rows, gw), BF),
            V((5, width, width), BF), V((tiles, width, width), BF), V((enc_rows, width), BF), V((enc_rows, width), BF),
            V((1, inner_width), F32), V((2, rows, width), BF), V((2, rows, width), BF),
            V((tiles, span, width), F32), V((tiles, span, width), BF), V((tiles, span, width), BF), V((span, width), F32), V((span, width), F32),
            V((2, 2, rows, width), BF), V((2, rows, width), BF),
            V((tiles,) + grid + shard, BF), V((tiles, 2, NX, NC) + w2_in.shape, BF),
            pltpu.SemaphoreType.DMA((FIRST_SEMS,)), pltpu.SemaphoreType.DMA((FIRST_SEMS,)),
            pltpu.SemaphoreType.DMA((len(FIRST_PARTS) + 3,)), pltpu.SemaphoreType.DMA((16,)),
        ],
        compiler_params=pltpu.CompilerParams(
            collective_id=0, has_side_effects=True, vmem_limit_bytes=63 << 20
        ),
        cost_estimate=pl.CostEstimate(flops=10**10, bytes_accessed=10**8, transcendentals=10**7),
        name="gather_and_forward",
    )(hid, g_in, enc, *params)


def norm_back(dz, gain, v):
    n, inv = norm_stats(v)
    dn = dz * gain
    result = (dn - jnp.mean(dn, axis=-1, keepdims=True) - n * jnp.mean(dn * n, axis=-1, keepdims=True)) * inv
    return result, jnp.sum(dz * n, axis=0, keepdims=True), jnp.sum(dz, axis=0, keepdims=True)


def column_total(v):
    return jnp.sum(v.astype(F32), axis=0, keepdims=True)


SQRT_HALF = 0.7071067811865476
DENSITY = 0.3989422804014327


def shard_loop(shape, fn):
    count = 1
    for n in shape:
        count *= n

    @pl.loop(0, count)
    def _(i):
        index = []
        for n in reversed(shape):
            index.append(i % n)
            i = i // n
        fn(tuple(reversed(index)))


def add_into(target, source):
    target[...] = (target[...].astype(F32) + source[...].astype(F32)).astype(BF)


WHOLE, PAIRED, SINGLE = ("y", "z", "x"), ("l", "z", "x"), ("z", "x")
EXTENT = {"y": NH, "l": NH, "z": NZ, "x": NX}


def reduce_stages(links, source, axes, order, here, bufs, local_sem, store, ydev=None):
    h, z, x, c = here
    every = slice(None)
    me = {"y": h, "z": z, "x": x}
    bufs = list(bufs)
    if local_sem is None:
        mine = source(c)
    else:
        mine = bufs.pop(0)
        local = pltpu.make_async_copy(source(c), mine, local_sem)
    from_core = bufs.pop(0)
    k_core = links.slot()
    core = device_at(h, z, x, 1 - c)

    def start():
        links.send(source(1 - c), from_core, k_core, core)
        if local_sem is not None:
            local.start()

    def after_core():
        if local_sem is not None:
            local.wait()
        links.copy(from_core, from_core, k_core, core).wait_recv()
        shard_loop([EXTENT[a] for a in axes], lambda i: add_into(mine.at[i], from_core.at[i]))

    fixed = {}
    stages = []
    for axis in order:
        buf = bufs.pop(0)
        open_axes = [a for a in axes if a not in fixed and a != axis]

        def at(**values):
            known = {**fixed, **values}
            return tuple(known.get(a, every) for a in axes)

        if axis == "z":
            routes = [
                (links.slot(), device_at(h, (z + d) % NZ, x, c), mine.at[at(z=(z + d) % NZ)], buf.at[d - 1])
                for d in (1, 2, 3)
            ]
        elif axis == "x":
            routes = [(links.slot(), device_at(h, z, 1 - x, c), mine.at[at(x=1 - x)], buf)]
        else:
            routes = [(links.slot(), device_at(1 - h, z, x, c), mine.at[at(y=1 - h)], buf)]

        def go(routes=routes):
            for k, device, away, target in routes:
                links.send(away, target, k, device)

        def come(routes=routes):
            for k, device, _away, target in routes:
                links.copy(target, target, k, device).wait_recv()

        fixed[axis] = me[axis]
        base = dict(fixed)

        def add(routes=routes, open_axes=open_axes, base=base):
            def one(i):
                known = {**base, **dict(zip(open_axes, i))}
                slot = mine.at[tuple(known[a] for a in axes)]
                total = slot[...].astype(F32)
                for _k, _device, _away, target in routes:
                    total = total + target[i].astype(F32)
                slot[...] = total.astype(BF)

            shard_loop([EXTENT[a] for a in open_axes], one)

        def total_of(lead, routes=routes, base=base):
            known = {**base, "l": lead}
            total = mine[tuple(known[a] for a in axes)].astype(F32)
            for _k, _device, _away, target in routes:
                total = total + (target[lead] if "l" in axes else target[...]).astype(F32)
            return total

        stages.append((go, come, add, total_of))

    made = [start, lambda: (after_core(), stages[0][0]())]
    for (_g, come, add, _t), (go, _c, _a, _t2) in zip(stages, stages[1:]):
        made.append(lambda come=come, add=add, go=go: (come(), add(), go()))
    _g, come, _a, total_of = stages[-1]
    if "l" not in axes:
        return made + [lambda: (come(), store(None, total_of(None)))]
    out, back = bufs
    k_swap = links.slot()

    def swap():
        come()
        store(h, total_of(h))
        out[...] = total_of(1 - h).astype(BF)
        links.send(out, back, k_swap, ydev)

    def finish():
        links.copy(back, back, k_swap, ydev).wait_recv()
        store(1 - h, back[...].astype(F32))

    return made + [swap, finish]


def reduce_bufs(shard, axes, order, own):
    sizes = [tuple(EXTENT[a] for a in axes)] * (2 if own else 1)
    left = list(axes)
    for axis in order:
        left.remove(axis)
        sizes.append((NZ - 1,) * (axis == "z") + tuple(EXTENT[a] for a in left))
    if "l" in axes:
        sizes += [(), ()]
    return [pltpu.VMEM(size + shard, BF) for size in sizes]


XYZ, YXZ = XY + ("z",), YX + ("z",)
LAST_PARTS = (
    (COLUMNS, 2, XYZ), (INNER_COLUMNS, 1, XZ), (COLUMNS, 3, YXZ), (ENCODED, 1, XYZ), (COLUMNS, 4, XYZ), (COLUMNS, 0, YXZ),
    (ROWS, 2, XZ), (ENCODED, 0, YXZ), (COLUMNS, 1, XYZ), (ROWS, 0, ZX), (INNER_COLUMNS, 0, ZX), (ROWS, 1, XZ),
)
LAST_ORDER = (
    (GO, 9), (DOC, 0), (GO, 9), (CROSS_PAIRS, 0), (CROSS_PAIRS, 1), (CROSS_PAIRS, 2), (DX1, 0), (GO, 9), (ENC, 0), (GO, 9),
    (ENC, 1), (GO, 1), (OWN, 0), (GO, 12), (GO, 13), (GO, 14), (GO, 1), (GO, 2), (BY_QUERY, 0), (BY_QUERY, 1), (BY_QUERY, 2),
    (GO, 12), (GO, 2), (GO, 15), (BY_QUERY, 3), (BY_QUERY, 4), (BY_QUERY, 5), (BY_QUERY, 6), (BY_QUERY, 7), (BY_QUERY, 8),
    (GO, 13), (BY_QUERY, 9), (GO, 1), (GO, 5), (GO, 12), (GO, 11), (BY_QUERY, 10), (BY_QUERY, 11), (QUERY_DONE, 0), (GO, 12),
    (GO, 16), (GO, 2), (GO, 14), (GO, 5), (GO, 13), (GO, 16), (GO, 8), (GO, 11), (GO, 13), (BY_KEY, 0), (GO, 15), (GO, 2),
    (GO, 8), (BY_KEY, 3), (GO, 14), (GO, 5), (GO, 1), (BY_KEY, 6), (GO, 14), (GO, 16), (GO, 1), (GO, 2), (GO, 3), (BY_KEY, 1),
    (GO, 0), (GO, 3), (GO, 6), (GO, 16), (GO, 11), (GO, 0), (GO, 15), (GO, 16), (GO, 6), (BY_KEY, 4), (GO, 15), (BY_KEY, 2),
    (GO, 4), (GO, 8), (GO, 11), (BY_KEY, 5), (GO, 4), (GO, 5), (GO, 8), (GO, 3), (GO, 10), (BY_KEY, 7), (GO, 10), (GO, 3),
    (GO, 5), (BY_KEY, 8), (GO, 0), (GO, 8), (BY_KEY, 9), (GO, 6), (BY_KEY, 10), (GO, 0), (BY_KEY, 11), (GO, 4), (KEY_DONE, 0),
    (GO, 17), (GO, 7), (GO, 10), (GO, 3), (GO, 17), (GO, 4), (GO, 7), (GO, 10), (GO, 6), (INPUT_GRAD, 0), (GO, 18), (GO, 0),
    (GO, 18), (GO, 7), (GO, 17), (GO, 4), (GO, 10), (GO, 18), (GO, 7), (GO, 18), (GO, 17), (GO, 7), (GO, 17), (GO, 18),
)

def last_kernel(
    hid, prm, a_span, o_wide, o_low, lse, x1, dx2, cn, qc, oc, cross_lse, row_sums,
    en_in, wq_in, keys_in, vals_in, queries_in, wc_in, kc_in, vc_in, gf1, gf2,
    hidden_grad, out_o, out_cq, out_ckv, out_co, out_fi, out_f, out_e, out_q, out_s,
    wk, pool, gc, ge, doc, dqc, dx1, do_low,
    do_all, st_all, q2, k2, v2, do2, dq2, dk2, dv2, dz_q, gq, gkv, gs, fbs, dz_send, dz_recv, send, recv, local, loads, *bufs,
):
    here = place()
    h, z, x, c = here
    links = Links(send, recv)
    every = slice(None)
    rows, width = hid.shape
    span = 2 * rows
    group = 4 * span
    gw = PAIRS * WIDE
    devices = NH * NZ * NX * NC
    feature = width // devices
    e_shard, f_shard = ge.shape[4], gf2.shape[3]
    enc_rows = devices * e_shard
    total_rows = keys_in.shape[0]
    ydev = device_at(1 - h, z, x, c)
    kc, vc, dkc, dvc = (pool.at[pl.ds(i * enc_rows, enc_rows)] for i in range(4))
    wc = [wk.at[pl.ds(i * width, width)] for i in range(5)]
    queries, wq = pool.at[:, pl.ds(0, gw)], [pool.at[pl.ds(i * width, width), pl.ds(gw, gw)] for i in range(3)]
    fetches = [pltpu.make_async_copy(wc_in.at[i], wc[i], loads.at[i]) for i in range(5)]
    fetches += [
        pltpu.make_async_copy(source, target, loads.at[5 + i])
        for i, (source, target) in enumerate([(kc_in, kc), (vc_in, vc), (en_in, ge)])
    ]
    for cp in fetches:
        cp.start()
    late = [
        pltpu.make_async_copy(source, wk.at[pl.ds(0, total_rows), pl.ds(lo, gw)], loads.at[8 + i])
        for i, (source, lo) in enumerate(((keys_in, 0), (vals_in, gw)))
    ]
    late.append(pltpu.make_async_copy(queries_in, pool.at[pl.ds(0, total_rows), pl.ds(0, gw)], loads.at[10]))
    late += [
        pltpu.make_async_copy(wq_in.at[:, pl.ds(i * gw, gw)], wq[i], loads.at[11 + i]) for i in range(3)
    ]
    greet(*here)

    cuts = [(out_o, 0), (out_cq, 0), (out_ckv, 0), (out_ckv, width), (out_co, 0)]
    pipes = Pipes()
    used = 0
    for i, (name, n, order) in enumerate(LAST_PARTS):
        if name == COLUMNS:
            out, lo = cuts[n]
            axes, view = WHOLE, lambda c, n=n: gc.at[n, :, :, :, c]

            def keep(_l, total, out=out, lo=lo):
                out[:, lo : lo + gw] = total[0:feature]
                out[:, lo + gw : lo + 2 * gw] = total[feature : 2 * feature]
        elif name == INNER_COLUMNS:
            axes, view = PAIRED, lambda c, n=n: gf1.at[n, :, :, :, c]

            def keep(lead, total, n=n):
                out_fi[lead, n] = total
        elif name == ROWS:
            size = f_shard // 3
            axes, view = SINGLE, lambda c, lo=n * size, size=size: gf2.at[:, :, c, pl.ds(lo, size)]

            def keep(_l, total, lo=n * size, size=size):
                out_f[lo : lo + size, :] = total
        else:
            size = e_shard // 2
            axes, view = WHOLE, lambda c, lo=n * size, size=size: ge.at[:, :, :, c, pl.ds(lo, size)]

            def keep(_l, total, lo=n * size, size=size):
                out_e[lo : lo + size, :] = total
        outside = name in (ROWS, INNER_COLUMNS)
        count = len(order) + 1 + outside + 2 * (axes == PAIRED)
        pipes.add(
            reduce_stages(
                links, view, axes, order, here, bufs[used : used + count], local.at[i] if outside else None, keep, ydev
            )
        )
        used += count
    q_bufs, kv_bufs, small_bufs = bufs[used : used + 5], bufs[used + 5 : used + 10], bufs[used + 10 :]

    sums = {}
    lane = lax.broadcasted_iota(jnp.int32, (span, 128), 1)

    def to_shards(n, left, right):
        for hh in range(NH):
            halves = [
                dot_tn(left(hh), right(half)).reshape(devices // 2, feature, gw) for half in range(2)
            ]
            gc[n, hh] = jnp.concatenate(halves, axis=1).astype(BF).reshape(NZ, NX, NC, 2 * feature, gw)

    def half_of(ref, i):
        return ref[:, i * gw : (i + 1) * gw]

    def step_doc():
        dy2 = dx2[...].astype(BF)
        sums[11] = column_total(dy2)
        for cp in fetches:
            cp.wait()
        doc[...] = dot_nt(dy2, wc[4][...]).astype(BF)
        to_shards(4, lambda hh: half_of(oc, hh), lambda i: half_of(dy2, i))

    def step_pairs(n):
        @pl.loop(2 * n, 2 * n + 2)
        def _(p):
            part = pl.ds(pl.multiple_of(p * WIDE, WIDE), WIDE)
            logs = jnp.sum(jnp.where(lane == p, cross_lse[...], 0.0), axis=-1, keepdims=True)
            q_pair = stack_pair(qc[:, part])
            w = jnp.exp(dot_nt(q_pair, kc[:, part]) - logs)
            do_pair = stack_pair(doc[:, part])
            dp = dot_nt(do_pair, vc[:, part])
            ds = (w * (dp - jnp.sum(w * dp, axis=-1, keepdims=True))).astype(BF)
            dqc[:, part] = (unstack_pair(dot(ds, kc[:, part])) * SCORE_SCALE).astype(BF)
            dkc[:, part] = dot_tn(ds, q_pair).astype(BF)
            dvc[:, part] = dot_tn(w.astype(BF), do_pair).astype(BF)

    ky = links.slot()

    def step_dx1():
        dq = dqc[...]
        sums[9] = column_total(dq)
        back, sums[1], sums[4] = norm_back(dot_nt(dq, wc[1][...]), prm[1:2], x1[...])
        total = dx2[...] + back
        dx1[...] = total
        dy1 = total.astype(BF)
        sums[8] = column_total(dy1)
        for i in range(2):
            do_low[i] = dot_nt(dy1, wc[0][i * gw : (i + 1) * gw, :]).astype(BF)
        links.send(do_low.at[1 - h], do_all.at[z, x, c, h], ky, ydev)
        do_all[z, x, c, h] = do_low[h]
        to_shards(1, lambda hh: half_of(cn, hh), lambda i: half_of(dq, i))
        to_shards(0, lambda hh: o_low[hh], lambda i: half_of(dy1, i))

    def step_enc(n):
        if n == 1:
            for i in range(NH):
                at = pl.ds(i * (enc_rows // NH), enc_rows // NH)
                de = dot_nt(dkc[at, :], wc[2][...]) + dot_nt(dvc[at, :], wc[3][...])
                ge[i] = de.astype(BF).reshape(ge.shape[1:])
            sums[10] = column_total(dvc[...])
            for cp in late:
                cp.start()
        else:
            e_all = ge[...].reshape(enc_rows, width)
            for n, d in ((2, dkc), (3, dvc)):
                to_shards(n, lambda hh: e_all[:, hh * gw : (hh + 1) * gw], lambda i: half_of(d, i))

    l_columns, d_columns = [], []
    own_place = (x * 2 + c) * span

    def step_own():
        got = do_all.at[z, x, c, 1 - h]
        links.copy(got, got, ky, ydev).wait_recv()
        for cp in late:
            cp.wait()
        first = lane_half((span, WIDE))
        deltas = jnp.zeros((span, 128), F32)
        logs = lse[...]
        start = pl.ds(pl.multiple_of(z * group + own_place, span), span)
        for p in range(PAIRS):
            part = pl.ds(p * WIDE, WIDE)
            do = do_all[z, x, c, :, :, part].reshape(span, WIDE)
            prod = do.astype(F32) * o_wide[:, part]
            low = jnp.sum(jnp.where(first, prod, 0.0), axis=-1, keepdims=True)
            high = jnp.sum(jnp.where(first, 0.0, prod), axis=-1, keepdims=True)
            deltas = jnp.where(lane == 2 * p, low, jnp.where(lane == 2 * p + 1, high, deltas))
            d_columns.append((low, high))
            l_columns.append((logs[:, 2 * p : 2 * p + 1], logs[:, 2 * p + 1 : 2 * p + 2]))
            q2[p] = stack_pair(pool[start, part])
            k2[p] = stack_pair(wk[start, part])
            v2[p] = stack_pair(wk[start, pl.ds(gw + p * WIDE, WIDE)])
            do2[p] = stack_pair(do)
            dq2[p] = jnp.zeros_like(dq2[p])
            dk2[p] = jnp.zeros_like(dk2[p])
            dv2[p] = jnp.zeros_like(dv2[p])
        st_all[z, x, c, 0:8] = jnp.transpose(logs)[0:8]
        st_all[z, x, c, 8:16] = jnp.transpose(deltas)[0:8]

    pipes.add(gather_stages(links, lambda *i: st_all.at[i[1:]], ZX, here))
    for p in range(PAIRS):
        part = pl.ds(p * WIDE, WIDE)
        pipes.add(gather_stages(links, lambda *i, part=part: do_all.at[i[1:] + (every, every, part)], ZX, here))

    def query_side(g, diagonal, p):
        at = pl.ds(pl.multiple_of(g * group, group), group)
        if True:
            for half in range(2):
                mine = pl.ds(half * span, span)
                k_pair, v_pair = wk[at, pl.ds(p * WIDE, WIDE)], wk[at, pl.ds(gw + p * WIDE, WIDE)]
                w = jnp.exp(dot_nt(q2[p, mine], k_pair) - l_columns[p][half])
                if diagonal:
                    place_q = own_place + lax.broadcasted_iota(jnp.int32, w.shape, 0)
                    w = jnp.where(lax.broadcasted_iota(jnp.int32, w.shape, 1) <= place_q, w, 0.0)
                ds = (w * (dot_nt(do2[p, mine], v_pair) - d_columns[p][half])).astype(BF)
                dq2[p, mine] += dot(ds, k_pair)

    def key_side(g, diagonal, p):
        at = pl.ds(pl.multiple_of(g * group, group), group)
        if True:
            part = pl.ds(p * WIDE, WIDE)
            for half in range(2):
                mine = pl.ds(half * span, span)
                head = 2 * p + half
                q_pair = pool[at, part]
                do_pair = do_all[g, :, :, :, :, part].reshape(group, WIDE)
                stats = [st_all[g, i // 2, i % 2] for i in range(4)]
                log_row = jnp.concatenate([s[head : head + 1] for s in stats], axis=1)
                delta_row = jnp.concatenate([s[8 + head : 9 + head] for s in stats], axis=1)
                w = jnp.exp(dot_nt(k2[p, mine], q_pair) - log_row)
                if diagonal:
                    place_k = own_place + lax.broadcasted_iota(jnp.int32, w.shape, 0)
                    w = jnp.where(place_k <= lax.broadcasted_iota(jnp.int32, w.shape, 1), w, 0.0)
                dv2[p, mine] += dot(w.astype(BF), do_pair)
                ds = (w * (dot_nt(v2[p, mine], do_pair) - delta_row)).astype(BF)
                dk2[p, mine] += dot(ds, q_pair)

    def side(fn, n, ahead):
        t, p = n // PAIRS, n % PAIRS
        if t == 0:
            fn(z, True, p)
        elif ahead:
            pl.when(z + t < NZ)(lambda: fn((z + t) % NZ, False, p))
        else:
            pl.when(z - t >= 0)(lambda: fn((z - t) % NZ, False, p))

    def keep_q(lead, total):
        out_q[lead, 0:feature] = total

    def keep_kv(lead, total):
        out_q[lead, feature : 3 * feature] = total

    def keep_small(_l, total):
        out_s[...] = total

    pipes.add(reduce_stages(links, lambda c: gq.at[:, :, :, c], PAIRED, XZ, here, q_bufs, None, keep_q, ydev))
    pipes.add(reduce_stages(links, lambda c: gkv.at[:, :, :, c], PAIRED, XZ, here, kv_bufs, None, keep_kv, ydev))
    pipes.add(reduce_stages(links, lambda c: gs.at[:, :, :, c], WHOLE, YXZ, here, small_bufs, None, keep_small))
    kz = links.slot()

    def query_done():
        dq = jnp.concatenate([unstack_pair(dq2[p]) * SCORE_SCALE for p in range(PAIRS)], axis=1).astype(BF)
        sums[6] = column_total(dq)
        gq[...] = dot_tn(a_span[...], dq).astype(BF).reshape(gq.shape)
        dz_q[...] = dot_nt(dq, wq[0][...])

    def key_done():
        dk = jnp.concatenate([unstack_pair(dk2[p]) for p in range(PAIRS)], axis=1).astype(BF)
        dv = jnp.concatenate([unstack_pair(dv2[p]) for p in range(PAIRS)], axis=1).astype(BF)
        sums[7] = column_total(dv)
        dz = dz_q[...] + dot_nt(dk, wq[1][...]) + dot_nt(dv, wq[2][...])
        dz_send[...] = dz.astype(BF).reshape(2, rows, width)
        links.send(dz_send.at[1 - h], dz_recv, kz, ydev)
        whole = [dot_tn(a_span[...], d).reshape(devices, feature, gw) for d in (dk, dv)]
        gkv[...] = jnp.concatenate(whole, axis=1).astype(BF).reshape(gkv.shape)

    def input_grad():
        links.copy(dz_recv, dz_recv, kz, ydev).wait_recv()
        dz_own = dz_send[h].astype(F32) + dz_recv[...].astype(F32)
        back, sums[0], sums[3] = norm_back(dz_own, prm[0:1], hid[...].astype(F32))
        hidden_grad[...] = dx1[...] + back
        for i in (6, 7):
            sums[i] = jnp.concatenate([jnp.where(h == k, sums[i], 0.0) for k in range(2)], axis=1)
        block = row_sums[0:16]
        row = lax.broadcasted_iota(jnp.int32, block.shape, 0)
        for i, value in sums.items():
            block = jnp.where(row == i, value, block)
        wide = jnp.concatenate([block, jnp.zeros((128 - 16, width), F32)], axis=0)
        by_feature = jnp.transpose(wide).reshape(devices, feature, 128)
        fbs[...] = jnp.zeros_like(fbs)
        each = width // f_shard
        for d in range(devices):
            at = 16 + 8 * (d // each)
            fbs[d : d + 1, 0:f_shard] = row_sums[at : at + 1, (d % each) * f_shard : (d % each + 1) * f_shard]
        fb = jnp.broadcast_to(fbs[...][:, None, :], (devices, 8, 128))
        gs[...] = jnp.concatenate([by_feature, fb], axis=1).astype(BF).reshape(gs.shape)

    steps = {
        GO: pipes.go, DOC: lambda n: step_doc(), CROSS_PAIRS: step_pairs, DX1: lambda n: step_dx1(), ENC: step_enc,
        OWN: lambda n: step_own(), BY_QUERY: lambda n: side(query_side, n, False), BY_KEY: lambda n: side(key_side, n, True),
        QUERY_DONE: lambda n: query_done(), KEY_DONE: lambda n: key_done(), INPUT_GRAD: lambda n: input_grad(),
    }
    for name, n in LAST_ORDER:
        steps[name](n)
    links.drain()


LAST_SEMS = 140


def run_last(vmem_args, hbm_args):
    hid, en, keys, gf1, gf2 = vmem_args[0], hbm_args[0], hbm_args[2], hbm_args[8], hbm_args[9]
    rows, width = hid.shape
    span = 2 * rows
    gw = PAIRS * WIDE
    grid = (NH, NZ, NX, NC)
    devices = NH * NZ * NX * NC
    feature = width // devices
    e_rows, f_rows = en.shape[4], gf2.shape[3]
    enc_rows = e_rows * devices
    hbm, vmem = pl.BlockSpec(memory_space=pl.ANY), pl.BlockSpec(memory_space=pltpu.VMEM)
    S = jax.ShapeDtypeStruct
    V = pltpu.VMEM
    outs = (
        S((rows, width), F32), S((feature, width), F32), S((feature, width), F32), S((feature, 2 * width), F32),
        S((feature, width), F32), S((NH, gf1.shape[0], 2 * feature, gw), F32), S((f_rows, width), F32), S((e_rows, width), F32),
        S((2, 3 * feature, gw), F32), S((32, 128), F32),
    )
    shard = (2 * feature, gw)
    bufs = []
    for name, n, order in LAST_PARTS:
        size = {COLUMNS: shard, INNER_COLUMNS: shard, ROWS: (f_rows // 3, width), ENCODED: (e_rows // 2, width)}[name]
        axes = {INNER_COLUMNS: PAIRED, ROWS: SINGLE}.get(name, WHOLE)
        bufs += reduce_bufs(size, axes, order, name in (ROWS, INNER_COLUMNS))
    q_shard, kv_shard = (feature, gw), (2 * feature, gw)
    bufs += reduce_bufs(q_shard, PAIRED, XZ, False) + reduce_bufs(kv_shard, PAIRED, XZ, False)
    bufs += reduce_bufs((32, 128), WHOLE, YXZ, False)
    stacked, stacked_f = V((PAIRS, 2 * span, WIDE), BF), V((PAIRS, 2 * span, WIDE), F32)
    D = pltpu.SemaphoreType.DMA
    return pl.pallas_call(
        last_kernel,
        out_shape=outs,
        in_specs=[vmem] * len(vmem_args) + [hbm] * len(hbm_args),
        out_specs=(vmem,) * len(outs),
        scratch_shapes=[
            V((max(keys.shape[0], 5 * width), width), BF), V((max(keys.shape[0], 4 * enc_rows), width), BF),
            V((5,) + grid + shard, BF), V(en.shape, BF), V((rows, width), BF), V((rows, width), BF), V((rows, width), F32), V((2, rows, gw), BF),
            V((NZ, NX, NC, 2, rows, gw), BF), V((NZ, NX, NC, 16, span), F32),
            stacked, stacked, stacked, stacked, stacked_f, stacked_f, stacked_f,
            V((span, width), F32), V(grid + q_shard, BF), V(grid + kv_shard, BF), V(grid + (32, 128), BF), V((devices, 128), F32),
            V((2, rows, width), BF), V((rows, width), BF),
            D((LAST_SEMS,)), D((LAST_SEMS,)), D((len(LAST_PARTS),)), D((14,)),
        ] + bufs,
        compiler_params=pltpu.CompilerParams(
            collective_id=1, has_side_effects=True, vmem_limit_bytes=63 << 20
        ),
        cost_estimate=pl.CostEstimate(flops=2 * 10**10, bytes_accessed=10**8, transcendentals=10**7),
        name="backward_and_reduce",
    )(*vmem_args, *hbm_args)


def deliver_kernel(
    hidden_out, hidden_grad, o, cq, ckv, co, fi_in, f, e, qkv_in, small_in,
    out_hidden, out_grad, out_e, gains, shifts, biases, out_qkv, out_o, out_cq, out_ckv, out_co, out_fi, out_bias, out_f,
    fi, qkv, small, sems,
):
    pairs = (
        (hidden_out, out_hidden.at[0, 0]), (hidden_grad, out_grad.at[0, 0]), (e, out_e.at[0]), (o, out_o), (cq, out_cq),
        (ckv, out_ckv), (co, out_co), (f, out_f), (fi_in, fi), (qkv_in, qkv), (small_in, small),
    )
    copies = [pltpu.make_async_copy(source, target, sems.at[i]) for i, (source, target) in enumerate(pairs)]
    for cp in copies:
        cp.start()
    for cp in copies:
        cp.wait()
    gw = qkv.shape[2]
    feature = qkv.shape[1] // 3
    for k in range(2):
        for i in range(3):
            lo = (2 * i + k) * gw
            out_qkv[:, lo : lo + gw] = qkv[k, i * feature : (i + 1) * feature, :]
    tiles = fi.shape[1]
    for k in range(2):
        for j in range(tiles):
            for half in range(2):
                lo = ((k * tiles + j) * 2 + half) * gw
                out_fi[:, lo : lo + gw] = fi[k, j, half * feature : (half + 1) * feature, :]
    by_row = jnp.transpose(jnp.concatenate([small[...], jnp.zeros((128 - small.shape[0], 128), F32)], axis=0))
    gains[...] = by_row[0:3, 0:feature]
    shifts[...] = by_row[3:6, 0:feature]
    biases[...] = by_row[6:13, 0:feature]
    out_bias[...] = small[feature : feature + 1, 0 : out_bias.shape[1]]


def run_deliver(hidden_out, hidden_grad, o, cq, ckv, co, fi, f, e, qkv, small):
    S = jax.ShapeDtypeStruct
    feature, width = o.shape
    inner = fi.shape[0] * fi.shape[1] * width
    outs = (
        S((1, 1) + hidden_out.shape, BF), S((1, 1) + hidden_grad.shape, F32), S((1,) + e.shape, F32),
        S((3, feature), F32), S((3, feature), F32), S((7, feature), F32), S((feature, 3 * width), F32),
        S(o.shape, F32), S(cq.shape, F32), S(ckv.shape, F32), S(co.shape, F32), S((feature, inner), F32), S((1, f.shape[0]), F32), S(f.shape, F32),
    )
    hbm, vmem = pl.BlockSpec(memory_space=pltpu.HBM), pl.BlockSpec(memory_space=pltpu.VMEM)
    return pl.pallas_call(
        deliver_kernel, out_shape=outs, in_specs=[hbm] * 11, out_specs=(vmem,) * len(outs),
        scratch_shapes=[
            pltpu.VMEM(fi.shape, F32), pltpu.VMEM(qkv.shape, F32), pltpu.VMEM(small.shape, F32), pltpu.SemaphoreType.DMA((11,)),
        ],
        compiler_params=pltpu.CompilerParams(vmem_limit_bytes=62 << 20), name="deliver",
    )(hidden_out, hidden_grad, o, cq, ckv, co, fi, f, e, qkv, small)


def fused_body(
    hidden_in, encoded, out_grad, ln_gain, ln_bias, biases, self_qkv, self_out, cross_q,
    cross_kv, cross_out, ffn_in, ffn_bias, ffn_out,
):
    got = run_first(
        hidden_in[0, 0], out_grad[0, 0], encoded[0], ln_gain, ln_bias, biases, self_qkv, self_out, cross_q, cross_kv,
        cross_out, ffn_in, ffn_bias[None], ffn_out,
    )
    prm, a_span, o_wide, o_low, lse, hidden_out, x1, dx2, cn, qc, oc, cross_lse, row_sums, en = got[9:]
    grads = run_last(
        (hidden_in[0, 0], prm, a_span, o_wide, o_low, lse, x1, dx2, cn, qc, oc, cross_lse, row_sums), (en,) + tuple(got[:9])
    )
    done = run_deliver(hidden_out, *grads)
    return done[:12] + (done[12][0], done[13])


def solution(mesh):
    fused = mesh.shape["head"] == NH and mesh.shape["blk"] == NZ * NX * NC
    return jax.shard_map(
        fused_body if fused else body,
        mesh=mesh,
        in_specs=(
            P(None, "blk", "head", None),
            P(None, ("head", "blk"), None),
            P(None, "blk", "head", None),
            P(None, ("head", "blk")),
            P(None, ("head", "blk")),
            P(None, ("head", "blk")),
            P(("head", "blk"), None),
            P(("head", "blk"), None),
            P(("head", "blk"), None),
            P(("head", "blk"), None),
            P(("head", "blk"), None),
            P(("head", "blk"), None),
            P(("head", "blk")),
            P(("head", "blk"), None),
        ),
        out_specs=(
            P(None, "blk", "head", None),
            P(None, "blk", "head", None),
            P(None, ("head", "blk"), None),
            P(None, ("head", "blk")),
            P(None, ("head", "blk")),
            P(None, ("head", "blk")),
            P(("head", "blk"), None),
            P(("head", "blk"), None),
            P(("head", "blk"), None),
            P(("head", "blk"), None),
            P(("head", "blk"), None),
            P(("head", "blk"), None),
            P(("head", "blk")),
            P(("head", "blk"), None),
        ),
        check_vma=False,
    )
```

```python
import jax
import jax.numpy as jnp
from jax import lax
from jax.experimental import pallas as pl
from jax.experimental.pallas import tpu as pltpu
from jax.sharding import PartitionSpec as P

HEADS = 12
HEAD_DIM = 64


EPSILON = 1e-05
SCORE_SCALE = 0.125


def from_behind(block, axis, distance):
    devices = range(lax.axis_size(axis))
    route = [((i - distance) % len(devices), i) for i in devices]
    return lax.ppermute(block, axis, route)


def layer_norm(values, gain_row, shift_row):
    centered = values - jnp.mean(values, axis=-1, keepdims=True)
    spread = jnp.mean(centered * centered, axis=-1, keepdims=True)
    return centered * lax.rsqrt(spread + EPSILON) * gain_row + shift_row


def norm_grads(values, gain_row, shift_row, upstream):
    result, pullback = jax.vjp(layer_norm, values, gain_row, shift_row)
    return pullback(upstream)


def exact_gelu(values):
    return jax.nn.gelu(values, approximate=False)


def project(left, right):
    return jnp.einsum("srk,kn->srn", left, right, preferred_element_type=jnp.float32)


def project_back(upstream, weight):
    return jnp.einsum("srn,kn->srk", upstream, weight, preferred_element_type=jnp.float32)


def weight_grad(left, upstream):
    return jnp.einsum("srk,srn->kn", left, upstream, preferred_element_type=jnp.float32)


def column_sum(upstream):
    return jnp.sum(upstream.astype(jnp.float32), axis=(0, 1))


def block_scores(queries, key_block, query_start, key_start):
    scores = (
        jnp.einsum("sqhd,skhd->shqk", queries, key_block, preferred_element_type=jnp.float32)
        * SCORE_SCALE
    )
    query_place = query_start + lax.iota(jnp.int32, queries.shape[1])
    key_place = key_start + lax.iota(jnp.int32, key_block.shape[1])
    allowed = key_place[None, :] <= query_place[:, None]
    return (scores, allowed)


def forward_block(carried, key_block, value_block, queries, query_start, key_start):
    row_top, row_total, weighted = carried
    scores, allowed = block_scores(queries, key_block, query_start, key_start)
    scores = jnp.where(allowed, scores, -jnp.inf)
    new_top = jnp.maximum(row_top, jnp.max(scores, axis=-1))
    weights = jnp.exp(scores - new_top[..., None])
    factor = jnp.exp(row_top - new_top)
    row_total = row_total * factor + jnp.sum(weights, axis=-1)
    addition = jnp.einsum(
        "shqk,skhd->sqhd",
        weights.astype(jnp.bfloat16),
        value_block,
        preferred_element_type=jnp.float32,
    )
    weighted = weighted * jnp.transpose(factor, (0, 2, 1))[..., None] + addition
    return (new_top, row_total, weighted)


def backward_block(
    queries, out_grads, log_total, row_delta, key_block, value_block, query_start, key_start
):
    scores, allowed = block_scores(queries, key_block, query_start, key_start)
    weights = jnp.where(allowed, jnp.exp(scores - log_total[..., None]), 0.0)
    value_grad = jnp.einsum(
        "shqk,sqhd->skhd",
        weights.astype(jnp.bfloat16),
        out_grads,
        preferred_element_type=jnp.float32,
    )
    prob_grad = jnp.einsum(
        "sqhd,skhd->shqk", out_grads, value_block, preferred_element_type=jnp.float32
    )
    score_grad = (weights * (prob_grad - row_delta[..., None])).astype(jnp.bfloat16)
    query_grad = jnp.einsum(
        "shqk,skhd->sqhd", score_grad, key_block, preferred_element_type=jnp.float32
    )
    key_grad = jnp.einsum(
        "shqk,sqhd->skhd", score_grad, queries, preferred_element_type=jnp.float32
    )
    return (query_grad, key_grad, value_grad)


def cross_forward(operands):
    queries, key_rows, value_rows = operands
    scores = (
        jnp.einsum("qhd,khd->hqk", queries, key_rows, preferred_element_type=jnp.float32)
        * SCORE_SCALE
    )
    row_top = jnp.max(scores, axis=-1, keepdims=True)
    weights = jnp.exp(scores - row_top)
    row_total = jnp.sum(weights, axis=-1, keepdims=True)
    weights_low = (weights / row_total).astype(jnp.bfloat16)
    attended = jnp.einsum(
        "hqk,khd->qhd", weights_low, value_rows, preferred_element_type=jnp.float32
    )
    return (attended, (row_top + jnp.log(row_total))[..., 0])


def cross_backward(operands):
    queries, key_rows, value_rows, log_total, out_grads = operands
    scores = (
        jnp.einsum("qhd,khd->hqk", queries, key_rows, preferred_element_type=jnp.float32)
        * SCORE_SCALE
    )
    weights = jnp.exp(scores - log_total[..., None])
    value_grad = jnp.einsum(
        "hqk,qhd->khd", weights.astype(jnp.bfloat16), out_grads, preferred_element_type=jnp.float32
    )
    prob_grad = jnp.einsum(
        "qhd,khd->hqk", out_grads, value_rows, preferred_element_type=jnp.float32
    )
    row_delta = jnp.sum(weights * prob_grad, axis=-1, keepdims=True)
    score_grad = (weights * (prob_grad - row_delta)).astype(jnp.bfloat16)
    query_grad = (
        jnp.einsum("hqk,khd->qhd", score_grad, key_rows, preferred_element_type=jnp.float32)
        * SCORE_SCALE
    )
    key_grad = (
        jnp.einsum("hqk,qhd->khd", score_grad, queries, preferred_element_type=jnp.float32)
        * SCORE_SCALE
    )
    return (query_grad, key_grad, value_grad)


def body(
    hidden_in,
    encoded,
    out_grad,
    ln_gain,
    ln_bias,
    biases,
    self_qkv,
    self_out,
    cross_q,
    cross_kv,
    cross_out,
    ffn_in,
    ffn_bias,
    ffn_out,
):
    seq_count = hidden_in.shape[0]
    row_count = hidden_in.shape[2]
    model_width = hidden_in.shape[3]
    groups = lax.axis_size("head")
    block_total = lax.axis_size("blk")
    span_rows = row_count * groups
    group_width = model_width // groups
    local_heads = HEADS // groups
    head_shape = (seq_count, span_rows, local_heads, HEAD_DIM)
    gathered = (
        lax.all_gather(ln_gain, ("head", "blk"), axis=1, tiled=True),
        lax.all_gather(ln_bias, ("head", "blk"), axis=1, tiled=True),
        lax.all_gather(biases, ("head", "blk"), axis=1, tiled=True),
        lax.all_gather(self_qkv, ("head", "blk"), axis=0, tiled=True),
        lax.all_gather(self_out, ("head", "blk"), axis=0, tiled=True),
        lax.all_gather(cross_q, ("head", "blk"), axis=0, tiled=True),
        lax.all_gather(cross_kv, ("head", "blk"), axis=0, tiled=True),
        lax.all_gather(cross_out, ("head", "blk"), axis=0, tiled=True),
        lax.all_gather(ffn_in, ("head", "blk"), axis=0, tiled=True),
        lax.all_gather(ffn_bias, ("head", "blk"), axis=0, tiled=True),
        lax.all_gather(ffn_out, ("head", "blk"), axis=0, tiled=True),
    )
    gain_rows = gathered[0].astype(jnp.float32)
    shift_rows = gathered[1].astype(jnp.float32)
    bias_rows = gathered[2].astype(jnp.float32)
    qkv_weight = gathered[3]
    out_weight = gathered[4]
    query_weight = gathered[5]
    memory_weight = gathered[6]
    cross_weight = gathered[7]
    inner_weight = gathered[8]
    inner_bias = gathered[9].astype(jnp.float32)
    outer_weight = gathered[10]
    hidden = hidden_in[:, 0].astype(jnp.float32)
    normed = layer_norm(hidden, gain_rows[0], shift_rows[0]).astype(jnp.bfloat16)
    mixed_qkv = project(normed, qkv_weight)
    mixed_qkv = mixed_qkv + jnp.concatenate(
        [bias_rows[0], jnp.zeros_like(bias_rows[0]), bias_rows[1]]
    )
    mixed_qkv = mixed_qkv.astype(jnp.bfloat16).reshape(seq_count, row_count, 3, groups, group_width)
    grouped = lax.all_to_all(mixed_qkv, "head", split_axis=3, concat_axis=1, tiled=True)
    self_queries = grouped[:, :, 0, 0].reshape(head_shape)
    self_keys = grouped[:, :, 1, 0]
    self_values = grouped[:, :, 2, 0]
    block_index = lax.axis_index("blk")
    own_start = block_index * span_rows
    stat_shape = (seq_count, local_heads, span_rows)
    initial = (
        jnp.full(stat_shape, -jnp.inf, jnp.float32),
        jnp.zeros(stat_shape, jnp.float32),
        jnp.zeros(head_shape, jnp.float32),
    )
    key_piece = lax.all_gather(self_keys, "blk", axis=1, tiled=True)
    value_piece = lax.all_gather(self_values, "blk", axis=1, tiled=True)
    piece_rows = key_piece.shape[1]
    block_count = piece_rows // span_rows
    layout = (seq_count, block_count, span_rows, local_heads, HEAD_DIM)
    key_blocks = jnp.moveaxis(key_piece.reshape(layout), 1, 0)
    value_blocks = jnp.moveaxis(value_piece.reshape(layout), 1, 0)
    block_starts = span_rows * lax.iota(jnp.int32, block_count)

    def visit(running, element):
        key_block, value_block, key_start = element

        def visit_compute(current):
            return forward_block(
                current, key_block, value_block, self_queries, own_start, key_start
            )

        def visit_unchanged(current):
            return current

        return (
            lax.cond(key_start < own_start + span_rows, visit_compute, visit_unchanged, running),
            None,
        )

    result, unused = lax.scan(visit, initial, (key_blocks, value_blocks, block_starts))
    running_top, running_total, running_sum = result
    log_total = running_top + jnp.log(running_total)
    attended = running_sum / jnp.transpose(running_total, (0, 2, 1))[..., None]
    attended_low = attended.astype(jnp.bfloat16).reshape(seq_count, span_rows, 1, group_width)
    self_mixed = lax.all_to_all(
        attended_low, "head", split_axis=1, concat_axis=2, tiled=True
    ).reshape(seq_count, row_count, model_width)
    after_self = hidden + project(self_mixed, out_weight) + bias_rows[2]
    cross_normed = layer_norm(after_self, gain_rows[1], shift_rows[1]).astype(jnp.bfloat16)
    cross_queries = (project(cross_normed, query_weight) + bias_rows[3]).astype(jnp.bfloat16)
    memory_mixed = project(encoded, memory_weight)
    memory_keys = memory_mixed[..., :model_width].astype(jnp.bfloat16)
    memory_values = (memory_mixed[..., model_width:] + bias_rows[4]).astype(jnp.bfloat16)
    all_keys, all_values = (
        lax.all_gather(memory_keys, ("head", "blk"), axis=1, tiled=True),
        lax.all_gather(memory_values, ("head", "blk"), axis=1, tiled=True),
    )
    query_heads = cross_queries.reshape(seq_count, row_count, HEADS, HEAD_DIM)
    key_heads = all_keys.reshape(seq_count, -1, HEADS, HEAD_DIM)
    value_heads = all_values.reshape(seq_count, -1, HEADS, HEAD_DIM)
    cross_result, cross_lse = lax.map(cross_forward, (query_heads, key_heads, value_heads))
    cross_mixed = cross_result.astype(jnp.bfloat16).reshape(seq_count, row_count, model_width)
    after_cross = after_self + project(cross_mixed, cross_weight) + bias_rows[5]
    ffn_normed = layer_norm(after_cross, gain_rows[2], shift_rows[2]).astype(jnp.bfloat16)
    inner_pre = project(ffn_normed, inner_weight) + inner_bias
    inner_act = exact_gelu(inner_pre).astype(jnp.bfloat16)
    output = after_cross + project(inner_act, outer_weight) + bias_rows[6]
    hidden_out = output.astype(jnp.bfloat16)[:, None]
    upstream = out_grad[:, 0].astype(jnp.float32)
    outer_low = upstream.astype(jnp.bfloat16)
    outer_weight_grad = weight_grad(inner_act, outer_low)
    act_grad = project_back(outer_low, outer_weight)
    unused_value, gelu_pull = jax.vjp(exact_gelu, inner_pre)
    pre_grad = gelu_pull(act_grad)[0].astype(jnp.bfloat16)
    inner_weight_grad = weight_grad(ffn_normed, pre_grad)
    inner_bias_grad = column_sum(pre_grad)
    back_cross, gain_grad_two, shift_grad_two = norm_grads(
        after_cross, gain_rows[2], shift_rows[2], project_back(pre_grad, inner_weight)
    )
    cross_total = upstream + back_cross
    cross_low = cross_total.astype(jnp.bfloat16)
    cross_weight_grad = weight_grad(cross_mixed, cross_low)
    cross_attn_grad = (
        project_back(cross_low, cross_weight)
        .astype(jnp.bfloat16)
        .reshape(seq_count, row_count, HEADS, HEAD_DIM)
    )
    cross_query_grads, cross_key_grads, cross_value_grads = lax.map(
        cross_backward, (query_heads, key_heads, value_heads, cross_lse, cross_attn_grad)
    )
    memory_key_grad, memory_value_grad = (
        lax.psum_scatter(
            cross_key_grads.reshape(seq_count, -1, model_width),
            ("head", "blk"),
            scatter_dimension=1,
            tiled=True,
        ),
        lax.psum_scatter(
            cross_value_grads.reshape(seq_count, -1, model_width),
            ("head", "blk"),
            scatter_dimension=1,
            tiled=True,
        ),
    )
    memory_key_low = memory_key_grad.astype(jnp.bfloat16)
    memory_value_low = memory_value_grad.astype(jnp.bfloat16)
    encoded_grad = project_back(memory_key_low, memory_weight[:, :model_width]) + project_back(
        memory_value_low, memory_weight[:, model_width:]
    )
    memory_weight_grad = weight_grad(
        encoded, jnp.concatenate([memory_key_low, memory_value_low], axis=-1)
    )
    cross_query_low = cross_query_grads.reshape(seq_count, row_count, model_width).astype(
        jnp.bfloat16
    )
    query_weight_grad = weight_grad(cross_normed, cross_query_low)
    back_self, gain_grad_one, shift_grad_one = norm_grads(
        after_self, gain_rows[1], shift_rows[1], project_back(cross_query_low, query_weight)
    )
    self_total = cross_total + back_self
    self_low = self_total.astype(jnp.bfloat16)
    out_weight_grad = weight_grad(self_mixed, self_low)
    attn_grad = (
        project_back(self_low, out_weight)
        .astype(jnp.bfloat16)
        .reshape(seq_count, row_count, groups, group_width)
    )
    grad_heads = lax.all_to_all(attn_grad, "head", split_axis=2, concat_axis=1, tiled=True).reshape(
        head_shape
    )
    row_delta = jnp.einsum("sqhd,sqhd->shq", grad_heads.astype(jnp.float32), attended)
    own_keys = self_keys.reshape(head_shape)
    own_values = self_values.reshape(head_shape)
    zero_grads = jnp.zeros(head_shape, jnp.float32)

    def key_turn(turn_index, carried):
        moving_keys, moving_values, moving_key_grads, moving_value_grads, query_grads = carried
        source = (block_index + turn_index) % block_total

        def key_compute(partial_grads):
            addition = backward_block(
                self_queries,
                grad_heads,
                log_total,
                row_delta,
                moving_keys,
                moving_values,
                own_start,
                source * span_rows,
            )
            return (
                partial_grads[0] + addition[0],
                partial_grads[1] + addition[1],
                partial_grads[2] + addition[2],
            )

        def key_unchanged(partial_grads):
            return partial_grads

        needed = (turn_index == 0) | (turn_index + block_index >= block_total)
        query_grads, moving_key_grads, moving_value_grads = lax.cond(
            needed, key_compute, key_unchanged, (query_grads, moving_key_grads, moving_value_grads)
        )
        moving_keys, moving_values = from_behind(
            (moving_keys, moving_values), "blk", block_total - 1
        )
        moving_key_grads, moving_value_grads = (
            from_behind(moving_key_grads.astype(jnp.bfloat16), "blk", block_total - 1).astype(
                moving_key_grads.dtype
            ),
            from_behind(moving_value_grads.astype(jnp.bfloat16), "blk", block_total - 1).astype(
                moving_value_grads.dtype
            ),
        )
        return (moving_keys, moving_values, moving_key_grads, moving_value_grads, query_grads)

    finished = lax.fori_loop(
        0, block_total, key_turn, (own_keys, own_values, zero_grads, zero_grads, zero_grads)
    )
    key_grads = finished[2]
    value_grads = finished[3]
    query_grads = finished[4]
    qkv_grads = jnp.stack([query_grads * SCORE_SCALE, key_grads * SCORE_SCALE, value_grads], axis=2)
    qkv_low = qkv_grads.astype(jnp.bfloat16).reshape(seq_count, span_rows, 3, 1, group_width)
    token_grads = lax.all_to_all(qkv_low, "head", split_axis=1, concat_axis=3, tiled=True).reshape(
        seq_count, row_count, 3 * model_width
    )
    qkv_weight_grad = weight_grad(normed, token_grads)
    back_input, gain_grad_zero, shift_grad_zero = norm_grads(
        hidden, gain_rows[0], shift_rows[0], project_back(token_grads, qkv_weight)
    )
    hidden_grad = (self_total + back_input)[:, None]
    bias_grad = jnp.stack(
        [
            column_sum(token_grads[..., :model_width]),
            column_sum(token_grads[..., 2 * model_width :]),
            column_sum(self_low),
            column_sum(cross_query_low),
            column_sum(memory_value_low),
            column_sum(cross_low),
            column_sum(outer_low),
        ]
    )
    gain_grad = jnp.stack([gain_grad_zero, gain_grad_one, gain_grad_two])
    shift_grad = jnp.stack([shift_grad_zero, shift_grad_one, shift_grad_two])
    reduced = (
        lax.psum_scatter(gain_grad, ("head", "blk"), scatter_dimension=1, tiled=True),
        lax.psum_scatter(shift_grad, ("head", "blk"), scatter_dimension=1, tiled=True),
        lax.psum_scatter(bias_grad, ("head", "blk"), scatter_dimension=1, tiled=True),
        lax.psum_scatter(qkv_weight_grad, ("head", "blk"), scatter_dimension=0, tiled=True),
        lax.psum_scatter(out_weight_grad, ("head", "blk"), scatter_dimension=0, tiled=True),
        lax.psum_scatter(query_weight_grad, ("head", "blk"), scatter_dimension=0, tiled=True),
        lax.psum_scatter(memory_weight_grad, ("head", "blk"), scatter_dimension=0, tiled=True),
        lax.psum_scatter(cross_weight_grad, ("head", "blk"), scatter_dimension=0, tiled=True),
        lax.psum_scatter(inner_weight_grad, ("head", "blk"), scatter_dimension=0, tiled=True),
        lax.psum_scatter(inner_bias_grad, ("head", "blk"), scatter_dimension=0, tiled=True),
        lax.psum_scatter(outer_weight_grad, ("head", "blk"), scatter_dimension=0, tiled=True),
    )
    return (
        hidden_out,
        hidden_grad,
        encoded_grad,
        reduced[0],
        reduced[1],
        reduced[2],
        reduced[3],
        reduced[4],
        reduced[5],
        reduced[6],
        reduced[7],
        reduced[8],
        reduced[9],
        reduced[10],
    )


MESH = pl.DeviceIdType.MESH
F32 = jnp.float32
BF = jnp.bfloat16
NZ, NX, NC, NH = 4, 2, 2, 2
PAIRS = 3
WIDE = 2 * HEAD_DIM


def place():
    h = lax.axis_index("head")
    b = lax.axis_index("blk")
    return h, b // 4, (b // 2) % 2, b % 2


def device_at(h, z, x, c):
    return (h, z * 4 + x * 2 + c)


def greet(h, z, x, c):
    barrier = pltpu.get_barrier_semaphore()
    others = [device_at(h, z, x, 1 - c), device_at(h, z, 1 - x, c), device_at(1 - h, z, x, c)]
    others += [device_at(h, (z + d) % NZ, x, c) for d in (1, 2, 3)]
    for other in others:
        pl.semaphore_signal(barrier, inc=1, device_id=other, device_id_type=MESH)
    pl.semaphore_wait(barrier, len(others))


def dot(a, b):
    return jnp.dot(a, b, preferred_element_type=F32)


def dot_nt(a, b):
    return lax.dot_general(a, b, (((1,), (1,)), ((), ())), preferred_element_type=F32)


def dot_tn(a, b):
    return lax.dot_general(a, b, (((0,), (0,)), ((), ())), preferred_element_type=F32)


def lane_half(shape):
    return lax.broadcasted_iota(jnp.int32, shape, len(shape) - 1) < HEAD_DIM


def stack_pair(values):
    first = lane_half(values.shape)
    zero = jnp.zeros_like(values)
    return jnp.concatenate([jnp.where(first, values, zero), jnp.where(first, zero, values)], axis=0)


def unstack_pair(stacked):
    rows = stacked.shape[0] // 2
    top, low = stacked[:rows], stacked[rows:]
    return jnp.where(lane_half(top.shape), top, low)


class Links:
    def __init__(self, send, recv):
        self.send_sems, self.recv_sems, self.count, self.open = send, recv, 0, []

    def slot(self):
        self.count += 1
        return self.count - 1

    def copy(self, source, target, k, device):
        return pltpu.make_async_remote_copy(
            source, target, self.send_sems.at[k], self.recv_sems.at[k],
            device_id=device, device_id_type=MESH,
        )

    def send(self, source, target, k, device):
        c = self.copy(source, target, k, device)
        c.start()
        self.open.append(c)

    def drain(self):
        for c in self.open:
            c.wait_send()
        self.open = []


def gather_stages(links, view, order, here, own=None, ready=None):
    h, z, x, c = here
    every = slice(None)
    known = {"y": h, "z": z, "x": x}
    stages = []

    def seen(core, **other):
        at = {**known, **other}
        return view(at["y"], at["z"], at["x"], core)

    for axis in order + ("c",):
        first = not stages
        sent = seen(c)
        source = own[0] if first and own is not None else sent
        if axis == "z":
            routes = [
                (links.slot(), device_at(h, (z + d) % NZ, x, c), seen(c, z=(z - d) % NZ)) for d in (1, 2, 3)
            ]
        elif axis == "x":
            routes = [(links.slot(), device_at(h, z, 1 - x, c), seen(c, x=1 - x))]
        elif axis == "y":
            routes = [(links.slot(), device_at(1 - h, z, x, c), seen(c, y=1 - h))]
        else:
            routes = [(links.slot(), device_at(h, z, x, 1 - c), seen(1 - c))]
        if axis != "c":
            known[axis] = every

        def start(first=first, sent=sent, source=source, routes=routes):
            if first and ready is not None:
                ready()
            for k, device, _got in routes:
                links.send(source, sent, k, device)

        def wait(first=first, routes=routes):
            if first and own is not None:
                own[1].wait()
            for k, device, got in routes:
                links.copy(got, got, k, device).wait_recv()

        stages.append((start, wait))

    made = [stages[0][0]]
    for (_s, wait), (start, _w) in zip(stages, stages[1:]):
        made.append(lambda wait=wait, start=start: (wait(), start()))
    return made + [stages[-1][1]]


class Pipes:
    def __init__(self):
        self.left = []

    def add(self, stages):
        self.left.append(list(stages))

    def go(self, i):
        self.left[i].pop(0)()


def norm_stats(v):
    centered = v - jnp.mean(v, axis=-1, keepdims=True)
    inv = lax.rsqrt(jnp.mean(centered * centered, axis=-1, keepdims=True) + EPSILON)
    return centered * inv, inv


(
    GO, PACK, SWAP, UNPACK, PROJECTION, WORK, SELF_DONE, RELAY, ENC, MID, CROSS, LATE, INNER, FINISH, DOC, CROSS_PAIRS, DX1, OWN,
    BY_QUERY, BY_KEY, HIDDEN_OUT, QUERY_DONE, KEY_DONE, INPUT_GRAD,
) = range(24)
SMALL, QKV, HIDDEN, ENCODED, COLUMNS, INNER_COLUMNS, ROWS = range(7)
XY, YX, X = ("x", "y"), ("y", "x"), ("x",)
ZXY, ZYX, ZX, XZ = ("z",) + XY, ("z",) + YX, ("z",) + X, X + ("z",)
XYZ, YXZ = XY + ("z",), YX + ("z",)
FIRST_PARTS = (
    (HIDDEN, 0, 8, ZXY), (HIDDEN, 2, 8, ZXY), (SMALL, 0, 1, ZXY), (HIDDEN, 7, 8, ZYX), (HIDDEN, 5, 8, ZXY), (HIDDEN, 1, 8, ZXY),
    (ENCODED, 1, 2, ZYX), (HIDDEN, 3, 8, ZYX), (HIDDEN, 6, 8, ZYX), (HIDDEN, 4, 8, ZXY), (COLUMNS, 1, 1, ZYX),
    (COLUMNS, 0, 1, ZXY), (COLUMNS, 3, 1, ZYX), (ENCODED, 0, 2, ZYX), (ROWS, 2, 3, XZ), (QKV, 0, 1, ZX),
    (INNER_COLUMNS, 0, 1, XZ), (COLUMNS, 2, 1, ZYX), (COLUMNS, 4, 1, ZYX), (ROWS, 1, 3, ZX), (INNER_COLUMNS, 1, 1, ZX),
    (ROWS, 0, 3, ZX),
)
FIRST_ORDER = (
    (GO, 0), (GO, 3), (GO, 4), (GO, 5), (GO, 7), (GO, 9), (PACK, 0), (GO, 1), (GO, 2), (GO, 15), (GO, 0), (SWAP, 0), (GO, 3),
    (GO, 0), (GO, 4), (GO, 3), (GO, 5), (GO, 8), (GO, 4), (GO, 7), (GO, 12), (GO, 0), (GO, 9), (GO, 0), (GO, 3), (GO, 1),
    (GO, 13), (GO, 2), (GO, 3), (GO, 4), (GO, 5), (GO, 17), (GO, 4), (GO, 7), (GO, 9), (GO, 14), (GO, 10), (GO, 1), (GO, 2),
    (GO, 5), (GO, 11), (GO, 5), (GO, 15), (GO, 7), (GO, 6), (GO, 9), (GO, 14), (GO, 7), (GO, 8), (GO, 9), (GO, 12), (GO, 1),
    (GO, 1), (GO, 13), (GO, 2), (GO, 2), (UNPACK, 0), (GO, 8), (SWAP, 1), (GO, 17), (GO, 15), (GO, 18), (GO, 12), (GO, 15),
    (GO, 10), (PROJECTION, 0), (GO, 8), (GO, 13), (GO, 19), (GO, 11), (GO, 8), (WORK, 0), (GO, 6), (GO, 20), (WORK, 1), (GO, 12),
    (WORK, 2), (GO, 17), (WORK, 3), (GO, 12), (WORK, 4), (GO, 6), (GO, 10), (GO, 13), (GO, 14), (GO, 21), (WORK, 5), (GO, 11),
    (GO, 13), (GO, 14), (GO, 18), (WORK, 6), (WORK, 7), (WORK, 8), (GO, 17), (GO, 19), (WORK, 9), (GO, 16), (GO, 11), (GO, 17),
    (WORK, 10), (GO, 6), (GO, 11), (WORK, 11), (GO, 6), (GO, 18), (GO, 20), (WORK, 12), (WORK, 13), (GO, 10), (GO, 21),
    (WORK, 14), (WORK, 15), (GO, 10), (SELF_DONE, 0), (RELAY, 0), (GO, 19), (RELAY, 1), (RELAY, 2), (GO, 16), (GO, 19),
    (RELAY, 3), (ENC, 0), (MID, 0), (CROSS, 0), (GO, 18), (CROSS, 1), (GO, 18), (CROSS, 2), (RELAY, 4), (LATE, 0), (GO, 20),
    (GO, 16), (GO, 20), (RELAY, 6), (GO, 21), (GO, 16), (RELAY, 5), (GO, 21), (INNER, 0), (INNER, 1), (INNER, 2), (FINISH, 0),
)

def first_kernel(
    hid, g_in, enc_in, gains_in, shifts_in, biases_in, qkv_in, out_in, cq_in, ckv_in, co_in, inner_in, bias_in, w2_in,
    wq_out, keys_out, vals_out, queries_out, wc_out, kc_out, vc_out, g1, g2,
    prm, a_span, o_wide, o_low, lse_out, out_part, out_send, x1, dx2_out, cn, qc, oc, cross_lse, row_sums, en,
    wq_in, wp_in, wf_in, sm_in, vec, xs, wq_all, sm_all, wp, wf, w2, wq, keys, vals, queries, q2, m_ref, l_ref, acc, o_tmp,
    wc, w1, kc, vc, fb, ff, dy3, slope, act, du, ya, dza, yz_send, yz_recv, g1_tile, g2_tile, send, recv, local, store,
):
    here = place()
    h, z, x, c = here
    links = Links(send, recv)
    every = slice(None)
    span = 2 * hid.shape[0]
    group = 4 * span
    width = hid.shape[1]
    gw = PAIRS * WIDE
    feature = width // (NH * NZ * NX * NC)

    tiles = wf.shape[0]
    core, xdev, ydev = device_at(h, z, x, 1 - c), device_at(h, z, 1 - x, c), device_at(1 - h, z, x, c)

    def part(name, i, n):
        if name == SMALL:
            return lambda *d: sm_all.at[d], sm_in
        if name == QKV:
            return lambda h, z, x, c: wq_all.at[every, z, x, c], None
        if name == COLUMNS:
            return lambda *d: wp.at[(i,) + d], wp_in.at[i]
        if name == INNER_COLUMNS:
            return lambda h, z, x, c: wf.at[i, every, z, x, c], None
        source = {HIDDEN: hid, ENCODED: enc_in, ROWS: w2_in}[name]
        size = source.shape[0] // n
        cut = pl.ds(i * size, size)
        if name == HIDDEN:
            return lambda h, z, x, c: xs.at[z, x, c, h, cut], source.at[cut]
        if name == ROWS:
            return lambda h, z, x, c: w2.at[z, x, c, cut], source.at[cut]
        return lambda *d: en.at[d + (cut,)], source.at[cut]

    made = [part(*p[:3]) for p in FIRST_PARTS]
    copies = [
        None if piece is None else pltpu.make_async_copy(piece, view(h, z, x, c), local.at[i])
        for i, (view, piece) in enumerate(made)
    ]
    count = len(made)
    own_q = pltpu.make_async_copy(wq_in.at[h], wq_all.at[h, z, x, c], local.at[count])
    own_f = pltpu.make_async_copy(wf_in.at[h], wf.at[every, h, z, x, c], local.at[count + 1])
    own_g = pltpu.make_async_copy(g_in, dy3.at[h], local.at[count + 2])
    packed_here = [name in (SMALL, COLUMNS) for name, *_rest in FIRST_PARTS]
    own_g.start()
    for cp, late in zip(copies, packed_here):
        if cp is not None and not late:
            cp.start()
    greet(*here)
    kq, kf, kg = links.slot(), links.slot(), links.slot()

    def pack():
        blocks = [(out_in, 0), (cq_in, 0), (ckv_in, 0), (ckv_in, width), (co_in, 0)]
        def stacked(source, lo):
            halves = [source[:, lo + k * gw : lo + (k + 1) * gw].astype(F32) for k in range(2)]
            return jnp.concatenate(halves, axis=0).astype(BF)

        for i, (source, lo) in enumerate(blocks):
            wp_in[i] = stacked(source, lo)
        for k in range(2):
            for j in range(tiles):
                wf_in[k, j] = stacked(inner_in, (k * tiles + j) * width)
        for k in range(2):
            for i in range(3):
                lo = i * width + k * gw
                wq_in[k, :, i * gw : (i + 1) * gw] = qkv_in[:, lo : lo + gw]
        vec[...] = jnp.zeros_like(vec)
        for source, lo in ((gains_in, 0), (shifts_in, 3), (biases_in, 6)):
            vec[lo : lo + source.shape[0], 0:feature] = source[...].astype(F32)
        packed = jnp.transpose(vec[...])[0 : sm_in.shape[0]]
        line = jnp.concatenate([bias_in[...].astype(F32), jnp.zeros((1, 128 - bias_in.shape[1]), F32)], axis=1)
        row = lax.broadcasted_iota(jnp.int32, packed.shape, 0)
        sm_in[...] = jnp.where(row == feature, line, packed).astype(BF)
        for cp in [own_q, own_f] + [cp for cp, late in zip(copies, packed_here) if late]:
            cp.start()
        links.send(wq_in.at[1 - h], wq_all.at[h, z, x, c], kq, ydev)

    def swapped_q():
        own_q.wait()
        got = wq_all.at[1 - h, z, x, c]
        links.copy(got, got, kq, ydev).wait_recv()

    waiting = [True]

    def swapped_f():
        if waiting:
            waiting.clear()
            own_f.wait()
            got = wf.at[every, 1 - h, z, x, c]
            links.copy(got, got, kf, ydev).wait_recv()

    pipes = Pipes()
    for (name, i, n, order), (view, piece), cp in zip(FIRST_PARTS, made, copies):
        ready = {QKV: swapped_q, INNER_COLUMNS: swapped_f}.get(name)
        pipes.add(gather_stages(links, view, order, here, None if piece is None else (piece, cp), ready))

    def swap(n):
        if n == 0:
            links.send(wf_in.at[1 - h], wf.at[every, h, z, x, c], kf, ydev)
        else:
            links.send(g_in, dy3.at[h], kg, ydev)

    def projection():
        wq[...] = wq_all[...].astype(F32).reshape(width, 3 * gw).astype(BF)
        keep(3, wq, wq_out)

    def small_done():
        sm = sm_all[...].astype(F32)
        devices = NH * NZ * NX * NC
        sm = sm.reshape(devices, sm.shape[-2], sm.shape[-1])
        prm[...] = jnp.transpose(sm[:, :feature, :].reshape(width, sm.shape[-1]))
        inner_part = w2_in.shape[0]
        for d in range(devices):
            fb[:, d * inner_part : (d + 1) * inner_part] = sm[d, feature : feature + 1, 0:inner_part]

    def project(g, keys_too, queries_too):
        gain, shift = prm[0:1, :], prm[3:4, :]
        lanes = pl.ds(pl.multiple_of(h * gw, 128), gw)
        q_bias, v_bias = prm[6:7, lanes], prm[7:8, lanes]

        @pl.loop(0, 4)
        def _(j):
            n, _unused = norm_stats(xs[g, j // 2, j % 2].reshape(span, width).astype(F32))
            a = (n * gain + shift).astype(BF)
            at = pl.ds(pl.multiple_of(g * group + j * span, span), span)
            if queries_too:
                queries[at, :] = ((dot(a, wq[:, 0:gw]) + q_bias).astype(BF).astype(F32) * SCORE_SCALE).astype(BF)
            if keys_too:
                keys[at, :] = dot(a, wq[:, gw : 2 * gw]).astype(BF)
                vals[at, :] = (dot(a, wq[:, 2 * gw : 3 * gw]) + v_bias).astype(BF)
            if keys_too and queries_too:
                @pl.when(j == x * 2 + c)
                def _():
                    a_span[...] = a

    def attend(g, diagonal, p):
        at = pl.ds(pl.multiple_of(g * group, group), group)
        if True:
            part = pl.ds(p * WIDE, WIDE)
            k_pair, v_pair = keys[at, part], vals[at, part]

            @pl.loop(0, 2)
            def _(half):
                mine = pl.ds(pl.multiple_of(half * span, span), span)
                s = dot_nt(q2[p, mine, :], k_pair)
                if diagonal:
                    query = (x * 2 + c) * span + lax.broadcasted_iota(jnp.int32, s.shape, 0)
                    s = jnp.where(lax.broadcasted_iota(jnp.int32, s.shape, 1) <= query, s, -jnp.inf)
                    top = jnp.max(s, axis=-1, keepdims=True)
                    w = jnp.exp(s - top)
                    m_ref[p, mine, :] = jnp.broadcast_to(top, (span, 128))
                    l_ref[p, mine, :] = jnp.broadcast_to(jnp.sum(w, axis=-1, keepdims=True), (span, 128))
                    acc[p, mine, :] = dot(w.astype(BF), v_pair)
                else:
                    old = m_ref[p, mine, :]
                    new = jnp.maximum(old, jnp.max(s, axis=-1, keepdims=True))
                    fade = jnp.exp(old - new)
                    w = jnp.exp(s - new[:, 0:1])
                    m_ref[p, mine, :] = new
                    l_ref[p, mine, :] = l_ref[p, mine, :] * fade + jnp.sum(w, axis=-1, keepdims=True)
                    acc[p, mine, :] = acc[p, mine, :] * fade + dot(w.astype(BF), v_pair)

    def work(n):
        t, p = n // 4, n % 4 - 1
        if t == 0 and p < 0:
            project(z, True, True)
            start = pl.ds(pl.multiple_of(z * group + (x * 2 + c) * span, span), span)
            for i in range(PAIRS):
                q2[i] = stack_pair(queries[start, pl.ds(i * WIDE, WIDE)])
        elif t == 0:
            attend(z, True, p)
        elif p < 0:
            pl.when(z - t >= 0)(lambda: project((z - t) % NZ, True, False))
            pl.when(z + t < NZ)(lambda: project((z + t) % NZ, False, True))
        else:
            pl.when(z - t >= 0)(lambda: attend((z - t) % NZ, False, p))

    lane = lax.broadcasted_iota(jnp.int32, (span, 128), 1)
    ko = links.slot()
    kept = []

    def keep(i, source, target):
        cp = pltpu.make_async_copy(source, target, store.at[i])
        cp.start()
        kept.append(cp)

    def self_done():
        keep(0, keys, keys_out)
        keep(1, vals, vals_out)
        keep(2, queries, queries_out)
        logs = jnp.zeros((span, 128), F32)
        for p in range(PAIRS):
            part = pl.ds(p * WIDE, WIDE)
            o_pair = unstack_pair(acc[p] / l_ref[p])
            o_wide[:, part] = o_pair
            o_tmp[:, :, part] = o_pair.astype(BF).reshape(2, span // 2, WIDE)
            total = m_ref[p] + jnp.log(l_ref[p])
            logs = jnp.where(lane == 2 * p, total[:span], logs)
            logs = jnp.where(lane == 2 * p + 1, total[span:], logs)
        lse_out[...] = logs
        links.send(o_tmp.at[1 - h], o_low.at[h], ko, ydev)
        o_low[h] = o_tmp[h]

    def unstack(v, hh, target):
        v = v.astype(F32).reshape(NZ * NX * NC, 2 * feature, gw)
        for half in range(2):
            target[hh * gw : (hh + 1) * gw, half * gw : (half + 1) * gw] = (
                v[:, half * feature : (half + 1) * feature, :].reshape(gw, gw).astype(BF)
            )

    def relay(i):
        for hh in range(NH):
            if i < 5:
                unstack(wp[i, hh], hh, wc.at[i])
            else:
                unstack(wf[i - 5, hh], hh, w1.at[i - 5])
        if i < 5:
            keep(4 + i, wc.at[i], wc_out.at[i])

    def encoder():
        enc_rows = kc.shape[0]

        @pl.loop(0, 2)
        def _(i):
            at = pl.ds(pl.multiple_of(i * (enc_rows // 2), 16), enc_rows // 2)
            e = en[i].reshape(enc_rows // 2, width)
            kc[at, :] = dot(e, wc[2]).astype(BF)
            vc[at, :] = (dot(e, wc[3]) + prm[10:11]).astype(BF)

        keep(9, kc, kc_out)
        keep(10, vc, vc_out)

    def after_self():
        links.copy(o_low.at[1 - h], o_low.at[1 - h], ko, ydev).wait_recv()
        total = hid[...].astype(F32) + dot(o_low[0], wc[0, 0:gw, :]) + dot(o_low[1], wc[0, gw:width, :]) + prm[8:9]
        x1[...] = total
        n, _unused = norm_stats(total)
        cn[...] = (n * prm[1:2] + prm[4:5]).astype(BF)
        qc[...] = ((dot(cn[...], wc[1]) + prm[9:10]).astype(BF).astype(F32) * SCORE_SCALE).astype(BF)
        cross_lse[...] = jnp.zeros_like(cross_lse)

    def cross(n):
        @pl.loop(2 * n, 2 * n + 2)
        def _(p):
            part = pl.ds(pl.multiple_of(p * WIDE, WIDE), WIDE)
            s = dot_nt(stack_pair(qc[:, part]), kc[:, part])
            top = jnp.max(s, axis=-1, keepdims=True)
            w = jnp.exp(s - top)
            total = jnp.sum(w, axis=-1, keepdims=True)
            cross_lse[...] = jnp.where(lane == p, top + jnp.log(total), cross_lse[...])
            oc[:, part] = unstack_pair(dot((w / total).astype(BF), vc[:, part])).astype(BF)

    def after_cross():
        total = x1[...] + dot(oc[...], wc[4]) + prm[11:12]
        dx2_out[...] = total
        n, _unused = norm_stats(total)
        ff[h] = (n * prm[2:3] + prm[5:6]).astype(BF)
        links.send(ff.at[h], ff.at[h], kn, ydev)
        row_sums[...] = jnp.zeros_like(row_sums)

    kn, kyz = links.slot(), links.slot()
    tile_copies = []

    def inner_start():
        own_g.wait()
        links.copy(dy3.at[1 - h], dy3.at[1 - h], kg, ydev).wait_recv()
        for j in range(tiles):
            w2_tile = w2[2 * j : 2 * j + 2].reshape(width, width)
            slope[j] = dot_nt(dy3[...].reshape(span, width), w2_tile)
        links.copy(ff.at[1 - h], ff.at[1 - h], kn, ydev).wait_recv()

    def inner_units():
        f_all = ff[...].reshape(span, width)
        for j in range(tiles):
            at = pl.multiple_of(h * (tiles * width) + j * width, 128)
            u = dot(f_all, w1[j]) + fb[:, pl.ds(at, width)]
            phi = 0.5 * (1.0 + lax.erf(u * SQRT_HALF))
            act[j] = (u * phi).astype(BF)
            du[j] = (slope[j] * (phi + u * (DENSITY * jnp.exp(-0.5 * u * u)))).astype(BF)
        for j in range(tiles):
            term = dot_nt(du[j], w1[j])
            dza[...] = term if j == 0 else dza[...] + term
        yz_send[...] = dza[...].astype(BF).reshape(2, span // 2, width)
        links.send(yz_send.at[1 - h], yz_recv, kyz, ydev)
        for j in range(tiles):
            term = dot(act[j], w2[2 * j : 2 * j + 2].reshape(width, width))
            ya[...] = term if j == 0 else ya[...] + term
        own_half = pl.ds(pl.multiple_of(h * (span // 2), 8), span // 2)
        other_half = pl.ds(pl.multiple_of((1 - h) * (span // 2), 8), span // 2)
        out_part[...] = dx2_out[...] + ya[own_half, :] + prm[12:13]
        out_send[...] = ya[other_half, :].astype(BF)

    def inner_grads():
        f_all = ff[...].reshape(span, width)
        for j in range(tiles):
            row_sums[pl.ds(pl.multiple_of(16 + 8 * (h * tiles + j), 8), 1), :] = column_total(du[j])
            for hh in range(NH):
                halves = [
                    dot_tn(f_all[:, hh * gw : (hh + 1) * gw], du[j, :, half * gw : (half + 1) * gw]).reshape(
                        NZ * NX * NC, feature, gw
                    )
                    for half in range(2)
                ]
                g1_tile[j, hh] = jnp.concatenate(halves, axis=1).astype(BF).reshape(NZ, NX, NC, 2 * feature, gw)
            tile_copies.append(pltpu.make_async_copy(g1_tile.at[j], g1.at[j], store.at[11 + 2 * j]))
            tile_copies[-1].start()
            g2_tile[j] = dot_tn(act[j], dy3[...].reshape(span, width)).astype(BF).reshape(g2_tile.shape[1:])
            tile_copies.append(pltpu.make_async_copy(g2_tile.at[j], g2.at[pl.ds(2 * j, 2)], store.at[12 + 2 * j]))
            tile_copies[-1].start()

    def finish():
        links.copy(yz_recv, yz_recv, kyz, ydev).wait_recv()
        mine = pl.ds(pl.multiple_of(h * (span // 2), 8), span // 2)
        x2 = dx2_out[...]
        back, d_gain, d_shift = norm_back(dza[mine, :] + yz_recv[...].astype(F32), prm[2:3], x2)
        row_sums[2:3, :], row_sums[5:6, :] = d_gain, d_shift
        row_sums[12:13, :] = column_total(g_in[...])
        dx2_out[...] = g_in[...].astype(F32) + back
        for cp in tile_copies + kept:
            cp.wait()

    steps = {
        GO: pipes.go, PACK: lambda n: pack(), SWAP: swap, UNPACK: lambda n: small_done(), PROJECTION: lambda n: projection(), WORK: work,
        SELF_DONE: lambda n: self_done(), RELAY: relay, ENC: lambda n: encoder(), MID: lambda n: after_self(),
        CROSS: cross, LATE: lambda n: after_cross(),
        INNER: lambda n: (inner_start, inner_units, inner_grads)[n](), FINISH: lambda n: finish(),
    }
    for name, n in FIRST_ORDER:
        steps[name](n)
    links.drain()


FIRST_SEMS = 150


def run_first(hid, g_in, enc, *params):
    rows, width = hid.shape
    w2_in = params[-1]
    span = 2 * rows
    total = span * NZ * NX * NC
    gw = PAIRS * WIDE
    grid = (NH, NZ, NX, NC)
    devices = NH * NZ * NX * NC
    feature = width // devices
    enc_rows = enc.shape[0] * devices
    inner_width = w2_in.shape[0] * devices
    tiles = inner_width // width // NH
    hbm, vmem = pl.BlockSpec(memory_space=pl.ANY), pl.BlockSpec(memory_space=pltpu.VMEM)
    S = jax.ShapeDtypeStruct
    shard = (2 * feature, gw)
    wq_shape = (feature, 3 * gw)
    outs_hbm = (
        S((width, 3 * gw), BF), S((total, gw), BF), S((total, gw), BF), S((total, gw), BF),
        S((5, width, width), BF), S((enc_rows, width), BF), S((enc_rows, width), BF),
        S((tiles,) + grid + shard, BF), S(grid[1:] + w2_in.shape, BF),
    )
    outs_vmem = (
        S((128, width), F32), S((span, width), BF), S((span, gw), F32), S((2, rows, gw), BF), S((span, 128), F32),
        S((rows, width), F32), S((rows, width), BF), S((rows, width), F32), S((rows, width), F32), S((rows, width), BF), S((rows, width), BF),
        S((rows, width), BF), S((span, 128), F32), S((16 + 8 * tiles * NH, width), F32), S(grid + enc.shape, BF),
    )
    V = pltpu.VMEM
    return pl.pallas_call(
        first_kernel,
        out_shape=outs_hbm + outs_vmem,
        in_specs=[vmem] * 14,
        out_specs=(hbm,) * len(outs_hbm) + (vmem,) * len(outs_vmem),
        scratch_shapes=[
            V((2,) + wq_shape, BF), V((5,) + shard, BF), V((2, tiles) + shard, BF), V((32, 128), BF), V((128, 128), F32),
            V((NZ, NX, NC, NH, rows, width), BF), V(grid + wq_shape, BF), V(grid + (32, 128), BF),
            V((5,) + grid + shard, BF), V((tiles,) + grid + shard, BF), V(grid[1:] + w2_in.shape, BF),
            V((width, 3 * gw), BF), V((total, gw), BF), V((total, gw), BF), V((total, gw), BF),
            V((PAIRS, 2 * span, WIDE), BF), V((PAIRS, 2 * span, 128), F32), V((PAIRS, 2 * span, 128), F32),
            V((PAIRS, 2 * span, WIDE), F32), V((2, rows, gw), BF),
            V((5, width, width), BF), V((tiles, width, width), BF), V((enc_rows, width), BF), V((enc_rows, width), BF),
            V((1, inner_width), F32), V((2, rows, width), BF), V((2, rows, width), BF),
            V((tiles, span, width), F32), V((tiles, span, width), BF), V((tiles, span, width), BF), V((span, width), F32), V((span, width), F32),
            V((2, rows, width), BF), V((rows, width), BF),
            V((tiles,) + grid + shard, BF), V((tiles, 2, NX, NC) + w2_in.shape, BF),
            pltpu.SemaphoreType.DMA((FIRST_SEMS,)), pltpu.SemaphoreType.DMA((FIRST_SEMS,)),
            pltpu.SemaphoreType.DMA((len(FIRST_PARTS) + 3,)), pltpu.SemaphoreType.DMA((16,)),
        ],
        compiler_params=pltpu.CompilerParams(
            collective_id=0, has_side_effects=True, vmem_limit_bytes=63 << 20
        ),
        cost_estimate=pl.CostEstimate(flops=10**10, bytes_accessed=10**8, transcendentals=10**7),
        name="gather_and_forward",
    )(hid, g_in, enc, *params)


def norm_back(dz, gain, v):
    n, inv = norm_stats(v)
    dn = dz * gain
    result = (dn - jnp.mean(dn, axis=-1, keepdims=True) - n * jnp.mean(dn * n, axis=-1, keepdims=True)) * inv
    return result, jnp.sum(dz * n, axis=0, keepdims=True), jnp.sum(dz, axis=0, keepdims=True)


def column_total(v):
    return jnp.sum(v.astype(F32), axis=0, keepdims=True)


SQRT_HALF = 0.7071067811865476
DENSITY = 0.3989422804014327


def shard_loop(shape, fn):
    count = 1
    for n in shape:
        count *= n

    @pl.loop(0, count)
    def _(i):
        index = []
        for n in reversed(shape):
            index.append(i % n)
            i = i // n
        fn(tuple(reversed(index)))


def add_into(target, source):
    target[...] = (target[...].astype(F32) + source[...].astype(F32)).astype(BF)


WHOLE, PAIRED, SINGLE = ("y", "z", "x"), ("l", "z", "x"), ("z", "x")
EXTENT = {"y": NH, "l": NH, "z": NZ, "x": NX}


def reduce_stages(links, source, axes, order, here, bufs, local_sem, store, ydev=None):
    h, z, x, c = here
    every = slice(None)
    me = {"y": h, "z": z, "x": x}
    bufs = list(bufs)
    if local_sem is None:
        mine = source(c)
    else:
        mine = bufs.pop(0)
        local = pltpu.make_async_copy(source(c), mine, local_sem)
    from_core = bufs.pop(0)
    k_core = links.slot()
    core = device_at(h, z, x, 1 - c)

    def start():
        links.send(source(1 - c), from_core, k_core, core)
        if local_sem is not None:
            local.start()

    def after_core():
        if local_sem is not None:
            local.wait()
        links.copy(from_core, from_core, k_core, core).wait_recv()
        shard_loop([EXTENT[a] for a in axes], lambda i: add_into(mine.at[i], from_core.at[i]))

    fixed = {}
    stages = []
    for axis in order:
        buf = bufs.pop(0)
        open_axes = [a for a in axes if a not in fixed and a != axis]

        def at(**values):
            known = {**fixed, **values}
            return tuple(known.get(a, every) for a in axes)

        if axis == "z":
            routes = [
                (links.slot(), device_at(h, (z + d) % NZ, x, c), mine.at[at(z=(z + d) % NZ)], buf.at[d - 1])
                for d in (1, 2, 3)
            ]
        elif axis == "x":
            routes = [(links.slot(), device_at(h, z, 1 - x, c), mine.at[at(x=1 - x)], buf)]
        else:
            routes = [(links.slot(), device_at(1 - h, z, x, c), mine.at[at(y=1 - h)], buf)]

        def go(routes=routes):
            for k, device, away, target in routes:
                links.send(away, target, k, device)

        def come(routes=routes):
            for k, device, _away, target in routes:
                links.copy(target, target, k, device).wait_recv()

        fixed[axis] = me[axis]
        base = dict(fixed)

        def add(routes=routes, open_axes=open_axes, base=base):
            def one(i):
                known = {**base, **dict(zip(open_axes, i))}
                slot = mine.at[tuple(known[a] for a in axes)]
                total = slot[...].astype(F32)
                for _k, _device, _away, target in routes:
                    total = total + target[i].astype(F32)
                slot[...] = total.astype(BF)

            shard_loop([EXTENT[a] for a in open_axes], one)

        def total_of(lead, routes=routes, base=base):
            known = {**base, "l": lead}
            total = mine[tuple(known[a] for a in axes)].astype(F32)
            for _k, _device, _away, target in routes:
                total = total + (target[lead] if "l" in axes else target[...]).astype(F32)
            return total

        stages.append((go, come, add, total_of))

    made = [start, lambda: (after_core(), stages[0][0]())]
    for (_g, come, add, _t), (go, _c, _a, _t2) in zip(stages, stages[1:]):
        made.append(lambda come=come, add=add, go=go: (come(), add(), go()))
    _g, come, _a, total_of = stages[-1]
    if "l" not in axes:
        return made + [lambda: (come(), store(None, total_of(None)))]
    out, back = bufs
    k_swap = links.slot()

    def swap():
        come()
        store(h, total_of(h))
        out[...] = total_of(1 - h).astype(BF)
        links.send(out, back, k_swap, ydev)

    def finish():
        links.copy(back, back, k_swap, ydev).wait_recv()
        store(1 - h, back[...].astype(F32))

    return made + [swap, finish]


def reduce_bufs(shard, axes, order, own):
    sizes = [tuple(EXTENT[a] for a in axes)] * (2 if own else 1)
    left = list(axes)
    for axis in order:
        left.remove(axis)
        sizes.append((NZ - 1,) * (axis == "z") + tuple(EXTENT[a] for a in left))
    if "l" in axes:
        sizes += [(), ()]
    return [pltpu.VMEM(size + shard, BF) for size in sizes]


XYZ, YXZ = XY + ("z",), YX + ("z",)
KV_ORDER = (XZ, XZ, XZ)
LAST_PARTS = (
    (ENCODED, 0, YXZ), (COLUMNS, 0, YXZ), (ROWS, 2, XZ), (INNER_COLUMNS, 0, XZ), (COLUMNS, 2, YXZ), (INNER_COLUMNS, 1, ZX),
    (ROWS, 0, ZX), (COLUMNS, 4, YXZ), (ENCODED, 1, YXZ), (COLUMNS, 3, XYZ), (COLUMNS, 1, YXZ), (ROWS, 1, ZX),
)
LAST_ORDER = (
    (GO, 2), (GO, 6), (DOC, 0), (GO, 2), (GO, 6), (CROSS_PAIRS, 0), (GO, 11), (CROSS_PAIRS, 1), (GO, 2), (GO, 11),
    (CROSS_PAIRS, 2), (DX1, 0), (GO, 1), (GO, 6), (ENC, 0), (GO, 1), (GO, 2), (GO, 6), (GO, 9), (GO, 10), (OWN, 0), (GO, 12),
    (GO, 13), (GO, 9), (GO, 10), (GO, 7), (ENC, 1), (GO, 12), (GO, 14), (GO, 1), (GO, 7), (GO, 11), (OWN, 1), (BY_QUERY, 0),
    (GO, 9), (BY_QUERY, 1), (GO, 12), (GO, 13), (GO, 15), (BY_QUERY, 2), (GO, 12), (GO, 4), (GO, 10), (BY_QUERY, 3),
    (BY_QUERY, 4), (GO, 1), (GO, 4), (GO, 11), (BY_QUERY, 5), (BY_QUERY, 6), (GO, 14), (GO, 8), (BY_QUERY, 7), (BY_QUERY, 8),
    (GO, 7), (GO, 8), (BY_QUERY, 9), (BY_QUERY, 10), (BY_QUERY, 11), (GO, 13), (GO, 9), (GO, 3), (GO, 5), (GO, 15),
    (QUERY_DONE, 0), (GO, 13), (GO, 16), (GO, 3), (GO, 10), (GO, 1), (GO, 16), (GO, 5), (BY_KEY, 0), (GO, 4), (GO, 9),
    (BY_KEY, 3), (GO, 14), (BY_KEY, 6), (GO, 8), (GO, 14), (GO, 10), (GO, 7), (BY_KEY, 9), (KEY_DONE, 0), (GO, 17), (BY_KEY, 1),
    (GO, 17), (BY_KEY, 4), (GO, 15), (BY_KEY, 7), (BY_KEY, 10), (GO, 15), (KEY_DONE, 1), (GO, 18), (BY_KEY, 2), (GO, 18),
    (GO, 3), (GO, 5), (GO, 0), (BY_KEY, 5), (GO, 7), (GO, 16), (GO, 0), (BY_KEY, 8), (BY_KEY, 11), (GO, 4), (KEY_DONE, 2),
    (GO, 19), (GO, 8), (KEY_DONE, 3), (GO, 3), (GO, 19), (GO, 0), (GO, 17), (GO, 16), (GO, 18), (GO, 5), (INPUT_GRAD, 0),
    (GO, 20), (GO, 19), (GO, 16), (GO, 3), (GO, 20), (GO, 0), (GO, 4), (GO, 5), (GO, 17), (GO, 8), (HIDDEN_OUT, 0), (GO, 20),
    (GO, 17), (GO, 18), (GO, 20), (GO, 18), (GO, 19), (GO, 0), (GO, 19), (GO, 20),
)

def last_kernel(
    out_part, out_send, hid, prm, a_span, o_wide, o_low, lse, x1, dx2, cn, qc, oc, cross_lse, row_sums,
    en_in, wq_in, keys_in, vals_in, queries_in, wc_in, kc_in, vc_in, gf1, gf2,
    hidden_out, hidden_grad, out_o, out_cq, out_ckv, out_co, out_fi, out_f, out_e, out_q, out_s,
    y_recv, wk, pool, gc, ge, doc, dqc, dx1, do_low,
    do_all, st_all, q2, k2, v2, do2, dq2, dk2, dv2, dz_q, gq, gkv, gs, fbs, dz_send, dz_recv, send, recv, local, loads, *bufs,
):
    here = place()
    h, z, x, c = here
    links = Links(send, recv)
    every = slice(None)
    rows, width = hid.shape
    span = 2 * rows
    group = 4 * span
    gw = PAIRS * WIDE
    devices = NH * NZ * NX * NC
    feature = width // devices
    e_shard, f_shard = ge.shape[4], gf2.shape[3]
    enc_rows = devices * e_shard
    total_rows = keys_in.shape[0]
    ydev = device_at(1 - h, z, x, c)
    kc, vc, dkc, dvc = (pool.at[pl.ds(i * enc_rows, enc_rows)] for i in range(4))
    wc = [wk.at[pl.ds(i * width, width)] for i in range(5)]
    queries, wq = pool.at[:, pl.ds(0, gw)], [pool.at[pl.ds(i * width, width), pl.ds(gw, gw)] for i in range(3)]
    fetches = [pltpu.make_async_copy(wc_in.at[i], wc[i], loads.at[i]) for i in range(5)]
    fetches += [
        pltpu.make_async_copy(source, target, loads.at[5 + i])
        for i, (source, target) in enumerate([(kc_in, kc), (vc_in, vc), (en_in, ge)])
    ]
    for cp in fetches:
        cp.start()
    late = [
        pltpu.make_async_copy(source, wk.at[pl.ds(0, total_rows), pl.ds(lo, gw)], loads.at[8 + i])
        for i, (source, lo) in enumerate(((keys_in, 0), (vals_in, gw)))
    ]
    late.append(pltpu.make_async_copy(queries_in, pool.at[pl.ds(0, total_rows), pl.ds(0, gw)], loads.at[10]))
    late += [
        pltpu.make_async_copy(wq_in.at[:, pl.ds(i * gw, gw)], wq[i], loads.at[11 + i]) for i in range(3)
    ]
    greet(*here)
    kh = links.slot()
    links.send(out_send, y_recv, kh, ydev)

    cuts = [(out_o, 0), (out_cq, 0), (out_ckv, 0), (out_ckv, width), (out_co, 0)]
    pipes = Pipes()
    used = 0
    for i, (name, n, order) in enumerate(LAST_PARTS):
        if name == COLUMNS:
            out, lo = cuts[n]
            axes, view = WHOLE, lambda c, n=n: gc.at[n, :, :, :, c]

            def keep(_l, total, out=out, lo=lo):
                out[:, lo : lo + gw] = total[0:feature]
                out[:, lo + gw : lo + 2 * gw] = total[feature : 2 * feature]
        elif name == INNER_COLUMNS:
            axes, view = PAIRED, lambda c, n=n: gf1.at[n, :, :, :, c]

            def keep(lead, total, n=n):
                out_fi[lead, n] = total
        elif name == ROWS:
            size = f_shard // 3
            axes, view = SINGLE, lambda c, lo=n * size, size=size: gf2.at[:, :, c, pl.ds(lo, size)]

            def keep(_l, total, lo=n * size, size=size):
                out_f[lo : lo + size, :] = total
        else:
            size = e_shard // 2
            axes, view = WHOLE, lambda c, lo=n * size, size=size: ge.at[:, :, :, c, pl.ds(lo, size)]

            def keep(_l, total, lo=n * size, size=size):
                out_e[lo : lo + size, :] = total
        outside = name in (ROWS, INNER_COLUMNS)
        count = len(order) + 1 + outside + 2 * (axes == PAIRED)
        pipes.add(
            reduce_stages(
                links, view, axes, order, here, bufs[used : used + count], local.at[i] if outside else None, keep, ydev
            )
        )
        used += count
    q_bufs, kv_bufs, small_bufs = bufs[used : used + 5], bufs[used + 5 : used + 20], bufs[used + 20 :]

    sums = {}
    lane = lax.broadcasted_iota(jnp.int32, (span, 128), 1)

    def to_shards(n, left, right):
        for hh in range(NH):
            halves = [
                dot_tn(left(hh), right(half)).reshape(devices // 2, feature, gw) for half in range(2)
            ]
            gc[n, hh] = jnp.concatenate(halves, axis=1).astype(BF).reshape(NZ, NX, NC, 2 * feature, gw)

    def half_of(ref, i):
        return ref[:, i * gw : (i + 1) * gw]

    def step_doc():
        dy2 = dx2[...].astype(BF)
        sums[11] = column_total(dy2)
        for cp in fetches:
            cp.wait()
        doc[...] = dot_nt(dy2, wc[4][...]).astype(BF)
        to_shards(4, lambda hh: half_of(oc, hh), lambda i: half_of(dy2, i))

    def step_pairs(n):
        @pl.loop(2 * n, 2 * n + 2)
        def _(p):
            part = pl.ds(pl.multiple_of(p * WIDE, WIDE), WIDE)
            logs = jnp.sum(jnp.where(lane == p, cross_lse[...], 0.0), axis=-1, keepdims=True)
            q_pair = stack_pair(qc[:, part])
            w = jnp.exp(dot_nt(q_pair, kc[:, part]) - logs)
            do_pair = stack_pair(doc[:, part])
            dp = dot_nt(do_pair, vc[:, part])
            ds = (w * (dp - jnp.sum(w * dp, axis=-1, keepdims=True))).astype(BF)
            dqc[:, part] = (unstack_pair(dot(ds, kc[:, part])) * SCORE_SCALE).astype(BF)
            dkc[:, part] = dot_tn(ds, q_pair).astype(BF)
            dvc[:, part] = dot_tn(w.astype(BF), do_pair).astype(BF)

    ky = links.slot()

    def step_dx1():
        dq = dqc[...]
        sums[9] = column_total(dq)
        back, sums[1], sums[4] = norm_back(dot_nt(dq, wc[1][...]), prm[1:2], x1[...])
        total = dx2[...] + back
        dx1[...] = total
        dy1 = total.astype(BF)
        sums[8] = column_total(dy1)
        for i in range(2):
            do = dot_nt(dy1, wc[0][i * gw : (i + 1) * gw, :]).astype(BF)
            for p in range(PAIRS):
                do_low[i, p] = do[:, p * WIDE : (p + 1) * WIDE]
        links.send(do_low.at[1 - h], do_all.at[every, z, x, c, h], ky, ydev)
        do_all[:, z, x, c, h] = do_low[h]
        to_shards(1, lambda hh: half_of(cn, hh), lambda i: half_of(dq, i))
        to_shards(0, lambda hh: o_low[hh], lambda i: half_of(dy1, i))

    def step_enc(n):
        if n == 1:
            for i in range(NH):
                at = pl.ds(i * (enc_rows // NH), enc_rows // NH)
                de = dot_nt(dkc[at, :], wc[2][...]) + dot_nt(dvc[at, :], wc[3][...])
                ge[i] = de.astype(BF).reshape(ge.shape[1:])
            sums[10] = column_total(dvc[...])
            for cp in late:
                cp.start()
        else:
            e_all = ge[...].reshape(enc_rows, width)
            for n, d in ((2, dkc), (3, dvc)):
                to_shards(n, lambda hh: e_all[:, hh * gw : (hh + 1) * gw], lambda i: half_of(d, i))

    l_columns, d_columns = [], []
    own_place = (x * 2 + c) * span

    def step_own(n):
        first = lane_half((span, WIDE))
        start = pl.ds(pl.multiple_of(z * group + own_place, span), span)
        if n == 1:
            for cp in late:
                cp.wait()
            for p in range(PAIRS):
                part = pl.ds(p * WIDE, WIDE)
                q2[p] = stack_pair(pool[start, part])
                k2[p] = stack_pair(wk[start, part])
                v2[p] = stack_pair(wk[start, pl.ds(gw + p * WIDE, WIDE)])
                dq2[p] = jnp.zeros_like(dq2[p])
                dk2[p] = jnp.zeros_like(dk2[p])
                dv2[p] = jnp.zeros_like(dv2[p])
            return
        got = do_all.at[every, z, x, c, 1 - h]
        links.copy(got, got, ky, ydev).wait_recv()
        deltas = jnp.zeros((span, 128), F32)
        logs = lse[...]
        for p in range(PAIRS):
            part = pl.ds(p * WIDE, WIDE)
            do = do_all[p, z, x, c].reshape(span, WIDE)
            prod = do.astype(F32) * o_wide[:, part]
            low = jnp.sum(jnp.where(first, prod, 0.0), axis=-1, keepdims=True)
            high = jnp.sum(jnp.where(first, 0.0, prod), axis=-1, keepdims=True)
            deltas = jnp.where(lane == 2 * p, low, jnp.where(lane == 2 * p + 1, high, deltas))
            d_columns.append((low, high))
            l_columns.append((logs[:, 2 * p : 2 * p + 1], logs[:, 2 * p + 1 : 2 * p + 2]))
            do2[p] = stack_pair(do)
        st_all[z, x, c, 0:8] = jnp.transpose(logs)[0:8]
        st_all[z, x, c, 8:16] = jnp.transpose(deltas)[0:8]

    pipes.add(gather_stages(links, lambda *i: st_all.at[i[1:]], ZX, here))
    for p in range(PAIRS):
        pipes.add(gather_stages(links, lambda *i, p=p: do_all.at[(p,) + i[1:]], ZX, here))

    def query_side(g, diagonal, p):
        at = pl.ds(pl.multiple_of(g * group, group), group)
        if True:
            for half in range(2):
                mine = pl.ds(half * span, span)
                k_pair, v_pair = wk[at, pl.ds(p * WIDE, WIDE)], wk[at, pl.ds(gw + p * WIDE, WIDE)]
                w = jnp.exp(dot_nt(q2[p, mine], k_pair) - l_columns[p][half])
                if diagonal:
                    place_q = own_place + lax.broadcasted_iota(jnp.int32, w.shape, 0)
                    w = jnp.where(lax.broadcasted_iota(jnp.int32, w.shape, 1) <= place_q, w, 0.0)
                ds = (w * (dot_nt(do2[p, mine], v_pair) - d_columns[p][half])).astype(BF)
                dq2[p, mine] += dot(ds, k_pair)

    def key_side(g, diagonal, p):
        at = pl.ds(pl.multiple_of(g * group, group), group)
        if True:
            part = pl.ds(p * WIDE, WIDE)
            for half in range(2):
                mine = pl.ds(half * span, span)
                head = 2 * p + half
                q_pair = pool[at, part]
                do_pair = do_all[p, g].reshape(group, WIDE)
                stats = [st_all[g, i // 2, i % 2] for i in range(4)]
                log_row = jnp.concatenate([s[head : head + 1] for s in stats], axis=1)
                delta_row = jnp.concatenate([s[8 + head : 9 + head] for s in stats], axis=1)
                w = jnp.exp(dot_nt(k2[p, mine], q_pair) - log_row)
                if diagonal:
                    place_k = own_place + lax.broadcasted_iota(jnp.int32, w.shape, 0)
                    w = jnp.where(place_k <= lax.broadcasted_iota(jnp.int32, w.shape, 1), w, 0.0)
                dv2[p, mine] += dot(w.astype(BF), do_pair)
                ds = (w * (dot_nt(v2[p, mine], do_pair) - delta_row)).astype(BF)
                dk2[p, mine] += dot(ds, q_pair)

    def side(fn, n, ahead):
        t, p = n // PAIRS, n % PAIRS
        if t == 0:
            fn(z, True, p)
        elif ahead:
            pl.when(z + t < NZ)(lambda: fn((z + t) % NZ, False, p))
        else:
            pl.when(z - t >= 0)(lambda: fn((z - t) % NZ, False, p))

    def keep_q(lead, total):
        out_q[lead, 0:feature] = total

    def keep_kv(p):
        def keep(lead, total):
            out_q[lead, feature : 3 * feature, p * WIDE : (p + 1) * WIDE] = total

        return keep

    def output():
        links.copy(y_recv, y_recv, kh, ydev).wait_recv()
        hidden_out[...] = (out_part[...] + y_recv[...].astype(F32)).astype(BF)

    def keep_small(_l, total):
        out_s[...] = total

    pipes.add(reduce_stages(links, lambda c: gq.at[:, :, :, c], PAIRED, XZ, here, q_bufs, None, keep_q, ydev))
    for p in range(PAIRS):
        view = lambda c, p=p: gkv.at[p, :, :, :, c]
        pipes.add(reduce_stages(links, view, PAIRED, KV_ORDER[p], here, kv_bufs[5 * p : 5 * p + 5], None, keep_kv(p), ydev))
    pipes.add(reduce_stages(links, lambda c: gs.at[:, :, :, c], WHOLE, YXZ, here, small_bufs, None, keep_small))
    kz = links.slot()

    def query_done():
        dq = jnp.concatenate([unstack_pair(dq2[p]) * SCORE_SCALE for p in range(PAIRS)], axis=1).astype(BF)
        sums[6] = column_total(dq)
        gq[...] = dot_tn(a_span[...], dq).astype(BF).reshape(gq.shape)
        dz_q[...] = dot_nt(dq, wq[0][...])

    v_sums = []

    def key_done(p):
        if p == PAIRS:
            sums[7] = jnp.concatenate(v_sums, axis=1)
            dz_send[...] = dz_q[...].astype(BF).reshape(2, rows, width)
            links.send(dz_send.at[1 - h], dz_recv, kz, ydev)
            return
        part = pl.ds(p * WIDE, WIDE)
        dk, dv = unstack_pair(dk2[p]).astype(BF), unstack_pair(dv2[p]).astype(BF)
        v_sums.append(column_total(dv))
        whole = [dot_tn(a_span[...], d).reshape(devices, feature, WIDE) for d in (dk, dv)]
        gkv[p] = jnp.concatenate(whole, axis=1).astype(BF).reshape(gkv.shape[1:])
        dz_q[...] += dot_nt(dk, wq[1][:, part]) + dot_nt(dv, wq[2][:, part])

    def input_grad():
        links.copy(dz_recv, dz_recv, kz, ydev).wait_recv()
        dz_own = dz_send[h].astype(F32) + dz_recv[...].astype(F32)
        back, sums[0], sums[3] = norm_back(dz_own, prm[0:1], hid[...].astype(F32))
        hidden_grad[...] = dx1[...] + back
        for i in (6, 7):
            sums[i] = jnp.concatenate([jnp.where(h == k, sums[i], 0.0) for k in range(2)], axis=1)
        block = row_sums[0:16]
        row = lax.broadcasted_iota(jnp.int32, block.shape, 0)
        for i, value in sums.items():
            block = jnp.where(row == i, value, block)
        wide = jnp.concatenate([block, jnp.zeros((128 - 16, width), F32)], axis=0)
        by_feature = jnp.transpose(wide).reshape(devices, feature, 128)
        fbs[...] = jnp.zeros_like(fbs)
        each = width // f_shard
        for d in range(devices):
            at = 16 + 8 * (d // each)
            fbs[d : d + 1, 0:f_shard] = row_sums[at : at + 1, (d % each) * f_shard : (d % each + 1) * f_shard]
        fb = jnp.broadcast_to(fbs[...][:, None, :], (devices, 8, 128))
        gs[...] = jnp.concatenate([by_feature, fb], axis=1).astype(BF).reshape(gs.shape)

    steps = {
        GO: pipes.go, DOC: lambda n: step_doc(), CROSS_PAIRS: step_pairs, DX1: lambda n: step_dx1(), ENC: step_enc,
        OWN: step_own, HIDDEN_OUT: lambda n: output(), BY_QUERY: lambda n: side(query_side, n, False), BY_KEY: lambda n: side(key_side, n, True),
        QUERY_DONE: lambda n: query_done(), KEY_DONE: key_done, INPUT_GRAD: lambda n: input_grad(),
    }
    for name, n in LAST_ORDER:
        steps[name](n)
    links.drain()


LAST_SEMS = 160


def run_last(vmem_args, hbm_args):
    hid, en, keys, gf1, gf2 = vmem_args[2], hbm_args[0], hbm_args[2], hbm_args[8], hbm_args[9]
    rows, width = hid.shape
    span = 2 * rows
    gw = PAIRS * WIDE
    grid = (NH, NZ, NX, NC)
    devices = NH * NZ * NX * NC
    feature = width // devices
    e_rows, f_rows = en.shape[4], gf2.shape[3]
    enc_rows = e_rows * devices
    hbm, vmem = pl.BlockSpec(memory_space=pl.ANY), pl.BlockSpec(memory_space=pltpu.VMEM)
    S = jax.ShapeDtypeStruct
    V = pltpu.VMEM
    outs = (
        S((rows, width), BF), S((rows, width), F32), S((feature, width), F32), S((feature, width), F32), S((feature, 2 * width), F32),
        S((feature, width), F32), S((NH, gf1.shape[0], 2 * feature, gw), F32), S((f_rows, width), F32), S((e_rows, width), F32),
        S((2, 3 * feature, gw), F32), S((32, 128), F32),
    )
    shard = (2 * feature, gw)
    bufs = []
    for name, n, order in LAST_PARTS:
        size = {COLUMNS: shard, INNER_COLUMNS: shard, ROWS: (f_rows // 3, width), ENCODED: (e_rows // 2, width)}[name]
        axes = {INNER_COLUMNS: PAIRED, ROWS: SINGLE}.get(name, WHOLE)
        bufs += reduce_bufs(size, axes, order, name in (ROWS, INNER_COLUMNS))
    q_shard, kv_shard = (feature, gw), (2 * feature, WIDE)
    bufs += reduce_bufs(q_shard, PAIRED, XZ, False)
    for p in range(PAIRS):
        bufs += reduce_bufs(kv_shard, PAIRED, KV_ORDER[p], False)
    bufs += reduce_bufs((32, 128), WHOLE, YXZ, False)
    stacked, stacked_f = V((PAIRS, 2 * span, WIDE), BF), V((PAIRS, 2 * span, WIDE), F32)
    D = pltpu.SemaphoreType.DMA
    return pl.pallas_call(
        last_kernel,
        out_shape=outs,
        in_specs=[vmem] * len(vmem_args) + [hbm] * len(hbm_args),
        out_specs=(vmem,) * len(outs),
        scratch_shapes=[
            V((rows, width), BF), V((max(keys.shape[0], 5 * width), width), BF), V((max(keys.shape[0], 4 * enc_rows), width), BF),
            V((5,) + grid + shard, BF), V(en.shape, BF), V((rows, width), BF), V((rows, width), BF), V((rows, width), F32), V((2, PAIRS, rows, WIDE), BF),
            V((PAIRS, NZ, NX, NC, 2, rows, WIDE), BF), V((NZ, NX, NC, 16, span), F32),
            stacked, stacked, stacked, stacked, stacked_f, stacked_f, stacked_f,
            V((span, width), F32), V(grid + q_shard, BF), V((PAIRS,) + grid + kv_shard, BF), V(grid + (32, 128), BF), V((devices, 128), F32),
            V((2, rows, width), BF), V((rows, width), BF),
            D((LAST_SEMS,)), D((LAST_SEMS,)), D((len(LAST_PARTS),)), D((14,)),
        ] + bufs,
        compiler_params=pltpu.CompilerParams(
            collective_id=1, has_side_effects=True, vmem_limit_bytes=63 << 20
        ),
        cost_estimate=pl.CostEstimate(flops=2 * 10**10, bytes_accessed=10**8, transcendentals=10**7),
        name="backward_and_reduce",
    )(*vmem_args, *hbm_args)


def deliver_kernel(
    hidden_out, hidden_grad, o, cq, ckv, co, fi_in, f, e, qkv_in, small_in,
    out_hidden, out_grad, out_e, gains, shifts, biases, out_qkv, out_o, out_cq, out_ckv, out_co, out_fi, out_bias, out_f,
    fi, qkv, small, sems,
):
    pairs = (
        (hidden_out, out_hidden.at[0, 0]), (hidden_grad, out_grad.at[0, 0]), (e, out_e.at[0]), (o, out_o), (cq, out_cq),
        (ckv, out_ckv), (co, out_co), (f, out_f), (fi_in, fi), (qkv_in, qkv), (small_in, small),
    )
    copies = [pltpu.make_async_copy(source, target, sems.at[i]) for i, (source, target) in enumerate(pairs)]
    for cp in copies:
        cp.start()
    for cp in copies:
        cp.wait()
    gw = qkv.shape[2]
    feature = qkv.shape[1] // 3
    for k in range(2):
        for i in range(3):
            lo = (2 * i + k) * gw
            out_qkv[:, lo : lo + gw] = qkv[k, i * feature : (i + 1) * feature, :]
    tiles = fi.shape[1]
    for k in range(2):
        for j in range(tiles):
            for half in range(2):
                lo = ((k * tiles + j) * 2 + half) * gw
                out_fi[:, lo : lo + gw] = fi[k, j, half * feature : (half + 1) * feature, :]
    by_row = jnp.transpose(jnp.concatenate([small[...], jnp.zeros((128 - small.shape[0], 128), F32)], axis=0))
    gains[...] = by_row[0:3, 0:feature]
    shifts[...] = by_row[3:6, 0:feature]
    biases[...] = by_row[6:13, 0:feature]
    out_bias[...] = small[feature : feature + 1, 0 : out_bias.shape[1]]


def run_deliver(hidden_out, hidden_grad, o, cq, ckv, co, fi, f, e, qkv, small):
    S = jax.ShapeDtypeStruct
    feature, width = o.shape
    inner = fi.shape[0] * fi.shape[1] * width
    outs = (
        S((1, 1) + hidden_out.shape, BF), S((1, 1) + hidden_grad.shape, F32), S((1,) + e.shape, F32),
        S((3, feature), F32), S((3, feature), F32), S((7, feature), F32), S((feature, 3 * width), F32),
        S(o.shape, F32), S(cq.shape, F32), S(ckv.shape, F32), S(co.shape, F32), S((feature, inner), F32), S((1, f.shape[0]), F32), S(f.shape, F32),
    )
    hbm, vmem = pl.BlockSpec(memory_space=pltpu.HBM), pl.BlockSpec(memory_space=pltpu.VMEM)
    return pl.pallas_call(
        deliver_kernel, out_shape=outs, in_specs=[hbm] * 11, out_specs=(vmem,) * len(outs),
        scratch_shapes=[
            pltpu.VMEM(fi.shape, F32), pltpu.VMEM(qkv.shape, F32), pltpu.VMEM(small.shape, F32), pltpu.SemaphoreType.DMA((11,)),
        ],
        compiler_params=pltpu.CompilerParams(vmem_limit_bytes=62 << 20), name="deliver",
    )(hidden_out, hidden_grad, o, cq, ckv, co, fi, f, e, qkv, small)


def fused_body(
    hidden_in, encoded, out_grad, ln_gain, ln_bias, biases, self_qkv, self_out, cross_q,
    cross_kv, cross_out, ffn_in, ffn_bias, ffn_out,
):
    got = run_first(
        hidden_in[0, 0], out_grad[0, 0], encoded[0], ln_gain, ln_bias, biases, self_qkv, self_out, cross_q, cross_kv,
        cross_out, ffn_in, ffn_bias[None], ffn_out,
    )
    prm, a_span, o_wide, o_low, lse, out_part, out_send, x1, dx2, cn, qc, oc, cross_lse, row_sums, en = got[9:]
    grads = run_last(
        (out_part, out_send, hidden_in[0, 0], prm, a_span, o_wide, o_low, lse, x1, dx2, cn, qc, oc, cross_lse, row_sums), (en,) + tuple(got[:9])
    )
    done = run_deliver(*grads)
    return done[:12] + (done[12][0], done[13])


def solution(mesh):
    fused = mesh.shape["head"] == NH and mesh.shape["blk"] == NZ * NX * NC
    return jax.shard_map(
        fused_body if fused else body,
        mesh=mesh,
        in_specs=(
            P(None, "blk", "head", None),
            P(None, ("head", "blk"), None),
            P(None, "blk", "head", None),
            P(None, ("head", "blk")),
            P(None, ("head", "blk")),
            P(None, ("head", "blk")),
            P(("head", "blk"), None),
            P(("head", "blk"), None),
            P(("head", "blk"), None),
            P(("head", "blk"), None),
            P(("head", "blk"), None),
            P(("head", "blk"), None),
            P(("head", "blk")),
            P(("head", "blk"), None),
        ),
        out_specs=(
            P(None, "blk", "head", None),
            P(None, "blk", "head", None),
            P(None, ("head", "blk"), None),
            P(None, ("head", "blk")),
            P(None, ("head", "blk")),
            P(None, ("head", "blk")),
            P(("head", "blk"), None),
            P(("head", "blk"), None),
            P(("head", "blk"), None),
            P(("head", "blk"), None),
            P(("head", "blk"), None),
            P(("head", "blk"), None),
            P(("head", "blk")),
            P(("head", "blk"), None),
        ),
        check_vma=False,
    )
```

```python
import jax
import jax.numpy as jnp
from jax import lax
from jax.experimental import pallas as pl
from jax.experimental.pallas import tpu as pltpu
from jax.sharding import PartitionSpec as P

HEADS = 12
HEAD_DIM = 64


EPSILON = 1e-05
SCORE_SCALE = 0.125


def from_behind(block, axis, distance):
    devices = range(lax.axis_size(axis))
    route = [((i - distance) % len(devices), i) for i in devices]
    return lax.ppermute(block, axis, route)


def layer_norm(values, gain_row, shift_row):
    centered = values - jnp.mean(values, axis=-1, keepdims=True)
    spread = jnp.mean(centered * centered, axis=-1, keepdims=True)
    return centered * lax.rsqrt(spread + EPSILON) * gain_row + shift_row


def norm_grads(values, gain_row, shift_row, upstream):
    result, pullback = jax.vjp(layer_norm, values, gain_row, shift_row)
    return pullback(upstream)


def exact_gelu(values):
    return jax.nn.gelu(values, approximate=False)


def project(left, right):
    return jnp.einsum("srk,kn->srn", left, right, preferred_element_type=jnp.float32)


def project_back(upstream, weight):
    return jnp.einsum("srn,kn->srk", upstream, weight, preferred_element_type=jnp.float32)


def weight_grad(left, upstream):
    return jnp.einsum("srk,srn->kn", left, upstream, preferred_element_type=jnp.float32)


def column_sum(upstream):
    return jnp.sum(upstream.astype(jnp.float32), axis=(0, 1))


def block_scores(queries, key_block, query_start, key_start):
    scores = (
        jnp.einsum("sqhd,skhd->shqk", queries, key_block, preferred_element_type=jnp.float32)
        * SCORE_SCALE
    )
    query_place = query_start + lax.iota(jnp.int32, queries.shape[1])
    key_place = key_start + lax.iota(jnp.int32, key_block.shape[1])
    allowed = key_place[None, :] <= query_place[:, None]
    return (scores, allowed)


def forward_block(carried, key_block, value_block, queries, query_start, key_start):
    row_top, row_total, weighted = carried
    scores, allowed = block_scores(queries, key_block, query_start, key_start)
    scores = jnp.where(allowed, scores, -jnp.inf)
    new_top = jnp.maximum(row_top, jnp.max(scores, axis=-1))
    weights = jnp.exp(scores - new_top[..., None])
    factor = jnp.exp(row_top - new_top)
    row_total = row_total * factor + jnp.sum(weights, axis=-1)
    addition = jnp.einsum(
        "shqk,skhd->sqhd",
        weights.astype(jnp.bfloat16),
        value_block,
        preferred_element_type=jnp.float32,
    )
    weighted = weighted * jnp.transpose(factor, (0, 2, 1))[..., None] + addition
    return (new_top, row_total, weighted)


def backward_block(
    queries, out_grads, log_total, row_delta, key_block, value_block, query_start, key_start
):
    scores, allowed = block_scores(queries, key_block, query_start, key_start)
    weights = jnp.where(allowed, jnp.exp(scores - log_total[..., None]), 0.0)
    value_grad = jnp.einsum(
        "shqk,sqhd->skhd",
        weights.astype(jnp.bfloat16),
        out_grads,
        preferred_element_type=jnp.float32,
    )
    prob_grad = jnp.einsum(
        "sqhd,skhd->shqk", out_grads, value_block, preferred_element_type=jnp.float32
    )
    score_grad = (weights * (prob_grad - row_delta[..., None])).astype(jnp.bfloat16)
    query_grad = jnp.einsum(
        "shqk,skhd->sqhd", score_grad, key_block, preferred_element_type=jnp.float32
    )
    key_grad = jnp.einsum(
        "shqk,sqhd->skhd", score_grad, queries, preferred_element_type=jnp.float32
    )
    return (query_grad, key_grad, value_grad)


def cross_forward(operands):
    queries, key_rows, value_rows = operands
    scores = (
        jnp.einsum("qhd,khd->hqk", queries, key_rows, preferred_element_type=jnp.float32)
        * SCORE_SCALE
    )
    row_top = jnp.max(scores, axis=-1, keepdims=True)
    weights = jnp.exp(scores - row_top)
    row_total = jnp.sum(weights, axis=-1, keepdims=True)
    weights_low = (weights / row_total).astype(jnp.bfloat16)
    attended = jnp.einsum(
        "hqk,khd->qhd", weights_low, value_rows, preferred_element_type=jnp.float32
    )
    return (attended, (row_top + jnp.log(row_total))[..., 0])


def cross_backward(operands):
    queries, key_rows, value_rows, log_total, out_grads = operands
    scores = (
        jnp.einsum("qhd,khd->hqk", queries, key_rows, preferred_element_type=jnp.float32)
        * SCORE_SCALE
    )
    weights = jnp.exp(scores - log_total[..., None])
    value_grad = jnp.einsum(
        "hqk,qhd->khd", weights.astype(jnp.bfloat16), out_grads, preferred_element_type=jnp.float32
    )
    prob_grad = jnp.einsum(
        "qhd,khd->hqk", out_grads, value_rows, preferred_element_type=jnp.float32
    )
    row_delta = jnp.sum(weights * prob_grad, axis=-1, keepdims=True)
    score_grad = (weights * (prob_grad - row_delta)).astype(jnp.bfloat16)
    query_grad = (
        jnp.einsum("hqk,khd->qhd", score_grad, key_rows, preferred_element_type=jnp.float32)
        * SCORE_SCALE
    )
    key_grad = (
        jnp.einsum("hqk,qhd->khd", score_grad, queries, preferred_element_type=jnp.float32)
        * SCORE_SCALE
    )
    return (query_grad, key_grad, value_grad)


def body(
    hidden_in,
    encoded,
    out_grad,
    ln_gain,
    ln_bias,
    biases,
    self_qkv,
    self_out,
    cross_q,
    cross_kv,
    cross_out,
    ffn_in,
    ffn_bias,
    ffn_out,
):
    seq_count = hidden_in.shape[0]
    row_count = hidden_in.shape[2]
    model_width = hidden_in.shape[3]
    groups = lax.axis_size("head")
    block_total = lax.axis_size("blk")
    span_rows = row_count * groups
    group_width = model_width // groups
    local_heads = HEADS // groups
    head_shape = (seq_count, span_rows, local_heads, HEAD_DIM)
    gathered = (
        lax.all_gather(ln_gain, ("head", "blk"), axis=1, tiled=True),
        lax.all_gather(ln_bias, ("head", "blk"), axis=1, tiled=True),
        lax.all_gather(biases, ("head", "blk"), axis=1, tiled=True),
        lax.all_gather(self_qkv, ("head", "blk"), axis=0, tiled=True),
        lax.all_gather(self_out, ("head", "blk"), axis=0, tiled=True),
        lax.all_gather(cross_q, ("head", "blk"), axis=0, tiled=True),
        lax.all_gather(cross_kv, ("head", "blk"), axis=0, tiled=True),
        lax.all_gather(cross_out, ("head", "blk"), axis=0, tiled=True),
        lax.all_gather(ffn_in, ("head", "blk"), axis=0, tiled=True),
        lax.all_gather(ffn_bias, ("head", "blk"), axis=0, tiled=True),
        lax.all_gather(ffn_out, ("head", "blk"), axis=0, tiled=True),
    )
    gain_rows = gathered[0].astype(jnp.float32)
    shift_rows = gathered[1].astype(jnp.float32)
    bias_rows = gathered[2].astype(jnp.float32)
    qkv_weight = gathered[3]
    out_weight = gathered[4]
    query_weight = gathered[5]
    memory_weight = gathered[6]
    cross_weight = gathered[7]
    inner_weight = gathered[8]
    inner_bias = gathered[9].astype(jnp.float32)
    outer_weight = gathered[10]
    hidden = hidden_in[:, 0].astype(jnp.float32)
    normed = layer_norm(hidden, gain_rows[0], shift_rows[0]).astype(jnp.bfloat16)
    mixed_qkv = project(normed, qkv_weight)
    mixed_qkv = mixed_qkv + jnp.concatenate(
        [bias_rows[0], jnp.zeros_like(bias_rows[0]), bias_rows[1]]
    )
    mixed_qkv = mixed_qkv.astype(jnp.bfloat16).reshape(seq_count, row_count, 3, groups, group_width)
    grouped = lax.all_to_all(mixed_qkv, "head", split_axis=3, concat_axis=1, tiled=True)
    self_queries = grouped[:, :, 0, 0].reshape(head_shape)
    self_keys = grouped[:, :, 1, 0]
    self_values = grouped[:, :, 2, 0]
    block_index = lax.axis_index("blk")
    own_start = block_index * span_rows
    stat_shape = (seq_count, local_heads, span_rows)
    initial = (
        jnp.full(stat_shape, -jnp.inf, jnp.float32),
        jnp.zeros(stat_shape, jnp.float32),
        jnp.zeros(head_shape, jnp.float32),
    )
    key_piece = lax.all_gather(self_keys, "blk", axis=1, tiled=True)
    value_piece = lax.all_gather(self_values, "blk", axis=1, tiled=True)
    piece_rows = key_piece.shape[1]
    block_count = piece_rows // span_rows
    layout = (seq_count, block_count, span_rows, local_heads, HEAD_DIM)
    key_blocks = jnp.moveaxis(key_piece.reshape(layout), 1, 0)
    value_blocks = jnp.moveaxis(value_piece.reshape(layout), 1, 0)
    block_starts = span_rows * lax.iota(jnp.int32, block_count)

    def visit(running, element):
        key_block, value_block, key_start = element

        def visit_compute(current):
            return forward_block(
                current, key_block, value_block, self_queries, own_start, key_start
            )

        def visit_unchanged(current):
            return current

        return (
            lax.cond(key_start < own_start + span_rows, visit_compute, visit_unchanged, running),
            None,
        )

    result, unused = lax.scan(visit, initial, (key_blocks, value_blocks, block_starts))
    running_top, running_total, running_sum = result
    log_total = running_top + jnp.log(running_total)
    attended = running_sum / jnp.transpose(running_total, (0, 2, 1))[..., None]
    attended_low = attended.astype(jnp.bfloat16).reshape(seq_count, span_rows, 1, group_width)
    self_mixed = lax.all_to_all(
        attended_low, "head", split_axis=1, concat_axis=2, tiled=True
    ).reshape(seq_count, row_count, model_width)
    after_self = hidden + project(self_mixed, out_weight) + bias_rows[2]
    cross_normed = layer_norm(after_self, gain_rows[1], shift_rows[1]).astype(jnp.bfloat16)
    cross_queries = (project(cross_normed, query_weight) + bias_rows[3]).astype(jnp.bfloat16)
    memory_mixed = project(encoded, memory_weight)
    memory_keys = memory_mixed[..., :model_width].astype(jnp.bfloat16)
    memory_values = (memory_mixed[..., model_width:] + bias_rows[4]).astype(jnp.bfloat16)
    all_keys, all_values = (
        lax.all_gather(memory_keys, ("head", "blk"), axis=1, tiled=True),
        lax.all_gather(memory_values, ("head", "blk"), axis=1, tiled=True),
    )
    query_heads = cross_queries.reshape(seq_count, row_count, HEADS, HEAD_DIM)
    key_heads = all_keys.reshape(seq_count, -1, HEADS, HEAD_DIM)
    value_heads = all_values.reshape(seq_count, -1, HEADS, HEAD_DIM)
    cross_result, cross_lse = lax.map(cross_forward, (query_heads, key_heads, value_heads))
    cross_mixed = cross_result.astype(jnp.bfloat16).reshape(seq_count, row_count, model_width)
    after_cross = after_self + project(cross_mixed, cross_weight) + bias_rows[5]
    ffn_normed = layer_norm(after_cross, gain_rows[2], shift_rows[2]).astype(jnp.bfloat16)
    inner_pre = project(ffn_normed, inner_weight) + inner_bias
    inner_act = exact_gelu(inner_pre).astype(jnp.bfloat16)
    output = after_cross + project(inner_act, outer_weight) + bias_rows[6]
    hidden_out = output.astype(jnp.bfloat16)[:, None]
    upstream = out_grad[:, 0].astype(jnp.float32)
    outer_low = upstream.astype(jnp.bfloat16)
    outer_weight_grad = weight_grad(inner_act, outer_low)
    act_grad = project_back(outer_low, outer_weight)
    unused_value, gelu_pull = jax.vjp(exact_gelu, inner_pre)
    pre_grad = gelu_pull(act_grad)[0].astype(jnp.bfloat16)
    inner_weight_grad = weight_grad(ffn_normed, pre_grad)
    inner_bias_grad = column_sum(pre_grad)
    back_cross, gain_grad_two, shift_grad_two = norm_grads(
        after_cross, gain_rows[2], shift_rows[2], project_back(pre_grad, inner_weight)
    )
    cross_total = upstream + back_cross
    cross_low = cross_total.astype(jnp.bfloat16)
    cross_weight_grad = weight_grad(cross_mixed, cross_low)
    cross_attn_grad = (
        project_back(cross_low, cross_weight)
        .astype(jnp.bfloat16)
        .reshape(seq_count, row_count, HEADS, HEAD_DIM)
    )
    cross_query_grads, cross_key_grads, cross_value_grads = lax.map(
        cross_backward, (query_heads, key_heads, value_heads, cross_lse, cross_attn_grad)
    )
    memory_key_grad, memory_value_grad = (
        lax.psum_scatter(
            cross_key_grads.reshape(seq_count, -1, model_width),
            ("head", "blk"),
            scatter_dimension=1,
            tiled=True,
        ),
        lax.psum_scatter(
            cross_value_grads.reshape(seq_count, -1, model_width),
            ("head", "blk"),
            scatter_dimension=1,
            tiled=True,
        ),
    )
    memory_key_low = memory_key_grad.astype(jnp.bfloat16)
    memory_value_low = memory_value_grad.astype(jnp.bfloat16)
    encoded_grad = project_back(memory_key_low, memory_weight[:, :model_width]) + project_back(
        memory_value_low, memory_weight[:, model_width:]
    )
    memory_weight_grad = weight_grad(
        encoded, jnp.concatenate([memory_key_low, memory_value_low], axis=-1)
    )
    cross_query_low = cross_query_grads.reshape(seq_count, row_count, model_width).astype(
        jnp.bfloat16
    )
    query_weight_grad = weight_grad(cross_normed, cross_query_low)
    back_self, gain_grad_one, shift_grad_one = norm_grads(
        after_self, gain_rows[1], shift_rows[1], project_back(cross_query_low, query_weight)
    )
    self_total = cross_total + back_self
    self_low = self_total.astype(jnp.bfloat16)
    out_weight_grad = weight_grad(self_mixed, self_low)
    attn_grad = (
        project_back(self_low, out_weight)
        .astype(jnp.bfloat16)
        .reshape(seq_count, row_count, groups, group_width)
    )
    grad_heads = lax.all_to_all(attn_grad, "head", split_axis=2, concat_axis=1, tiled=True).reshape(
        head_shape
    )
    row_delta = jnp.einsum("sqhd,sqhd->shq", grad_heads.astype(jnp.float32), attended)
    own_keys = self_keys.reshape(head_shape)
    own_values = self_values.reshape(head_shape)
    zero_grads = jnp.zeros(head_shape, jnp.float32)

    def key_turn(turn_index, carried):
        moving_keys, moving_values, moving_key_grads, moving_value_grads, query_grads = carried
        source = (block_index + turn_index) % block_total

        def key_compute(partial_grads):
            addition = backward_block(
                self_queries,
                grad_heads,
                log_total,
                row_delta,
                moving_keys,
                moving_values,
                own_start,
                source * span_rows,
            )
            return (
                partial_grads[0] + addition[0],
                partial_grads[1] + addition[1],
                partial_grads[2] + addition[2],
            )

        def key_unchanged(partial_grads):
            return partial_grads

        needed = (turn_index == 0) | (turn_index + block_index >= block_total)
        query_grads, moving_key_grads, moving_value_grads = lax.cond(
            needed, key_compute, key_unchanged, (query_grads, moving_key_grads, moving_value_grads)
        )
        moving_keys, moving_values = from_behind(
            (moving_keys, moving_values), "blk", block_total - 1
        )
        moving_key_grads, moving_value_grads = (
            from_behind(moving_key_grads.astype(jnp.bfloat16), "blk", block_total - 1).astype(
                moving_key_grads.dtype
            ),
            from_behind(moving_value_grads.astype(jnp.bfloat16), "blk", block_total - 1).astype(
                moving_value_grads.dtype
            ),
        )
        return (moving_keys, moving_values, moving_key_grads, moving_value_grads, query_grads)

    finished = lax.fori_loop(
        0, block_total, key_turn, (own_keys, own_values, zero_grads, zero_grads, zero_grads)
    )
    key_grads = finished[2]
    value_grads = finished[3]
    query_grads = finished[4]
    qkv_grads = jnp.stack([query_grads * SCORE_SCALE, key_grads * SCORE_SCALE, value_grads], axis=2)
    qkv_low = qkv_grads.astype(jnp.bfloat16).reshape(seq_count, span_rows, 3, 1, group_width)
    token_grads = lax.all_to_all(qkv_low, "head", split_axis=1, concat_axis=3, tiled=True).reshape(
        seq_count, row_count, 3 * model_width
    )
    qkv_weight_grad = weight_grad(normed, token_grads)
    back_input, gain_grad_zero, shift_grad_zero = norm_grads(
        hidden, gain_rows[0], shift_rows[0], project_back(token_grads, qkv_weight)
    )
    hidden_grad = (self_total + back_input)[:, None]
    bias_grad = jnp.stack(
        [
            column_sum(token_grads[..., :model_width]),
            column_sum(token_grads[..., 2 * model_width :]),
            column_sum(self_low),
            column_sum(cross_query_low),
            column_sum(memory_value_low),
            column_sum(cross_low),
            column_sum(outer_low),
        ]
    )
    gain_grad = jnp.stack([gain_grad_zero, gain_grad_one, gain_grad_two])
    shift_grad = jnp.stack([shift_grad_zero, shift_grad_one, shift_grad_two])
    reduced = (
        lax.psum_scatter(gain_grad, ("head", "blk"), scatter_dimension=1, tiled=True),
        lax.psum_scatter(shift_grad, ("head", "blk"), scatter_dimension=1, tiled=True),
        lax.psum_scatter(bias_grad, ("head", "blk"), scatter_dimension=1, tiled=True),
        lax.psum_scatter(qkv_weight_grad, ("head", "blk"), scatter_dimension=0, tiled=True),
        lax.psum_scatter(out_weight_grad, ("head", "blk"), scatter_dimension=0, tiled=True),
        lax.psum_scatter(query_weight_grad, ("head", "blk"), scatter_dimension=0, tiled=True),
        lax.psum_scatter(memory_weight_grad, ("head", "blk"), scatter_dimension=0, tiled=True),
        lax.psum_scatter(cross_weight_grad, ("head", "blk"), scatter_dimension=0, tiled=True),
        lax.psum_scatter(inner_weight_grad, ("head", "blk"), scatter_dimension=0, tiled=True),
        lax.psum_scatter(inner_bias_grad, ("head", "blk"), scatter_dimension=0, tiled=True),
        lax.psum_scatter(outer_weight_grad, ("head", "blk"), scatter_dimension=0, tiled=True),
    )
    return (
        hidden_out,
        hidden_grad,
        encoded_grad,
        reduced[0],
        reduced[1],
        reduced[2],
        reduced[3],
        reduced[4],
        reduced[5],
        reduced[6],
        reduced[7],
        reduced[8],
        reduced[9],
        reduced[10],
    )


MESH = pl.DeviceIdType.MESH
F32 = jnp.float32
BF = jnp.bfloat16
NZ, NX, NC, NH = 4, 2, 2, 2
PAIRS = 3
WIDE = 2 * HEAD_DIM


def place():
    h = lax.axis_index("head")
    b = lax.axis_index("blk")
    return h, b // 4, (b // 2) % 2, b % 2


def device_at(h, z, x, c):
    return (h, z * 4 + x * 2 + c)


def corner(h, z, x, c, k):
    flip = lambda v, bit: 1 - v if k >> bit & 1 else v
    return device_at(flip(h, 2), z, flip(x, 1), flip(c, 0))


def greet(h, z, x, c, corners=False):
    barrier = pltpu.get_barrier_semaphore()
    others = [device_at(h, z, x, 1 - c), device_at(h, z, 1 - x, c), device_at(1 - h, z, x, c)]
    others += [device_at(h, (z + d) % NZ, x, c) for d in (1, 2, 3)]
    if corners:
        others += [corner(h, z, x, c, k) for k in (3, 5, 6, 7)]
    for other in others:
        pl.semaphore_signal(barrier, inc=1, device_id=other, device_id_type=MESH)
    pl.semaphore_wait(barrier, len(others))


def dot(a, b):
    return jnp.dot(a, b, preferred_element_type=F32)


def dot_nt(a, b):
    return lax.dot_general(a, b, (((1,), (1,)), ((), ())), preferred_element_type=F32)


def dot_tn(a, b):
    return lax.dot_general(a, b, (((0,), (0,)), ((), ())), preferred_element_type=F32)


def lane_half(shape):
    return lax.broadcasted_iota(jnp.int32, shape, len(shape) - 1) < HEAD_DIM


def stack_pair(values):
    first = lane_half(values.shape)
    zero = jnp.zeros_like(values)
    return jnp.concatenate([jnp.where(first, values, zero), jnp.where(first, zero, values)], axis=0)


def unstack_pair(stacked):
    rows = stacked.shape[0] // 2
    top, low = stacked[:rows], stacked[rows:]
    return jnp.where(lane_half(top.shape), top, low)


class Links:
    def __init__(self, send, recv):
        self.send_sems, self.recv_sems, self.count, self.open = send, recv, 0, []

    def slot(self):
        self.count += 1
        return self.count - 1

    def copy(self, source, target, k, device):
        return pltpu.make_async_remote_copy(
            source, target, self.send_sems.at[k], self.recv_sems.at[k],
            device_id=device, device_id_type=MESH,
        )

    def send(self, source, target, k, device):
        c = self.copy(source, target, k, device)
        c.start()
        self.open.append(c)

    def drain(self):
        for c in self.open:
            c.wait_send()
        self.open = []


def gather_stages(links, view, order, here, own=None, ready=None):
    h, z, x, c = here
    every = slice(None)
    known = {"y": h, "z": z, "x": x}
    stages = []

    def seen(core, **other):
        at = {**known, **other}
        return view(at["y"], at["z"], at["x"], core)

    for axis in order + ("c",):
        first = not stages
        sent = seen(c)
        source = own[0] if first and own is not None else sent
        if axis == "z":
            routes = [
                (links.slot(), device_at(h, (z + d) % NZ, x, c), seen(c, z=(z - d) % NZ)) for d in (1, 2, 3)
            ]
        elif axis == "x":
            routes = [(links.slot(), device_at(h, z, 1 - x, c), seen(c, x=1 - x))]
        elif axis == "y":
            routes = [(links.slot(), device_at(1 - h, z, x, c), seen(c, y=1 - h))]
        else:
            routes = [(links.slot(), device_at(h, z, x, 1 - c), seen(1 - c))]
        if axis != "c":
            known[axis] = every

        def start(first=first, sent=sent, source=source, routes=routes):
            if first and ready is not None:
                ready()
            for k, device, _got in routes:
                links.send(source, sent, k, device)

        def wait(first=first, routes=routes):
            if first and own is not None:
                own[1].wait()
            for k, device, got in routes:
                links.copy(got, got, k, device).wait_recv()

        stages.append((start, wait))

    made = [stages[0][0]]
    for (_s, wait), (start, _w) in zip(stages, stages[1:]):
        made.append(lambda wait=wait, start=start: (wait(), start()))
    return made + [stages[-1][1]]


class Pipes:
    def __init__(self):
        self.left = []

    def add(self, stages):
        self.left.append(list(stages))

    def go(self, i):
        self.left[i].pop(0)()


def norm_stats(v):
    centered = v - jnp.mean(v, axis=-1, keepdims=True)
    inv = lax.rsqrt(jnp.mean(centered * centered, axis=-1, keepdims=True) + EPSILON)
    return centered * inv, inv


(
    GO, PACK, SWAP, UNPACK, PROJECTION, WORK, SELF_DONE, RELAY, ENC, MID, CROSS, LATE, INNER, FINISH, DOC, CROSS_PAIRS, DX1, OWN,
    BY_QUERY, BY_KEY, HIDDEN_OUT, QUERY_DONE, KEY_DONE, INPUT_GRAD,
) = range(24)
SMALL, QKV, HIDDEN, ENCODED, COLUMNS, INNER_COLUMNS, ROWS = range(7)
XY, YX, X = ("x", "y"), ("y", "x"), ("x",)
ZXY, ZYX, ZX, XZ = ("z",) + XY, ("z",) + YX, ("z",) + X, X + ("z",)
XYZ, YXZ = XY + ("z",), YX + ("z",)
XZY, YZX = ("x", "z", "y"), ("y", "z", "x")
FIRST_PARTS = (
    (HIDDEN, 4, 8, ZXY), (ENCODED, 0, 2, ZYX), (HIDDEN, 2, 8, ZYX), (HIDDEN, 1, 8, ZXY), (HIDDEN, 5, 8, ZXY),
    (HIDDEN, 3, 8, YZX), (HIDDEN, 6, 8, ZYX), (HIDDEN, 0, 8, ZXY), (QKV, 0, 1, ZX), (HIDDEN, 7, 8, ZXY), (COLUMNS, 3, 1, ZYX),
    (SMALL, 0, 1, XZY), (COLUMNS, 2, 1, ZXY), (COLUMNS, 4, 1, ZYX), (COLUMNS, 1, 1, XZY), (ENCODED, 1, 2, ZYX),
    (COLUMNS, 0, 1, YZX), (ROWS, 1, 3, ZX), (INNER_COLUMNS, 1, 1, ZX), (ROWS, 0, 3, ZX), (ROWS, 2, 3, ZX),
    (INNER_COLUMNS, 0, 1, XZ),
)
FIRST_ORDER = (
    (GO, 0), (GO, 2), (GO, 3), (GO, 4), (GO, 9), (PACK, 0), (GO, 6), (SWAP, 0), (GO, 0), (GO, 7), (GO, 2), (GO, 5), (GO, 8),
    (GO, 11), (GO, 0), (GO, 3), (GO, 11), (GO, 2), (GO, 5), (GO, 4), (GO, 3), (GO, 9), (GO, 0), (GO, 6), (GO, 2), (GO, 0),
    (GO, 7), (GO, 2), (GO, 4), (GO, 3), (GO, 9), (GO, 3), (GO, 6), (GO, 7), (GO, 1), (GO, 10), (GO, 4), (GO, 8), (GO, 16),
    (GO, 6), (GO, 4), (GO, 12), (GO, 11), (GO, 6), (GO, 9), (GO, 9), (GO, 15), (GO, 5), (GO, 7), (GO, 16), (GO, 1), (GO, 7),
    (GO, 14), (GO, 11), (GO, 8), (GO, 11), (GO, 10), (UNPACK, 0), (GO, 1), (SWAP, 1), (GO, 8), (PROJECTION, 0), (GO, 5),
    (GO, 12), (GO, 13), (GO, 10), (GO, 14), (GO, 15), (GO, 5), (WORK, 0), (WORK, 1), (WORK, 2), (WORK, 3), (GO, 1), (GO, 12),
    (GO, 15), (GO, 16), (GO, 18), (WORK, 4), (GO, 1), (GO, 13), (WORK, 5), (WORK, 6), (WORK, 7), (GO, 10), (GO, 12), (GO, 17),
    (GO, 14), (GO, 21), (WORK, 8), (GO, 10), (RELAY, 3), (GO, 12), (GO, 13), (GO, 15), (GO, 19), (WORK, 9), (WORK, 10), (GO, 15),
    (GO, 16), (GO, 18), (GO, 20), (WORK, 11), (GO, 14), (GO, 16), (RELAY, 0), (GO, 17), (GO, 21), (WORK, 12), (GO, 14),
    (WORK, 13), (GO, 19), (GO, 13), (WORK, 14), (WORK, 15), (SELF_DONE, 0), (GO, 13), (RELAY, 4), (GO, 20), (RELAY, 1),
    (RELAY, 2), (ENC, 0), (MID, 0), (CROSS, 0), (CROSS, 1), (CROSS, 2), (LATE, 0), (GO, 17), (GO, 18), (GO, 19), (GO, 21),
    (GO, 17), (GO, 20), (GO, 18), (RELAY, 6), (GO, 19), (GO, 21), (RELAY, 5), (GO, 20), (INNER, 0), (INNER, 1), (INNER, 2),
    (FINISH, 0),
)

def first_kernel(
    hid, g_in, enc_in, gains_in, shifts_in, biases_in, qkv_in, out_in, cq_in, ckv_in, co_in, inner_in, bias_in, w2_in,
    wq_out, keys_out, vals_out, queries_out, wc_out, kc_out, vc_out, g1, g2,
    prm_out, a_span_out, o_wide_out, o_low_out, logs_out, x1_out, cn_out, qc_out, oc_out, cross_out, en_out,
    out_part, out_send, dx2_out, row_sums,
    prm, a_span, o_wide, o_low, lse_out, x1, cn, qc, oc, cross_lse, en,
    wq_in, wp_in, wf_in, sm_in, vec, xs, wq_all, sm_all, wp, wf, w2, wq, keys, vals, queries, q2, m_ref, l_ref, acc, o_tmp,
    wc, w1, kc, vc, fb, ff, dy3, slope, act, du, ya, dza, yz_send, yz_recv, g1_tile, g2_tile, send, recv, local, store,
):
    here = place()
    h, z, x, c = here
    links = Links(send, recv)
    every = slice(None)
    span = 2 * hid.shape[0]
    group = 4 * span
    width = hid.shape[1]
    gw = PAIRS * WIDE
    feature = width // (NH * NZ * NX * NC)

    tiles = wf.shape[0]
    core, xdev, ydev = device_at(h, z, x, 1 - c), device_at(h, z, 1 - x, c), device_at(1 - h, z, x, c)

    def part(name, i, n):
        if name == SMALL:
            return lambda *d: sm_all.at[d], sm_in
        if name == QKV:
            return lambda h, z, x, c: wq_all.at[every, z, x, c], None
        if name == COLUMNS:
            return lambda *d: wp.at[(i,) + d], wp_in.at[i]
        if name == INNER_COLUMNS:
            return lambda h, z, x, c: wf.at[i, every, z, x, c], None
        source = {HIDDEN: hid, ENCODED: enc_in, ROWS: w2_in}[name]
        size = source.shape[0] // n
        cut = pl.ds(i * size, size)
        if name == HIDDEN:
            return lambda h, z, x, c: xs.at[z, x, c, h, cut], source.at[cut]
        if name == ROWS:
            return lambda h, z, x, c: w2.at[z, x, c, cut], source.at[cut]
        return lambda *d: en.at[d + (cut,)], source.at[cut]

    made = [part(*p[:3]) for p in FIRST_PARTS]
    copies = [
        None if piece is None else pltpu.make_async_copy(piece, view(h, z, x, c), local.at[i])
        for i, (view, piece) in enumerate(made)
    ]
    count = len(made)
    own_q = pltpu.make_async_copy(wq_in.at[h], wq_all.at[h, z, x, c], local.at[count])
    own_f = pltpu.make_async_copy(wf_in.at[h], wf.at[every, h, z, x, c], local.at[count + 1])
    own_g = pltpu.make_async_copy(g_in, dy3.at[h], local.at[count + 2])
    packed_here = [name in (SMALL, COLUMNS) for name, *_rest in FIRST_PARTS]
    own_g.start()
    for cp, late in zip(copies, packed_here):
        if cp is not None and not late:
            cp.start()
    greet(*here)
    kq, kf, kg = links.slot(), links.slot(), links.slot()

    def pack():
        blocks = [(out_in, 0), (cq_in, 0), (ckv_in, 0), (ckv_in, width), (co_in, 0)]
        def stacked(source, lo):
            halves = [source[:, lo + k * gw : lo + (k + 1) * gw].astype(F32) for k in range(2)]
            return jnp.concatenate(halves, axis=0).astype(BF)

        for i, (source, lo) in enumerate(blocks):
            wp_in[i] = stacked(source, lo)
        for k in range(2):
            for j in range(tiles):
                wf_in[k, j] = stacked(inner_in, (k * tiles + j) * width)
        for k in range(2):
            for i in range(3):
                lo = i * width + k * gw
                wq_in[k, :, i * gw : (i + 1) * gw] = qkv_in[:, lo : lo + gw]
        vec[...] = jnp.zeros_like(vec)
        for source, lo in ((gains_in, 0), (shifts_in, 3), (biases_in, 6)):
            vec[lo : lo + source.shape[0], 0:feature] = source[...].astype(F32)
        packed = jnp.transpose(vec[...])[0 : sm_in.shape[0]]
        line = jnp.concatenate([bias_in[...].astype(F32), jnp.zeros((1, 128 - bias_in.shape[1]), F32)], axis=1)
        row = lax.broadcasted_iota(jnp.int32, packed.shape, 0)
        sm_in[...] = jnp.where(row == feature, line, packed).astype(BF)
        for cp in [own_q, own_f] + [cp for cp, late in zip(copies, packed_here) if late]:
            cp.start()
        links.send(wq_in.at[1 - h], wq_all.at[h, z, x, c], kq, ydev)

    def swapped_q():
        own_q.wait()
        got = wq_all.at[1 - h, z, x, c]
        links.copy(got, got, kq, ydev).wait_recv()

    waiting = [True]

    def swapped_f():
        if waiting:
            waiting.clear()
            own_f.wait()
            got = wf.at[every, 1 - h, z, x, c]
            links.copy(got, got, kf, ydev).wait_recv()

    pipes = Pipes()
    for (name, i, n, order), (view, piece), cp in zip(FIRST_PARTS, made, copies):
        ready = {QKV: swapped_q, INNER_COLUMNS: swapped_f}.get(name)
        pipes.add(gather_stages(links, view, order, here, None if piece is None else (piece, cp), ready))

    def swap(n):
        if n == 0:
            links.send(wf_in.at[1 - h], wf.at[every, h, z, x, c], kf, ydev)
        else:
            links.send(g_in, dy3.at[h], kg, ydev)

    def projection():
        wq[...] = wq_all[...].astype(F32).reshape(width, 3 * gw).astype(BF)
        keep(3, wq, wq_out)

    def small_done():
        sm = sm_all[...].astype(F32)
        devices = NH * NZ * NX * NC
        sm = sm.reshape(devices, sm.shape[-2], sm.shape[-1])
        prm[...] = jnp.transpose(sm[:, :feature, :].reshape(width, sm.shape[-1]))
        inner_part = w2_in.shape[0]
        for d in range(devices):
            fb[:, d * inner_part : (d + 1) * inner_part] = sm[d, feature : feature + 1, 0:inner_part]

    def project(g, keys_too, queries_too):
        gain, shift = prm[0:1, :], prm[3:4, :]
        lanes = pl.ds(pl.multiple_of(h * gw, 128), gw)
        q_bias, v_bias = prm[6:7, lanes], prm[7:8, lanes]

        @pl.loop(0, 4)
        def _(j):
            n, _unused = norm_stats(xs[g, j // 2, j % 2].reshape(span, width).astype(F32))
            a = (n * gain + shift).astype(BF)
            at = pl.ds(pl.multiple_of(g * group + j * span, span), span)
            if queries_too:
                queries[at, :] = ((dot(a, wq[:, 0:gw]) + q_bias).astype(BF).astype(F32) * SCORE_SCALE).astype(BF)
            if keys_too:
                keys[at, :] = dot(a, wq[:, gw : 2 * gw]).astype(BF)
                vals[at, :] = (dot(a, wq[:, 2 * gw : 3 * gw]) + v_bias).astype(BF)
            if keys_too and queries_too:
                @pl.when(j == x * 2 + c)
                def _():
                    a_span[...] = a

    def attend(g, diagonal, p):
        at = pl.ds(pl.multiple_of(g * group, group), group)
        if True:
            part = pl.ds(p * WIDE, WIDE)
            k_pair, v_pair = keys[at, part], vals[at, part]

            @pl.loop(0, 2)
            def _(half):
                mine = pl.ds(pl.multiple_of(half * span, span), span)
                s = dot_nt(q2[p, mine, :], k_pair)
                if diagonal:
                    query = (x * 2 + c) * span + lax.broadcasted_iota(jnp.int32, s.shape, 0)
                    s = jnp.where(lax.broadcasted_iota(jnp.int32, s.shape, 1) <= query, s, -jnp.inf)
                    top = jnp.max(s, axis=-1, keepdims=True)
                    w = jnp.exp(s - top)
                    m_ref[p, mine, :] = jnp.broadcast_to(top, (span, 128))
                    l_ref[p, mine, :] = jnp.broadcast_to(jnp.sum(w, axis=-1, keepdims=True), (span, 128))
                    acc[p, mine, :] = dot(w.astype(BF), v_pair)
                else:
                    old = m_ref[p, mine, :]
                    new = jnp.maximum(old, jnp.max(s, axis=-1, keepdims=True))
                    fade = jnp.exp(old - new)
                    w = jnp.exp(s - new[:, 0:1])
                    m_ref[p, mine, :] = new
                    l_ref[p, mine, :] = l_ref[p, mine, :] * fade + jnp.sum(w, axis=-1, keepdims=True)
                    acc[p, mine, :] = acc[p, mine, :] * fade + dot(w.astype(BF), v_pair)

    def work(n):
        t, p = n // 4, n % 4 - 1
        if t == 0 and p < 0:
            project(z, True, True)
            start = pl.ds(pl.multiple_of(z * group + (x * 2 + c) * span, span), span)
            for i in range(PAIRS):
                q2[i] = stack_pair(queries[start, pl.ds(i * WIDE, WIDE)])
        elif t == 0:
            attend(z, True, p)
        elif p < 0:
            pl.when(z - t >= 0)(lambda: project((z - t) % NZ, True, False))
            pl.when(z + t < NZ)(lambda: project((z + t) % NZ, False, True))
        else:
            pl.when(z - t >= 0)(lambda: attend((z - t) % NZ, False, p))

    lane = lax.broadcasted_iota(jnp.int32, (span, 128), 1)
    ko = links.slot()
    kept = []

    def keep(i, source, target):
        cp = pltpu.make_async_copy(source, target, store.at[i])
        cp.start()
        kept.append(cp)

    def self_done():
        keep(0, keys, keys_out)
        keep(1, vals, vals_out)
        keep(2, queries, queries_out)
        logs = jnp.zeros((span, 128), F32)
        for p in range(PAIRS):
            part = pl.ds(p * WIDE, WIDE)
            o_pair = unstack_pair(acc[p] / l_ref[p])
            o_wide[:, part] = o_pair
            o_tmp[:, :, part] = o_pair.astype(BF).reshape(2, span // 2, WIDE)
            total = m_ref[p] + jnp.log(l_ref[p])
            logs = jnp.where(lane == 2 * p, total[:span], logs)
            logs = jnp.where(lane == 2 * p + 1, total[span:], logs)
        lse_out[...] = logs
        links.send(o_tmp.at[1 - h], o_low.at[h], ko, ydev)
        o_low[h] = o_tmp[h]

    def unstack(v, hh, target):
        v = v.astype(F32).reshape(NZ * NX * NC, 2 * feature, gw)
        for half in range(2):
            target[hh * gw : (hh + 1) * gw, half * gw : (half + 1) * gw] = (
                v[:, half * feature : (half + 1) * feature, :].reshape(gw, gw).astype(BF)
            )

    def relay(i):
        for hh in range(NH):
            if i < 5:
                unstack(wp[i, hh], hh, wc.at[i])
            else:
                unstack(wf[i - 5, hh], hh, w1.at[i - 5])
        if i < 5:
            keep(4 + i, wc.at[i], wc_out.at[i])

    def encoder():
        enc_rows = kc.shape[0]

        @pl.loop(0, 2)
        def _(i):
            at = pl.ds(pl.multiple_of(i * (enc_rows // 2), 16), enc_rows // 2)
            e = en[i].reshape(enc_rows // 2, width)
            kc[at, :] = dot(e, wc[2]).astype(BF)
            vc[at, :] = (dot(e, wc[3]) + prm[10:11]).astype(BF)

        keep(9, kc, kc_out)
        keep(10, vc, vc_out)

    def after_self():
        links.copy(o_low.at[1 - h], o_low.at[1 - h], ko, ydev).wait_recv()
        total = hid[...].astype(F32) + dot(o_low[0], wc[0, 0:gw, :]) + dot(o_low[1], wc[0, gw:width, :]) + prm[8:9]
        x1[...] = total
        n, _unused = norm_stats(total)
        cn[...] = (n * prm[1:2] + prm[4:5]).astype(BF)
        qc[...] = ((dot(cn[...], wc[1]) + prm[9:10]).astype(BF).astype(F32) * SCORE_SCALE).astype(BF)
        cross_lse[...] = jnp.zeros_like(cross_lse)

    def cross(n):
        @pl.loop(2 * n, 2 * n + 2)
        def _(p):
            part = pl.ds(pl.multiple_of(p * WIDE, WIDE), WIDE)
            s = dot_nt(stack_pair(qc[:, part]), kc[:, part])
            top = jnp.max(s, axis=-1, keepdims=True)
            w = jnp.exp(s - top)
            total = jnp.sum(w, axis=-1, keepdims=True)
            cross_lse[...] = jnp.where(lane == p, top + jnp.log(total), cross_lse[...])
            oc[:, part] = unstack_pair(dot((w / total).astype(BF), vc[:, part])).astype(BF)

    def after_cross():
        total = x1[...] + dot(oc[...], wc[4]) + prm[11:12]
        dx2_out[...] = total
        n, _unused = norm_stats(total)
        ff[h] = (n * prm[2:3] + prm[5:6]).astype(BF)
        links.send(ff.at[h], ff.at[h], kn, ydev)
        results = (
            (prm, prm_out), (a_span, a_span_out), (o_wide, o_wide_out), (o_low, o_low_out), (lse_out, logs_out), (x1, x1_out),
            (cn, cn_out), (qc, qc_out), (oc, oc_out), (cross_lse, cross_out), (en, en_out),
        )
        for i, (source, target) in enumerate(results):
            keep(16 + i, source, target)
        row_sums[...] = jnp.zeros_like(row_sums)

    kn, kyz = links.slot(), links.slot()
    tile_copies = []

    def inner_start():
        own_g.wait()
        links.copy(dy3.at[1 - h], dy3.at[1 - h], kg, ydev).wait_recv()
        for j in range(tiles):
            w2_tile = w2[2 * j : 2 * j + 2].reshape(width, width)
            slope[j] = dot_nt(dy3[...].reshape(span, width), w2_tile)
        links.copy(ff.at[1 - h], ff.at[1 - h], kn, ydev).wait_recv()

    def inner_units():
        f_all = ff[...].reshape(span, width)
        for j in range(tiles):
            at = pl.multiple_of(h * (tiles * width) + j * width, 128)
            u = dot(f_all, w1[j]) + fb[:, pl.ds(at, width)]
            phi = 0.5 * (1.0 + lax.erf(u * SQRT_HALF))
            act[j] = (u * phi).astype(BF)
            du[j] = (slope[j] * (phi + u * (DENSITY * jnp.exp(-0.5 * u * u)))).astype(BF)
        for j in range(tiles):
            term = dot_nt(du[j], w1[j])
            dza[...] = term if j == 0 else dza[...] + term
        yz_send[...] = dza[...].astype(BF).reshape(2, span // 2, width)
        links.send(yz_send.at[1 - h], yz_recv, kyz, ydev)
        for j in range(tiles):
            term = dot(act[j], w2[2 * j : 2 * j + 2].reshape(width, width))
            ya[...] = term if j == 0 else ya[...] + term
        own_half = pl.ds(pl.multiple_of(h * (span // 2), 8), span // 2)
        other_half = pl.ds(pl.multiple_of((1 - h) * (span // 2), 8), span // 2)
        out_part[...] = dx2_out[...] + ya[own_half, :] + prm[12:13]
        out_send[...] = ya[other_half, :].astype(BF)

    def inner_grads():
        f_all = ff[...].reshape(span, width)
        for j in range(tiles):
            row_sums[pl.ds(pl.multiple_of(16 + 8 * (h * tiles + j), 8), 1), :] = column_total(du[j])
            for hh in range(NH):
                halves = [
                    dot_tn(f_all[:, hh * gw : (hh + 1) * gw], du[j, :, half * gw : (half + 1) * gw]).reshape(
                        NZ * NX * NC, feature, gw
                    )
                    for half in range(2)
                ]
                g1_tile[j, hh] = jnp.concatenate(halves, axis=1).astype(BF).reshape(NZ, NX, NC, 2 * feature, gw)
            tile_copies.append(pltpu.make_async_copy(g1_tile.at[j], g1.at[j], store.at[11 + 2 * j]))
            tile_copies[-1].start()
            g2_tile[j] = dot_tn(act[j], dy3[...].reshape(span, width)).astype(BF).reshape(g2_tile.shape[1:])
            tile_copies.append(pltpu.make_async_copy(g2_tile.at[j], g2.at[pl.ds(2 * j, 2)], store.at[12 + 2 * j]))
            tile_copies[-1].start()

    def finish():
        links.copy(yz_recv, yz_recv, kyz, ydev).wait_recv()
        mine = pl.ds(pl.multiple_of(h * (span // 2), 8), span // 2)
        x2 = dx2_out[...]
        back, d_gain, d_shift = norm_back(dza[mine, :] + yz_recv[...].astype(F32), prm[2:3], x2)
        row_sums[2:3, :], row_sums[5:6, :] = d_gain, d_shift
        row_sums[12:13, :] = column_total(g_in[...])
        dx2_out[...] = g_in[...].astype(F32) + back
        for cp in tile_copies + kept:
            cp.wait()

    steps = {
        GO: pipes.go, PACK: lambda n: pack(), SWAP: swap, UNPACK: lambda n: small_done(), PROJECTION: lambda n: projection(), WORK: work,
        SELF_DONE: lambda n: self_done(), RELAY: relay, ENC: lambda n: encoder(), MID: lambda n: after_self(),
        CROSS: cross, LATE: lambda n: after_cross(),
        INNER: lambda n: (inner_start, inner_units, inner_grads)[n](), FINISH: lambda n: finish(),
    }
    for name, n in FIRST_ORDER:
        steps[name](n)
    links.drain()


FIRST_SEMS = 150


def run_first(hid, g_in, enc, *params):
    rows, width = hid.shape
    w2_in = params[-1]
    span = 2 * rows
    total = span * NZ * NX * NC
    gw = PAIRS * WIDE
    grid = (NH, NZ, NX, NC)
    devices = NH * NZ * NX * NC
    feature = width // devices
    enc_rows = enc.shape[0] * devices
    inner_width = w2_in.shape[0] * devices
    tiles = inner_width // width // NH
    hbm, vmem = pl.BlockSpec(memory_space=pl.ANY), pl.BlockSpec(memory_space=pltpu.VMEM)
    S = jax.ShapeDtypeStruct
    shard = (2 * feature, gw)
    wq_shape = (feature, 3 * gw)
    outs_hbm = (
        S((width, 3 * gw), BF), S((total, gw), BF), S((total, gw), BF), S((total, gw), BF),
        S((5, width, width), BF), S((enc_rows, width), BF), S((enc_rows, width), BF),
        S((tiles,) + grid + shard, BF), S(grid[1:] + w2_in.shape, BF),
    )
    middle = (
        S((128, width), F32), S((span, width), BF), S((span, gw), F32), S((2, rows, gw), BF), S((span, 128), F32),
        S((rows, width), F32), S((rows, width), BF), S((rows, width), BF), S((rows, width), BF), S((span, 128), F32), S(grid + enc.shape, BF),
    )
    outs_hbm += middle
    outs_vmem = (
        S((rows, width), F32), S((rows, width), BF), S((rows, width), F32), S((16 + 8 * tiles * NH, width), F32),
    )
    V = pltpu.VMEM
    return pl.pallas_call(
        first_kernel,
        out_shape=outs_hbm + outs_vmem,
        in_specs=[vmem] * 14,
        out_specs=(hbm,) * len(outs_hbm) + (vmem,) * len(outs_vmem),
        scratch_shapes=[V(m.shape, m.dtype) for m in middle] + [
            V((2,) + wq_shape, BF), V((5,) + shard, BF), V((2, tiles) + shard, BF), V((32, 128), BF), V((128, 128), F32),
            V((NZ, NX, NC, NH, rows, width), BF), V(grid + wq_shape, BF), V(grid + (32, 128), BF),
            V((5,) + grid + shard, BF), V((tiles,) + grid + shard, BF), V(grid[1:] + w2_in.shape, BF),
            V((width, 3 * gw), BF), V((total, gw), BF), V((total, gw), BF), V((total, gw), BF),
            V((PAIRS, 2 * span, WIDE), BF), V((PAIRS, 2 * span, 128), F32), V((PAIRS, 2 * span, 128), F32),
            V((PAIRS, 2 * span, WIDE), F32), V((2, rows, gw), BF),
            V((5, width, width), BF), V((tiles, width, width), BF), V((enc_rows, width), BF), V((enc_rows, width), BF),
            V((1, inner_width), F32), V((2, rows, width), BF), V((2, rows, width), BF),
            V((tiles, span, width), F32), V((tiles, span, width), BF), V((tiles, span, width), BF), V((span, width), F32), V((span, width), F32),
            V((2, rows, width), BF), V((rows, width), BF),
            V((tiles,) + grid + shard, BF), V((tiles, 2, NX, NC) + w2_in.shape, BF),
            pltpu.SemaphoreType.DMA((FIRST_SEMS,)), pltpu.SemaphoreType.DMA((FIRST_SEMS,)),
            pltpu.SemaphoreType.DMA((len(FIRST_PARTS) + 3,)), pltpu.SemaphoreType.DMA((28,)),
        ],
        compiler_params=pltpu.CompilerParams(
            collective_id=0, has_side_effects=True, vmem_limit_bytes=63 << 20
        ),
        cost_estimate=pl.CostEstimate(flops=10**10, bytes_accessed=10**8, transcendentals=10**7),
        name="gather_and_forward",
    )(hid, g_in, enc, *params)


def norm_back(dz, gain, v):
    n, inv = norm_stats(v)
    dn = dz * gain
    result = (dn - jnp.mean(dn, axis=-1, keepdims=True) - n * jnp.mean(dn * n, axis=-1, keepdims=True)) * inv
    return result, jnp.sum(dz * n, axis=0, keepdims=True), jnp.sum(dz, axis=0, keepdims=True)


def column_total(v):
    return jnp.sum(v.astype(F32), axis=0, keepdims=True)


SQRT_HALF = 0.7071067811865476
DENSITY = 0.3989422804014327


def shard_loop(shape, fn):
    count = 1
    for n in shape:
        count *= n

    @pl.loop(0, count)
    def _(i):
        index = []
        for n in reversed(shape):
            index.append(i % n)
            i = i // n
        fn(tuple(reversed(index)))


def add_into(target, source):
    target[...] = (target[...].astype(F32) + source[...].astype(F32)).astype(BF)


WHOLE, PAIRED, SINGLE = ("y", "z", "x"), ("l", "z", "x"), ("z", "x")
EXTENT = {"y": NH, "l": NH, "z": NZ, "x": NX}


def reduce_stages(links, source, axes, order, here, bufs, local_sem, store, ydev=None):
    h, z, x, c = here
    every = slice(None)
    me = {"y": h, "z": z, "x": x}
    bufs = list(bufs)
    if local_sem is None:
        mine = source(c)
    else:
        mine = bufs.pop(0)
        local = pltpu.make_async_copy(source(c), mine, local_sem)
    from_core = bufs.pop(0)
    k_core = links.slot()
    core = device_at(h, z, x, 1 - c)

    def start():
        links.send(source(1 - c), from_core, k_core, core)
        if local_sem is not None:
            local.start()

    def after_core():
        if local_sem is not None:
            local.wait()
        links.copy(from_core, from_core, k_core, core).wait_recv()
        shard_loop([EXTENT[a] for a in axes], lambda i: add_into(mine.at[i], from_core.at[i]))

    fixed = {}
    stages = []
    for axis in order:
        buf = bufs.pop(0)
        open_axes = [a for a in axes if a not in fixed and a != axis]

        def at(**values):
            known = {**fixed, **values}
            return tuple(known.get(a, every) for a in axes)

        if axis == "z":
            routes = [
                (links.slot(), device_at(h, (z + d) % NZ, x, c), mine.at[at(z=(z + d) % NZ)], buf.at[d - 1])
                for d in (1, 2, 3)
            ]
        elif axis == "x":
            routes = [(links.slot(), device_at(h, z, 1 - x, c), mine.at[at(x=1 - x)], buf)]
        else:
            routes = [(links.slot(), device_at(1 - h, z, x, c), mine.at[at(y=1 - h)], buf)]

        def go(routes=routes):
            for k, device, away, target in routes:
                links.send(away, target, k, device)

        def come(routes=routes):
            for k, device, _away, target in routes:
                links.copy(target, target, k, device).wait_recv()

        fixed[axis] = me[axis]
        base = dict(fixed)

        def add(routes=routes, open_axes=open_axes, base=base):
            def one(i):
                known = {**base, **dict(zip(open_axes, i))}
                slot = mine.at[tuple(known[a] for a in axes)]
                total = slot[...].astype(F32)
                for _k, _device, _away, target in routes:
                    total = total + target[i].astype(F32)
                slot[...] = total.astype(BF)

            shard_loop([EXTENT[a] for a in open_axes], one)

        def total_of(lead, routes=routes, base=base):
            known = {**base, "l": lead}
            total = mine[tuple(known[a] for a in axes)].astype(F32)
            for _k, _device, _away, target in routes:
                total = total + (target[lead] if "l" in axes else target[...]).astype(F32)
            return total

        stages.append((go, come, add, total_of))

    made = [start, lambda: (after_core(), stages[0][0]())]
    for (_g, come, add, _t), (go, _c, _a, _t2) in zip(stages, stages[1:]):
        made.append(lambda come=come, add=add, go=go: (come(), add(), go()))
    _g, come, _a, total_of = stages[-1]
    if "l" not in axes:
        return made + [lambda: (come(), store(None, total_of(None)))]
    out, back = bufs
    k_swap = links.slot()

    def swap():
        come()
        store(h, total_of(h))
        out[...] = total_of(1 - h).astype(BF)
        links.send(out, back, k_swap, ydev)

    def finish():
        links.copy(back, back, k_swap, ydev).wait_recv()
        store(1 - h, back[...].astype(F32))

    return made + [swap, finish]


def reduce_bufs(shard, axes, order, own):
    sizes = [tuple(EXTENT[a] for a in axes)] * (2 if own else 1)
    left = list(axes)
    for axis in order:
        left.remove(axis)
        sizes.append((NZ - 1,) * (axis == "z") + tuple(EXTENT[a] for a in left))
    if "l" in axes:
        sizes += [(), ()]
    return [pltpu.VMEM(size + shard, BF) for size in sizes]


XYZ, YXZ = XY + ("z",), YX + ("z",)
KV_ORDER = (XZ, XZ, XZ)
LAST_PARTS = (
    (ROWS, 0, XZ), (COLUMNS, 0, YXZ), (COLUMNS, 2, YXZ), (ROWS, 2, XZ), (COLUMNS, 1, YXZ), (COLUMNS, 4, XYZ), (ENCODED, 1, YZX),
    (INNER_COLUMNS, 0, ZX), (ENCODED, 0, YXZ), (ROWS, 1, XZ), (COLUMNS, 3, YXZ), (INNER_COLUMNS, 1, XZ),
)
LAST_ORDER = (
    (GO, 0), (GO, 7), (GO, 9), (DOC, 0), (GO, 0), (GO, 5), (GO, 7), (GO, 9), (CROSS_PAIRS, 0), (GO, 3), (GO, 5),
    (CROSS_PAIRS, 1), (GO, 0), (GO, 3), (GO, 11), (CROSS_PAIRS, 2), (DX1, 0), (ENC, 0), (GO, 4), (OWN, 0), (GO, 12), (GO, 13),
    (GO, 14), (GO, 0), (GO, 3), (GO, 4), (GO, 5), (GO, 7), (GO, 9), (GO, 12), (GO, 10), (GO, 11), (ENC, 1), (GO, 12), (GO, 7),
    (GO, 10), (GO, 12), (GO, 13), (OWN, 1), (BY_QUERY, 0), (BY_QUERY, 1), (BY_QUERY, 2), (BY_QUERY, 3), (GO, 1), (GO, 15),
    (GO, 4), (GO, 5), (GO, 7), (GO, 14), (GO, 11), (GO, 1), (BY_QUERY, 4), (BY_QUERY, 5), (BY_QUERY, 6), (GO, 2), (BY_QUERY, 7),
    (BY_QUERY, 8), (BY_QUERY, 9), (GO, 13), (GO, 2), (GO, 3), (GO, 10), (BY_QUERY, 10), (GO, 13), (GO, 4), (BY_QUERY, 11),
    (GO, 9), (QUERY_DONE, 0), (GO, 16), (BY_KEY, 0), (GO, 16), (GO, 1), (BY_KEY, 3), (GO, 14), (GO, 15), (BY_KEY, 6),
    (BY_KEY, 9), (GO, 14), (BY_KEY, 10), (GO, 2), (GO, 5), (GO, 6), (GO, 16), (GO, 8), (GO, 10), (KEY_DONE, 0), (GO, 17),
    (GO, 6), (GO, 8), (GO, 17), (GO, 1), (GO, 11), (BY_KEY, 1), (BY_KEY, 4), (GO, 4), (BY_KEY, 7), (GO, 15), (GO, 6),
    (KEY_DONE, 1), (GO, 15), (BY_KEY, 2), (BY_KEY, 5), (BY_KEY, 8), (BY_KEY, 11), (KEY_DONE, 2), (KEY_DONE, 3), (GO, 17),
    (GO, 18), (GO, 19), (GO, 16), (GO, 1), (GO, 18), (GO, 19), (GO, 2), (GO, 6), (GO, 8), (GO, 10), (GO, 11), (GO, 17), (GO, 18),
    (INPUT_GRAD, 0), (GO, 20), (GO, 17), (GO, 19), (GO, 16), (GO, 2), (GO, 6), (HIDDEN_OUT, 0), (GO, 18), (GO, 8), (GO, 20),
    (GO, 18), (GO, 19), (GO, 8), (GO, 19), (GO, 20),
)

def last_kernel(
    out_part, out_send, dx2, oc, qc, cross_lse,
    hid_in, prm_in, a_span_in, o_wide_in, o_low_in, lse_in, x1_in, cn_in, row_sums_in,
    en_in, wq_in, keys_in, vals_in, queries_in, wc_in, kc_in, vc_in, gf1, gf2,
    hidden_out, hidden_grad, out_o, out_cq, out_ckv, out_co, out_fi, out_f, out_e, out_q, out_s,
    hid, prm, a_span, o_wide, o_low, lse, x1, cn, row_sums,
    y_recv, wk, pool, gc, ge, doc, dqc, dx1, do_low,
    do_all, st_all, q2, k2, v2, do2, dq2, dk2, dv2, dz_q, gq, gkv, gs, fbs, dz_send, dz_recv, send, recv, local, loads, *bufs,
):
    here = place()
    h, z, x, c = here
    links = Links(send, recv)
    every = slice(None)
    rows, width = hid.shape
    span = 2 * rows
    group = 4 * span
    gw = PAIRS * WIDE
    devices = NH * NZ * NX * NC
    feature = width // devices
    e_shard, f_shard = ge.shape[4], gf2.shape[3]
    enc_rows = devices * e_shard
    total_rows = keys_in.shape[0]
    ydev = device_at(1 - h, z, x, c)
    kc, vc, dkc, dvc = (pool.at[pl.ds(i * enc_rows, enc_rows)] for i in range(4))
    wc = [wk.at[pl.ds(i * width, width)] for i in range(5)]
    queries, wq = pool.at[:, pl.ds(0, gw)], [pool.at[pl.ds(i * width, width), pl.ds(gw, gw)] for i in range(3)]
    plan = [(wc_in.at[4], wc[4]), (kc_in, kc), (vc_in, vc), (wc_in.at[1], wc[1]), (wc_in.at[0], wc[0])]
    plan += [(x1_in, x1), (prm_in, prm), (cn_in, cn), (o_low_in, o_low), (lse_in, lse), (o_wide_in, o_wide)]
    plan += [(en_in, ge), (wc_in.at[2], wc[2]), (wc_in.at[3], wc[3]), (a_span_in, a_span), (hid_in, hid), (row_sums_in, row_sums)]
    fetches = [pltpu.make_async_copy(source, target, loads.at[14 + i]) for i, (source, target) in enumerate(plan)]
    for cp in fetches:
        cp.start()

    def fetched(lo, hi):
        for cp in fetches[lo:hi]:
            cp.wait()

    late = [
        pltpu.make_async_copy(source, wk.at[pl.ds(0, total_rows), pl.ds(lo, gw)], loads.at[8 + i])
        for i, (source, lo) in enumerate(((keys_in, 0), (vals_in, gw)))
    ]
    late.append(pltpu.make_async_copy(queries_in, pool.at[pl.ds(0, total_rows), pl.ds(0, gw)], loads.at[10]))
    late += [
        pltpu.make_async_copy(wq_in.at[:, pl.ds(i * gw, gw)], wq[i], loads.at[11 + i]) for i in range(3)
    ]
    greet(*here, corners=True)
    kh = links.slot()
    links.send(out_send, y_recv, kh, ydev)

    cuts = [(out_o, 0), (out_cq, 0), (out_ckv, 0), (out_ckv, width), (out_co, 0)]
    pipes = Pipes()
    used = 0
    for i, (name, n, order) in enumerate(LAST_PARTS):
        if name == COLUMNS:
            out, lo = cuts[n]
            axes, view = WHOLE, lambda c, n=n: gc.at[n, :, :, :, c]

            def keep(_l, total, out=out, lo=lo):
                out[:, lo : lo + gw] = total[0:feature]
                out[:, lo + gw : lo + 2 * gw] = total[feature : 2 * feature]
        elif name == INNER_COLUMNS:
            axes, view = PAIRED, lambda c, n=n: gf1.at[n, :, :, :, c]

            def keep(lead, total, n=n):
                out_fi[lead, n] = total
        elif name == ROWS:
            size = f_shard // 3
            axes, view = SINGLE, lambda c, lo=n * size, size=size: gf2.at[:, :, c, pl.ds(lo, size)]

            def keep(_l, total, lo=n * size, size=size):
                out_f[lo : lo + size, :] = total
        else:
            size = e_shard // 2
            axes, view = WHOLE, lambda c, lo=n * size, size=size: ge.at[:, :, :, c, pl.ds(lo, size)]

            def keep(_l, total, lo=n * size, size=size):
                out_e[lo : lo + size, :] = total
        outside = name in (ROWS, INNER_COLUMNS)
        count = len(order) + 1 + outside + 2 * (axes == PAIRED)
        pipes.add(
            reduce_stages(
                links, view, axes, order, here, bufs[used : used + count], local.at[i] if outside else None, keep, ydev
            )
        )
        used += count
    q_bufs, kv_bufs, small_bufs = bufs[used : used + 5], bufs[used + 5 : used + 20], bufs[used + 20 :]

    sums = {}
    lane = lax.broadcasted_iota(jnp.int32, (span, 128), 1)

    def to_shards(n, left, right):
        for hh in range(NH):
            halves = [
                dot_tn(left(hh), right(half)).reshape(devices // 2, feature, gw) for half in range(2)
            ]
            gc[n, hh] = jnp.concatenate(halves, axis=1).astype(BF).reshape(NZ, NX, NC, 2 * feature, gw)

    def half_of(ref, i):
        return ref[:, i * gw : (i + 1) * gw]

    def step_doc():
        dy2 = dx2[...].astype(BF)
        sums[11] = column_total(dy2)
        fetched(0, 1)
        doc[...] = dot_nt(dy2, wc[4][...]).astype(BF)
        to_shards(4, lambda hh: half_of(oc, hh), lambda i: half_of(dy2, i))

    def step_pairs(n):
        if n == 0:
            fetched(1, 3)

        @pl.loop(2 * n, 2 * n + 2)
        def _(p):
            part = pl.ds(pl.multiple_of(p * WIDE, WIDE), WIDE)
            logs = jnp.sum(jnp.where(lane == p, cross_lse[...], 0.0), axis=-1, keepdims=True)
            q_pair = stack_pair(qc[:, part])
            w = jnp.exp(dot_nt(q_pair, kc[:, part]) - logs)
            do_pair = stack_pair(doc[:, part])
            dp = dot_nt(do_pair, vc[:, part])
            ds = (w * (dp - jnp.sum(w * dp, axis=-1, keepdims=True))).astype(BF)
            dqc[:, part] = (unstack_pair(dot(ds, kc[:, part])) * SCORE_SCALE).astype(BF)
            dkc[:, part] = dot_tn(ds, q_pair).astype(BF)
            dvc[:, part] = dot_tn(w.astype(BF), do_pair).astype(BF)

    ky = links.slot()

    def step_dx1():
        fetched(3, 9)
        dq = dqc[...]
        sums[9] = column_total(dq)
        back, sums[1], sums[4] = norm_back(dot_nt(dq, wc[1][...]), prm[1:2], x1[...])
        total = dx2[...] + back
        dx1[...] = total
        dy1 = total.astype(BF)
        sums[8] = column_total(dy1)
        for i in range(2):
            do = dot_nt(dy1, wc[0][i * gw : (i + 1) * gw, :]).astype(BF)
            for p in range(PAIRS):
                do_low[i, p] = do[:, p * WIDE : (p + 1) * WIDE]
        links.send(do_low.at[1 - h], do_all.at[every, z, x, c, h], ky, ydev)
        do_all[:, z, x, c, h] = do_low[h]
        to_shards(1, lambda hh: half_of(cn, hh), lambda i: half_of(dq, i))
        to_shards(0, lambda hh: o_low[hh], lambda i: half_of(dy1, i))

    def step_enc(n):
        if n == 1:
            for i in range(NH):
                at = pl.ds(i * (enc_rows // NH), enc_rows // NH)
                de = dot_nt(dkc[at, :], wc[2][...]) + dot_nt(dvc[at, :], wc[3][...])
                ge[i] = de.astype(BF).reshape(ge.shape[1:])
            sums[10] = column_total(dvc[...])
            for cp in late:
                cp.start()
        else:
            fetched(11, 14)
            e_all = ge[...].reshape(enc_rows, width)
            for n, d in ((2, dkc), (3, dvc)):
                to_shards(n, lambda hh: e_all[:, hh * gw : (hh + 1) * gw], lambda i: half_of(d, i))

    l_columns, d_columns = [], []
    own_place = (x * 2 + c) * span

    def step_own(n):
        first = lane_half((span, WIDE))
        start = pl.ds(pl.multiple_of(z * group + own_place, span), span)
        if n == 1:
            for cp in late:
                cp.wait()
            for p in range(PAIRS):
                part = pl.ds(p * WIDE, WIDE)
                q2[p] = stack_pair(pool[start, part])
                k2[p] = stack_pair(wk[start, part])
                v2[p] = stack_pair(wk[start, pl.ds(gw + p * WIDE, WIDE)])
                dq2[p] = jnp.zeros_like(dq2[p])
                dk2[p] = jnp.zeros_like(dk2[p])
                dv2[p] = jnp.zeros_like(dv2[p])
            return
        fetched(9, 11)
        got = do_all.at[every, z, x, c, 1 - h]
        links.copy(got, got, ky, ydev).wait_recv()
        deltas = jnp.zeros((span, 128), F32)
        logs = lse[...]
        for p in range(PAIRS):
            part = pl.ds(p * WIDE, WIDE)
            do = do_all[p, z, x, c].reshape(span, WIDE)
            prod = do.astype(F32) * o_wide[:, part]
            low = jnp.sum(jnp.where(first, prod, 0.0), axis=-1, keepdims=True)
            high = jnp.sum(jnp.where(first, 0.0, prod), axis=-1, keepdims=True)
            deltas = jnp.where(lane == 2 * p, low, jnp.where(lane == 2 * p + 1, high, deltas))
            d_columns.append((low, high))
            l_columns.append((logs[:, 2 * p : 2 * p + 1], logs[:, 2 * p + 1 : 2 * p + 2]))
            do2[p] = stack_pair(do)
        st_all[z, x, c, 0:8] = jnp.transpose(logs)[0:8]
        st_all[z, x, c, 8:16] = jnp.transpose(deltas)[0:8]

    pipes.add(gather_stages(links, lambda *i: st_all.at[i[1:]], ZX, here))
    for p in range(PAIRS):
        pipes.add(gather_stages(links, lambda *i, p=p: do_all.at[(p,) + i[1:]], ZX, here))

    def query_side(g, diagonal, p):
        at = pl.ds(pl.multiple_of(g * group, group), group)
        if True:
            for half in range(2):
                mine = pl.ds(half * span, span)
                k_pair, v_pair = wk[at, pl.ds(p * WIDE, WIDE)], wk[at, pl.ds(gw + p * WIDE, WIDE)]
                w = jnp.exp(dot_nt(q2[p, mine], k_pair) - l_columns[p][half])
                if diagonal:
                    place_q = own_place + lax.broadcasted_iota(jnp.int32, w.shape, 0)
                    w = jnp.where(lax.broadcasted_iota(jnp.int32, w.shape, 1) <= place_q, w, 0.0)
                ds = (w * (dot_nt(do2[p, mine], v_pair) - d_columns[p][half])).astype(BF)
                dq2[p, mine] += dot(ds, k_pair)

    def key_side(g, diagonal, p):
        at = pl.ds(pl.multiple_of(g * group, group), group)
        if True:
            part = pl.ds(p * WIDE, WIDE)
            for half in range(2):
                mine = pl.ds(half * span, span)
                head = 2 * p + half
                q_pair = pool[at, part]
                do_pair = do_all[p, g].reshape(group, WIDE)
                stats = [st_all[g, i // 2, i % 2] for i in range(4)]
                log_row = jnp.concatenate([s[head : head + 1] for s in stats], axis=1)
                delta_row = jnp.concatenate([s[8 + head : 9 + head] for s in stats], axis=1)
                w = jnp.exp(dot_nt(k2[p, mine], q_pair) - log_row)
                if diagonal:
                    place_k = own_place + lax.broadcasted_iota(jnp.int32, w.shape, 0)
                    w = jnp.where(place_k <= lax.broadcasted_iota(jnp.int32, w.shape, 1), w, 0.0)
                dv2[p, mine] += dot(w.astype(BF), do_pair)
                ds = (w * (dot_nt(v2[p, mine], do_pair) - delta_row)).astype(BF)
                dk2[p, mine] += dot(ds, q_pair)

    def side(fn, n, ahead):
        t, p = n // PAIRS, n % PAIRS
        if t == 0:
            fn(z, True, p)
        elif ahead:
            pl.when(z + t < NZ)(lambda: fn((z + t) % NZ, False, p))
        else:
            pl.when(z - t >= 0)(lambda: fn((z - t) % NZ, False, p))

    def keep_q(lead, total):
        out_q[lead, 0:feature] = total

    def keep_kv(p):
        def keep(lead, total):
            out_q[lead, feature : 3 * feature, p * WIDE : (p + 1) * WIDE] = total

        return keep

    def output():
        links.copy(y_recv, y_recv, kh, ydev).wait_recv()
        hidden_out[...] = (out_part[...] + y_recv[...].astype(F32)).astype(BF)

    pipes.add(reduce_stages(links, lambda c: gq.at[:, :, :, c], PAIRED, XZ, here, q_bufs, None, keep_q, ydev))
    for p in range(PAIRS):
        view = lambda c, p=p: gkv.at[p, :, :, :, c]
        pipes.add(reduce_stages(links, view, PAIRED, KV_ORDER[p], here, kv_bufs[5 * p : 5 * p + 5], None, keep_kv(p), ydev))
    from_corners, by_z, small_z = small_bufs
    k_corner, k_small = [links.slot() for _ in range(7)], [links.slot() for _ in range(3)]
    flip = lambda v, k, bit: 1 - v if k >> bit & 1 else v

    def small_start():
        for k in range(1, 8):
            away = gs.at[flip(h, k, 2), :, flip(x, k, 1), flip(c, k, 0)]
            links.send(away, from_corners.at[k - 1], k_corner[k - 1], corner(h, z, x, c, k))

    def small_middle():
        total = gs[h, :, x, c].astype(F32)
        for k in range(1, 8):
            got = from_corners.at[k - 1]
            links.copy(got, got, k_corner[k - 1], corner(h, z, x, c, k)).wait_recv()
            total = total + from_corners[k - 1].astype(F32)
        by_z[...] = total.astype(BF)
        for d, k in zip((1, 2, 3), k_small):
            to = (z + d) % NZ
            links.send(by_z.at[to], small_z.at[d - 1], k, device_at(h, to, x, c))

    def small_finish():
        total = by_z[z].astype(F32)
        for d, k in zip((1, 2, 3), k_small):
            links.copy(small_z.at[d - 1], small_z.at[d - 1], k, device_at(h, (z + d) % NZ, x, c)).wait_recv()
            total = total + small_z[d - 1].astype(F32)
        out_s[...] = total

    pipes.add([small_start, small_middle, small_finish])
    kz = links.slot()

    def query_done():
        dq = jnp.concatenate([unstack_pair(dq2[p]) * SCORE_SCALE for p in range(PAIRS)], axis=1).astype(BF)
        fetched(14, 17)
        sums[6] = column_total(dq)
        gq[...] = dot_tn(a_span[...], dq).astype(BF).reshape(gq.shape)
        dz_q[...] = dot_nt(dq, wq[0][...])

    v_sums = []

    def key_done(p):
        if p == PAIRS:
            sums[7] = jnp.concatenate(v_sums, axis=1)
            dz_send[...] = dz_q[...].astype(BF).reshape(2, rows, width)
            links.send(dz_send.at[1 - h], dz_recv, kz, ydev)
            return
        part = pl.ds(p * WIDE, WIDE)
        dk, dv = unstack_pair(dk2[p]).astype(BF), unstack_pair(dv2[p]).astype(BF)
        v_sums.append(column_total(dv))
        whole = [dot_tn(a_span[...], d).reshape(devices, feature, WIDE) for d in (dk, dv)]
        gkv[p] = jnp.concatenate(whole, axis=1).astype(BF).reshape(gkv.shape[1:])
        dz_q[...] += dot_nt(dk, wq[1][:, part]) + dot_nt(dv, wq[2][:, part])

    def input_grad():
        links.copy(dz_recv, dz_recv, kz, ydev).wait_recv()
        dz_own = dz_send[h].astype(F32) + dz_recv[...].astype(F32)
        back, sums[0], sums[3] = norm_back(dz_own, prm[0:1], hid[...].astype(F32))
        hidden_grad[...] = dx1[...] + back
        for i in (6, 7):
            sums[i] = jnp.concatenate([jnp.where(h == k, sums[i], 0.0) for k in range(2)], axis=1)
        block = row_sums[0:16]
        row = lax.broadcasted_iota(jnp.int32, block.shape, 0)
        for i, value in sums.items():
            block = jnp.where(row == i, value, block)
        wide = jnp.concatenate([block, jnp.zeros((128 - 16, width), F32)], axis=0)
        by_feature = jnp.transpose(wide).reshape(devices, feature, 128)
        fbs[...] = jnp.zeros_like(fbs)
        each = width // f_shard
        for d in range(devices):
            at = 16 + 8 * (d // each)
            fbs[d : d + 1, 0:f_shard] = row_sums[at : at + 1, (d % each) * f_shard : (d % each + 1) * f_shard]
        fb = jnp.broadcast_to(fbs[...][:, None, :], (devices, 8, 128))
        gs[...] = jnp.concatenate([by_feature, fb], axis=1).astype(BF).reshape(gs.shape)

    steps = {
        GO: pipes.go, DOC: lambda n: step_doc(), CROSS_PAIRS: step_pairs, DX1: lambda n: step_dx1(), ENC: step_enc,
        OWN: step_own, HIDDEN_OUT: lambda n: output(), BY_QUERY: lambda n: side(query_side, n, False), BY_KEY: lambda n: side(key_side, n, True),
        QUERY_DONE: lambda n: query_done(), KEY_DONE: key_done, INPUT_GRAD: lambda n: input_grad(),
    }
    for name, n in LAST_ORDER:
        steps[name](n)
    links.drain()


LAST_SEMS = 170


def run_last(vmem_args, hbm_args):
    hid, en, keys, gf1, gf2 = hbm_args[0], hbm_args[9], hbm_args[11], hbm_args[17], hbm_args[18]
    rows, width = hid.shape
    span = 2 * rows
    gw = PAIRS * WIDE
    grid = (NH, NZ, NX, NC)
    devices = NH * NZ * NX * NC
    feature = width // devices
    e_rows, f_rows = en.shape[4], gf2.shape[3]
    enc_rows = e_rows * devices
    hbm, vmem = pl.BlockSpec(memory_space=pl.ANY), pl.BlockSpec(memory_space=pltpu.VMEM)
    S = jax.ShapeDtypeStruct
    V = pltpu.VMEM
    outs = (
        S((rows, width), BF), S((rows, width), F32), S((feature, width), F32), S((feature, width), F32), S((feature, 2 * width), F32),
        S((feature, width), F32), S((NH, gf1.shape[0], 2 * feature, gw), F32), S((f_rows, width), F32), S((e_rows, width), F32),
        S((2, 3 * feature, gw), F32), S((32, 128), F32),
    )
    shard = (2 * feature, gw)
    bufs = []
    for name, n, order in LAST_PARTS:
        size = {COLUMNS: shard, INNER_COLUMNS: shard, ROWS: (f_rows // 3, width), ENCODED: (e_rows // 2, width)}[name]
        axes = {INNER_COLUMNS: PAIRED, ROWS: SINGLE}.get(name, WHOLE)
        bufs += reduce_bufs(size, axes, order, name in (ROWS, INNER_COLUMNS))
    q_shard, kv_shard = (feature, gw), (2 * feature, WIDE)
    bufs += reduce_bufs(q_shard, PAIRED, XZ, False)
    for p in range(PAIRS):
        bufs += reduce_bufs(kv_shard, PAIRED, KV_ORDER[p], False)
    bufs += [V((7, NZ, 32, 128), BF), V((NZ, 32, 128), BF), V((3, 32, 128), BF)]
    stacked, stacked_f = V((PAIRS, 2 * span, WIDE), BF), V((PAIRS, 2 * span, WIDE), F32)
    D = pltpu.SemaphoreType.DMA
    return pl.pallas_call(
        last_kernel,
        out_shape=outs,
        in_specs=[vmem] * len(vmem_args) + [hbm] * len(hbm_args),
        out_specs=(vmem,) * len(outs),
        scratch_shapes=[V(m.shape, m.dtype) for m in hbm_args[:9]] + [
            V((rows, width), BF), V((max(keys.shape[0], 5 * width), width), BF), V((max(keys.shape[0], 4 * enc_rows), width), BF),
            V((5,) + grid + shard, BF), V(en.shape, BF), V((rows, width), BF), V((rows, width), BF), V((rows, width), F32), V((2, PAIRS, rows, WIDE), BF),
            V((PAIRS, NZ, NX, NC, 2, rows, WIDE), BF), V((NZ, NX, NC, 16, span), F32),
            stacked, stacked, stacked, stacked, stacked_f, stacked_f, stacked_f,
            V((span, width), F32), V(grid + q_shard, BF), V((PAIRS,) + grid + kv_shard, BF), V(grid + (32, 128), BF), V((devices, 128), F32),
            V((2, rows, width), BF), V((rows, width), BF),
            D((LAST_SEMS,)), D((LAST_SEMS,)), D((len(LAST_PARTS),)), D((32,)),
        ] + bufs,
        compiler_params=pltpu.CompilerParams(
            collective_id=1, has_side_effects=True, vmem_limit_bytes=63 << 20
        ),
        cost_estimate=pl.CostEstimate(flops=2 * 10**10, bytes_accessed=10**8, transcendentals=10**7),
        name="backward_and_reduce",
    )(*vmem_args, *hbm_args)


def deliver_kernel(
    hidden_out, hidden_grad, o, cq, ckv, co, fi_in, f, e, qkv_in, small_in,
    out_hidden, out_grad, out_e, gains, shifts, biases, out_qkv, out_o, out_cq, out_ckv, out_co, out_fi, out_bias, out_f,
    fi, qkv, small, sems,
):
    pairs = (
        (hidden_out, out_hidden.at[0, 0]), (hidden_grad, out_grad.at[0, 0]), (e, out_e.at[0]), (o, out_o), (cq, out_cq),
        (ckv, out_ckv), (co, out_co), (f, out_f), (fi_in, fi), (qkv_in, qkv), (small_in, small),
    )
    copies = [pltpu.make_async_copy(source, target, sems.at[i]) for i, (source, target) in enumerate(pairs)]
    for cp in copies:
        cp.start()
    for cp in copies:
        cp.wait()
    gw = qkv.shape[2]
    feature = qkv.shape[1] // 3
    for k in range(2):
        for i in range(3):
            lo = (2 * i + k) * gw
            out_qkv[:, lo : lo + gw] = qkv[k, i * feature : (i + 1) * feature, :]
    tiles = fi.shape[1]
    for k in range(2):
        for j in range(tiles):
            for half in range(2):
                lo = ((k * tiles + j) * 2 + half) * gw
                out_fi[:, lo : lo + gw] = fi[k, j, half * feature : (half + 1) * feature, :]
    by_row = jnp.transpose(jnp.concatenate([small[...], jnp.zeros((128 - small.shape[0], 128), F32)], axis=0))
    gains[...] = by_row[0:3, 0:feature]
    shifts[...] = by_row[3:6, 0:feature]
    biases[...] = by_row[6:13, 0:feature]
    out_bias[...] = small[feature : feature + 1, 0 : out_bias.shape[1]]


def run_deliver(hidden_out, hidden_grad, o, cq, ckv, co, fi, f, e, qkv, small):
    S = jax.ShapeDtypeStruct
    feature, width = o.shape
    inner = fi.shape[0] * fi.shape[1] * width
    outs = (
        S((1, 1) + hidden_out.shape, BF), S((1, 1) + hidden_grad.shape, F32), S((1,) + e.shape, F32),
        S((3, feature), F32), S((3, feature), F32), S((7, feature), F32), S((feature, 3 * width), F32),
        S(o.shape, F32), S(cq.shape, F32), S(ckv.shape, F32), S(co.shape, F32), S((feature, inner), F32), S((1, f.shape[0]), F32), S(f.shape, F32),
    )
    hbm, vmem = pl.BlockSpec(memory_space=pltpu.HBM), pl.BlockSpec(memory_space=pltpu.VMEM)
    return pl.pallas_call(
        deliver_kernel, out_shape=outs, in_specs=[hbm] * 11, out_specs=(vmem,) * len(outs),
        scratch_shapes=[
            pltpu.VMEM(fi.shape, F32), pltpu.VMEM(qkv.shape, F32), pltpu.VMEM(small.shape, F32), pltpu.SemaphoreType.DMA((11,)),
        ],
        compiler_params=pltpu.CompilerParams(vmem_limit_bytes=62 << 20), name="deliver",
    )(hidden_out, hidden_grad, o, cq, ckv, co, fi, f, e, qkv, small)


def fused_body(
    hidden_in, encoded, out_grad, ln_gain, ln_bias, biases, self_qkv, self_out, cross_q,
    cross_kv, cross_out, ffn_in, ffn_bias, ffn_out,
):
    got = run_first(
        hidden_in[0, 0], out_grad[0, 0], encoded[0], ln_gain, ln_bias, biases, self_qkv, self_out, cross_q, cross_kv,
        cross_out, ffn_in, ffn_bias[None], ffn_out,
    )
    wide, (prm, a_span, o_wide, o_low, lse, x1, cn, qc, oc, cross_lse, en) = got[:9], got[9:20]
    out_part, out_send, dx2, row_sums = got[20:]
    grads = run_last(
        (out_part, out_send, dx2, oc, qc, cross_lse),
        (hidden_in[0, 0], prm, a_span, o_wide, o_low, lse, x1, cn, row_sums, en) + tuple(wide),
    )
    done = run_deliver(*grads)
    return done[:12] + (done[12][0], done[13])


def solution(mesh):
    fused = mesh.shape["head"] == NH and mesh.shape["blk"] == NZ * NX * NC
    return jax.shard_map(
        fused_body if fused else body,
        mesh=mesh,
        in_specs=(
            P(None, "blk", "head", None),
            P(None, ("head", "blk"), None),
            P(None, "blk", "head", None),
            P(None, ("head", "blk")),
            P(None, ("head", "blk")),
            P(None, ("head", "blk")),
            P(("head", "blk"), None),
            P(("head", "blk"), None),
            P(("head", "blk"), None),
            P(("head", "blk"), None),
            P(("head", "blk"), None),
            P(("head", "blk"), None),
            P(("head", "blk")),
            P(("head", "blk"), None),
        ),
        out_specs=(
            P(None, "blk", "head", None),
            P(None, "blk", "head", None),
            P(None, ("head", "blk"), None),
            P(None, ("head", "blk")),
            P(None, ("head", "blk")),
            P(None, ("head", "blk")),
            P(("head", "blk"), None),
            P(("head", "blk"), None),
            P(("head", "blk"), None),
            P(("head", "blk"), None),
            P(("head", "blk"), None),
            P(("head", "blk"), None),
            P(("head", "blk")),
            P(("head", "blk"), None),
        ),
        check_vma=False,
    )
```

```python
import jax
import jax.numpy as jnp
from jax import lax
from jax.experimental import pallas as pl
from jax.experimental.pallas import tpu as pltpu
from jax.sharding import PartitionSpec as P

HEADS = 12
HEAD_DIM = 64


EPSILON = 1e-05
SCORE_SCALE = 0.125


def from_behind(block, axis, distance):
    devices = range(lax.axis_size(axis))
    route = [((i - distance) % len(devices), i) for i in devices]
    return lax.ppermute(block, axis, route)


def layer_norm(values, gain_row, shift_row):
    centered = values - jnp.mean(values, axis=-1, keepdims=True)
    spread = jnp.mean(centered * centered, axis=-1, keepdims=True)
    return centered * lax.rsqrt(spread + EPSILON) * gain_row + shift_row


def norm_grads(values, gain_row, shift_row, upstream):
    result, pullback = jax.vjp(layer_norm, values, gain_row, shift_row)
    return pullback(upstream)


def exact_gelu(values):
    return jax.nn.gelu(values, approximate=False)


def project(left, right):
    return jnp.einsum("srk,kn->srn", left, right, preferred_element_type=jnp.float32)


def project_back(upstream, weight):
    return jnp.einsum("srn,kn->srk", upstream, weight, preferred_element_type=jnp.float32)


def weight_grad(left, upstream):
    return jnp.einsum("srk,srn->kn", left, upstream, preferred_element_type=jnp.float32)


def column_sum(upstream):
    return jnp.sum(upstream.astype(jnp.float32), axis=(0, 1))


def block_scores(queries, key_block, query_start, key_start):
    scores = (
        jnp.einsum("sqhd,skhd->shqk", queries, key_block, preferred_element_type=jnp.float32)
        * SCORE_SCALE
    )
    query_place = query_start + lax.iota(jnp.int32, queries.shape[1])
    key_place = key_start + lax.iota(jnp.int32, key_block.shape[1])
    allowed = key_place[None, :] <= query_place[:, None]
    return (scores, allowed)


def forward_block(carried, key_block, value_block, queries, query_start, key_start):
    row_top, row_total, weighted = carried
    scores, allowed = block_scores(queries, key_block, query_start, key_start)
    scores = jnp.where(allowed, scores, -jnp.inf)
    new_top = jnp.maximum(row_top, jnp.max(scores, axis=-1))
    weights = jnp.exp(scores - new_top[..., None])
    factor = jnp.exp(row_top - new_top)
    row_total = row_total * factor + jnp.sum(weights, axis=-1)
    addition = jnp.einsum(
        "shqk,skhd->sqhd",
        weights.astype(jnp.bfloat16),
        value_block,
        preferred_element_type=jnp.float32,
    )
    weighted = weighted * jnp.transpose(factor, (0, 2, 1))[..., None] + addition
    return (new_top, row_total, weighted)


def backward_block(
    queries, out_grads, log_total, row_delta, key_block, value_block, query_start, key_start
):
    scores, allowed = block_scores(queries, key_block, query_start, key_start)
    weights = jnp.where(allowed, jnp.exp(scores - log_total[..., None]), 0.0)
    value_grad = jnp.einsum(
        "shqk,sqhd->skhd",
        weights.astype(jnp.bfloat16),
        out_grads,
        preferred_element_type=jnp.float32,
    )
    prob_grad = jnp.einsum(
        "sqhd,skhd->shqk", out_grads, value_block, preferred_element_type=jnp.float32
    )
    score_grad = (weights * (prob_grad - row_delta[..., None])).astype(jnp.bfloat16)
    query_grad = jnp.einsum(
        "shqk,skhd->sqhd", score_grad, key_block, preferred_element_type=jnp.float32
    )
    key_grad = jnp.einsum(
        "shqk,sqhd->skhd", score_grad, queries, preferred_element_type=jnp.float32
    )
    return (query_grad, key_grad, value_grad)


def cross_forward(operands):
    queries, key_rows, value_rows = operands
    scores = (
        jnp.einsum("qhd,khd->hqk", queries, key_rows, preferred_element_type=jnp.float32)
        * SCORE_SCALE
    )
    row_top = jnp.max(scores, axis=-1, keepdims=True)
    weights = jnp.exp(scores - row_top)
    row_total = jnp.sum(weights, axis=-1, keepdims=True)
    weights_low = (weights / row_total).astype(jnp.bfloat16)
    attended = jnp.einsum(
        "hqk,khd->qhd", weights_low, value_rows, preferred_element_type=jnp.float32
    )
    return (attended, (row_top + jnp.log(row_total))[..., 0])


def cross_backward(operands):
    queries, key_rows, value_rows, log_total, out_grads = operands
    scores = (
        jnp.einsum("qhd,khd->hqk", queries, key_rows, preferred_element_type=jnp.float32)
        * SCORE_SCALE
    )
    weights = jnp.exp(scores - log_total[..., None])
    value_grad = jnp.einsum(
        "hqk,qhd->khd", weights.astype(jnp.bfloat16), out_grads, preferred_element_type=jnp.float32
    )
    prob_grad = jnp.einsum(
        "qhd,khd->hqk", out_grads, value_rows, preferred_element_type=jnp.float32
    )
    row_delta = jnp.sum(weights * prob_grad, axis=-1, keepdims=True)
    score_grad = (weights * (prob_grad - row_delta)).astype(jnp.bfloat16)
    query_grad = (
        jnp.einsum("hqk,khd->qhd", score_grad, key_rows, preferred_element_type=jnp.float32)
        * SCORE_SCALE
    )
    key_grad = (
        jnp.einsum("hqk,qhd->khd", score_grad, queries, preferred_element_type=jnp.float32)
        * SCORE_SCALE
    )
    return (query_grad, key_grad, value_grad)


def body(
    hidden_in,
    encoded,
    out_grad,
    ln_gain,
    ln_bias,
    biases,
    self_qkv,
    self_out,
    cross_q,
    cross_kv,
    cross_out,
    ffn_in,
    ffn_bias,
    ffn_out,
):
    seq_count = hidden_in.shape[0]
    row_count = hidden_in.shape[2]
    model_width = hidden_in.shape[3]
    groups = lax.axis_size("head")
    block_total = lax.axis_size("blk")
    span_rows = row_count * groups
    group_width = model_width // groups
    local_heads = HEADS // groups
    head_shape = (seq_count, span_rows, local_heads, HEAD_DIM)
    gathered = (
        lax.all_gather(ln_gain, ("head", "blk"), axis=1, tiled=True),
        lax.all_gather(ln_bias, ("head", "blk"), axis=1, tiled=True),
        lax.all_gather(biases, ("head", "blk"), axis=1, tiled=True),
        lax.all_gather(self_qkv, ("head", "blk"), axis=0, tiled=True),
        lax.all_gather(self_out, ("head", "blk"), axis=0, tiled=True),
        lax.all_gather(cross_q, ("head", "blk"), axis=0, tiled=True),
        lax.all_gather(cross_kv, ("head", "blk"), axis=0, tiled=True),
        lax.all_gather(cross_out, ("head", "blk"), axis=0, tiled=True),
        lax.all_gather(ffn_in, ("head", "blk"), axis=0, tiled=True),
        lax.all_gather(ffn_bias, ("head", "blk"), axis=0, tiled=True),
        lax.all_gather(ffn_out, ("head", "blk"), axis=0, tiled=True),
    )
    gain_rows = gathered[0].astype(jnp.float32)
    shift_rows = gathered[1].astype(jnp.float32)
    bias_rows = gathered[2].astype(jnp.float32)
    qkv_weight = gathered[3]
    out_weight = gathered[4]
    query_weight = gathered[5]
    memory_weight = gathered[6]
    cross_weight = gathered[7]
    inner_weight = gathered[8]
    inner_bias = gathered[9].astype(jnp.float32)
    outer_weight = gathered[10]
    hidden = hidden_in[:, 0].astype(jnp.float32)
    normed = layer_norm(hidden, gain_rows[0], shift_rows[0]).astype(jnp.bfloat16)
    mixed_qkv = project(normed, qkv_weight)
    mixed_qkv = mixed_qkv + jnp.concatenate(
        [bias_rows[0], jnp.zeros_like(bias_rows[0]), bias_rows[1]]
    )
    mixed_qkv = mixed_qkv.astype(jnp.bfloat16).reshape(seq_count, row_count, 3, groups, group_width)
    grouped = lax.all_to_all(mixed_qkv, "head", split_axis=3, concat_axis=1, tiled=True)
    self_queries = grouped[:, :, 0, 0].reshape(head_shape)
    self_keys = grouped[:, :, 1, 0]
    self_values = grouped[:, :, 2, 0]
    block_index = lax.axis_index("blk")
    own_start = block_index * span_rows
    stat_shape = (seq_count, local_heads, span_rows)
    initial = (
        jnp.full(stat_shape, -jnp.inf, jnp.float32),
        jnp.zeros(stat_shape, jnp.float32),
        jnp.zeros(head_shape, jnp.float32),
    )
    key_piece = lax.all_gather(self_keys, "blk", axis=1, tiled=True)
    value_piece = lax.all_gather(self_values, "blk", axis=1, tiled=True)
    piece_rows = key_piece.shape[1]
    block_count = piece_rows // span_rows
    layout = (seq_count, block_count, span_rows, local_heads, HEAD_DIM)
    key_blocks = jnp.moveaxis(key_piece.reshape(layout), 1, 0)
    value_blocks = jnp.moveaxis(value_piece.reshape(layout), 1, 0)
    block_starts = span_rows * lax.iota(jnp.int32, block_count)

    def visit(running, element):
        key_block, value_block, key_start = element

        def visit_compute(current):
            return forward_block(
                current, key_block, value_block, self_queries, own_start, key_start
            )

        def visit_unchanged(current):
            return current

        return (
            lax.cond(key_start < own_start + span_rows, visit_compute, visit_unchanged, running),
            None,
        )

    result, unused = lax.scan(visit, initial, (key_blocks, value_blocks, block_starts))
    running_top, running_total, running_sum = result
    log_total = running_top + jnp.log(running_total)
    attended = running_sum / jnp.transpose(running_total, (0, 2, 1))[..., None]
    attended_low = attended.astype(jnp.bfloat16).reshape(seq_count, span_rows, 1, group_width)
    self_mixed = lax.all_to_all(
        attended_low, "head", split_axis=1, concat_axis=2, tiled=True
    ).reshape(seq_count, row_count, model_width)
    after_self = hidden + project(self_mixed, out_weight) + bias_rows[2]
    cross_normed = layer_norm(after_self, gain_rows[1], shift_rows[1]).astype(jnp.bfloat16)
    cross_queries = (project(cross_normed, query_weight) + bias_rows[3]).astype(jnp.bfloat16)
    memory_mixed = project(encoded, memory_weight)
    memory_keys = memory_mixed[..., :model_width].astype(jnp.bfloat16)
    memory_values = (memory_mixed[..., model_width:] + bias_rows[4]).astype(jnp.bfloat16)
    all_keys, all_values = (
        lax.all_gather(memory_keys, ("head", "blk"), axis=1, tiled=True),
        lax.all_gather(memory_values, ("head", "blk"), axis=1, tiled=True),
    )
    query_heads = cross_queries.reshape(seq_count, row_count, HEADS, HEAD_DIM)
    key_heads = all_keys.reshape(seq_count, -1, HEADS, HEAD_DIM)
    value_heads = all_values.reshape(seq_count, -1, HEADS, HEAD_DIM)
    cross_result, cross_lse = lax.map(cross_forward, (query_heads, key_heads, value_heads))
    cross_mixed = cross_result.astype(jnp.bfloat16).reshape(seq_count, row_count, model_width)
    after_cross = after_self + project(cross_mixed, cross_weight) + bias_rows[5]
    ffn_normed = layer_norm(after_cross, gain_rows[2], shift_rows[2]).astype(jnp.bfloat16)
    inner_pre = project(ffn_normed, inner_weight) + inner_bias
    inner_act = exact_gelu(inner_pre).astype(jnp.bfloat16)
    output = after_cross + project(inner_act, outer_weight) + bias_rows[6]
    hidden_out = output.astype(jnp.bfloat16)[:, None]
    upstream = out_grad[:, 0].astype(jnp.float32)
    outer_low = upstream.astype(jnp.bfloat16)
    outer_weight_grad = weight_grad(inner_act, outer_low)
    act_grad = project_back(outer_low, outer_weight)
    unused_value, gelu_pull = jax.vjp(exact_gelu, inner_pre)
    pre_grad = gelu_pull(act_grad)[0].astype(jnp.bfloat16)
    inner_weight_grad = weight_grad(ffn_normed, pre_grad)
    inner_bias_grad = column_sum(pre_grad)
    back_cross, gain_grad_two, shift_grad_two = norm_grads(
        after_cross, gain_rows[2], shift_rows[2], project_back(pre_grad, inner_weight)
    )
    cross_total = upstream + back_cross
    cross_low = cross_total.astype(jnp.bfloat16)
    cross_weight_grad = weight_grad(cross_mixed, cross_low)
    cross_attn_grad = (
        project_back(cross_low, cross_weight)
        .astype(jnp.bfloat16)
        .reshape(seq_count, row_count, HEADS, HEAD_DIM)
    )
    cross_query_grads, cross_key_grads, cross_value_grads = lax.map(
        cross_backward, (query_heads, key_heads, value_heads, cross_lse, cross_attn_grad)
    )
    memory_key_grad, memory_value_grad = (
        lax.psum_scatter(
            cross_key_grads.reshape(seq_count, -1, model_width),
            ("head", "blk"),
            scatter_dimension=1,
            tiled=True,
        ),
        lax.psum_scatter(
            cross_value_grads.reshape(seq_count, -1, model_width),
            ("head", "blk"),
            scatter_dimension=1,
            tiled=True,
        ),
    )
    memory_key_low = memory_key_grad.astype(jnp.bfloat16)
    memory_value_low = memory_value_grad.astype(jnp.bfloat16)
    encoded_grad = project_back(memory_key_low, memory_weight[:, :model_width]) + project_back(
        memory_value_low, memory_weight[:, model_width:]
    )
    memory_weight_grad = weight_grad(
        encoded, jnp.concatenate([memory_key_low, memory_value_low], axis=-1)
    )
    cross_query_low = cross_query_grads.reshape(seq_count, row_count, model_width).astype(
        jnp.bfloat16
    )
    query_weight_grad = weight_grad(cross_normed, cross_query_low)
    back_self, gain_grad_one, shift_grad_one = norm_grads(
        after_self, gain_rows[1], shift_rows[1], project_back(cross_query_low, query_weight)
    )
    self_total = cross_total + back_self
    self_low = self_total.astype(jnp.bfloat16)
    out_weight_grad = weight_grad(self_mixed, self_low)
    attn_grad = (
        project_back(self_low, out_weight)
        .astype(jnp.bfloat16)
        .reshape(seq_count, row_count, groups, group_width)
    )
    grad_heads = lax.all_to_all(attn_grad, "head", split_axis=2, concat_axis=1, tiled=True).reshape(
        head_shape
    )
    row_delta = jnp.einsum("sqhd,sqhd->shq", grad_heads.astype(jnp.float32), attended)
    own_keys = self_keys.reshape(head_shape)
    own_values = self_values.reshape(head_shape)
    zero_grads = jnp.zeros(head_shape, jnp.float32)

    def key_turn(turn_index, carried):
        moving_keys, moving_values, moving_key_grads, moving_value_grads, query_grads = carried
        source = (block_index + turn_index) % block_total

        def key_compute(partial_grads):
            addition = backward_block(
                self_queries,
                grad_heads,
                log_total,
                row_delta,
                moving_keys,
                moving_values,
                own_start,
                source * span_rows,
            )
            return (
                partial_grads[0] + addition[0],
                partial_grads[1] + addition[1],
                partial_grads[2] + addition[2],
            )

        def key_unchanged(partial_grads):
            return partial_grads

        needed = (turn_index == 0) | (turn_index + block_index >= block_total)
        query_grads, moving_key_grads, moving_value_grads = lax.cond(
            needed, key_compute, key_unchanged, (query_grads, moving_key_grads, moving_value_grads)
        )
        moving_keys, moving_values = from_behind(
            (moving_keys, moving_values), "blk", block_total - 1
        )
        moving_key_grads, moving_value_grads = (
            from_behind(moving_key_grads.astype(jnp.bfloat16), "blk", block_total - 1).astype(
                moving_key_grads.dtype
            ),
            from_behind(moving_value_grads.astype(jnp.bfloat16), "blk", block_total - 1).astype(
                moving_value_grads.dtype
            ),
        )
        return (moving_keys, moving_values, moving_key_grads, moving_value_grads, query_grads)

    finished = lax.fori_loop(
        0, block_total, key_turn, (own_keys, own_values, zero_grads, zero_grads, zero_grads)
    )
    key_grads = finished[2]
    value_grads = finished[3]
    query_grads = finished[4]
    qkv_grads = jnp.stack([query_grads * SCORE_SCALE, key_grads * SCORE_SCALE, value_grads], axis=2)
    qkv_low = qkv_grads.astype(jnp.bfloat16).reshape(seq_count, span_rows, 3, 1, group_width)
    token_grads = lax.all_to_all(qkv_low, "head", split_axis=1, concat_axis=3, tiled=True).reshape(
        seq_count, row_count, 3 * model_width
    )
    qkv_weight_grad = weight_grad(normed, token_grads)
    back_input, gain_grad_zero, shift_grad_zero = norm_grads(
        hidden, gain_rows[0], shift_rows[0], project_back(token_grads, qkv_weight)
    )
    hidden_grad = (self_total + back_input)[:, None]
    bias_grad = jnp.stack(
        [
            column_sum(token_grads[..., :model_width]),
            column_sum(token_grads[..., 2 * model_width :]),
            column_sum(self_low),
            column_sum(cross_query_low),
            column_sum(memory_value_low),
            column_sum(cross_low),
            column_sum(outer_low),
        ]
    )
    gain_grad = jnp.stack([gain_grad_zero, gain_grad_one, gain_grad_two])
    shift_grad = jnp.stack([shift_grad_zero, shift_grad_one, shift_grad_two])
    reduced = (
        lax.psum_scatter(gain_grad, ("head", "blk"), scatter_dimension=1, tiled=True),
        lax.psum_scatter(shift_grad, ("head", "blk"), scatter_dimension=1, tiled=True),
        lax.psum_scatter(bias_grad, ("head", "blk"), scatter_dimension=1, tiled=True),
        lax.psum_scatter(qkv_weight_grad, ("head", "blk"), scatter_dimension=0, tiled=True),
        lax.psum_scatter(out_weight_grad, ("head", "blk"), scatter_dimension=0, tiled=True),
        lax.psum_scatter(query_weight_grad, ("head", "blk"), scatter_dimension=0, tiled=True),
        lax.psum_scatter(memory_weight_grad, ("head", "blk"), scatter_dimension=0, tiled=True),
        lax.psum_scatter(cross_weight_grad, ("head", "blk"), scatter_dimension=0, tiled=True),
        lax.psum_scatter(inner_weight_grad, ("head", "blk"), scatter_dimension=0, tiled=True),
        lax.psum_scatter(inner_bias_grad, ("head", "blk"), scatter_dimension=0, tiled=True),
        lax.psum_scatter(outer_weight_grad, ("head", "blk"), scatter_dimension=0, tiled=True),
    )
    return (
        hidden_out,
        hidden_grad,
        encoded_grad,
        reduced[0],
        reduced[1],
        reduced[2],
        reduced[3],
        reduced[4],
        reduced[5],
        reduced[6],
        reduced[7],
        reduced[8],
        reduced[9],
        reduced[10],
    )


MESH = pl.DeviceIdType.MESH
F32 = jnp.float32
BF = jnp.bfloat16
NZ, NX, NC, NH = 4, 2, 2, 2
PAIRS = 3
WIDE = 2 * HEAD_DIM


def place():
    h = lax.axis_index("head")
    b = lax.axis_index("blk")
    return h, b // 4, (b // 2) % 2, b % 2


def device_at(h, z, x, c):
    return (h, z * 4 + x * 2 + c)


def corner(h, z, x, c, k):
    flip = lambda v, bit: 1 - v if k >> bit & 1 else v
    return device_at(flip(h, 2), z, flip(x, 1), flip(c, 0))


def greet(h, z, x, c, corners=False):
    barrier = pltpu.get_barrier_semaphore()
    others = [device_at(h, z, x, 1 - c), device_at(h, z, 1 - x, c), device_at(1 - h, z, x, c)]
    others += [device_at(h, (z + d) % NZ, x, c) for d in (1, 2, 3)]
    if corners:
        others += [corner(h, z, x, c, k) for k in (3, 5, 6, 7)]
    for other in others:
        pl.semaphore_signal(barrier, inc=1, device_id=other, device_id_type=MESH)
    pl.semaphore_wait(barrier, len(others))


def dot(a, b):
    return jnp.dot(a, b, preferred_element_type=F32)


def dot_nt(a, b):
    return lax.dot_general(a, b, (((1,), (1,)), ((), ())), preferred_element_type=F32)


def dot_tn(a, b):
    return lax.dot_general(a, b, (((0,), (0,)), ((), ())), preferred_element_type=F32)


def lane_half(shape):
    return lax.broadcasted_iota(jnp.int32, shape, len(shape) - 1) < HEAD_DIM


def stack_pair(values):
    first = lane_half(values.shape)
    zero = jnp.zeros_like(values)
    return jnp.concatenate([jnp.where(first, values, zero), jnp.where(first, zero, values)], axis=0)


def unstack_pair(stacked):
    rows = stacked.shape[0] // 2
    top, low = stacked[:rows], stacked[rows:]
    return jnp.where(lane_half(top.shape), top, low)


class Links:
    def __init__(self, send, recv):
        self.send_sems, self.recv_sems, self.count, self.open = send, recv, 0, []

    def slot(self):
        self.count += 1
        return self.count - 1

    def copy(self, source, target, k, device):
        return pltpu.make_async_remote_copy(
            source, target, self.send_sems.at[k], self.recv_sems.at[k],
            device_id=device, device_id_type=MESH,
        )

    def send(self, source, target, k, device):
        c = self.copy(source, target, k, device)
        c.start()
        self.open.append(c)

    def drain(self):
        for c in self.open:
            c.wait_send()
        self.open = []


def gather_stages(links, view, order, here, own=None, ready=None):
    h, z, x, c = here
    every = slice(None)
    known = {"y": h, "z": z, "x": x}
    stages = []

    def seen(core, **other):
        at = {**known, **other}
        return view(at["y"], at["z"], at["x"], core)

    for axis in order + ("c",):
        first = not stages
        sent = seen(c)
        source = own[0] if first and own is not None else sent
        if axis == "z":
            routes = [
                (links.slot(), device_at(h, (z + d) % NZ, x, c), seen(c, z=(z - d) % NZ)) for d in (1, 2, 3)
            ]
        elif axis == "x":
            routes = [(links.slot(), device_at(h, z, 1 - x, c), seen(c, x=1 - x))]
        elif axis == "y":
            routes = [(links.slot(), device_at(1 - h, z, x, c), seen(c, y=1 - h))]
        else:
            routes = [(links.slot(), device_at(h, z, x, 1 - c), seen(1 - c))]
        if axis != "c":
            known[axis] = every

        def start(first=first, sent=sent, source=source, routes=routes):
            if first and ready is not None:
                ready()
            for k, device, _got in routes:
                links.send(source, sent, k, device)

        def wait(first=first, routes=routes):
            if first and own is not None:
                own[1].wait()
            for k, device, got in routes:
                links.copy(got, got, k, device).wait_recv()

        stages.append((start, wait))

    made = [stages[0][0]]
    for (_s, wait), (start, _w) in zip(stages, stages[1:]):
        made.append(lambda wait=wait, start=start: (wait(), start()))
    return made + [stages[-1][1]]


class Pipes:
    def __init__(self):
        self.left = []

    def add(self, stages):
        self.left.append(list(stages))

    def go(self, i):
        self.left[i].pop(0)()


def norm_stats(v):
    centered = v - jnp.mean(v, axis=-1, keepdims=True)
    inv = lax.rsqrt(jnp.mean(centered * centered, axis=-1, keepdims=True) + EPSILON)
    return centered * inv, inv


(
    GO, PACK, SWAP, UNPACK, PROJECTION, WORK, SELF_DONE, RELAY, ENC, MID, CROSS, LATE, INNER, FINISH, DOC, CROSS_PAIRS, DX1, OWN,
    BY_QUERY, BY_KEY, HIDDEN_OUT, QUERY_DONE, KEY_DONE, INPUT_GRAD,
) = range(24)
SMALL, QKV, HIDDEN, ENCODED, COLUMNS, INNER_COLUMNS, ROWS = range(7)
XY, YX, X = ("x", "y"), ("y", "x"), ("x",)
ZXY, ZYX, ZX, XZ = ("z",) + XY, ("z",) + YX, ("z",) + X, X + ("z",)
XYZ, YXZ = XY + ("z",), YX + ("z",)
XZY, YZX = ("x", "z", "y"), ("y", "z", "x")
FIRST_PARTS = (
    (HIDDEN, 4, 8, ZXY), (ENCODED, 0, 2, ZYX), (HIDDEN, 2, 8, ZYX), (HIDDEN, 1, 8, ZXY), (HIDDEN, 5, 8, ZXY),
    (HIDDEN, 3, 8, YZX), (HIDDEN, 6, 8, ZYX), (HIDDEN, 0, 8, ZXY), (QKV, 0, 1, ZX), (HIDDEN, 7, 8, ZXY), (COLUMNS, 3, 1, ZYX),
    (SMALL, 0, 1, XZY), (COLUMNS, 2, 1, ZXY), (COLUMNS, 4, 1, ZYX), (COLUMNS, 1, 1, XZY), (ENCODED, 1, 2, ZYX),
    (COLUMNS, 0, 1, YZX), (ROWS, 1, 3, ZX), (INNER_COLUMNS, 1, 1, ZX), (ROWS, 0, 3, ZX), (ROWS, 2, 3, ZX),
    (INNER_COLUMNS, 0, 1, XZ),
)
FIRST_ORDER = (
    (GO, 0), (GO, 2), (GO, 3), (GO, 4), (GO, 9), (PACK, 0), (GO, 6), (SWAP, 0), (GO, 0), (GO, 7), (GO, 2), (GO, 5), (GO, 8),
    (GO, 11), (GO, 0), (GO, 3), (GO, 11), (GO, 2), (GO, 5), (GO, 4), (GO, 3), (GO, 9), (GO, 0), (GO, 6), (GO, 2), (GO, 0),
    (GO, 7), (GO, 2), (GO, 4), (GO, 3), (GO, 9), (GO, 3), (GO, 6), (GO, 7), (GO, 1), (GO, 10), (GO, 4), (GO, 8), (GO, 16),
    (GO, 6), (GO, 4), (GO, 12), (GO, 11), (GO, 6), (GO, 9), (GO, 9), (GO, 15), (GO, 5), (GO, 7), (GO, 16), (GO, 1), (GO, 7),
    (GO, 14), (GO, 11), (GO, 8), (GO, 11), (GO, 10), (UNPACK, 0), (GO, 1), (SWAP, 1), (GO, 8), (PROJECTION, 0), (GO, 5),
    (GO, 12), (GO, 13), (GO, 10), (GO, 14), (GO, 15), (GO, 5), (WORK, 0), (WORK, 1), (WORK, 2), (WORK, 3), (GO, 1), (GO, 12),
    (GO, 15), (GO, 16), (GO, 18), (WORK, 4), (GO, 1), (GO, 13), (WORK, 5), (WORK, 6), (WORK, 7), (GO, 10), (GO, 12), (GO, 17),
    (GO, 14), (GO, 21), (WORK, 8), (GO, 10), (RELAY, 3), (GO, 12), (GO, 13), (GO, 15), (GO, 19), (WORK, 9), (WORK, 10), (GO, 15),
    (GO, 16), (GO, 18), (GO, 20), (WORK, 11), (GO, 14), (GO, 16), (RELAY, 0), (GO, 17), (GO, 21), (WORK, 12), (GO, 14),
    (WORK, 13), (GO, 19), (GO, 13), (WORK, 14), (WORK, 15), (SELF_DONE, 0), (GO, 13), (RELAY, 4), (GO, 20), (RELAY, 1),
    (RELAY, 2), (ENC, 0), (MID, 0), (CROSS, 0), (CROSS, 1), (CROSS, 2), (LATE, 0), (GO, 17), (GO, 18), (GO, 19), (GO, 21),
    (GO, 17), (GO, 20), (GO, 18), (RELAY, 6), (GO, 19), (GO, 21), (RELAY, 5), (GO, 20), (INNER, 0), (INNER, 1), (INNER, 2),
    (FINISH, 0),
)

def first_kernel(
    hid, g_in, enc_in, gains_in, shifts_in, biases_in, qkv_in, out_in, cq_in, ckv_in, co_in, inner_in, bias_in, w2_in,
    wq_out, keys_out, vals_out, queries_out, wc_out, kc_out, vc_out, g1, g2,
    prm_out, a_span_out, o_wide_out, o_low_out, logs_out, x1_out, cn_out, qc_out, oc_out, cross_out, en_out,
    out_part, out_send, dx2_out, row_sums,
    prm, a_span, o_wide, o_low, lse_out, x1, cn, qc, oc, cross_lse, en,
    wq_in, wp_in, wf_in, sm_in, vec, xs, wq_all, sm_all, wp, wf, w2, wq, keys, vals, queries, q2, m_ref, l_ref, acc, o_tmp,
    wc, w1, kc, vc, fb, ff, dy3, slope, act, du, ya, dza, yz_send, yz_recv, g1_tile, g2_tile, send, recv, local, store,
):
    here = place()
    h, z, x, c = here
    links = Links(send, recv)
    every = slice(None)
    span = 2 * hid.shape[0]
    group = 4 * span
    width = hid.shape[1]
    gw = PAIRS * WIDE
    feature = width // (NH * NZ * NX * NC)

    tiles = wf.shape[0]
    core, xdev, ydev = device_at(h, z, x, 1 - c), device_at(h, z, 1 - x, c), device_at(1 - h, z, x, c)

    def part(name, i, n):
        if name == SMALL:
            return lambda *d: sm_all.at[d], sm_in
        if name == QKV:
            return lambda h, z, x, c: wq_all.at[every, z, x, c], None
        if name == COLUMNS:
            return lambda *d: wp.at[(i,) + d], wp_in.at[i]
        if name == INNER_COLUMNS:
            return lambda h, z, x, c: wf.at[i, every, z, x, c], None
        source = {HIDDEN: hid, ENCODED: enc_in, ROWS: w2_in}[name]
        size = source.shape[0] // n
        cut = pl.ds(i * size, size)
        if name == HIDDEN:
            return lambda h, z, x, c: xs.at[z, x, c, h, cut], source.at[cut]
        if name == ROWS:
            return lambda h, z, x, c: w2.at[z, x, c, cut], source.at[cut]
        return lambda *d: en.at[d + (cut,)], source.at[cut]

    made = [part(*p[:3]) for p in FIRST_PARTS]
    copies = [
        None if piece is None else pltpu.make_async_copy(piece, view(h, z, x, c), local.at[i])
        for i, (view, piece) in enumerate(made)
    ]
    count = len(made)
    own_q = pltpu.make_async_copy(wq_in.at[h], wq_all.at[h, z, x, c], local.at[count])
    own_f = pltpu.make_async_copy(wf_in.at[h], wf.at[every, h, z, x, c], local.at[count + 1])
    own_g = pltpu.make_async_copy(g_in, dy3.at[h], local.at[count + 2])
    packed_here = [name in (SMALL, COLUMNS) for name, *_rest in FIRST_PARTS]
    own_g.start()
    for cp, late in zip(copies, packed_here):
        if cp is not None and not late:
            cp.start()
    greet(*here)
    kq, kf, kg = links.slot(), links.slot(), links.slot()

    def pack():
        blocks = [(out_in, 0), (cq_in, 0), (ckv_in, 0), (ckv_in, width), (co_in, 0)]
        def stacked(source, lo):
            halves = [source[:, lo + k * gw : lo + (k + 1) * gw].astype(F32) for k in range(2)]
            return jnp.concatenate(halves, axis=0).astype(BF)

        for i, (source, lo) in enumerate(blocks):
            wp_in[i] = stacked(source, lo)
        for k in range(2):
            for j in range(tiles):
                wf_in[k, j] = stacked(inner_in, (k * tiles + j) * width)
        for k in range(2):
            for i in range(3):
                lo = i * width + k * gw
                wq_in[k, :, i * gw : (i + 1) * gw] = qkv_in[:, lo : lo + gw]
        vec[...] = jnp.zeros_like(vec)
        for source, lo in ((gains_in, 0), (shifts_in, 3), (biases_in, 6)):
            vec[lo : lo + source.shape[0], 0:feature] = source[...].astype(F32)
        packed = jnp.transpose(vec[...])[0 : sm_in.shape[0]]
        line = jnp.concatenate([bias_in[...].astype(F32), jnp.zeros((1, 128 - bias_in.shape[1]), F32)], axis=1)
        row = lax.broadcasted_iota(jnp.int32, packed.shape, 0)
        sm_in[...] = jnp.where(row == feature, line, packed).astype(BF)
        for cp in [own_q, own_f] + [cp for cp, late in zip(copies, packed_here) if late]:
            cp.start()
        links.send(wq_in.at[1 - h], wq_all.at[h, z, x, c], kq, ydev)

    def swapped_q():
        own_q.wait()
        got = wq_all.at[1 - h, z, x, c]
        links.copy(got, got, kq, ydev).wait_recv()

    waiting = [True]

    def swapped_f():
        if waiting:
            waiting.clear()
            own_f.wait()
            got = wf.at[every, 1 - h, z, x, c]
            links.copy(got, got, kf, ydev).wait_recv()

    pipes = Pipes()
    for (name, i, n, order), (view, piece), cp in zip(FIRST_PARTS, made, copies):
        ready = {QKV: swapped_q, INNER_COLUMNS: swapped_f}.get(name)
        pipes.add(gather_stages(links, view, order, here, None if piece is None else (piece, cp), ready))

    def swap(n):
        if n == 0:
            links.send(wf_in.at[1 - h], wf.at[every, h, z, x, c], kf, ydev)
        else:
            links.send(g_in, dy3.at[h], kg, ydev)

    def projection():
        wq[...] = wq_all[...].astype(F32).reshape(width, 3 * gw).astype(BF)
        keep(3, wq, wq_out)

    def small_done():
        sm = sm_all[...].astype(F32)
        devices = NH * NZ * NX * NC
        sm = sm.reshape(devices, sm.shape[-2], sm.shape[-1])
        prm[...] = jnp.transpose(sm[:, :feature, :].reshape(width, sm.shape[-1]))
        inner_part = w2_in.shape[0]
        for d in range(devices):
            fb[:, d * inner_part : (d + 1) * inner_part] = sm[d, feature : feature + 1, 0:inner_part]

    def project(g, keys_too, queries_too):
        gain, shift = prm[0:1, :], prm[3:4, :]
        lanes = pl.ds(pl.multiple_of(h * gw, 128), gw)
        q_bias, v_bias = prm[6:7, lanes], prm[7:8, lanes]

        @pl.loop(0, 4)
        def _(j):
            n, _unused = norm_stats(xs[g, j // 2, j % 2].reshape(span, width).astype(F32))
            a = (n * gain + shift).astype(BF)
            at = pl.ds(pl.multiple_of(g * group + j * span, span), span)
            if queries_too:
                queries[at, :] = ((dot(a, wq[:, 0:gw]) + q_bias).astype(BF).astype(F32) * SCORE_SCALE).astype(BF)
            if keys_too:
                keys[at, :] = dot(a, wq[:, gw : 2 * gw]).astype(BF)
                vals[at, :] = (dot(a, wq[:, 2 * gw : 3 * gw]) + v_bias).astype(BF)
            if keys_too and queries_too:
                @pl.when(j == x * 2 + c)
                def _():
                    a_span[...] = a

    def attend(g, diagonal, p):
        at = pl.ds(pl.multiple_of(g * group, group), group)
        if True:
            part = pl.ds(p * WIDE, WIDE)
            k_pair, v_pair = keys[at, part], vals[at, part]

            @pl.loop(0, 2)
            def _(half):
                mine = pl.ds(pl.multiple_of(half * span, span), span)
                s = dot_nt(q2[p, mine, :], k_pair)
                if diagonal:
                    query = (x * 2 + c) * span + lax.broadcasted_iota(jnp.int32, s.shape, 0)
                    s = jnp.where(lax.broadcasted_iota(jnp.int32, s.shape, 1) <= query, s, -jnp.inf)
                    top = jnp.max(s, axis=-1, keepdims=True)
                    w = jnp.exp(s - top)
                    m_ref[p, mine, :] = jnp.broadcast_to(top, (span, 128))
                    l_ref[p, mine, :] = jnp.broadcast_to(jnp.sum(w, axis=-1, keepdims=True), (span, 128))
                    acc[p, mine, :] = dot(w.astype(BF), v_pair)
                else:
                    old = m_ref[p, mine, :]
                    new = jnp.maximum(old, jnp.max(s, axis=-1, keepdims=True))
                    fade = jnp.exp(old - new)
                    w = jnp.exp(s - new[:, 0:1])
                    m_ref[p, mine, :] = new
                    l_ref[p, mine, :] = l_ref[p, mine, :] * fade + jnp.sum(w, axis=-1, keepdims=True)
                    acc[p, mine, :] = acc[p, mine, :] * fade + dot(w.astype(BF), v_pair)

    def work(n):
        t, p = n // 4, n % 4 - 1
        if t == 0 and p < 0:
            project(z, True, True)
            start = pl.ds(pl.multiple_of(z * group + (x * 2 + c) * span, span), span)
            for i in range(PAIRS):
                q2[i] = stack_pair(queries[start, pl.ds(i * WIDE, WIDE)])
        elif t == 0:
            attend(z, True, p)
        elif p < 0:
            pl.when(z - t >= 0)(lambda: project((z - t) % NZ, True, False))
            pl.when(z + t < NZ)(lambda: project((z + t) % NZ, False, True))
        else:
            pl.when(z - t >= 0)(lambda: attend((z - t) % NZ, False, p))

    lane = lax.broadcasted_iota(jnp.int32, (span, 128), 1)
    ko = links.slot()
    kept = []

    def keep(i, source, target):
        cp = pltpu.make_async_copy(source, target, store.at[i])
        cp.start()
        kept.append(cp)

    def self_done():
        keep(0, keys, keys_out)
        keep(1, vals, vals_out)
        keep(2, queries, queries_out)
        logs = jnp.zeros((span, 128), F32)
        for p in range(PAIRS):
            part = pl.ds(p * WIDE, WIDE)
            o_pair = unstack_pair(acc[p] / l_ref[p])
            o_wide[:, part] = o_pair
            o_tmp[:, :, part] = o_pair.astype(BF).reshape(2, span // 2, WIDE)
            total = m_ref[p] + jnp.log(l_ref[p])
            logs = jnp.where(lane == 2 * p, total[:span], logs)
            logs = jnp.where(lane == 2 * p + 1, total[span:], logs)
        lse_out[...] = logs
        links.send(o_tmp.at[1 - h], o_low.at[h], ko, ydev)
        o_low[h] = o_tmp[h]

    def unstack(v, hh, target):
        v = v.astype(F32).reshape(NZ * NX * NC, 2 * feature, gw)
        for half in range(2):
            target[hh * gw : (hh + 1) * gw, half * gw : (half + 1) * gw] = (
                v[:, half * feature : (half + 1) * feature, :].reshape(gw, gw).astype(BF)
            )

    def relay(i):
        for hh in range(NH):
            if i < 5:
                unstack(wp[i, hh], hh, wc.at[i])
            else:
                unstack(wf[i - 5, hh], hh, w1.at[i - 5])
        if i < 5:
            keep(4 + i, wc.at[i], wc_out.at[i])

    def encoder():
        enc_rows = kc.shape[0]

        @pl.loop(0, 2)
        def _(i):
            at = pl.ds(pl.multiple_of(i * (enc_rows // 2), 16), enc_rows // 2)
            e = en[i].reshape(enc_rows // 2, width)
            kc[at, :] = dot(e, wc[2]).astype(BF)
            vc[at, :] = (dot(e, wc[3]) + prm[10:11]).astype(BF)

        keep(9, kc, kc_out)
        keep(10, vc, vc_out)

    def after_self():
        links.copy(o_low.at[1 - h], o_low.at[1 - h], ko, ydev).wait_recv()
        total = hid[...].astype(F32) + dot(o_low[0], wc[0, 0:gw, :]) + dot(o_low[1], wc[0, gw:width, :]) + prm[8:9]
        x1[...] = total
        n, _unused = norm_stats(total)
        cn[...] = (n * prm[1:2] + prm[4:5]).astype(BF)
        qc[...] = ((dot(cn[...], wc[1]) + prm[9:10]).astype(BF).astype(F32) * SCORE_SCALE).astype(BF)
        cross_lse[...] = jnp.zeros_like(cross_lse)

    def cross(n):
        @pl.loop(2 * n, 2 * n + 2)
        def _(p):
            part = pl.ds(pl.multiple_of(p * WIDE, WIDE), WIDE)
            s = dot_nt(stack_pair(qc[:, part]), kc[:, part])
            top = jnp.max(s, axis=-1, keepdims=True)
            w = jnp.exp(s - top)
            total = jnp.sum(w, axis=-1, keepdims=True)
            cross_lse[...] = jnp.where(lane == p, top + jnp.log(total), cross_lse[...])
            oc[:, part] = unstack_pair(dot((w / total).astype(BF), vc[:, part])).astype(BF)

    def after_cross():
        total = x1[...] + dot(oc[...], wc[4]) + prm[11:12]
        dx2_out[...] = total
        n, _unused = norm_stats(total)
        ff[h] = (n * prm[2:3] + prm[5:6]).astype(BF)
        links.send(ff.at[h], ff.at[h], kn, ydev)
        results = (
            (prm, prm_out), (a_span, a_span_out), (o_wide, o_wide_out), (o_low, o_low_out), (lse_out, logs_out), (x1, x1_out),
            (cn, cn_out), (qc, qc_out), (oc, oc_out), (cross_lse, cross_out), (en, en_out),
        )
        for i, (source, target) in enumerate(results):
            keep(16 + i, source, target)
        row_sums[...] = jnp.zeros_like(row_sums)

    kn, kyz = links.slot(), links.slot()
    tile_copies = []

    def inner_start():
        own_g.wait()
        links.copy(dy3.at[1 - h], dy3.at[1 - h], kg, ydev).wait_recv()
        for j in range(tiles):
            w2_tile = w2[2 * j : 2 * j + 2].reshape(width, width)
            slope[j] = dot_nt(dy3[...].reshape(span, width), w2_tile)
        hidden_units(h)

    def hidden_units(i):
        at_rows = pl.ds(pl.multiple_of(i * (span // 2), 16), span // 2)
        for j in range(tiles):
            at = pl.multiple_of(h * (tiles * width) + j * width, 128)
            u = dot(ff[i], w1[j]) + fb[:, pl.ds(at, width)]
            phi = 0.5 * (1.0 + lax.erf(u * SQRT_HALF))
            act[j, at_rows, :] = (u * phi).astype(BF)
            du[j, at_rows, :] = (slope[j, at_rows, :] * (phi + u * (DENSITY * jnp.exp(-0.5 * u * u)))).astype(BF)

    def inner_units():
        links.copy(ff.at[1 - h], ff.at[1 - h], kn, ydev).wait_recv()
        hidden_units(1 - h)
        for j in range(tiles):
            term = dot_nt(du[j], w1[j])
            dza[...] = term if j == 0 else dza[...] + term
        yz_send[...] = dza[...].astype(BF).reshape(2, span // 2, width)
        links.send(yz_send.at[1 - h], yz_recv, kyz, ydev)
        for j in range(tiles):
            term = dot(act[j], w2[2 * j : 2 * j + 2].reshape(width, width))
            ya[...] = term if j == 0 else ya[...] + term
        own_half = pl.ds(pl.multiple_of(h * (span // 2), 8), span // 2)
        other_half = pl.ds(pl.multiple_of((1 - h) * (span // 2), 8), span // 2)
        out_part[...] = dx2_out[...] + ya[own_half, :] + prm[12:13]
        out_send[...] = ya[other_half, :].astype(BF)

    def inner_grads():
        f_all = ff[...].reshape(span, width)
        for j in range(tiles):
            row_sums[pl.ds(pl.multiple_of(16 + 8 * (h * tiles + j), 8), 1), :] = column_total(du[j])
            for hh in range(NH):
                halves = [
                    dot_tn(f_all[:, hh * gw : (hh + 1) * gw], du[j, :, half * gw : (half + 1) * gw]).reshape(
                        NZ * NX * NC, feature, gw
                    )
                    for half in range(2)
                ]
                g1_tile[j, hh] = jnp.concatenate(halves, axis=1).astype(BF).reshape(NZ, NX, NC, 2 * feature, gw)
            tile_copies.append(pltpu.make_async_copy(g1_tile.at[j], g1.at[j], store.at[11 + 2 * j]))
            tile_copies[-1].start()
            g2_tile[j] = dot_tn(act[j], dy3[...].reshape(span, width)).astype(BF).reshape(g2_tile.shape[1:])
            tile_copies.append(pltpu.make_async_copy(g2_tile.at[j], g2.at[pl.ds(2 * j, 2)], store.at[12 + 2 * j]))
            tile_copies[-1].start()

    def finish():
        links.copy(yz_recv, yz_recv, kyz, ydev).wait_recv()
        mine = pl.ds(pl.multiple_of(h * (span // 2), 8), span // 2)
        x2 = dx2_out[...]
        back, d_gain, d_shift = norm_back(dza[mine, :] + yz_recv[...].astype(F32), prm[2:3], x2)
        row_sums[2:3, :], row_sums[5:6, :] = d_gain, d_shift
        row_sums[12:13, :] = column_total(g_in[...])
        dx2_out[...] = g_in[...].astype(F32) + back
        for cp in tile_copies + kept:
            cp.wait()

    steps = {
        GO: pipes.go, PACK: lambda n: pack(), SWAP: swap, UNPACK: lambda n: small_done(), PROJECTION: lambda n: projection(), WORK: work,
        SELF_DONE: lambda n: self_done(), RELAY: relay, ENC: lambda n: encoder(), MID: lambda n: after_self(),
        CROSS: cross, LATE: lambda n: after_cross(),
        INNER: lambda n: (inner_start, inner_units, inner_grads)[n](), FINISH: lambda n: finish(),
    }
    for name, n in FIRST_ORDER:
        steps[name](n)
    links.drain()


FIRST_SEMS = 150


def run_first(hid, g_in, enc, *params):
    rows, width = hid.shape
    w2_in = params[-1]
    span = 2 * rows
    total = span * NZ * NX * NC
    gw = PAIRS * WIDE
    grid = (NH, NZ, NX, NC)
    devices = NH * NZ * NX * NC
    feature = width // devices
    enc_rows = enc.shape[0] * devices
    inner_width = w2_in.shape[0] * devices
    tiles = inner_width // width // NH
    hbm, vmem = pl.BlockSpec(memory_space=pl.ANY), pl.BlockSpec(memory_space=pltpu.VMEM)
    S = jax.ShapeDtypeStruct
    shard = (2 * feature, gw)
    wq_shape = (feature, 3 * gw)
    outs_hbm = (
        S((width, 3 * gw), BF), S((total, gw), BF), S((total, gw), BF), S((total, gw), BF),
        S((5, width, width), BF), S((enc_rows, width), BF), S((enc_rows, width), BF),
        S((tiles,) + grid + shard, BF), S(grid[1:] + w2_in.shape, BF),
    )
    middle = (
        S((128, width), F32), S((span, width), BF), S((span, gw), F32), S((2, rows, gw), BF), S((span, 128), F32),
        S((rows, width), F32), S((rows, width), BF), S((rows, width), BF), S((rows, width), BF), S((span, 128), F32), S(grid + enc.shape, BF),
    )
    outs_hbm += middle
    outs_vmem = (
        S((rows, width), F32), S((rows, width), BF), S((rows, width), F32), S((16 + 8 * tiles * NH, width), F32),
    )
    V = pltpu.VMEM
    return pl.pallas_call(
        first_kernel,
        out_shape=outs_hbm + outs_vmem,
        in_specs=[vmem] * 14,
        out_specs=(hbm,) * len(outs_hbm) + (vmem,) * len(outs_vmem),
        scratch_shapes=[V(m.shape, m.dtype) for m in middle] + [
            V((2,) + wq_shape, BF), V((5,) + shard, BF), V((2, tiles) + shard, BF), V((32, 128), BF), V((128, 128), F32),
            V((NZ, NX, NC, NH, rows, width), BF), V(grid + wq_shape, BF), V(grid + (32, 128), BF),
            V((5,) + grid + shard, BF), V((tiles,) + grid + shard, BF), V(grid[1:] + w2_in.shape, BF),
            V((width, 3 * gw), BF), V((total, gw), BF), V((total, gw), BF), V((total, gw), BF),
            V((PAIRS, 2 * span, WIDE), BF), V((PAIRS, 2 * span, 128), F32), V((PAIRS, 2 * span, 128), F32),
            V((PAIRS, 2 * span, WIDE), F32), V((2, rows, gw), BF),
            V((5, width, width), BF), V((tiles, width, width), BF), V((enc_rows, width), BF), V((enc_rows, width), BF),
            V((1, inner_width), F32), V((2, rows, width), BF), V((2, rows, width), BF),
            V((tiles, span, width), F32), V((tiles, span, width), BF), V((tiles, span, width), BF), V((span, width), F32), V((span, width), F32),
            V((2, rows, width), BF), V((rows, width), BF),
            V((tiles,) + grid + shard, BF), V((tiles, 2, NX, NC) + w2_in.shape, BF),
            pltpu.SemaphoreType.DMA((FIRST_SEMS,)), pltpu.SemaphoreType.DMA((FIRST_SEMS,)),
            pltpu.SemaphoreType.DMA((len(FIRST_PARTS) + 3,)), pltpu.SemaphoreType.DMA((28,)),
        ],
        compiler_params=pltpu.CompilerParams(
            collective_id=0, has_side_effects=True, vmem_limit_bytes=63 << 20
        ),
        cost_estimate=pl.CostEstimate(flops=10**10, bytes_accessed=10**8, transcendentals=10**7),
        name="gather_and_forward",
    )(hid, g_in, enc, *params)


def norm_back(dz, gain, v):
    n, inv = norm_stats(v)
    dn = dz * gain
    result = (dn - jnp.mean(dn, axis=-1, keepdims=True) - n * jnp.mean(dn * n, axis=-1, keepdims=True)) * inv
    return result, jnp.sum(dz * n, axis=0, keepdims=True), jnp.sum(dz, axis=0, keepdims=True)


def column_total(v):
    return jnp.sum(v.astype(F32), axis=0, keepdims=True)


SQRT_HALF = 0.7071067811865476
DENSITY = 0.3989422804014327


def shard_loop(shape, fn):
    count = 1
    for n in shape:
        count *= n

    @pl.loop(0, count)
    def _(i):
        index = []
        for n in reversed(shape):
            index.append(i % n)
            i = i // n
        fn(tuple(reversed(index)))


def add_into(target, source):
    target[...] = (target[...].astype(F32) + source[...].astype(F32)).astype(BF)


WHOLE, PAIRED, SINGLE = ("y", "z", "x"), ("l", "z", "x"), ("z", "x")
EXTENT = {"y": NH, "l": NH, "z": NZ, "x": NX}


def reduce_stages(links, source, axes, order, here, bufs, local_sem, store, ydev=None):
    h, z, x, c = here
    every = slice(None)
    me = {"y": h, "z": z, "x": x}
    bufs = list(bufs)
    if local_sem is None:
        mine = source(c)
    else:
        mine = bufs.pop(0)
        local = pltpu.make_async_copy(source(c), mine, local_sem)
    from_core = bufs.pop(0)
    k_core = links.slot()
    core = device_at(h, z, x, 1 - c)

    def start():
        links.send(source(1 - c), from_core, k_core, core)
        if local_sem is not None:
            local.start()

    def after_core():
        if local_sem is not None:
            local.wait()
        links.copy(from_core, from_core, k_core, core).wait_recv()
        shard_loop([EXTENT[a] for a in axes], lambda i: add_into(mine.at[i], from_core.at[i]))

    fixed = {}
    stages = []
    for axis in order:
        buf = bufs.pop(0)
        open_axes = [a for a in axes if a not in fixed and a != axis]

        def at(**values):
            known = {**fixed, **values}
            return tuple(known.get(a, every) for a in axes)

        if axis == "z":
            routes = [
                (links.slot(), device_at(h, (z + d) % NZ, x, c), mine.at[at(z=(z + d) % NZ)], buf.at[d - 1])
                for d in (1, 2, 3)
            ]
        elif axis == "x":
            routes = [(links.slot(), device_at(h, z, 1 - x, c), mine.at[at(x=1 - x)], buf)]
        else:
            routes = [(links.slot(), device_at(1 - h, z, x, c), mine.at[at(y=1 - h)], buf)]

        def go(routes=routes):
            for k, device, away, target in routes:
                links.send(away, target, k, device)

        def come(routes=routes):
            for k, device, _away, target in routes:
                links.copy(target, target, k, device).wait_recv()

        fixed[axis] = me[axis]
        base = dict(fixed)

        def add(routes=routes, open_axes=open_axes, base=base):
            def one(i):
                known = {**base, **dict(zip(open_axes, i))}
                slot = mine.at[tuple(known[a] for a in axes)]
                total = slot[...].astype(F32)
                for _k, _device, _away, target in routes:
                    total = total + target[i].astype(F32)
                slot[...] = total.astype(BF)

            shard_loop([EXTENT[a] for a in open_axes], one)

        def total_of(lead, routes=routes, base=base):
            known = {**base, "l": lead}
            total = mine[tuple(known[a] for a in axes)].astype(F32)
            for _k, _device, _away, target in routes:
                total = total + (target[lead] if "l" in axes else target[...]).astype(F32)
            return total

        stages.append((go, come, add, total_of))

    made = [start, lambda: (after_core(), stages[0][0]())]
    for (_g, come, add, _t), (go, _c, _a, _t2) in zip(stages, stages[1:]):
        made.append(lambda come=come, add=add, go=go: (come(), add(), go()))
    _g, come, _a, total_of = stages[-1]
    if "l" not in axes:
        return made + [lambda: (come(), store(None, total_of(None)))]
    out, back = bufs
    k_swap = links.slot()

    def swap():
        come()
        store(h, total_of(h))
        out[...] = total_of(1 - h).astype(BF)
        links.send(out, back, k_swap, ydev)

    def finish():
        links.copy(back, back, k_swap, ydev).wait_recv()
        store(1 - h, back[...].astype(F32))

    return made + [swap, finish]


def reduce_bufs(shard, axes, order, own):
    sizes = [tuple(EXTENT[a] for a in axes)] * (2 if own else 1)
    left = list(axes)
    for axis in order:
        left.remove(axis)
        sizes.append((NZ - 1,) * (axis == "z") + tuple(EXTENT[a] for a in left))
    if "l" in axes:
        sizes += [(), ()]
    return [pltpu.VMEM(size + shard, BF) for size in sizes]


XYZ, YXZ = XY + ("z",), YX + ("z",)
KV_ORDER = (XZ, XZ, XZ)
LAST_PARTS = (
    (ROWS, 0, XZ), (COLUMNS, 0, YXZ), (COLUMNS, 2, YXZ), (ROWS, 2, XZ), (COLUMNS, 1, YXZ), (COLUMNS, 4, XYZ), (ENCODED, 1, YZX),
    (INNER_COLUMNS, 0, ZX), (ENCODED, 0, YXZ), (ROWS, 1, XZ), (COLUMNS, 3, YXZ), (INNER_COLUMNS, 1, XZ),
)
LAST_ORDER = (
    (GO, 0), (GO, 7), (GO, 9), (DOC, 0), (GO, 0), (GO, 5), (GO, 7), (GO, 9), (CROSS_PAIRS, 0), (GO, 3), (GO, 5),
    (CROSS_PAIRS, 1), (GO, 0), (GO, 3), (GO, 11), (CROSS_PAIRS, 2), (DX1, 0), (ENC, 0), (GO, 4), (OWN, 0), (GO, 12), (GO, 13),
    (GO, 14), (GO, 0), (GO, 3), (GO, 4), (GO, 5), (GO, 7), (GO, 9), (GO, 12), (GO, 10), (GO, 11), (ENC, 1), (GO, 12), (GO, 7),
    (GO, 10), (GO, 12), (GO, 13), (OWN, 1), (BY_QUERY, 0), (BY_QUERY, 1), (BY_QUERY, 2), (BY_QUERY, 3), (GO, 1), (GO, 15),
    (GO, 4), (GO, 5), (GO, 7), (GO, 14), (GO, 11), (GO, 1), (BY_QUERY, 4), (BY_QUERY, 5), (BY_QUERY, 6), (GO, 2), (BY_QUERY, 7),
    (BY_QUERY, 8), (BY_QUERY, 9), (GO, 13), (GO, 2), (GO, 3), (GO, 10), (BY_QUERY, 10), (GO, 13), (GO, 4), (BY_QUERY, 11),
    (GO, 9), (QUERY_DONE, 0), (GO, 16), (BY_KEY, 0), (GO, 16), (GO, 1), (BY_KEY, 3), (GO, 14), (GO, 15), (BY_KEY, 6),
    (BY_KEY, 9), (GO, 14), (BY_KEY, 10), (GO, 2), (GO, 5), (GO, 6), (GO, 16), (GO, 8), (GO, 10), (KEY_DONE, 0), (GO, 17),
    (GO, 6), (GO, 8), (GO, 17), (GO, 1), (GO, 11), (BY_KEY, 1), (BY_KEY, 4), (GO, 4), (BY_KEY, 7), (GO, 15), (GO, 6),
    (KEY_DONE, 1), (GO, 15), (BY_KEY, 2), (BY_KEY, 5), (BY_KEY, 8), (BY_KEY, 11), (KEY_DONE, 2), (KEY_DONE, 3), (GO, 17),
    (GO, 18), (GO, 19), (GO, 16), (GO, 1), (GO, 18), (GO, 19), (GO, 2), (GO, 6), (GO, 8), (GO, 10), (GO, 11), (GO, 17), (GO, 18),
    (INPUT_GRAD, 0), (GO, 20), (GO, 17), (GO, 19), (GO, 16), (GO, 2), (GO, 6), (HIDDEN_OUT, 0), (GO, 18), (GO, 8), (GO, 20),
    (GO, 18), (GO, 19), (GO, 8), (GO, 19), (GO, 20),
)

def last_kernel(
    out_part, out_send, dx2, oc, qc, cross_lse,
    hid_in, prm_in, a_span_in, o_wide_in, o_low_in, lse_in, x1_in, cn_in, row_sums_in,
    en_in, wq_in, keys_in, vals_in, queries_in, wc_in, kc_in, vc_in, gf1, gf2,
    hidden_out, hidden_grad, out_o, out_cq, out_ckv, out_co, out_fi, out_f, out_e, out_q, out_s,
    hid, prm, a_span, o_wide, o_low, lse, x1, cn, row_sums,
    y_recv, wk, pool, gc, ge, doc, dqc, dx1, do_low,
    do_all, st_all, q2, k2, v2, do2, dq2, dk2, dv2, dz_q, gq, gkv, gs, fbs, dz_send, dz_recv, send, recv, local, loads, *bufs,
):
    here = place()
    h, z, x, c = here
    links = Links(send, recv)
    every = slice(None)
    rows, width = hid.shape
    span = 2 * rows
    group = 4 * span
    gw = PAIRS * WIDE
    devices = NH * NZ * NX * NC
    feature = width // devices
    e_shard, f_shard = ge.shape[4], gf2.shape[3]
    enc_rows = devices * e_shard
    total_rows = keys_in.shape[0]
    ydev = device_at(1 - h, z, x, c)
    kc, vc, dkc, dvc = (pool.at[pl.ds(i * enc_rows, enc_rows)] for i in range(4))
    wc = [wk.at[pl.ds(i * width, width)] for i in range(5)]
    queries, wq = pool.at[:, pl.ds(0, gw)], [pool.at[pl.ds(i * width, width), pl.ds(gw, gw)] for i in range(3)]
    plan = [(wc_in.at[4], wc[4]), (kc_in, kc), (vc_in, vc), (wc_in.at[1], wc[1]), (wc_in.at[0], wc[0])]
    plan += [(x1_in, x1), (prm_in, prm), (cn_in, cn), (o_low_in, o_low), (lse_in, lse), (o_wide_in, o_wide)]
    plan += [(en_in, ge), (wc_in.at[2], wc[2]), (wc_in.at[3], wc[3]), (a_span_in, a_span), (hid_in, hid), (row_sums_in, row_sums)]
    fetches = [pltpu.make_async_copy(source, target, loads.at[14 + i]) for i, (source, target) in enumerate(plan)]
    for cp in fetches:
        cp.start()

    def fetched(lo, hi):
        for cp in fetches[lo:hi]:
            cp.wait()

    late = [
        pltpu.make_async_copy(source, wk.at[pl.ds(0, total_rows), pl.ds(lo, gw)], loads.at[8 + i])
        for i, (source, lo) in enumerate(((keys_in, 0), (vals_in, gw)))
    ]
    late.append(pltpu.make_async_copy(queries_in, pool.at[pl.ds(0, total_rows), pl.ds(0, gw)], loads.at[10]))
    late += [
        pltpu.make_async_copy(wq_in.at[:, pl.ds(i * gw, gw)], wq[i], loads.at[11 + i]) for i in range(3)
    ]
    greet(*here, corners=True)
    kh = links.slot()
    links.send(out_send, y_recv, kh, ydev)

    cuts = [(out_o, 0), (out_cq, 0), (out_ckv, 0), (out_ckv, width), (out_co, 0)]
    pipes = Pipes()
    used = 0
    for i, (name, n, order) in enumerate(LAST_PARTS):
        if name == COLUMNS:
            out, lo = cuts[n]
            axes, view = WHOLE, lambda c, n=n: gc.at[n, :, :, :, c]

            def keep(_l, total, out=out, lo=lo):
                out[:, lo : lo + gw] = total[0:feature]
                out[:, lo + gw : lo + 2 * gw] = total[feature : 2 * feature]
        elif name == INNER_COLUMNS:
            axes, view = PAIRED, lambda c, n=n: gf1.at[n, :, :, :, c]

            def keep(lead, total, n=n):
                out_fi[lead, n] = total
        elif name == ROWS:
            size = f_shard // 3
            axes, view = SINGLE, lambda c, lo=n * size, size=size: gf2.at[:, :, c, pl.ds(lo, size)]

            def keep(_l, total, lo=n * size, size=size):
                out_f[lo : lo + size, :] = total
        else:
            size = e_shard // 2
            axes, view = WHOLE, lambda c, lo=n * size, size=size: ge.at[:, :, :, c, pl.ds(lo, size)]

            def keep(_l, total, lo=n * size, size=size):
                out_e[lo : lo + size, :] = total
        outside = name in (ROWS, INNER_COLUMNS)
        count = len(order) + 1 + outside + 2 * (axes == PAIRED)
        pipes.add(
            reduce_stages(
                links, view, axes, order, here, bufs[used : used + count], local.at[i] if outside else None, keep, ydev
            )
        )
        used += count
    q_bufs, kv_bufs, small_bufs = bufs[used : used + 5], bufs[used + 5 : used + 20], bufs[used + 20 :]

    sums = {}
    lane = lax.broadcasted_iota(jnp.int32, (span, 128), 1)

    def to_shards(n, left, right):
        for hh in range(NH):
            halves = [
                dot_tn(left(hh), right(half)).reshape(devices // 2, feature, gw) for half in range(2)
            ]
            gc[n, hh] = jnp.concatenate(halves, axis=1).astype(BF).reshape(NZ, NX, NC, 2 * feature, gw)

    def half_of(ref, i):
        return ref[:, i * gw : (i + 1) * gw]

    def step_doc():
        dy2 = dx2[...].astype(BF)
        sums[11] = column_total(dy2)
        fetched(0, 1)
        doc[...] = dot_nt(dy2, wc[4][...]).astype(BF)
        to_shards(4, lambda hh: half_of(oc, hh), lambda i: half_of(dy2, i))

    def step_pairs(n):
        if n == 0:
            fetched(1, 3)

        @pl.loop(2 * n, 2 * n + 2)
        def _(p):
            part = pl.ds(pl.multiple_of(p * WIDE, WIDE), WIDE)
            logs = jnp.sum(jnp.where(lane == p, cross_lse[...], 0.0), axis=-1, keepdims=True)
            q_pair = stack_pair(qc[:, part])
            w = jnp.exp(dot_nt(q_pair, kc[:, part]) - logs)
            do_pair = stack_pair(doc[:, part])
            dp = dot_nt(do_pair, vc[:, part])
            ds = (w * (dp - jnp.sum(w * dp, axis=-1, keepdims=True))).astype(BF)
            dqc[:, part] = (unstack_pair(dot(ds, kc[:, part])) * SCORE_SCALE).astype(BF)
            dkc[:, part] = dot_tn(ds, q_pair).astype(BF)
            dvc[:, part] = dot_tn(w.astype(BF), do_pair).astype(BF)

    ky = links.slot()

    def step_dx1():
        fetched(3, 9)
        dq = dqc[...]
        sums[9] = column_total(dq)
        back, sums[1], sums[4] = norm_back(dot_nt(dq, wc[1][...]), prm[1:2], x1[...])
        total = dx2[...] + back
        dx1[...] = total
        dy1 = total.astype(BF)
        sums[8] = column_total(dy1)
        for i in range(2):
            do = dot_nt(dy1, wc[0][i * gw : (i + 1) * gw, :]).astype(BF)
            for p in range(PAIRS):
                do_low[i, p] = do[:, p * WIDE : (p + 1) * WIDE]
        links.send(do_low.at[1 - h], do_all.at[every, z, x, c, h], ky, ydev)
        do_all[:, z, x, c, h] = do_low[h]
        to_shards(1, lambda hh: half_of(cn, hh), lambda i: half_of(dq, i))
        to_shards(0, lambda hh: o_low[hh], lambda i: half_of(dy1, i))

    def step_enc(n):
        if n == 1:
            for i in range(NH):
                at = pl.ds(i * (enc_rows // NH), enc_rows // NH)
                de = dot_nt(dkc[at, :], wc[2][...]) + dot_nt(dvc[at, :], wc[3][...])
                ge[i] = de.astype(BF).reshape(ge.shape[1:])
            sums[10] = column_total(dvc[...])
            for cp in late:
                cp.start()
        else:
            fetched(11, 14)
            e_all = ge[...].reshape(enc_rows, width)
            for n, d in ((2, dkc), (3, dvc)):
                to_shards(n, lambda hh: e_all[:, hh * gw : (hh + 1) * gw], lambda i: half_of(d, i))

    l_columns, d_columns = [], []
    own_place = (x * 2 + c) * span

    def step_own(n):
        first = lane_half((span, WIDE))
        start = pl.ds(pl.multiple_of(z * group + own_place, span), span)
        if n == 1:
            for cp in late:
                cp.wait()
            for p in range(PAIRS):
                part = pl.ds(p * WIDE, WIDE)
                q2[p] = stack_pair(pool[start, part])
                k2[p] = stack_pair(wk[start, part])
                v2[p] = stack_pair(wk[start, pl.ds(gw + p * WIDE, WIDE)])
                dq2[p] = jnp.zeros_like(dq2[p])
                dk2[p] = jnp.zeros_like(dk2[p])
                dv2[p] = jnp.zeros_like(dv2[p])
            return
        fetched(9, 11)
        got = do_all.at[every, z, x, c, 1 - h]
        links.copy(got, got, ky, ydev).wait_recv()
        deltas = jnp.zeros((span, 128), F32)
        logs = lse[...]
        for p in range(PAIRS):
            part = pl.ds(p * WIDE, WIDE)
            do = do_all[p, z, x, c].reshape(span, WIDE)
            prod = do.astype(F32) * o_wide[:, part]
            low = jnp.sum(jnp.where(first, prod, 0.0), axis=-1, keepdims=True)
            high = jnp.sum(jnp.where(first, 0.0, prod), axis=-1, keepdims=True)
            deltas = jnp.where(lane == 2 * p, low, jnp.where(lane == 2 * p + 1, high, deltas))
            d_columns.append((low, high))
            l_columns.append((logs[:, 2 * p : 2 * p + 1], logs[:, 2 * p + 1 : 2 * p + 2]))
            do2[p] = stack_pair(do)
        st_all[z, x, c, 0:8] = jnp.transpose(logs)[0:8]
        st_all[z, x, c, 8:16] = jnp.transpose(deltas)[0:8]

    pipes.add(gather_stages(links, lambda *i: st_all.at[i[1:]], ZX, here))
    for p in range(PAIRS):
        pipes.add(gather_stages(links, lambda *i, p=p: do_all.at[(p,) + i[1:]], ZX, here))

    def query_side(g, diagonal, p):
        at = pl.ds(pl.multiple_of(g * group, group), group)
        if True:
            for half in range(2):
                mine = pl.ds(half * span, span)
                k_pair, v_pair = wk[at, pl.ds(p * WIDE, WIDE)], wk[at, pl.ds(gw + p * WIDE, WIDE)]
                w = jnp.exp(dot_nt(q2[p, mine], k_pair) - l_columns[p][half])
                if diagonal:
                    place_q = own_place + lax.broadcasted_iota(jnp.int32, w.shape, 0)
                    w = jnp.where(lax.broadcasted_iota(jnp.int32, w.shape, 1) <= place_q, w, 0.0)
                ds = (w * (dot_nt(do2[p, mine], v_pair) - d_columns[p][half])).astype(BF)
                dq2[p, mine] += dot(ds, k_pair)

    def key_side(g, diagonal, p):
        at = pl.ds(pl.multiple_of(g * group, group), group)
        if True:
            part = pl.ds(p * WIDE, WIDE)
            for half in range(2):
                mine = pl.ds(half * span, span)
                head = 2 * p + half
                q_pair = pool[at, part]
                do_pair = do_all[p, g].reshape(group, WIDE)
                stats = [st_all[g, i // 2, i % 2] for i in range(4)]
                log_row = jnp.concatenate([s[head : head + 1] for s in stats], axis=1)
                delta_row = jnp.concatenate([s[8 + head : 9 + head] for s in stats], axis=1)
                w = jnp.exp(dot_nt(k2[p, mine], q_pair) - log_row)
                if diagonal:
                    place_k = own_place + lax.broadcasted_iota(jnp.int32, w.shape, 0)
                    w = jnp.where(place_k <= lax.broadcasted_iota(jnp.int32, w.shape, 1), w, 0.0)
                dv2[p, mine] += dot(w.astype(BF), do_pair)
                ds = (w * (dot_nt(v2[p, mine], do_pair) - delta_row)).astype(BF)
                dk2[p, mine] += dot(ds, q_pair)

    def side(fn, n, ahead):
        t, p = n // PAIRS, n % PAIRS
        if t == 0:
            fn(z, True, p)
        elif ahead:
            pl.when(z + t < NZ)(lambda: fn((z + t) % NZ, False, p))
        else:
            pl.when(z - t >= 0)(lambda: fn((z - t) % NZ, False, p))

    def keep_q(lead, total):
        out_q[lead, 0:feature] = total

    def keep_kv(p):
        def keep(lead, total):
            out_q[lead, feature : 3 * feature, p * WIDE : (p + 1) * WIDE] = total

        return keep

    def output():
        links.copy(y_recv, y_recv, kh, ydev).wait_recv()
        hidden_out[...] = (out_part[...] + y_recv[...].astype(F32)).astype(BF)

    pipes.add(reduce_stages(links, lambda c: gq.at[:, :, :, c], PAIRED, XZ, here, q_bufs, None, keep_q, ydev))
    for p in range(PAIRS):
        view = lambda c, p=p: gkv.at[p, :, :, :, c]
        pipes.add(reduce_stages(links, view, PAIRED, KV_ORDER[p], here, kv_bufs[5 * p : 5 * p + 5], None, keep_kv(p), ydev))
    from_corners, by_z, small_z = small_bufs
    k_corner, k_small = [links.slot() for _ in range(7)], [links.slot() for _ in range(3)]
    flip = lambda v, k, bit: 1 - v if k >> bit & 1 else v

    def small_start():
        for k in range(1, 8):
            away = gs.at[flip(h, k, 2), :, flip(x, k, 1), flip(c, k, 0)]
            links.send(away, from_corners.at[k - 1], k_corner[k - 1], corner(h, z, x, c, k))

    def small_middle():
        total = gs[h, :, x, c].astype(F32)
        for k in range(1, 8):
            got = from_corners.at[k - 1]
            links.copy(got, got, k_corner[k - 1], corner(h, z, x, c, k)).wait_recv()
            total = total + from_corners[k - 1].astype(F32)
        by_z[...] = total.astype(BF)
        for d, k in zip((1, 2, 3), k_small):
            to = (z + d) % NZ
            links.send(by_z.at[to], small_z.at[d - 1], k, device_at(h, to, x, c))

    def small_finish():
        total = by_z[z].astype(F32)
        for d, k in zip((1, 2, 3), k_small):
            links.copy(small_z.at[d - 1], small_z.at[d - 1], k, device_at(h, (z + d) % NZ, x, c)).wait_recv()
            total = total + small_z[d - 1].astype(F32)
        out_s[...] = total

    pipes.add([small_start, small_middle, small_finish])
    kz = links.slot()

    def query_done():
        dq = jnp.concatenate([unstack_pair(dq2[p]) * SCORE_SCALE for p in range(PAIRS)], axis=1).astype(BF)
        fetched(14, 17)
        sums[6] = column_total(dq)
        gq[...] = dot_tn(a_span[...], dq).astype(BF).reshape(gq.shape)
        dz_q[...] = dot_nt(dq, wq[0][...])

    v_sums = []

    def key_done(p):
        if p == PAIRS:
            sums[7] = jnp.concatenate(v_sums, axis=1)
            dz_send[...] = dz_q[...].astype(BF).reshape(2, rows, width)
            links.send(dz_send.at[1 - h], dz_recv, kz, ydev)
            return
        part = pl.ds(p * WIDE, WIDE)
        dk, dv = unstack_pair(dk2[p]).astype(BF), unstack_pair(dv2[p]).astype(BF)
        v_sums.append(column_total(dv))
        whole = [dot_tn(a_span[...], d).reshape(devices, feature, WIDE) for d in (dk, dv)]
        gkv[p] = jnp.concatenate(whole, axis=1).astype(BF).reshape(gkv.shape[1:])
        dz_q[...] += dot_nt(dk, wq[1][:, part]) + dot_nt(dv, wq[2][:, part])

    def input_grad():
        links.copy(dz_recv, dz_recv, kz, ydev).wait_recv()
        dz_own = dz_send[h].astype(F32) + dz_recv[...].astype(F32)
        back, sums[0], sums[3] = norm_back(dz_own, prm[0:1], hid[...].astype(F32))
        hidden_grad[...] = dx1[...] + back
        for i in (6, 7):
            sums[i] = jnp.concatenate([jnp.where(h == k, sums[i], 0.0) for k in range(2)], axis=1)
        block = row_sums[0:16]
        row = lax.broadcasted_iota(jnp.int32, block.shape, 0)
        for i, value in sums.items():
            block = jnp.where(row == i, value, block)
        wide = jnp.concatenate([block, jnp.zeros((128 - 16, width), F32)], axis=0)
        by_feature = jnp.transpose(wide).reshape(devices, feature, 128)
        fbs[...] = jnp.zeros_like(fbs)
        each = width // f_shard
        for d in range(devices):
            at = 16 + 8 * (d // each)
            fbs[d : d + 1, 0:f_shard] = row_sums[at : at + 1, (d % each) * f_shard : (d % each + 1) * f_shard]
        fb = jnp.broadcast_to(fbs[...][:, None, :], (devices, 8, 128))
        gs[...] = jnp.concatenate([by_feature, fb], axis=1).astype(BF).reshape(gs.shape)

    steps = {
        GO: pipes.go, DOC: lambda n: step_doc(), CROSS_PAIRS: step_pairs, DX1: lambda n: step_dx1(), ENC: step_enc,
        OWN: step_own, HIDDEN_OUT: lambda n: output(), BY_QUERY: lambda n: side(query_side, n, False), BY_KEY: lambda n: side(key_side, n, True),
        QUERY_DONE: lambda n: query_done(), KEY_DONE: key_done, INPUT_GRAD: lambda n: input_grad(),
    }
    for name, n in LAST_ORDER:
        steps[name](n)
    links.drain()


LAST_SEMS = 170


def run_last(vmem_args, hbm_args):
    hid, en, keys, gf1, gf2 = hbm_args[0], hbm_args[9], hbm_args[11], hbm_args[17], hbm_args[18]
    rows, width = hid.shape
    span = 2 * rows
    gw = PAIRS * WIDE
    grid = (NH, NZ, NX, NC)
    devices = NH * NZ * NX * NC
    feature = width // devices
    e_rows, f_rows = en.shape[4], gf2.shape[3]
    enc_rows = e_rows * devices
    hbm, vmem = pl.BlockSpec(memory_space=pl.ANY), pl.BlockSpec(memory_space=pltpu.VMEM)
    S = jax.ShapeDtypeStruct
    V = pltpu.VMEM
    outs = (
        S((rows, width), BF), S((rows, width), F32), S((feature, width), F32), S((feature, width), F32), S((feature, 2 * width), F32),
        S((feature, width), F32), S((NH, gf1.shape[0], 2 * feature, gw), F32), S((f_rows, width), F32), S((e_rows, width), F32),
        S((2, 3 * feature, gw), F32), S((32, 128), F32),
    )
    shard = (2 * feature, gw)
    bufs = []
    for name, n, order in LAST_PARTS:
        size = {COLUMNS: shard, INNER_COLUMNS: shard, ROWS: (f_rows // 3, width), ENCODED: (e_rows // 2, width)}[name]
        axes = {INNER_COLUMNS: PAIRED, ROWS: SINGLE}.get(name, WHOLE)
        bufs += reduce_bufs(size, axes, order, name in (ROWS, INNER_COLUMNS))
    q_shard, kv_shard = (feature, gw), (2 * feature, WIDE)
    bufs += reduce_bufs(q_shard, PAIRED, XZ, False)
    for p in range(PAIRS):
        bufs += reduce_bufs(kv_shard, PAIRED, KV_ORDER[p], False)
    bufs += [V((7, NZ, 32, 128), BF), V((NZ, 32, 128), BF), V((3, 32, 128), BF)]
    stacked, stacked_f = V((PAIRS, 2 * span, WIDE), BF), V((PAIRS, 2 * span, WIDE), F32)
    D = pltpu.SemaphoreType.DMA
    return pl.pallas_call(
        last_kernel,
        out_shape=outs,
        in_specs=[vmem] * len(vmem_args) + [hbm] * len(hbm_args),
        out_specs=(vmem,) * len(outs),
        scratch_shapes=[V(m.shape, m.dtype) for m in hbm_args[:9]] + [
            V((rows, width), BF), V((max(keys.shape[0], 5 * width), width), BF), V((max(keys.shape[0], 4 * enc_rows), width), BF),
            V((5,) + grid + shard, BF), V(en.shape, BF), V((rows, width), BF), V((rows, width), BF), V((rows, width), F32), V((2, PAIRS, rows, WIDE), BF),
            V((PAIRS, NZ, NX, NC, 2, rows, WIDE), BF), V((NZ, NX, NC, 16, span), F32),
            stacked, stacked, stacked, stacked, stacked_f, stacked_f, stacked_f,
            V((span, width), F32), V(grid + q_shard, BF), V((PAIRS,) + grid + kv_shard, BF), V(grid + (32, 128), BF), V((devices, 128), F32),
            V((2, rows, width), BF), V((rows, width), BF),
            D((LAST_SEMS,)), D((LAST_SEMS,)), D((len(LAST_PARTS),)), D((32,)),
        ] + bufs,
        compiler_params=pltpu.CompilerParams(
            collective_id=1, has_side_effects=True, vmem_limit_bytes=63 << 20
        ),
        cost_estimate=pl.CostEstimate(flops=2 * 10**10, bytes_accessed=10**8, transcendentals=10**7),
        name="backward_and_reduce",
    )(*vmem_args, *hbm_args)


def deliver_kernel(
    hidden_out, hidden_grad, o, cq, ckv, co, fi_in, f, e, qkv_in, small_in,
    out_hidden, out_grad, out_e, gains, shifts, biases, out_qkv, out_o, out_cq, out_ckv, out_co, out_fi, out_bias, out_f,
    fi, qkv, small, sems,
):
    pairs = (
        (hidden_out, out_hidden.at[0, 0]), (hidden_grad, out_grad.at[0, 0]), (e, out_e.at[0]), (o, out_o), (cq, out_cq),
        (ckv, out_ckv), (co, out_co), (f, out_f), (fi_in, fi), (qkv_in, qkv), (small_in, small),
    )
    copies = [pltpu.make_async_copy(source, target, sems.at[i]) for i, (source, target) in enumerate(pairs)]
    for cp in copies:
        cp.start()
    for cp in copies:
        cp.wait()
    gw = qkv.shape[2]
    feature = qkv.shape[1] // 3
    for k in range(2):
        for i in range(3):
            lo = (2 * i + k) * gw
            out_qkv[:, lo : lo + gw] = qkv[k, i * feature : (i + 1) * feature, :]
    tiles = fi.shape[1]
    for k in range(2):
        for j in range(tiles):
            for half in range(2):
                lo = ((k * tiles + j) * 2 + half) * gw
                out_fi[:, lo : lo + gw] = fi[k, j, half * feature : (half + 1) * feature, :]
    by_row = jnp.transpose(jnp.concatenate([small[...], jnp.zeros((128 - small.shape[0], 128), F32)], axis=0))
    gains[...] = by_row[0:3, 0:feature]
    shifts[...] = by_row[3:6, 0:feature]
    biases[...] = by_row[6:13, 0:feature]
    out_bias[...] = small[feature : feature + 1, 0 : out_bias.shape[1]]


def run_deliver(hidden_out, hidden_grad, o, cq, ckv, co, fi, f, e, qkv, small):
    S = jax.ShapeDtypeStruct
    feature, width = o.shape
    inner = fi.shape[0] * fi.shape[1] * width
    outs = (
        S((1, 1) + hidden_out.shape, BF), S((1, 1) + hidden_grad.shape, F32), S((1,) + e.shape, F32),
        S((3, feature), F32), S((3, feature), F32), S((7, feature), F32), S((feature, 3 * width), F32),
        S(o.shape, F32), S(cq.shape, F32), S(ckv.shape, F32), S(co.shape, F32), S((feature, inner), F32), S((1, f.shape[0]), F32), S(f.shape, F32),
    )
    hbm, vmem = pl.BlockSpec(memory_space=pltpu.HBM), pl.BlockSpec(memory_space=pltpu.VMEM)
    return pl.pallas_call(
        deliver_kernel, out_shape=outs, in_specs=[hbm] * 11, out_specs=(vmem,) * len(outs),
        scratch_shapes=[
            pltpu.VMEM(fi.shape, F32), pltpu.VMEM(qkv.shape, F32), pltpu.VMEM(small.shape, F32), pltpu.SemaphoreType.DMA((11,)),
        ],
        compiler_params=pltpu.CompilerParams(vmem_limit_bytes=62 << 20), name="deliver",
    )(hidden_out, hidden_grad, o, cq, ckv, co, fi, f, e, qkv, small)


def fused_body(
    hidden_in, encoded, out_grad, ln_gain, ln_bias, biases, self_qkv, self_out, cross_q,
    cross_kv, cross_out, ffn_in, ffn_bias, ffn_out,
):
    got = run_first(
        hidden_in[0, 0], out_grad[0, 0], encoded[0], ln_gain, ln_bias, biases, self_qkv, self_out, cross_q, cross_kv,
        cross_out, ffn_in, ffn_bias[None], ffn_out,
    )
    wide, (prm, a_span, o_wide, o_low, lse, x1, cn, qc, oc, cross_lse, en) = got[:9], got[9:20]
    out_part, out_send, dx2, row_sums = got[20:]
    grads = run_last(
        (out_part, out_send, dx2, oc, qc, cross_lse),
        (hidden_in[0, 0], prm, a_span, o_wide, o_low, lse, x1, cn, row_sums, en) + tuple(wide),
    )
    done = run_deliver(*grads)
    return done[:12] + (done[12][0], done[13])


def solution(mesh):
    fused = mesh.shape["head"] == NH and mesh.shape["blk"] == NZ * NX * NC
    return jax.shard_map(
        fused_body if fused else body,
        mesh=mesh,
        in_specs=(
            P(None, "blk", "head", None),
            P(None, ("head", "blk"), None),
            P(None, "blk", "head", None),
            P(None, ("head", "blk")),
            P(None, ("head", "blk")),
            P(None, ("head", "blk")),
            P(("head", "blk"), None),
            P(("head", "blk"), None),
            P(("head", "blk"), None),
            P(("head", "blk"), None),
            P(("head", "blk"), None),
            P(("head", "blk"), None),
            P(("head", "blk")),
            P(("head", "blk"), None),
        ),
        out_specs=(
            P(None, "blk", "head", None),
            P(None, "blk", "head", None),
            P(None, ("head", "blk"), None),
            P(None, ("head", "blk")),
            P(None, ("head", "blk")),
            P(None, ("head", "blk")),
            P(("head", "blk"), None),
            P(("head", "blk"), None),
            P(("head", "blk"), None),
            P(("head", "blk"), None),
            P(("head", "blk"), None),
            P(("head", "blk"), None),
            P(("head", "blk")),
            P(("head", "blk"), None),
        ),
        check_vma=False,
    )
```
